32 devices in a mesh: leaf: 2 (over y), node: 8 (over z, x), tensor: 2 (over core).
Axes of the slice: x: 2, y: 2, z: 4, core: 2. Of those that a mesh axis runs over, the one named last changes fastest.
Arguments:
- queries: bfloat16 [2048, 64, 128], P(('leaf', 'node'), 'tensor'), parts along dimension 0, may hold values from -6 to 6
- keys: bfloat16 [2048, 8, 128], P(('leaf', 'node'), 'tensor'), parts along dimension 0, may hold values from -6 to 6
- values: bfloat16 [2048, 8, 128], P(('leaf', 'node'), 'tensor'), parts along dimension 0, may hold values from -6 to 6
- grad_out: bfloat16 [2048, 64, 128], P(('leaf', 'node'), 'tensor'), parts along dimension 0, may hold values from -6 to 6
- parents: int32 [128], P('leaf'), parts along dimension 0, may hold values from -1 to 62, as said below
- lengths: int32 [128], P('leaf'), parts along dimension 0, may hold values from 8 to 16, as said below
Outputs:
- grad_queries: bfloat16 [2048, 64, 128], P(('leaf', 'node'), 'tensor'), parts along dimension 0
- grad_keys: float32 [2048, 8, 128], P(('leaf', 'node'), 'tensor'), parts along dimension 0
- grad_values: float32 [2048, 8, 128], P(('leaf', 'node'), 'tensor'), parts along dimension 0
The draws below stay inside these ranges and needn't reach their ends.
There are 2 independent parts, one for each index of `leaf`. The reference program is written for one: setup_inputs(seed, part) draws one part's arguments, and reference() takes and returns one part's arrays. A program takes and returns all parts, laid end to end along the dimension named above; each array names one. Nothing has to cross between parts.
Inputs may be any that keep to these rules, and one draw needn't show every extreme that they name: `parents`: node t has parent t - 1 unless t is the first of the 8 nodes of a device. The first node of device 0 is the root. The first node of any other device has as parent either node 7 or one of the first 2 nodes of a lower device; every ancestor of a node outside device 0 lies on device 0 or on one of the 7 devices below its own, and every such node descends from node 7. `lengths`: the nodes of device 0 are full.
All inputs are finite; a program needn't handle non-finite values.
Results may differ from the reference program's by a relative error of at most 0.0097.
Values may be sent and summed in bfloat16 or wider, within the bound.
No kernel may reach another device: no remote copies, remote signals or barrier semaphores. Data moves between devices by JAX's collectives and lax.ppermute only.
A program may use at most 64 MiB of HBM per device.

```python
import jax
import jax.numpy as jnp
from jax import lax

QUERY_HEADS = 64
KEY_VALUE_HEADS = 8
HEAD_WIDTH = 128
TILE = 16
TD = 8
CAP = 2
W = 7
TILES = 64
TOKEN_SLOTS = 1024
N_NODE = 8


def draw_queries(key, part):
    key = jax.random.fold_in(key, 11)
    tensor_shape = (TOKEN_SLOTS, QUERY_HEADS, HEAD_WIDTH)
    drawn = jax.random.truncated_normal(key, -6.0, 6.0, tensor_shape, jnp.float32)
    return drawn.astype(jnp.bfloat16)


def draw_keys(key, part):
    key = jax.random.fold_in(key, 13)
    tensor_shape = (TOKEN_SLOTS, KEY_VALUE_HEADS, HEAD_WIDTH)
    drawn = jax.random.truncated_normal(key, -6.0, 6.0, tensor_shape, jnp.float32)
    return drawn.astype(jnp.bfloat16)


def draw_parents(key, part):
    key = jax.random.fold_in(key, 21)
    device_count = TILES // TD
    devices = jnp.arange(device_count, dtype=jnp.int32)
    extra = (jax.random.randint(jax.random.fold_in(key, 1), (device_count,), 0, 3) == 0) & ((devices - 1) % (W + 1) >= 2)
    starts = (devices >= 1) & (((devices - 1) % (W + 1) == 0) | extra)
    group_start = lax.cummax(jnp.where(starts, devices, 0), axis=0)
    span_size = jnp.maximum(devices - group_start, 1)
    first_pick = jax.random.randint(jax.random.fold_in(key, 2), (device_count,), 0, 1 << 20) % span_size
    second_pick = jax.random.randint(jax.random.fold_in(key, 3), (device_count,), 0, 1 << 20) % span_size
    near = jax.random.randint(jax.random.fold_in(key, 5), (device_count,), 0, 2) > 0
    parent_device = jnp.where(near, devices - 1, group_start + jnp.maximum(first_pick, second_pick))
    attach = jax.random.randint(jax.random.fold_in(key, 4), (device_count,), 0, CAP)
    first_parent = jnp.where(starts, TD - 1, parent_device * TD + attach)
    first_parent = jnp.where(devices == 0, -1, first_parent)
    tile_index = jnp.arange(TILES, dtype=jnp.int32)
    return jnp.where(tile_index % TD > 0, tile_index - 1, first_parent[tile_index // TD]).astype(jnp.int32)


def draw_lengths(key, part):
    key = jax.random.fold_in(key, 31)
    drawn = jax.random.randint(key, (TILES,), TILE // 2, TILE + 1)
    return jnp.where(jnp.arange(TILES) < TD, TILE, drawn).astype(jnp.int32)


def steps_of(key, dims, split, smallest, largest):
    def one(axis_at, parts):
        heights = jax.random.uniform(jax.random.fold_in(jax.random.fold_in(key, 6), axis_at), (parts,), jnp.float32, smallest / len(split), largest / len(split))
        return jnp.repeat(jnp.exp(heights), dims[axis_at] // parts).reshape((-1,) + (1,) * (len(dims) - axis_at - 1))

    factor_of = one(*split[0])
    for cut in split[1:]:
        factor_of = factor_of * one(*cut)
    return factor_of


def gaussian(stream_key, dims, width, most, shards=(), held_as=jnp.bfloat16):
    result = width * jax.random.normal(stream_key, dims, jnp.float32)
    if shards:
        result = result * steps_of(stream_key, dims, shards, -0.22, 0.18)
    return jnp.clip(result, -most, most).astype(held_as)


def setup_inputs(seed: int = 0, part: int = 0) -> dict:
    seeds = jax.random.split(jax.random.key(seed), 7)
    own_keys = jax.random.split(jax.random.fold_in(seeds[6], part), 7)
    return {
        "queries": draw_queries(jax.random.fold_in(jax.random.fold_in(seeds[6], part), 71), part),
        "keys": draw_keys(jax.random.fold_in(jax.random.fold_in(seeds[6], part), 71), part),
        "values": gaussian(own_keys[2], (TOKEN_SLOTS, KEY_VALUE_HEADS, HEAD_WIDTH), 1.0, 6.0, ((0, 8), (1, 2))),
        "grad_out": gaussian(own_keys[3], (TOKEN_SLOTS, QUERY_HEADS, HEAD_WIDTH), 1.0, 6.0, ((0, 8), (1, 2))),
        "parents": draw_parents(jax.random.fold_in(jax.random.fold_in(seeds[6], part), 71), part),
        "lengths": draw_lengths(jax.random.fold_in(jax.random.fold_in(seeds[6], part), 71), part),
    }


def ancestry(parents):
    tile_count = parents.shape[0]
    reach_table = jax.nn.one_hot(parents, tile_count, dtype=jnp.float32)
    for _ in range(tile_count.bit_length()):
        reach_table = jnp.minimum(reach_table + jnp.dot(reach_table, reach_table, precision=lax.Precision.HIGHEST), 1.0)
    return reach_table


def reference(queries, keys, values, grad_out, parents, lengths):
    tokens_per_device = TD * TILE
    front_rows = CAP * TILE
    row_total = queries.shape[0]
    score_scale = HEAD_WIDTH ** -0.5
    heads_per_group = QUERY_HEADS // KEY_VALUE_HEADS
    reach_table = ancestry(parents)
    row_ids = jnp.arange(row_total, dtype=jnp.int32)
    live_all = (row_ids % TILE) < jnp.repeat(lengths, TILE, total_repeat_length=row_total)
    gradient_live = jnp.where(live_all[:, None, None], grad_out, jnp.zeros_like(grad_out))
    base_rows = jnp.arange(tokens_per_device, dtype=jnp.int32)
    head_rows = jnp.arange(front_rows, dtype=jnp.int32)

    def block_step(carried, current_device):
        grad_k_all, grad_v_all = carried
        row_pieces = [base_rows]
        ok_pieces = [(current_device >= 1) & ((base_rows >= front_rows) | (current_device > W))]
        for distance in range(1, W + 1):
            owner_dev = current_device - distance
            row_pieces.append(owner_dev * tokens_per_device + head_rows)
            ok_pieces.append(jnp.broadcast_to(owner_dev >= 0, (front_rows,)))
        row_pieces.append(current_device * tokens_per_device + base_rows)
        ok_pieces.append(jnp.ones((tokens_per_device,), bool))
        key_rows = jnp.clip(jnp.concatenate(row_pieces), 0, row_total - 1).astype(jnp.int32)
        segment_ok = jnp.concatenate(ok_pieces)
        query_rows = (current_device * tokens_per_device + base_rows).astype(jnp.int32)
        query_tile = query_rows // TILE
        key_tile = key_rows // TILE
        ancestor = jnp.take(jnp.take(reach_table, query_tile, axis=0), key_tile, axis=1) > 0.5
        same_tile = (query_tile[:, None] == key_tile[None, :]) & ((key_rows % TILE)[None, :] <= (query_rows % TILE)[:, None])
        visible = (ancestor | same_tile) & segment_ok[None, :] & live_all[key_rows][None, :]
        query_rows_block = lax.dynamic_slice_in_dim(queries, current_device * tokens_per_device, tokens_per_device, 0).astype(jnp.float32).reshape(tokens_per_device, KEY_VALUE_HEADS, heads_per_group, HEAD_WIDTH)
        gradient_block = lax.dynamic_slice_in_dim(gradient_live, current_device * tokens_per_device, tokens_per_device, 0).astype(jnp.float32).reshape(tokens_per_device, KEY_VALUE_HEADS, heads_per_group, HEAD_WIDTH)
        key_block = jnp.take(keys, key_rows, axis=0).astype(jnp.float32)
        value_block = jnp.take(values, key_rows, axis=0).astype(jnp.float32)
        scores = jnp.einsum("tgrd,kgd->grtk", query_rows_block, key_block) * score_scale
        scores = jnp.where(visible[None, None], scores, -jnp.inf)
        row_top = jnp.max(scores, axis=-1, keepdims=True)
        probs = jnp.exp(scores - row_top)
        probs = probs / jnp.sum(probs, axis=-1, keepdims=True)
        probs_low = lax.optimization_barrier(probs.astype(jnp.bfloat16)).astype(jnp.float32)
        grad_probs = jnp.einsum("tgrd,kgd->grtk", gradient_block, value_block)
        row_delta = jnp.sum(probs * grad_probs, axis=-1, keepdims=True)
        grad_scores = lax.optimization_barrier((probs * (grad_probs - row_delta) * score_scale).astype(jnp.bfloat16)).astype(jnp.float32)
        grad_q = jnp.einsum("grtk,kgd->tgrd", grad_scores, key_block).reshape(tokens_per_device, QUERY_HEADS, HEAD_WIDTH).astype(jnp.bfloat16)
        grad_k = jnp.einsum("grtk,tgrd->kgd", grad_scores, query_rows_block)
        grad_v = jnp.einsum("grtk,tgrd->kgd", probs_low, gradient_block)
        return (grad_k_all.at[key_rows].add(grad_k), grad_v_all.at[key_rows].add(grad_v)), grad_q

    start_offset = (jnp.zeros((row_total, KEY_VALUE_HEADS, HEAD_WIDTH), jnp.float32), jnp.zeros((row_total, KEY_VALUE_HEADS, HEAD_WIDTH), jnp.float32))
    finals, grad_q_blocks = lax.scan(block_step, start_offset, jnp.arange(N_NODE, dtype=jnp.int32))
    return grad_q_blocks.reshape(row_total, QUERY_HEADS, HEAD_WIDTH), finals[0], finals[1]
```

```python
import functools
import math

import jax
import jax.numpy as jnp
from jax import lax
from jax.experimental import pallas as pl
from jax.experimental.pallas import tpu as pltpu
from jax.sharding import PartitionSpec as P

TILE = 16
TD = 8
CAP = 2
W = 7
GROUPS_PER_STEP = 2
CHUNK = 32
MASKED = -1e30
BF16 = jnp.bfloat16
F32 = jnp.float32


def shifted(block, distance, size):
    route = [(i - distance, i) for i in range(size) if 0 <= i - distance < size]
    return lax.ppermute(block, "node", route)


def tree_strides(size):
    strides = []
    stride = 1
    while stride < size:
        strides.append(stride)
        stride *= 2
    return strides


def column_limits(device, window, parents, lengths):
    cursor = parents[device * TD]
    need = [jnp.int32(0)] * (window + 1)
    for _ in range(W):
        owner = jnp.where(cursor < 0, -1, lax.div(jnp.maximum(cursor, 0), TD))
        distance = device - owner
        active = (owner >= 1) & (distance >= 1) & (distance <= W)
        depth = lax.rem(jnp.maximum(cursor, 0), TD) + 1
        for k in range(1, window + 1):
            need[k] = jnp.where(active & (distance == k), depth, need[k])
        cursor = jnp.where(active, parents[jnp.maximum(owner, 0) * TD], cursor)
    limits = [jnp.where(device >= 1, lengths[t], 0) for t in range(TD)]
    for k in range(1, window + 1):
        owner = device - k
        for c in range(CAP):
            seen = (owner >= 1) & (c < need[k])
            limits.append(jnp.where(seen, lengths[jnp.maximum(owner, 0) * TD + c], 0))
    limits += [lengths[device * TD + t] for t in range(TD)]
    return limits


def attention_kernel(rounds, window, heads_kv, scale, *refs):
    parents, lengths = refs[:2]
    prompt = refs[2 : 2 + rounds]
    behind = refs[2 + rounds : 2 + rounds + window]
    keys, values, q_ref, g_ref = refs[2 + rounds + window : 6 + rounds + window]
    dq_ref, dprompt_ref, dbehind_ref, dk_ref, dv_ref = refs[6 + rounds + window : 11 + rounds + window]
    kh, vh, bias, acc_k, acc_v, wide = refs[11 + rounds + window :]
    tokens = TD * TILE
    front = CAP * TILE
    before = tokens + window * front
    step = pl.program_id(0)
    device = lax.axis_index("node")

    @pl.when(step == 0)
    def _():
        def split(block, heads_ref, start, count):
            wide[: count * heads_kv] = block
            for h in range(heads_kv):
                heads_ref[h, start : start + count] = wide[pl.ds(h, count, stride=heads_kv), :].astype(BF16)

        for side, heads_ref, own in ((0, kh, keys), (1, vh, values)):
            block = prompt[0][side].astype(F32)
            for r in range(1, rounds):
                block = block + prompt[r][side].astype(F32)
            split(block, heads_ref, 0, tokens)
            for k in range(window):
                split(behind[k][side].astype(F32), heads_ref, tokens + k * front, front)
            split(own[...].astype(F32), heads_ref, before, tokens)
        place = lax.broadcasted_iota(jnp.int32, (TILE, 128), 0)
        for t, limit in enumerate(column_limits(device, window, parents, lengths)):
            bias[t * TILE : (t + 1) * TILE] = jnp.where(place < limit, 0.0, MASKED)

    columns = CHUNK * 8
    column_token = lax.broadcasted_iota(jnp.int32, (CHUNK, columns), 1) // 8
    causal = jnp.where(lax.broadcasted_iota(jnp.int32, (CHUNK, columns), 0) <= column_token, 0.0, MASKED)
    lane_place = lax.broadcasted_iota(jnp.int32, (1, 128), 1) // 8

    for c in reversed(range(tokens // CHUNK)):
        rows = before + (c + 1) * CHUNK
        live = jnp.concatenate(
            [
                jnp.where(lane_place < lengths[device * TD + c * (CHUNK // TILE) + t], 1.0, 0.0)
                for t in range(CHUNK // TILE)
            ],
            axis=1,
        )
        q_all = q_ref[c * CHUNK : (c + 1) * CHUNK].astype(F32)
        g_all = g_ref[c * CHUNK : (c + 1) * CHUNK].astype(F32)
        dq_parts = []
        for part in range(GROUPS_PER_STEP):
            head = step * GROUPS_PER_STEP + part
            q = q_all[:, part * 8 : (part + 1) * 8].reshape(columns, 128).astype(BF16)
            g = g_all[:, part * 8 : (part + 1) * 8].reshape(columns, 128).astype(BF16)
            k = kh[head, :rows]
            v = vh[head, :rows]
            s = lax.dot_general(k, q, (((1,), (1,)), ((), ())), preferred_element_type=F32)
            column_bias = bias[:rows]
            s = s + jnp.concatenate([column_bias] * (columns // 128), axis=1)
            s = jnp.concatenate([s[: rows - CHUNK], s[rows - CHUNK :] + causal], axis=0)
            top = jnp.max(s, axis=0, keepdims=True)
            e = jnp.exp2((s - top) * (scale * math.log2(math.e)))
            total = jnp.sum(e, axis=0, keepdims=True)
            dp = lax.dot_general(v, g, (((1,), (1,)), ((), ())), preferred_element_type=F32)
            weight = live / total
            p = e * weight
            delta = jnp.sum(p * dp, axis=0, keepdims=True)
            ds = (p * (dp - delta) * scale).astype(BF16)
            p = p.astype(BF16)
            dk = jnp.dot(ds, q, preferred_element_type=F32)
            dv = jnp.dot(p, g, preferred_element_type=F32)
            if c == tokens // CHUNK - 1:
                acc_k[head, :rows] = dk
                acc_v[head, :rows] = dv
            else:
                acc_k[head, :rows] += dk
                acc_v[head, :rows] += dv
            dq = lax.dot_general(k, ds, (((0,), (0,)), ((), ())), preferred_element_type=F32)
            dq_parts.append(dq.T.reshape(CHUNK, 8, 128))
        dq_ref[c * CHUNK : (c + 1) * CHUNK] = jnp.concatenate(dq_parts, axis=1).astype(BF16)

    @pl.when(step == pl.num_programs(0) - 1)
    def _():
        def join(acc, start, count):
            for h in range(heads_kv):
                wide[pl.ds(h, count, stride=heads_kv), :] = acc[h, start : start + count]
            return wide[: count * heads_kv]

        for side, acc, own in ((0, acc_k, dk_ref), (1, acc_v, dv_ref)):
            dprompt_ref[side] = join(acc, 0, tokens).astype(BF16)
            for k in range(window):
                dbehind_ref[k, side] = join(acc, tokens + k * front, front).astype(BF16)
            own[...] = join(acc, before, tokens)


def attention(prompt, behind, keys, values, queries, grad_out, parents, lengths, heads_kv):
    tokens, heads_q, head_size = queries.shape
    window = len(behind)
    rounds = len(prompt)
    front = CAP * TILE
    all_rows = 2 * tokens + window * front
    step_heads = 8 * GROUPS_PER_STEP
    smem = pl.BlockSpec(memory_space=pltpu.SMEM)

    def whole(shape):
        return pl.BlockSpec(shape, lambda i: (0,) * len(shape))

    by_heads = pl.BlockSpec((tokens, step_heads, head_size), lambda i: (0, i, 0))
    products = 5 * 2 * tokens * heads_q * head_size * all_rows
    return pl.pallas_call(
        functools.partial(attention_kernel, rounds, window, heads_kv, head_size**-0.5),
        grid=(heads_q // step_heads,),
        in_specs=[smem, smem]
        + [whole(a.shape) for a in (*prompt, *behind, keys, values)]
        + [by_heads, by_heads],
        out_specs=[
            by_heads,
            whole((2, tokens * heads_kv, head_size)),
            whole((window, 2, front * heads_kv, head_size)),
            whole((tokens * heads_kv, head_size)),
            whole((tokens * heads_kv, head_size)),
        ],
        out_shape=[
            jax.ShapeDtypeStruct(queries.shape, BF16),
            jax.ShapeDtypeStruct((2, tokens * heads_kv, head_size), BF16),
            jax.ShapeDtypeStruct((window, 2, front * heads_kv, head_size), BF16),
            jax.ShapeDtypeStruct((tokens * heads_kv, head_size), F32),
            jax.ShapeDtypeStruct((tokens * heads_kv, head_size), F32),
        ],
        scratch_shapes=[
            pltpu.VMEM((heads_kv, all_rows, head_size), BF16),
            pltpu.VMEM((heads_kv, all_rows, head_size), BF16),
            pltpu.VMEM((all_rows, 128), F32),
            pltpu.VMEM((heads_kv, all_rows, head_size), F32),
            pltpu.VMEM((heads_kv, all_rows, head_size), F32),
            pltpu.VMEM((tokens * heads_kv, head_size), F32),
        ],
        compiler_params=pltpu.CompilerParams(vmem_limit_bytes=40 * 1024 * 1024),
        cost_estimate=pl.CostEstimate(
            flops=products, bytes_accessed=4 * 1024 * 1024, transcendentals=tokens * heads_q * all_rows
        ),
        name="tree_attention_backward",
    )(parents, lengths, *prompt, *behind, keys, values, queries, grad_out)


def per_device(size, queries, keys, values, grad_out, parents, lengths):
    tokens, heads_kv, head_size = keys.shape
    rows = tokens * heads_kv
    front = CAP * TILE * heads_kv
    window = max(1, min(W, size - 2))
    device = lax.axis_index("node")
    keys = keys.reshape(rows, head_size)
    values = values.reshape(rows, head_size)
    pair = jnp.stack([keys, values])
    strides = tree_strides(size)

    prompt = []
    held = pair
    for stride in reversed(strides):
        route = [(i, i + stride) for i in range(0, size, 2 * stride) if i + stride < size]
        arrived = lax.ppermute(held, "node", route)
        prompt.append(arrived)
        if stride > 1:
            held = jnp.where(lax.rem(device, 2 * stride) == 0, held, arrived)
    head = pair[:, :front]
    behind = [shifted(head, k, size) for k in range(1, window + 1)]

    grad_queries, dprompt, dbehind, dk, dv = attention(
        prompt, behind, keys, values, queries, grad_out, parents, lengths, heads_kv
    )

    total = dprompt
    for stride in strides:
        route = [(i + stride, i) for i in range(0, size, 2 * stride) if i + stride < size]
        arrived = lax.ppermute(total, "node", route)
        total = (total.astype(F32) + arrived.astype(F32)).astype(BF16 if stride < strides[-1] else F32)
    back = sum(shifted(dbehind[k - 1], -k, size).astype(F32) for k in range(1, window + 1))
    total = jnp.where(device == 0, total, 0.0)
    own = []
    for side, local in ((0, dk), (1, dv)):
        whole = local + total[side]
        own.append(whole.at[:front].add(back[side]).reshape(tokens, heads_kv, head_size))
    return grad_queries, own[0], own[1]


def solution(mesh):
    by_token = P(("leaf", "node"), "tensor", None)
    return jax.shard_map(
        functools.partial(per_device, mesh.shape["node"]),
        mesh=mesh,
        in_specs=(by_token, by_token, by_token, by_token, P("leaf"), P("leaf")),
        out_specs=(by_token, by_token, by_token),
        check_vma=False,
    )
```

```python
import functools
import math

import jax
import jax.numpy as jnp
from jax import lax
from jax.experimental import pallas as pl
from jax.experimental.pallas import tpu as pltpu
from jax.sharding import PartitionSpec as P

TILE = 16
TD = 8
CAP = 2
W = 7
GROUPS_PER_STEP = 2
CHUNK = 32
MASKED = -1e30
BF16 = jnp.bfloat16
F32 = jnp.float32


def shifted(block, distance, size):
    route = [(i - distance, i) for i in range(size) if 0 <= i - distance < size]
    return lax.ppermute(block, "node", route)


def permuted(block, route):
    return lax.ppermute(block, "node", route)


def after(arrays, *earlier):
    return lax.optimization_barrier((*arrays, *earlier))[: len(arrays)]


def column_limits(device, window, parents, lengths):
    cursor = parents[device * TD]
    need = [jnp.int32(0)] * (window + 1)
    for _ in range(W):
        owner = jnp.where(cursor < 0, -1, lax.div(jnp.maximum(cursor, 0), TD))
        distance = device - owner
        active = (owner >= 1) & (distance >= 1) & (distance <= W)
        depth = lax.rem(jnp.maximum(cursor, 0), TD) + 1
        for k in range(1, window + 1):
            need[k] = jnp.where(active & (distance == k), depth, need[k])
        cursor = jnp.where(active, parents[jnp.maximum(owner, 0) * TD], cursor)
    limits = [jnp.where(device >= 1, lengths[t], 0) for t in range(TD)]
    for k in range(1, window + 1):
        owner = device - k
        for c in range(CAP):
            seen = (owner >= 1) & (c < need[k])
            limits.append(jnp.where(seen, lengths[jnp.maximum(owner, 0) * TD + c], 0))
    limits += [lengths[device * TD + t] for t in range(TD)]
    return limits


def attention_kernel(rounds, window, heads_kv, scale, *refs):
    parents, lengths = refs[:2]
    prompt = refs[2 : 2 + rounds]
    behind = refs[2 + rounds : 2 + rounds + window]
    keys, values, q_ref, g_ref = refs[2 + rounds + window : 6 + rounds + window]
    dq_ref, dprompt_ref, dbehind_ref, dk_ref, dv_ref = refs[6 + rounds + window : 11 + rounds + window]
    kh, vh, bias, acc_k, acc_v, wide = refs[11 + rounds + window :]
    tokens = TD * TILE
    front = CAP * TILE
    before = tokens + window * front
    step = pl.program_id(0)
    device = lax.axis_index("node")

    @pl.when(step == 0)
    def _():
        def split(block, heads_ref, start, count):
            wide[: count * heads_kv] = block
            for h in range(heads_kv):
                heads_ref[h, start : start + count] = wide[pl.ds(h, count, stride=heads_kv), :].astype(BF16)

        for side, heads_ref, own in ((0, kh, keys), (1, vh, values)):
            block = prompt[0][side].astype(F32)
            for r in range(1, rounds):
                block = block + prompt[r][side].astype(F32)
            split(block, heads_ref, 0, tokens)
            for k in range(window):
                split(behind[k][side].astype(F32), heads_ref, tokens + k * front, front)
            split(own[...].astype(F32), heads_ref, before, tokens)
        place = lax.broadcasted_iota(jnp.int32, (TILE, 128), 0)
        for t, limit in enumerate(column_limits(device, window, parents, lengths)):
            bias[t * TILE : (t + 1) * TILE] = jnp.where(place < limit, 0.0, MASKED)

    columns = CHUNK * 8
    column_token = lax.broadcasted_iota(jnp.int32, (CHUNK, columns), 1) // 8
    causal = jnp.where(lax.broadcasted_iota(jnp.int32, (CHUNK, columns), 0) <= column_token, 0.0, MASKED)
    lane_place = lax.broadcasted_iota(jnp.int32, (1, 128), 1) // 8

    for c in reversed(range(tokens // CHUNK)):
        rows = before + (c + 1) * CHUNK
        live = jnp.concatenate(
            [
                jnp.where(lane_place < lengths[device * TD + c * (CHUNK // TILE) + t], 1.0, 0.0)
                for t in range(CHUNK // TILE)
            ],
            axis=1,
        )
        q_all = q_ref[c * CHUNK : (c + 1) * CHUNK].astype(F32)
        g_all = g_ref[c * CHUNK : (c + 1) * CHUNK].astype(F32)
        dq_parts = []
        for part in range(GROUPS_PER_STEP):
            head = step * GROUPS_PER_STEP + part
            q = q_all[:, part * 8 : (part + 1) * 8].reshape(columns, 128).astype(BF16)
            g = g_all[:, part * 8 : (part + 1) * 8].reshape(columns, 128).astype(BF16)
            k = kh[head, :rows]
            v = vh[head, :rows]
            s = lax.dot_general(k, q, (((1,), (1,)), ((), ())), preferred_element_type=F32)
            column_bias = bias[:rows]
            s = s + jnp.concatenate([column_bias] * (columns // 128), axis=1)
            s = jnp.concatenate([s[: rows - CHUNK], s[rows - CHUNK :] + causal], axis=0)
            top = jnp.max(s, axis=0, keepdims=True)
            e = jnp.exp2((s - top) * (scale * math.log2(math.e)))
            total = jnp.sum(e, axis=0, keepdims=True)
            dp = lax.dot_general(v, g, (((1,), (1,)), ((), ())), preferred_element_type=F32)
            weight = live / total
            p = e * weight
            delta = jnp.sum(p * dp, axis=0, keepdims=True)
            ds = (p * (dp - delta) * scale).astype(BF16)
            p = p.astype(BF16)
            dk = jnp.dot(ds, q, preferred_element_type=F32)
            dv = jnp.dot(p, g, preferred_element_type=F32)
            if c == tokens // CHUNK - 1:
                acc_k[head, :rows] = dk
                acc_v[head, :rows] = dv
            else:
                acc_k[head, :rows] += dk
                acc_v[head, :rows] += dv
            dq = lax.dot_general(k, ds, (((0,), (0,)), ((), ())), preferred_element_type=F32)
            dq_parts.append(dq.T.reshape(CHUNK, 8, 128))
        dq_ref[c * CHUNK : (c + 1) * CHUNK] = jnp.concatenate(dq_parts, axis=1).astype(BF16)

    @pl.when(step == pl.num_programs(0) - 1)
    def _():
        def join(acc, start, count):
            for h in range(heads_kv):
                wide[pl.ds(h, count, stride=heads_kv), :] = acc[h, start : start + count]
            return wide[: count * heads_kv]

        for side, acc, own in ((0, acc_k, dk_ref), (1, acc_v, dv_ref)):
            dprompt_ref[side] = join(acc, 0, tokens).astype(BF16)
            for k in range(window):
                dbehind_ref[k, side] = join(acc, tokens + k * front, front).astype(BF16)
            own[...] = join(acc, before, tokens)


def attention(prompt, behind, keys, values, queries, grad_out, parents, lengths, heads_kv):
    tokens, heads_q, head_size = queries.shape
    window = len(behind)
    rounds = len(prompt)
    front = CAP * TILE
    all_rows = 2 * tokens + window * front
    step_heads = 8 * GROUPS_PER_STEP
    smem = pl.BlockSpec(memory_space=pltpu.SMEM)

    def whole(shape):
        return pl.BlockSpec(shape, lambda i: (0,) * len(shape))

    by_heads = pl.BlockSpec((tokens, step_heads, head_size), lambda i: (0, i, 0))
    products = 5 * 2 * tokens * heads_q * head_size * all_rows
    return pl.pallas_call(
        functools.partial(attention_kernel, rounds, window, heads_kv, head_size**-0.5),
        grid=(heads_q // step_heads,),
        in_specs=[smem, smem]
        + [whole(a.shape) for a in (*prompt, *behind, keys, values)]
        + [by_heads, by_heads],
        out_specs=[
            by_heads,
            whole((2, tokens * heads_kv, head_size)),
            whole((window, 2, front * heads_kv, head_size)),
            whole((tokens * heads_kv, head_size)),
            whole((tokens * heads_kv, head_size)),
        ],
        out_shape=[
            jax.ShapeDtypeStruct(queries.shape, BF16),
            jax.ShapeDtypeStruct((2, tokens * heads_kv, head_size), BF16),
            jax.ShapeDtypeStruct((window, 2, front * heads_kv, head_size), BF16),
            jax.ShapeDtypeStruct((tokens * heads_kv, head_size), F32),
            jax.ShapeDtypeStruct((tokens * heads_kv, head_size), F32),
        ],
        scratch_shapes=[
            pltpu.VMEM((heads_kv, all_rows, head_size), BF16),
            pltpu.VMEM((heads_kv, all_rows, head_size), BF16),
            pltpu.VMEM((all_rows, 128), F32),
            pltpu.VMEM((heads_kv, all_rows, head_size), F32),
            pltpu.VMEM((heads_kv, all_rows, head_size), F32),
            pltpu.VMEM((tokens * heads_kv, head_size), F32),
        ],
        compiler_params=pltpu.CompilerParams(vmem_limit_bytes=40 * 1024 * 1024),
        cost_estimate=pl.CostEstimate(
            flops=products, bytes_accessed=4 * 1024 * 1024, transcendentals=tokens * heads_q * all_rows
        ),
        name="tree_attention_backward",
    )(parents, lengths, *prompt, *behind, keys, values, queries, grad_out)


def per_device(size, queries, keys, values, grad_out, parents, lengths):
    tokens, heads_kv, head_size = keys.shape
    rows = tokens * heads_kv
    front = CAP * TILE * heads_kv
    window = max(1, min(W, size - 2))
    device = lax.axis_index("node")
    keys = keys.reshape(rows, head_size)
    values = values.reshape(rows, head_size)
    pair = jnp.stack([keys, values])
    half = size // 2
    strides = []
    stride = half // 2
    while stride > 1:
        strides.append(stride)
        stride //= 2
    head = pair[:, :front]
    behind = {}

    def fetch(count):
        for k in range(len(behind) + 1, min(len(behind) + count, window) + 1):
            behind[k] = shifted(head, k, size)
        return list(behind.values())

    keys_1 = permuted(keys, [(0, half)])
    values_1 = permuted(values, [(0, 1)])
    keys_1, values_1 = after((keys_1, values_1), *fetch(2))
    keys_2 = permuted(jnp.where(device == 0, keys, keys_1), [(0, 1), (half, half + 1)])
    values_2 = permuted(jnp.where(device == 0, values, values_1), [(0, half), (1, half + 1)])
    keys_2, values_2 = after((keys_2, values_2), *fetch(2))
    held = jnp.stack(
        [
            jnp.where(device == 0, keys, jnp.where(device == half, keys_1, keys_2)),
            jnp.where(device == 0, values, jnp.where(device == 1, values_1, values_2)),
        ]
    )
    prompt = [held]
    for stride in strides:
        route = [(i + j, i + j + stride) for i in range(0, size, 2 * stride) for j in (0, 1)]
        arrived = permuted(held, route)
        prompt.append(arrived)
        if stride > 2:
            held = held + arrived
    fetch(window)

    grad_queries, dprompt, dbehind, dk, dv = attention(
        prompt, list(behind.values()), keys, values, queries, grad_out, parents, lengths, heads_kv
    )

    back = {}

    def send_back(count):
        for k in range(len(back) + 1, min(len(back) + count, window) + 1):
            back[k] = shifted(dbehind[k - 1], -k, size)
        return list(back.values())

    def added(total, arrived):
        return (total.astype(F32) + arrived.astype(F32)).astype(BF16)

    total = dprompt
    for stride in reversed(strides):
        route = [(i + j + stride, i + j) for i in range(0, size, 2 * stride) for j in (0, 1)]
        total = added(total, permuted(total, route))
    total, = after((total,), *send_back(2))
    total_k, total_v = total[0], total[1]
    moved_k = permuted(total_k, [(1, 0), (half + 1, half)])
    moved_v = permuted(total_v, [(half, 0), (half + 1, 1)])
    moved_k, moved_v = after((moved_k, moved_v), *send_back(2))
    total_k = added(total_k, moved_k)
    total_v = added(total_v, moved_v)
    last_k = permuted(total_k, [(half, 0)])
    last_v = permuted(total_v, [(1, 0)])
    send_back(window)
    own = []
    for side, local, total, last in ((0, dk, total_k, last_k), (1, dv, total_v, last_v)):
        whole = local + jnp.where(device == 0, total.astype(F32) + last.astype(F32), 0.0)
        received = sum(block[side].astype(F32) for block in back.values())
        own.append(whole.at[:front].add(received).reshape(tokens, heads_kv, head_size))
    return grad_queries, own[0], own[1]


def solution(mesh):
    by_token = P(("leaf", "node"), "tensor", None)
    return jax.shard_map(
        functools.partial(per_device, mesh.shape["node"]),
        mesh=mesh,
        in_specs=(by_token, by_token, by_token, by_token, P("leaf"), P("leaf")),
        out_specs=(by_token, by_token, by_token),
        check_vma=False,
    )
```

```python
import functools
import math

import jax
import jax.numpy as jnp
from jax import lax
from jax.experimental import pallas as pl
from jax.experimental.pallas import tpu as pltpu
from jax.sharding import PartitionSpec as P

TILE = 16
TD = 8
CAP = 2
W = 7
GROUPS_PER_STEP = 2
CHUNK = 32
MASKED = -1e30
BF16 = jnp.bfloat16
F32 = jnp.float32


def permuted(block, route):
    return lax.ppermute(block, "node", route)


def column_limits(device, window, parents, lengths):
    cursor = parents[device * TD]
    need = [jnp.int32(0)] * (window + 1)
    for _ in range(W):
        owner = jnp.where(cursor < 0, -1, lax.div(jnp.maximum(cursor, 0), TD))
        distance = device - owner
        active = (owner >= 1) & (distance >= 1) & (distance <= W)
        depth = lax.rem(jnp.maximum(cursor, 0), TD) + 1
        for k in range(1, window + 1):
            need[k] = jnp.where(active & (distance == k), depth, need[k])
        cursor = jnp.where(active, parents[jnp.maximum(owner, 0) * TD], cursor)
    limits = [jnp.where(device >= 1, lengths[t], 0) for t in range(TD)]
    for k in range(1, window + 1):
        owner = device - k
        for c in range(CAP):
            seen = (owner >= 1) & (c < need[k])
            limits.append(jnp.where(seen, lengths[jnp.maximum(owner, 0) * TD + c], 0))
    limits += [lengths[device * TD + t] for t in range(TD)]
    return limits


def attention_kernel(slots, heads_kv, scale, *refs):
    parents, lengths, prompt_k, prompt_v, keys, values, q_ref, g_ref = refs[:8]
    blocks = refs[8 : 8 + 1 + max(source for source, _ in slots)]
    dq_ref, send_ref, keep_ref, dk_ref, dv_ref = refs[8 + len(blocks) : 13 + len(blocks)]
    kh, vh, bias, acc_k, acc_v, wide = refs[13 + len(blocks) :]
    window = len(slots)
    tokens = TD * TILE
    front = CAP * TILE
    before = tokens + window * front
    step = pl.program_id(0)
    device = lax.axis_index("node")

    @pl.when(step == 0)
    def _():
        def split(block, heads_ref, start, count):
            wide[: count * heads_kv] = block
            for h in range(heads_kv):
                heads_ref[h, start : start + count] = wide[pl.ds(h, count, stride=heads_kv), :].astype(BF16)

        for side, heads_ref, prompt, own in ((0, kh, prompt_k, keys), (1, vh, prompt_v, values)):
            split(prompt[...].astype(F32), heads_ref, 0, tokens)
            for k, (source, start) in enumerate(slots):
                start += side * front * heads_kv
                block = blocks[source][start : start + front * heads_kv]
                split(block.astype(F32), heads_ref, tokens + k * front, front)
            split(own[...].astype(F32), heads_ref, before, tokens)
        place = lax.broadcasted_iota(jnp.int32, (TILE, 128), 0)
        for t, limit in enumerate(column_limits(device, window, parents, lengths)):
            bias[t * TILE : (t + 1) * TILE] = jnp.where(place < limit, 0.0, MASKED)

    columns = CHUNK * 8
    column_token = lax.broadcasted_iota(jnp.int32, (CHUNK, columns), 1) // 8
    causal = jnp.where(lax.broadcasted_iota(jnp.int32, (CHUNK, columns), 0) <= column_token, 0.0, MASKED)
    lane_place = lax.broadcasted_iota(jnp.int32, (1, 128), 1) // 8

    for c in reversed(range(tokens // CHUNK)):
        rows = before + (c + 1) * CHUNK
        live = jnp.concatenate(
            [
                jnp.where(lane_place < lengths[device * TD + c * (CHUNK // TILE) + t], 1.0, 0.0)
                for t in range(CHUNK // TILE)
            ],
            axis=1,
        )
        q_all = q_ref[c * CHUNK : (c + 1) * CHUNK].astype(F32)
        g_all = g_ref[c * CHUNK : (c + 1) * CHUNK].astype(F32)
        dq_parts = []
        for part in range(GROUPS_PER_STEP):
            head = step * GROUPS_PER_STEP + part
            q = q_all[:, part * 8 : (part + 1) * 8].reshape(columns, 128).astype(BF16)
            g = g_all[:, part * 8 : (part + 1) * 8].reshape(columns, 128).astype(BF16)
            k = kh[head, :rows]
            v = vh[head, :rows]
            s = lax.dot_general(k, q, (((1,), (1,)), ((), ())), preferred_element_type=F32)
            column_bias = bias[:rows]
            s = s + jnp.concatenate([column_bias] * (columns // 128), axis=1)
            s = jnp.concatenate([s[: rows - CHUNK], s[rows - CHUNK :] + causal], axis=0)
            top = jnp.max(s, axis=0, keepdims=True)
            e = jnp.exp2((s - top) * (scale * math.log2(math.e)))
            total = jnp.sum(e, axis=0, keepdims=True)
            dp = lax.dot_general(v, g, (((1,), (1,)), ((), ())), preferred_element_type=F32)
            weight = live / total
            p = e * weight
            delta = jnp.sum(p * dp, axis=0, keepdims=True)
            ds = (p * (dp - delta) * scale).astype(BF16)
            p = p.astype(BF16)
            dk = jnp.dot(ds, q, preferred_element_type=F32)
            dv = jnp.dot(p, g, preferred_element_type=F32)
            if c == tokens // CHUNK - 1:
                acc_k[head, :rows] = dk
                acc_v[head, :rows] = dv
            else:
                acc_k[head, :rows] += dk
                acc_v[head, :rows] += dv
            dq = lax.dot_general(k, ds, (((0,), (0,)), ((), ())), preferred_element_type=F32)
            dq_parts.append(dq.T.reshape(CHUNK, 8, 128))
        dq_ref[c * CHUNK : (c + 1) * CHUNK] = jnp.concatenate(dq_parts, axis=1).astype(BF16)

    @pl.when(step == pl.num_programs(0) - 1)
    def _():
        def join(acc, start, count):
            for h in range(heads_kv):
                wide[pl.ds(h, count, stride=heads_kv), :] = acc[h, start : start + count]
            return wide[: count * heads_kv]

        rows = tokens * heads_kv
        rows_front = front * heads_kv
        even = lax.rem(device, 2) == 0
        for side, acc, own in ((0, acc_k, dk_ref), (1, acc_v, dv_ref)):
            dprompt = join(acc, 0, tokens).astype(BF16)
            kept = even if side == 0 else jnp.logical_not(even)

            @pl.when(kept)
            def _():
                keep_ref[:rows] = dprompt

            @pl.when(jnp.logical_not(kept))
            def _():
                send_ref[:rows] = dprompt

            for k in range(window):
                block = join(acc, tokens + k * front, front).astype(BF16)
                start = rows + (k // 2 * 2 + side) * rows_front
                (send_ref, keep_ref)[k % 2][start : start + rows_front] = block
            own[...] = join(acc, before, tokens)


def attention(prompt_k, prompt_v, slots, blocks, keys, values, queries, grad_out, parents, lengths):
    tokens, heads_q, head_size = queries.shape
    window = len(slots)
    rows = keys.shape[0]
    heads_kv = rows // tokens
    front = CAP * TILE
    all_rows = 2 * tokens + window * front
    step_heads = 8 * GROUPS_PER_STEP
    smem = pl.BlockSpec(memory_space=pltpu.SMEM)
    sent = rows + (window + 1) // 2 * 2 * front * heads_kv
    kept = rows + window // 2 * 2 * front * heads_kv

    def whole(shape):
        return pl.BlockSpec(shape, lambda i: (0,) * len(shape))

    by_heads = pl.BlockSpec((tokens, step_heads, head_size), lambda i: (0, i, 0))
    products = 5 * 2 * tokens * heads_q * head_size * all_rows
    return pl.pallas_call(
        functools.partial(attention_kernel, slots, heads_kv, head_size**-0.5),
        grid=(heads_q // step_heads,),
        in_specs=[smem, smem]
        + [whole(a.shape) for a in (prompt_k, prompt_v, keys, values)]
        + [by_heads, by_heads]
        + [whole(a.shape) for a in blocks],
        out_specs=[
            by_heads,
            whole((sent, head_size)),
            whole((kept, head_size)),
            whole((rows, head_size)),
            whole((rows, head_size)),
        ],
        out_shape=[
            jax.ShapeDtypeStruct(queries.shape, BF16),
            jax.ShapeDtypeStruct((sent, head_size), BF16),
            jax.ShapeDtypeStruct((kept, head_size), BF16),
            jax.ShapeDtypeStruct((rows, head_size), F32),
            jax.ShapeDtypeStruct((rows, head_size), F32),
        ],
        scratch_shapes=[
            pltpu.VMEM((heads_kv, all_rows, head_size), BF16),
            pltpu.VMEM((heads_kv, all_rows, head_size), BF16),
            pltpu.VMEM((all_rows, 128), F32),
            pltpu.VMEM((heads_kv, all_rows, head_size), F32),
            pltpu.VMEM((heads_kv, all_rows, head_size), F32),
            pltpu.VMEM((rows, head_size), F32),
        ],
        compiler_params=pltpu.CompilerParams(vmem_limit_bytes=40 * 1024 * 1024),
        cost_estimate=pl.CostEstimate(
            flops=products, bytes_accessed=4 * 1024 * 1024, transcendentals=tokens * heads_q * all_rows
        ),
        name="tree_attention_backward",
    )(parents, lengths, prompt_k, prompt_v, keys, values, queries, grad_out, *blocks)


def shift_route(distance, size):
    return [(i, i + distance) for i in range(size - distance)]


def back(route):
    return [(j, i) for i, j in route]


def added(*blocks):
    total = blocks[0].astype(F32)
    for block in blocks[1:]:
        total = total + block.astype(F32)
    return total


def per_device(size, queries, keys, values, grad_out, parents, lengths):
    tokens, heads_kv, head_size = keys.shape
    rows = tokens * heads_kv
    unit = 2 * CAP * TILE * heads_kv
    one = CAP * TILE * heads_kv
    near = size <= W + 1
    window = min(W, size - 2) if near else W
    device = lax.axis_index("node")
    even = lax.rem(device, 2) == 0
    keys = keys.reshape(rows, head_size)
    values = values.reshape(rows, head_size)
    strides = [2**i for i in range(2, size.bit_length()) if 2**i < size]
    neighbours = [(i, i ^ 1) for i in range(size)]
    far_route = shift_route(4, size)[1:]
    near_route = shift_route(2, size)

    def prompt_route(stride):
        return [(i + j, i + j + stride) for i in range(0, size, 2 * stride) for j in (0, 1)]

    head = jnp.concatenate([keys[:one], values[:one]])
    held = jnp.where(device == 0, keys, permuted(values, [(0, 1)]))
    far = permuted(head, far_route)
    for stride in reversed(strides):
        held = added(held, permuted(held, prompt_route(stride))).astype(BF16)
    second = permuted(jnp.concatenate([held, head, far]), near_route)
    held = jnp.where(lax.rem(device, 4) < 2, held, second[:rows])
    two, four, six = second[rows : rows + unit], far, second[rows + unit :]
    if near:
        even_slots = jnp.where(even, jnp.concatenate([head, two, four]), jnp.concatenate([two, four, six]))
        third = permuted(jnp.concatenate([held, even_slots]), neighbours)
        other, start = third[:rows], rows
    else:
        third = permuted(jnp.concatenate([head, two, four, six]), shift_route(1, size))
        other, start = permuted(held, neighbours), 0
    slots = [(0, start), (1, rows), (0, start + unit), (2, 0), (0, start + 2 * unit), (1, rows + unit), (0, start + 3 * unit)]
    slots = slots[:window]

    grad_queries, send, keep, dk, dv = attention(
        jnp.where(even, held, other), jnp.where(even, other, held), slots, (third, second, far),
        keys, values, queries, grad_out, parents, lengths,
    )

    def slot(array, index):
        return array[rows + index * unit : rows + (index + 1) * unit]

    if near:
        third = permuted(send, neighbours)
        total = added(keep[:rows], third[:rows])
        from_third = [slot(third, i) for i in range(3)]
        none = jnp.zeros_like(from_third[0])
        mine = jnp.where(even, from_third[0], none)
        two = added(slot(keep, 0), jnp.where(even, from_third[1], from_third[0]))
        four = added(slot(keep, 1), jnp.where(even, from_third[2], from_third[1]))
        six = added(slot(keep, 2), jnp.where(even, none, from_third[2]))
    else:
        third = permuted(send[rows:], back(shift_route(1, size)))
        total = added(keep[:rows], permuted(send[:rows], neighbours))
        mine = third[:unit]
        two = added(slot(keep, 0), third[unit : 2 * unit])
        four = added(slot(keep, 1), third[2 * unit : 3 * unit])
        six = added(slot(keep, 2), third[3 * unit :])
    second = permuted(jnp.concatenate([total.astype(BF16), two.astype(BF16), six.astype(BF16)]), back(near_route))
    total = added(total.astype(BF16), jnp.where(lax.rem(device, 4) < 2, second[:rows], 0)).astype(BF16)
    mine = added(mine, slot(second, 0))
    four = added(four, slot(second, 1)).astype(BF16)
    for stride in strides:
        total = added(total, permuted(total, back(prompt_route(stride)))).astype(BF16)
    mine = added(mine, permuted(four, back(far_route)))
    last = permuted(total, [(1, 0)])
    own = []
    for side, local, prompt in ((0, dk, total), (1, dv, last)):
        whole = local + jnp.where(device == 0, prompt.astype(F32), 0.0)
        own.append(whole.at[:one].add(mine[side * one : (side + 1) * one]).reshape(tokens, heads_kv, head_size))
    return grad_queries, own[0], own[1]


def solution(mesh):
    by_token = P(("leaf", "node"), "tensor", None)
    return jax.shard_map(
        functools.partial(per_device, mesh.shape["node"]),
        mesh=mesh,
        in_specs=(by_token, by_token, by_token, by_token, P("leaf"), P("leaf")),
        out_specs=(by_token, by_token, by_token),
        check_vma=False,
    )
```

```python
import functools
import math

import jax
import jax.numpy as jnp
from jax import lax
from jax.experimental import pallas as pl
from jax.experimental.pallas import tpu as pltpu
from jax.sharding import PartitionSpec as P

TILE = 16
TD = 8
CAP = 2
W = 7
CHUNK = 32
MASKED = -1e30
BF16 = jnp.bfloat16
F32 = jnp.float32


def permuted(block, route):
    return lax.ppermute(block, "node", route)


def column_limits(device, window, parents, lengths):
    cursor = parents[device * TD]
    need = [jnp.int32(0)] * (window + 1)
    for _ in range(W):
        owner = jnp.where(cursor < 0, -1, lax.div(jnp.maximum(cursor, 0), TD))
        distance = device - owner
        active = (owner >= 1) & (distance >= 1) & (distance <= W)
        depth = lax.rem(jnp.maximum(cursor, 0), TD) + 1
        for k in range(1, window + 1):
            need[k] = jnp.where(active & (distance == k), depth, need[k])
        cursor = jnp.where(active, parents[jnp.maximum(owner, 0) * TD], cursor)
    limits = [jnp.where(device >= 1, lengths[t], 0) for t in range(TD)]
    for k in range(1, window + 1):
        owner = device - k
        for c in range(CAP):
            seen = (owner >= 1) & (c < need[k])
            limits.append(jnp.where(seen, lengths[jnp.maximum(owner, 0) * TD + c], 0))
    limits += [lengths[device * TD + t] for t in range(TD)]
    return limits


def split_heads(block, heads_ref, start, count, heads_kv, wide):
    wide[: count * heads_kv] = block.astype(F32)
    for h in range(heads_kv):
        heads_ref[h, start : start + count] = wide[pl.ds(h, count, stride=heads_kv), :].astype(BF16)


def join_heads(blocks, count, heads_kv, wide):
    for h in range(heads_kv):
        wide[pl.ds(h, count, stride=heads_kv), :] = blocks[h]
    return wide[: count * heads_kv]


def prepare_kernel(window, heads_kv, *refs):
    parents, lengths, keys, values, q_ref, g_ref, qh, gh, own_k, own_v, bias, weight, wide = refs
    tokens = TD * TILE
    device = lax.axis_index("node")
    for pair in range(heads_kv // 2):
        for ref, out in ((q_ref, qh), (g_ref, gh)):
            both = ref[:, pair * 16 : (pair + 1) * 16].astype(F32)
            for part in range(2):
                out[2 * pair + part] = both[:, part * 8 : (part + 1) * 8].reshape(tokens * 8, 128).astype(BF16)
    split_heads(keys[...], own_k, 0, tokens, heads_kv, wide)
    split_heads(values[...], own_v, 0, tokens, heads_kv, wide)
    place = lax.broadcasted_iota(jnp.int32, (TILE, 128), 0)
    for t, limit in enumerate(column_limits(device, window, parents, lengths)):
        bias[t * TILE : (t + 1) * TILE] = jnp.where(place < limit, 0.0, MASKED)
    lane_place = lax.broadcasted_iota(jnp.int32, (8, 128), 1) // 8
    for t in range(TD):
        weight[:, t * 128 : (t + 1) * 128] = jnp.where(lane_place < lengths[device * TD + t], 1.0, 0.0)


def probs_kernel(slots, heads_kv, scale, *refs):
    prompt_k, prompt_v, own_k, own_v, qh, gh, bias, weight_ref = refs[:8]
    blocks = refs[8 : 8 + 1 + max(source for source, _ in slots)]
    send_ref, keep_ref, kh, ds_ref, p_own = refs[8 + len(blocks) : 13 + len(blocks)]
    vh, p_ref, grads, wide = refs[13 + len(blocks) :]
    window = len(slots)
    tokens = TD * TILE
    front = CAP * TILE
    before = tokens + window * front
    columns = CHUNK * 8
    device = lax.axis_index("node")

    for side, heads_ref, prompt, own in ((0, kh, prompt_k, own_k), (1, vh, prompt_v, own_v)):
        split_heads(prompt[...], heads_ref, 0, tokens, heads_kv, wide)
        for k, (source, start) in enumerate(slots):
            start += side * front * heads_kv
            block = blocks[source][start : start + front * heads_kv]
            split_heads(block, heads_ref, tokens + k * front, front, heads_kv, wide)
        heads_ref[:, before:] = own[...]

    column_token = lax.broadcasted_iota(jnp.int32, (CHUNK, columns), 1) // 8
    causal = jnp.where(lax.broadcasted_iota(jnp.int32, (CHUNK, columns), 0) <= column_token, 0.0, MASKED)
    for head in range(heads_kv):
        for c in range(tokens // CHUNK):
            rows = before + (c + 1) * CHUNK
            span = slice(c * columns, (c + 1) * columns)
            q = qh[head, span]
            g = gh[head, span]
            s = lax.dot_general(kh[head, :rows], q, (((1,), (1,)), ((), ())), preferred_element_type=F32)
            dp = lax.dot_general(vh[head, :rows], g, (((1,), (1,)), ((), ())), preferred_element_type=F32)
            s = s + jnp.concatenate([bias[:rows]] * (columns // 128), axis=1)
            s = jnp.concatenate([s[: rows - CHUNK], s[rows - CHUNK :] + causal], axis=0)
            top = jnp.max(s, axis=0, keepdims=True)
            e = jnp.exp2((s - top) * (scale * math.log2(math.e)))
            total = jnp.sum(e, axis=0, keepdims=True)
            p = e * (weight_ref[:1, span] / total)
            delta = jnp.sum(p * dp, axis=0, keepdims=True)
            ds_ref[head, :rows, span] = (p * (dp - delta) * scale).astype(BF16)
            p_ref[:, span] = p[:before].astype(BF16)
            p_own[head, : rows - before, span] = p[before:].astype(BF16)
        grads[0, head] = jnp.dot(ds_ref[head, :before], qh[head], preferred_element_type=F32)
        grads[1, head] = jnp.dot(p_ref[...], gh[head], preferred_element_type=F32)

    rows = tokens * heads_kv
    rows_front = front * heads_kv
    even = lax.rem(device, 2) == 0
    for side in range(2):
        dprompt = join_heads([grads[side, h, :tokens] for h in range(heads_kv)], tokens, heads_kv, wide).astype(BF16)
        kept = even if side == 0 else jnp.logical_not(even)

        @pl.when(kept)
        def _():
            keep_ref[:rows] = dprompt

        @pl.when(jnp.logical_not(kept))
        def _():
            send_ref[:rows] = dprompt

        for k in range(window):
            span = slice(tokens + k * front, tokens + (k + 1) * front)
            block = join_heads([grads[side, h, span] for h in range(heads_kv)], front, heads_kv, wide).astype(BF16)
            start = rows + (k // 2 * 2 + side) * rows_front
            (send_ref, keep_ref)[k % 2][start : start + rows_front] = block


def grads_kernel(heads_kv, *refs):
    qh, gh, kh, ds_ref, p_own, dq_ref, dk_ref, dv_ref, wide = refs
    tokens = TD * TILE
    before = kh.shape[1] - tokens
    columns = CHUNK * 8
    dk = []
    dv = []
    for pair in range(heads_kv // 2):
        for c in range(tokens // CHUNK):
            rows = before + (c + 1) * CHUNK
            span = slice(c * columns, (c + 1) * columns)
            parts = []
            for head in (2 * pair, 2 * pair + 1):
                dq = lax.dot_general(
                    kh[head, :rows], ds_ref[head, :rows, span], (((0,), (0,)), ((), ())), preferred_element_type=F32
                )
                parts.append(dq.T.reshape(CHUNK, 8, 128))
            dq_ref[c * CHUNK : (c + 1) * CHUNK, pair * 16 : (pair + 1) * 16] = jnp.concatenate(parts, axis=1).astype(BF16)
        for head in (2 * pair, 2 * pair + 1):
            for source, factor, out in ((ds_ref.at[head, before:], qh, dk), (p_own.at[head], gh, dv)):
                pieces = []
                for c in range(tokens // CHUNK):
                    start = c * columns
                    pieces.append(
                        jnp.dot(
                            source[c * CHUNK : (c + 1) * CHUNK, start:], factor[head, start:], preferred_element_type=F32
                        )
                    )
                out.append(jnp.concatenate(pieces, axis=0))
    dk_ref[...] = join_heads(dk, tokens, heads_kv, wide)
    dv_ref[...] = join_heads(dv, tokens, heads_kv, wide)


VMEM = pl.BlockSpec(memory_space=pltpu.VMEM)
SMEM = pl.BlockSpec(memory_space=pltpu.SMEM)


def call(kernel, name, operands, outputs, scratch, flops, transcendentals=0, scalars=0):
    sizes = [a.size * a.dtype.itemsize for a in (*operands, *outputs)]
    return pl.pallas_call(
        kernel,
        in_specs=[SMEM] * scalars + [VMEM] * (len(operands) - scalars),
        out_specs=[VMEM] * len(outputs),
        out_shape=outputs,
        scratch_shapes=scratch,
        compiler_params=pltpu.CompilerParams(vmem_limit_bytes=28 * 1024 * 1024),
        cost_estimate=pl.CostEstimate(flops=flops, bytes_accessed=sum(sizes), transcendentals=transcendentals),
        name=name,
    )(*operands)


def prepare(window, queries, grad_out, keys, values, parents, lengths):
    tokens, heads_q, head_size = queries.shape
    rows = keys.shape[0]
    heads_kv = rows // tokens
    array = jax.ShapeDtypeStruct
    return call(
        functools.partial(prepare_kernel, window, heads_kv),
        "prepare",
        (parents, lengths, keys, values, queries, grad_out),
        [array((heads_kv, tokens * 8, head_size), BF16)] * 2
        + [array((heads_kv, tokens, head_size), BF16)] * 2
        + [array((2 * tokens + window * CAP * TILE, 128), F32), array((8, tokens * 8), F32)],
        [pltpu.VMEM((rows, head_size), F32)],
        flops=1 << 20,
        scalars=2,
    )


def probs(slots, prompt_k, prompt_v, prepared, blocks):
    qh, gh, own_k, own_v, bias, weight = prepared
    heads_kv, tokens, head_size = own_k.shape
    window = len(slots)
    rows = tokens * heads_kv
    front = CAP * TILE
    before = tokens + window * front
    sent = rows + (window + 1) // 2 * 2 * front * heads_kv
    kept = rows + window // 2 * 2 * front * heads_kv
    array = jax.ShapeDtypeStruct
    work = heads_kv * tokens * 8 * (before + tokens)
    return call(
        functools.partial(probs_kernel, slots, heads_kv, head_size**-0.5),
        "probs",
        (prompt_k, prompt_v, own_k, own_v, qh, gh, bias, weight, *blocks),
        [
            array((sent, head_size), BF16),
            array((kept, head_size), BF16),
            array((heads_kv, before + tokens, head_size), BF16),
            array((heads_kv, before + tokens, tokens * 8), BF16),
            array((heads_kv, tokens, tokens * 8), BF16),
        ],
        [
            pltpu.VMEM((heads_kv, before + tokens, head_size), BF16),
            pltpu.VMEM((before, tokens * 8), BF16),
            pltpu.VMEM((2, heads_kv, before, head_size), F32),
            pltpu.VMEM((rows, head_size), F32),
        ],
        flops=8 * work * head_size,
        transcendentals=work,
    )


def grads(qh, gh, kh, ds, p_own):
    heads_kv, tokens, _ = p_own.shape
    head_size = kh.shape[2]
    array = jax.ShapeDtypeStruct
    return call(
        functools.partial(grads_kernel, heads_kv),
        "grads",
        (qh, gh, kh, ds, p_own),
        [
            array((tokens, heads_kv * 8, head_size), BF16),
            array((tokens * heads_kv, head_size), F32),
            array((tokens * heads_kv, head_size), F32),
        ],
        [pltpu.VMEM((tokens * heads_kv, head_size), F32)],
        flops=4 * heads_kv * tokens * 8 * kh.shape[1] * head_size,
    )


def shift_route(distance, size):
    return [(i, i + distance) for i in range(size - distance)]


def back(route):
    return [(j, i) for i, j in route]


def added(*blocks):
    total = blocks[0].astype(F32)
    for block in blocks[1:]:
        total = total + block.astype(F32)
    return total


def per_device(size, queries, keys, values, grad_out, parents, lengths):
    tokens, heads_kv, head_size = keys.shape
    rows = tokens * heads_kv
    unit = 2 * CAP * TILE * heads_kv
    one = CAP * TILE * heads_kv
    near = size <= W + 1
    window = min(W, size - 2) if near else W
    device = lax.axis_index("node")
    even = lax.rem(device, 2) == 0
    keys = keys.reshape(rows, head_size)
    values = values.reshape(rows, head_size)
    strides = [2**i for i in range(2, size.bit_length()) if 2**i < size]
    neighbours = [(i, i ^ 1) for i in range(size)]
    far_route = shift_route(4, size)[1:]
    near_route = shift_route(2, size)

    def prompt_route(stride):
        return [(i + j, i + j + stride) for i in range(0, size, 2 * stride) for j in (0, 1)]

    top = strides[-1]
    prepared = prepare(window, queries, grad_out, keys, values, parents, lengths)
    values_far = permuted(values, [(0, top + 1)])
    keys_far = permuted(keys, [(0, top)])
    values_next = permuted(values, [(0, 1)])
    head = jnp.concatenate([keys[:one], values[:one]])
    far = permuted(head, far_route)
    held = jnp.where(device == 0, keys, added(values_far, keys_far, values_next).astype(BF16))
    for stride in reversed(strides[:-1]):
        held = added(held, permuted(held, prompt_route(stride))).astype(BF16)
    second = permuted(jnp.concatenate([held, head, far]), near_route)
    held = jnp.where(lax.rem(device, 4) < 2, held, second[:rows])
    two, four, six = second[rows : rows + unit], far, second[rows + unit :]
    if near:
        even_slots = jnp.where(even, jnp.concatenate([head, two, four]), jnp.concatenate([two, four, six]))
        third = permuted(jnp.concatenate([held, even_slots]), neighbours)
        other, start = third[:rows], rows
    else:
        third = permuted(jnp.concatenate([head, two, four, six]), shift_route(1, size))
        other, start = permuted(held, neighbours), 0
    slots = [(0, start), (1, rows), (0, start + unit), (2, 0), (0, start + 2 * unit), (1, rows + unit), (0, start + 3 * unit)]
    slots = slots[:window]

    send, keep, kh, ds, p_own = probs(
        slots, jnp.where(even, held, other), jnp.where(even, other, held), prepared, (third, second, far)
    )
    grad_queries, dk, dv = grads(*prepared[:2], kh, ds, p_own)

    def slot(array, index):
        return array[rows + index * unit : rows + (index + 1) * unit]

    if near:
        third = permuted(send, neighbours)
        total = added(keep[:rows], third[:rows])
        from_third = [slot(third, i) for i in range(3)]
        none = jnp.zeros_like(from_third[0])
        mine = jnp.where(even, from_third[0], none)
        two = added(slot(keep, 0), jnp.where(even, from_third[1], from_third[0]))
        four = added(slot(keep, 1), jnp.where(even, from_third[2], from_third[1]))
        six = added(slot(keep, 2), jnp.where(even, none, from_third[2]))
    else:
        third = permuted(send[rows:], back(shift_route(1, size)))
        total = added(keep[:rows], permuted(send[:rows], neighbours))
        mine = third[:unit]
        two = added(slot(keep, 0), third[unit : 2 * unit])
        four = added(slot(keep, 1), third[2 * unit : 3 * unit])
        six = added(slot(keep, 2), third[3 * unit :])
    second = permuted(jnp.concatenate([total.astype(BF16), two.astype(BF16), six.astype(BF16)]), back(near_route))
    total = added(total.astype(BF16), jnp.where(lax.rem(device, 4) < 2, second[:rows], 0)).astype(BF16)
    mine = added(mine, slot(second, 0))
    four = added(four, slot(second, 1)).astype(BF16)
    for stride in strides[:-1]:
        total = added(total, permuted(total, back(prompt_route(stride)))).astype(BF16)
    values_far = permuted(total, [(top + 1, 0)])
    keys_far = permuted(total, [(top, 0)])
    values_next = permuted(total, [(1, 0)])
    mine = added(mine, permuted(four, back(far_route)))
    own = []
    for side, local, prompt in ((0, dk, added(total, keys_far)), (1, dv, added(values_far, values_next))):
        whole = local + jnp.where(device == 0, prompt, 0.0)
        own.append(whole.at[:one].add(mine[side * one : (side + 1) * one]).reshape(tokens, heads_kv, head_size))
    return grad_queries, own[0], own[1]


def solution(mesh):
    by_token = P(("leaf", "node"), "tensor", None)
    return jax.shard_map(
        functools.partial(per_device, mesh.shape["node"]),
        mesh=mesh,
        in_specs=(by_token, by_token, by_token, by_token, P("leaf"), P("leaf")),
        out_specs=(by_token, by_token, by_token),
        check_vma=False,
    )
```

```python
import functools
import math

import jax
import jax.numpy as jnp
from jax import lax
from jax.experimental import pallas as pl
from jax.experimental.pallas import tpu as pltpu
from jax.sharding import PartitionSpec as P

TILE = 16
TD = 8
CAP = 2
W = 7
CHUNK = 32
MASKED = -1e30
BF16 = jnp.bfloat16
F32 = jnp.float32


def permuted(block, route):
    return lax.ppermute(block, "node", route)


def column_limits(device, window, parents, lengths):
    cursor = parents[device * TD]
    need = [jnp.int32(0)] * (window + 1)
    for _ in range(W):
        owner = jnp.where(cursor < 0, -1, lax.div(jnp.maximum(cursor, 0), TD))
        distance = device - owner
        active = (owner >= 1) & (distance >= 1) & (distance <= W)
        depth = lax.rem(jnp.maximum(cursor, 0), TD) + 1
        for k in range(1, window + 1):
            need[k] = jnp.where(active & (distance == k), depth, need[k])
        cursor = jnp.where(active, parents[jnp.maximum(owner, 0) * TD], cursor)
    prompt = [jnp.where(device >= 1, lengths[t], 0) for t in range(TD)]
    behind = []
    for k in range(1, window + 1):
        owner = device - k
        seen = [(owner >= 1) & (c < need[k]) for c in range(CAP)]
        behind.append([jnp.where(seen[c], lengths[jnp.maximum(owner, 0) * TD + c], 0) for c in range(CAP)])
    return prompt, behind, [lengths[device * TD + t] for t in range(TD)]


def split_heads(block, heads_ref, start, count, heads_kv, wide):
    wide[: count * heads_kv] = block.astype(F32)
    for h in range(heads_kv):
        heads_ref[h, start : start + count] = wide[pl.ds(h, count, stride=heads_kv), :].astype(BF16)


def join_heads(blocks, count, heads_kv, wide):
    for h in range(heads_kv):
        wide[pl.ds(h, count, stride=heads_kv), :] = blocks[h]
    return wide[: count * heads_kv]


def prepare_kernel(order, heads_kv, *refs):
    parents, lengths, keys, values, q_ref, g_ref, qh, gh, own_k, own_v, bias, weight, wide = refs
    tokens = TD * TILE
    device = lax.axis_index("node")
    for pair in range(heads_kv // 2):
        for ref, out in ((q_ref, qh), (g_ref, gh)):
            both = ref[:, pair * 16 : (pair + 1) * 16].astype(F32)
            for part in range(2):
                out[2 * pair + part] = both[:, part * 8 : (part + 1) * 8].reshape(tokens * 8, 128).astype(BF16)
    split_heads(keys[...], own_k, 0, tokens, heads_kv, wide)
    split_heads(values[...], own_v, 0, tokens, heads_kv, wide)
    place = lax.broadcasted_iota(jnp.int32, (TILE, 128), 0)
    prompt, behind, own = column_limits(device, len(order), parents, lengths)
    even = lax.rem(device, 2) == 0
    limits = prompt
    for on_even, on_odd in order:
        limits = limits + [jnp.where(even, x, y) for x, y in zip(behind[on_even - 1], behind[on_odd - 1])]
    for t, limit in enumerate(limits + own):
        bias[t * TILE : (t + 1) * TILE] = jnp.where(place < limit, 0.0, MASKED)
    lane_place = lax.broadcasted_iota(jnp.int32, (8, 128), 1) // 8
    for t in range(TD):
        weight[:, t * 128 : (t + 1) * 128] = jnp.where(lane_place < lengths[device * TD + t], 1.0, 0.0)


def probs_kernel(sources, targets, heads_kv, scale, *refs):
    prompt_k, prompt_v, own_k, own_v, qh, gh, bias, weight_ref = refs[:8]
    n_in = 1 + max(source for source, _ in sources)
    n_out = 1 + max(target for target, _ in targets)
    blocks = refs[8 : 8 + n_in]
    outs = refs[8 + n_in : 8 + n_in + n_out]
    kh, ds_ref, p_own, vh, p_ref, grads, wide = refs[8 + n_in + n_out :]
    window = len(sources)
    tokens = TD * TILE
    front = CAP * TILE
    before = tokens + window * front
    columns = CHUNK * 8
    device = lax.axis_index("node")

    for side, heads_ref, prompt, own in ((0, kh, prompt_k, own_k), (1, vh, prompt_v, own_v)):
        split_heads(prompt[...], heads_ref, 0, tokens, heads_kv, wide)
        for k, (source, start) in enumerate(sources):
            start += side * front * heads_kv
            block = blocks[source][start : start + front * heads_kv]
            split_heads(block, heads_ref, tokens + k * front, front, heads_kv, wide)
        heads_ref[:, before:] = own[...]

    column_token = lax.broadcasted_iota(jnp.int32, (CHUNK, columns), 1) // 8
    causal = jnp.where(lax.broadcasted_iota(jnp.int32, (CHUNK, columns), 0) <= column_token, 0.0, MASKED)
    for head in range(heads_kv):
        for c in range(tokens // CHUNK):
            rows = before + (c + 1) * CHUNK
            span = slice(c * columns, (c + 1) * columns)
            q = qh[head, span]
            g = gh[head, span]
            s = lax.dot_general(kh[head, :rows], q, (((1,), (1,)), ((), ())), preferred_element_type=F32)
            dp = lax.dot_general(vh[head, :rows], g, (((1,), (1,)), ((), ())), preferred_element_type=F32)
            s = s + jnp.concatenate([bias[:rows]] * (columns // 128), axis=1)
            s = jnp.concatenate([s[: rows - CHUNK], s[rows - CHUNK :] + causal], axis=0)
            top = jnp.max(s, axis=0, keepdims=True)
            e = jnp.exp2((s - top) * (scale * math.log2(math.e)))
            total = jnp.sum(e, axis=0, keepdims=True)
            p = e * (weight_ref[:1, span] / total)
            delta = jnp.sum(p * dp, axis=0, keepdims=True)
            ds_ref[head, :rows, span] = (p * (dp - delta) * scale).astype(BF16)
            p_ref[:, span] = p[:before].astype(BF16)
            p_own[head, : rows - before, span] = p[before:].astype(BF16)
        grads[0, head] = jnp.dot(ds_ref[head, :before], qh[head], preferred_element_type=F32)
        grads[1, head] = jnp.dot(p_ref[...], gh[head], preferred_element_type=F32)

    rows = tokens * heads_kv
    rows_front = front * heads_kv
    even = lax.rem(device, 2) == 0
    for side in range(2):
        dprompt = join_heads([grads[side, h, :tokens] for h in range(heads_kv)], tokens, heads_kv, wide).astype(BF16)
        kept = even if side == 0 else jnp.logical_not(even)

        @pl.when(kept)
        def _():
            outs[1][:rows] = dprompt

        @pl.when(jnp.logical_not(kept))
        def _():
            outs[0][:rows] = dprompt

        for k, (target, start) in enumerate(targets):
            span = slice(tokens + k * front, tokens + (k + 1) * front)
            block = join_heads([grads[side, h, span] for h in range(heads_kv)], front, heads_kv, wide).astype(BF16)
            start += side * rows_front
            outs[target][start : start + rows_front] = block


def grads_kernel(heads_kv, *refs):
    qh, gh, kh, ds_ref, p_own, dq_ref, dk_ref, dv_ref, wide = refs
    tokens = TD * TILE
    before = kh.shape[1] - tokens
    columns = CHUNK * 8
    dk = []
    dv = []
    for pair in range(heads_kv // 2):
        for c in range(tokens // CHUNK):
            rows = before + (c + 1) * CHUNK
            span = slice(c * columns, (c + 1) * columns)
            parts = []
            for head in (2 * pair, 2 * pair + 1):
                dq = lax.dot_general(
                    kh[head, :rows], ds_ref[head, :rows, span], (((0,), (0,)), ((), ())), preferred_element_type=F32
                )
                parts.append(dq.T.reshape(CHUNK, 8, 128))
            dq_ref[c * CHUNK : (c + 1) * CHUNK, pair * 16 : (pair + 1) * 16] = jnp.concatenate(parts, axis=1).astype(BF16)
        for head in (2 * pair, 2 * pair + 1):
            for source, factor, out in ((ds_ref.at[head, before:], qh, dk), (p_own.at[head], gh, dv)):
                pieces = []
                for c in range(tokens // CHUNK):
                    start = c * columns
                    pieces.append(
                        jnp.dot(
                            source[c * CHUNK : (c + 1) * CHUNK, start:], factor[head, start:], preferred_element_type=F32
                        )
                    )
                out.append(jnp.concatenate(pieces, axis=0))
    dk_ref[...] = join_heads(dk, tokens, heads_kv, wide)
    dv_ref[...] = join_heads(dv, tokens, heads_kv, wide)


VMEM = pl.BlockSpec(memory_space=pltpu.VMEM)
SMEM = pl.BlockSpec(memory_space=pltpu.SMEM)


def call(kernel, name, operands, outputs, scratch, flops, transcendentals=0, scalars=0):
    sizes = [a.size * a.dtype.itemsize for a in (*operands, *outputs)]
    return pl.pallas_call(
        kernel,
        in_specs=[SMEM] * scalars + [VMEM] * (len(operands) - scalars),
        out_specs=[VMEM] * len(outputs),
        out_shape=outputs,
        scratch_shapes=scratch,
        compiler_params=pltpu.CompilerParams(vmem_limit_bytes=28 * 1024 * 1024),
        cost_estimate=pl.CostEstimate(flops=flops, bytes_accessed=sum(sizes), transcendentals=transcendentals),
        name=name,
    )(*operands)


def prepare(order, queries, grad_out, keys, values, parents, lengths):
    tokens, heads_q, head_size = queries.shape
    rows = keys.shape[0]
    heads_kv = rows // tokens
    array = jax.ShapeDtypeStruct
    return call(
        functools.partial(prepare_kernel, order, heads_kv),
        "prepare",
        (parents, lengths, keys, values, queries, grad_out),
        [array((heads_kv, tokens * 8, head_size), BF16)] * 2
        + [array((heads_kv, tokens, head_size), BF16)] * 2
        + [array((2 * tokens + len(order) * CAP * TILE, 128), F32), array((8, tokens * 8), F32)],
        [pltpu.VMEM((rows, head_size), F32)],
        flops=1 << 20,
        scalars=2,
    )


def probs(sources, targets, prompt_k, prompt_v, prepared, blocks):
    qh, gh, own_k, own_v, bias, weight = prepared
    heads_kv, tokens, head_size = own_k.shape
    rows = tokens * heads_kv
    front = CAP * TILE
    unit = 2 * front * heads_kv
    before = tokens + len(sources) * front
    sizes = [max(start for target, start in targets if target == t) + unit for t in range(1 + max(targets)[0])]
    array = jax.ShapeDtypeStruct
    work = heads_kv * tokens * 8 * (before + tokens)
    return call(
        functools.partial(probs_kernel, sources, targets, heads_kv, head_size**-0.5),
        "probs",
        (prompt_k, prompt_v, own_k, own_v, qh, gh, bias, weight, *blocks),
        [array((size, head_size), BF16) for size in sizes]
        + [
            array((heads_kv, before + tokens, head_size), BF16),
            array((heads_kv, before + tokens, tokens * 8), BF16),
            array((heads_kv, tokens, tokens * 8), BF16),
        ],
        [
            pltpu.VMEM((heads_kv, before + tokens, head_size), BF16),
            pltpu.VMEM((before, tokens * 8), BF16),
            pltpu.VMEM((2, heads_kv, before, head_size), F32),
            pltpu.VMEM((rows, head_size), F32),
        ],
        flops=8 * work * head_size,
        transcendentals=work,
    )


def grads(qh, gh, kh, ds, p_own):
    heads_kv, tokens, _ = p_own.shape
    head_size = kh.shape[2]
    array = jax.ShapeDtypeStruct
    return call(
        functools.partial(grads_kernel, heads_kv),
        "grads",
        (qh, gh, kh, ds, p_own),
        [
            array((tokens, heads_kv * 8, head_size), BF16),
            array((tokens * heads_kv, head_size), F32),
            array((tokens * heads_kv, head_size), F32),
        ],
        [pltpu.VMEM((tokens * heads_kv, head_size), F32)],
        flops=4 * heads_kv * tokens * 8 * kh.shape[1] * head_size,
    )


def shift_route(distance, size):
    return [(i, i + distance) for i in range(size - distance)]


def back(route):
    return [(j, i) for i, j in route]


def added(*blocks):
    total = blocks[0].astype(F32)
    for block in blocks[1:]:
        total = total + block.astype(F32)
    return total


def after(array, *earlier):
    return lax.optimization_barrier((array, *earlier))[0]


def per_device(size, queries, keys, values, grad_out, parents, lengths):
    tokens, heads_kv, head_size = keys.shape
    rows = tokens * heads_kv
    one = CAP * TILE * heads_kv
    unit = 2 * one
    device = lax.axis_index("node")
    even = lax.rem(device, 2) == 0
    lower = lax.rem(device, 4) < 2
    keys = keys.reshape(rows, head_size)
    values = values.reshape(rows, head_size)
    strides = [2**i for i in range(2, size.bit_length()) if 2**i < size]
    top = strides[-1]
    neighbours = [(i, i ^ 1) for i in range(size)]
    far_route = shift_route(4, size)[1:]
    near_route = shift_route(2, size)
    six_route = [(1, 7)]
    small = size == W + 1
    if small:
        order = [(1, 3), (2, 2), (3, 1), (4, 4), (5, 5), (6, 6)]
        sources = [(0, rows), (1, rows), (2, 0), (3, 0), (2, unit), (4, 0)]
        targets = [(0, rows), (1, rows), (2, 0), (1, rows + unit), (2, unit), (1, rows + 2 * unit)]
    else:
        order = [(k, k) for k in range(1, W + 1)]
        sources = [(0, 0), (1, rows), (0, unit), (2, 0), (0, 2 * unit), (1, rows + unit), (0, 3 * unit)]
        targets = [(1 - k % 2, rows + (k - 1) // 2 * unit) for k in range(1, W + 1)]

    def prompt_route(stride):
        return [(i + j, i + j + stride) for i in range(0, size, 2 * stride) for j in (0, 1)]

    def units(array, start, count):
        return [array[start + i * unit : start + (i + 1) * unit] for i in range(count)]

    prepared = prepare(order, queries, grad_out, keys, values, parents, lengths)
    held = lax.optimization_barrier(jnp.where(device == 0, keys, jnp.zeros_like(keys)))
    keys_far = permuted(keys, [(0, top)])
    values_far = permuted(values, [(0, top + 1)])
    values_next = permuted(values, [(0, 1)])
    head = after(jnp.concatenate([keys[:one], values[:one]]), keys_far)
    far = permuted(head, far_route)
    held = added(held, values_next, values_far, keys_far).astype(BF16)
    for stride in reversed(strides[:-1]):
        held = added(held, permuted(held, prompt_route(stride))).astype(BF16)
    if small:
        six = permuted(head, six_route)
        held = after(held, far, six)
        second = permuted(jnp.concatenate([held, head]), near_route)
        crossed = jnp.where(even, jnp.concatenate([head, far]), jnp.concatenate([far, six]))
        crossed = permuted(crossed, neighbours)
        held = jnp.where(lower, held, second[:rows])
        third = permuted(after(jnp.concatenate([held, second[rows:]]), crossed), neighbours)
        other = third[:rows]
        blocks = (third, second, crossed, far, six)
    else:
        second = permuted(jnp.concatenate([held, head, far]), near_route)
        held = jnp.where(lower, held, second[:rows])
        third = permuted(jnp.concatenate([head, second[rows : rows + unit], far, second[rows + unit :]]), shift_route(1, size))
        other = permuted(held, neighbours)
        blocks = (third, second, far)

    *sent, kh, ds, p_own = probs(
        sources, targets, jnp.where(even, held, other), jnp.where(even, other, held), prepared, blocks
    )
    grad_queries, dk, dv = grads(*prepared[:2], kh, ds, p_own)

    send, keep = sent[:2]
    two, four, six = units(keep, rows, 3)
    if small:
        third = permuted(send, neighbours)
        total = added(keep[:rows], third[:rows]).astype(BF16)
        two = added(two, third[rows:])
        total = after(total, dk)
        second = permuted(after(jnp.concatenate([total, two.astype(BF16)])), back(near_route))
        first, last = units(permuted(after(sent[2], third), neighbours), 0, 2)
        four, six, first, last, second = lax.optimization_barrier((four, six, first, last, second))
        none = jnp.zeros_like(first)
        mine = added(jnp.where(even, first, none), second[rows:])
        four = added(four, jnp.where(even, last, first))
        six = added(six, jnp.where(even, none, last)).astype(BF16)
    else:
        zero, *third = units(permuted(send[rows:], back(shift_route(1, size))), 0, 4)
        total = added(keep[:rows], permuted(send[:rows], neighbours)).astype(BF16)
        two, four, six = (added(x, y).astype(BF16) for x, y in zip((two, four, six), third))
        second = permuted(jnp.concatenate([total, two, six]), back(near_route))
        mine = added(zero, second[rows : rows + unit])
        four = added(four, second[rows + unit :])
    total = added(total, jnp.where(lower, second[:rows], jnp.zeros_like(total))).astype(BF16)
    for stride in strides[:-1]:
        total = added(total, permuted(total, back(prompt_route(stride)))).astype(BF16)
    keys_far = permuted(total, [(top, 0)])
    values_far = permuted(total, [(top + 1, 0)])
    values_next = permuted(total, [(1, 0)])
    four = after(four.astype(BF16), values_next)
    mine = added(mine, permuted(four, back(far_route)))
    if small:
        mine = added(mine, permuted(after(six, values_next), back(six_route)))
    own = []
    for side, local, prompt in ((0, dk, added(total, keys_far)), (1, dv, added(values_far, values_next))):
        whole = local + jnp.where(device == 0, prompt, 0.0)
        own.append(whole.at[:one].add(mine[side * one : (side + 1) * one]).reshape(tokens, heads_kv, head_size))
    return grad_queries, own[0], own[1]


def solution(mesh):
    by_token = P(("leaf", "node"), "tensor", None)
    return jax.shard_map(
        functools.partial(per_device, mesh.shape["node"]),
        mesh=mesh,
        in_specs=(by_token, by_token, by_token, by_token, P("leaf"), P("leaf")),
        out_specs=(by_token, by_token, by_token),
        check_vma=False,
    )
```

```python
import functools
import math

import jax
import jax.numpy as jnp
from jax import lax
from jax.experimental import pallas as pl
from jax.experimental.pallas import tpu as pltpu
from jax.sharding import PartitionSpec as P

TILE = 16
TD = 8
CAP = 2
W = 7
CHUNK = 32
MASKED = -1e30
BF16 = jnp.bfloat16
F32 = jnp.float32


def permuted(block, route):
    return lax.ppermute(block, "node", route)


def column_limits(device, window, parents, lengths):
    cursor = parents[device * TD]
    need = [jnp.int32(0)] * (window + 1)
    for _ in range(W):
        owner = jnp.where(cursor < 0, -1, lax.div(jnp.maximum(cursor, 0), TD))
        distance = device - owner
        active = (owner >= 1) & (distance >= 1) & (distance <= W)
        depth = lax.rem(jnp.maximum(cursor, 0), TD) + 1
        for k in range(1, window + 1):
            need[k] = jnp.where(active & (distance == k), depth, need[k])
        cursor = jnp.where(active, parents[jnp.maximum(owner, 0) * TD], cursor)
    prompt = [jnp.where(device >= 1, lengths[t], 0) for t in range(TD)]
    behind = []
    for k in range(1, window + 1):
        owner = device - k
        seen = [(owner >= 1) & (c < need[k]) for c in range(CAP)]
        behind.append([jnp.where(seen[c], lengths[jnp.maximum(owner, 0) * TD + c], 0) for c in range(CAP)])
    return prompt, behind, [lengths[device * TD + t] for t in range(TD)]


def split_heads(block, heads_ref, start, count, heads_kv, wide):
    wide[: count * heads_kv] = block.astype(F32)
    for h in range(heads_kv):
        heads_ref[h, start : start + count] = wide[pl.ds(h, count, stride=heads_kv), :].astype(BF16)


def join_heads(blocks, count, heads_kv, wide):
    for h in range(heads_kv):
        wide[pl.ds(h, count, stride=heads_kv), :] = blocks[h]
    return wide[: count * heads_kv]


def load_kernel(order, heads_kv, *refs):
    sources, outs, scratch = refs[:4], refs[4:10], refs[10:]
    head, held, own_k, own_v, bias, weight = outs
    parents, lengths, keys, values, wide, arrived = scratch
    copies = [pltpu.make_async_copy(a, b, arrived.at[i]) for i, (a, b) in enumerate(zip(sources, scratch))]
    for copy in copies:
        copy.start()
    tokens = TD * TILE
    front = CAP * TILE * heads_kv
    device = lax.axis_index("node")
    for copy in copies:
        copy.wait()
    head[:front] = keys[:front]
    head[front:] = values[:front]
    held[...] = jnp.where(device == 0, keys[...], jnp.zeros_like(keys))
    split_heads(keys[...], own_k, 0, tokens, heads_kv, wide)
    split_heads(values[...], own_v, 0, tokens, heads_kv, wide)
    place = lax.broadcasted_iota(jnp.int32, (TILE, 128), 0)
    prompt, behind, own = column_limits(device, len(order), parents, lengths)
    even = lax.rem(device, 2) == 0
    limits = prompt
    for on_even, on_odd in order:
        limits = limits + [jnp.where(even, x, y) for x, y in zip(behind[on_even - 1], behind[on_odd - 1])]
    for t, limit in enumerate(limits + own):
        bias[t * TILE : (t + 1) * TILE] = jnp.where(place < limit, 0.0, MASKED)
    lane_place = lax.broadcasted_iota(jnp.int32, (8, 128), 1) // 8
    for t in range(TD):
        weight[:, t * 128 : (t + 1) * 128] = jnp.where(lane_place < lengths[device * TD + t], 1.0, 0.0)


def pack_kernel(heads_kv, q_ref, g_ref, qh, gh, blocks, arrived):
    tokens = TD * TILE
    copies = []
    for pair in range(heads_kv // 2):
        for ref, out in ((q_ref, qh), (g_ref, gh)):
            i = len(copies)
            copy = pltpu.make_async_copy(ref.at[:, pair * 16 : (pair + 1) * 16], blocks.at[i], arrived.at[i])
            copy.start()
            copies.append((copy, out, pair))
    for i, (copy, out, pair) in enumerate(copies):
        copy.wait()
        both = blocks[i].astype(F32)
        for part in range(2):
            out[2 * pair + part] = both[:, part * 8 : (part + 1) * 8].reshape(tokens * 8, 128).astype(BF16)


def probs_kernel(sources, targets, heads_kv, scale, *refs):
    prompt_k, prompt_v, own_k, own_v, qh, gh, bias, weight_ref = refs[:8]
    n_in = 1 + max(source for source, _ in sources)
    n_out = 1 + max(target for target, _ in targets)
    blocks = refs[8 : 8 + n_in]
    outs = refs[8 + n_in : 8 + n_in + n_out]
    kh, ds_ref, p_own, vh, p_ref, grads, wide = refs[8 + n_in + n_out :]
    window = len(sources)
    tokens = TD * TILE
    front = CAP * TILE
    before = tokens + window * front
    columns = CHUNK * 8
    device = lax.axis_index("node")

    for side, heads_ref, prompt, own in ((0, kh, prompt_k, own_k), (1, vh, prompt_v, own_v)):
        split_heads(prompt[...], heads_ref, 0, tokens, heads_kv, wide)
        for k, (source, start) in enumerate(sources):
            start += side * front * heads_kv
            block = blocks[source][start : start + front * heads_kv]
            split_heads(block, heads_ref, tokens + k * front, front, heads_kv, wide)
        heads_ref[:, before:] = own[...]

    column_token = lax.broadcasted_iota(jnp.int32, (CHUNK, columns), 1) // 8
    causal = jnp.where(lax.broadcasted_iota(jnp.int32, (CHUNK, columns), 0) <= column_token, 0.0, MASKED)
    for head in range(heads_kv):
        for c in range(tokens // CHUNK):
            rows = before + (c + 1) * CHUNK
            span = slice(c * columns, (c + 1) * columns)
            q = qh[head, span]
            g = gh[head, span]
            s = lax.dot_general(kh[head, :rows], q, (((1,), (1,)), ((), ())), preferred_element_type=F32)
            dp = lax.dot_general(vh[head, :rows], g, (((1,), (1,)), ((), ())), preferred_element_type=F32)
            s = s + jnp.concatenate([bias[:rows]] * (columns // 128), axis=1)
            s = jnp.concatenate([s[: rows - CHUNK], s[rows - CHUNK :] + causal], axis=0)
            top = jnp.max(s, axis=0, keepdims=True)
            e = jnp.exp2((s - top) * (scale * math.log2(math.e)))
            total = jnp.sum(e, axis=0, keepdims=True)
            p = e * (weight_ref[:1, span] / total)
            delta = jnp.sum(p * dp, axis=0, keepdims=True)
            ds_ref[head, :rows, span] = (p * (dp - delta) * scale).astype(BF16)
            p_ref[:, span] = p[:before].astype(BF16)
            p_own[head, : rows - before, span] = p[before:].astype(BF16)
        grads[0, head] = jnp.dot(ds_ref[head, :before], qh[head], preferred_element_type=F32)
        grads[1, head] = jnp.dot(p_ref[...], gh[head], preferred_element_type=F32)

    rows = tokens * heads_kv
    rows_front = front * heads_kv
    even = lax.rem(device, 2) == 0
    for side in range(2):
        dprompt = join_heads([grads[side, h, :tokens] for h in range(heads_kv)], tokens, heads_kv, wide).astype(BF16)
        kept = even if side == 0 else jnp.logical_not(even)

        @pl.when(kept)
        def _():
            outs[1][:rows] = dprompt

        @pl.when(jnp.logical_not(kept))
        def _():
            outs[0][:rows] = dprompt

        for k, (target, start) in enumerate(targets):
            span = slice(tokens + k * front, tokens + (k + 1) * front)
            block = join_heads([grads[side, h, span] for h in range(heads_kv)], front, heads_kv, wide).astype(BF16)
            start += side * rows_front
            outs[target][start : start + rows_front] = block


def grads_kernel(heads_kv, *refs):
    qh, gh, kh, ds_ref, p_own, dq_ref, dk_ref, dv_ref, wide = refs
    tokens = TD * TILE
    before = kh.shape[1] - tokens
    columns = CHUNK * 8
    dk = []
    dv = []
    for pair in range(heads_kv // 2):
        for c in range(tokens // CHUNK):
            rows = before + (c + 1) * CHUNK
            span = slice(c * columns, (c + 1) * columns)
            parts = []
            for head in (2 * pair, 2 * pair + 1):
                dq = lax.dot_general(
                    kh[head, :rows], ds_ref[head, :rows, span], (((0,), (0,)), ((), ())), preferred_element_type=F32
                )
                parts.append(dq.T.reshape(CHUNK, 8, 128))
            dq_ref[c * CHUNK : (c + 1) * CHUNK, pair * 16 : (pair + 1) * 16] = jnp.concatenate(parts, axis=1).astype(BF16)
        for head in (2 * pair, 2 * pair + 1):
            for source, factor, out in ((ds_ref.at[head, before:], qh, dk), (p_own.at[head], gh, dv)):
                pieces = []
                for c in range(tokens // CHUNK):
                    start = c * columns
                    pieces.append(
                        jnp.dot(
                            source[c * CHUNK : (c + 1) * CHUNK, start:], factor[head, start:], preferred_element_type=F32
                        )
                    )
                out.append(jnp.concatenate(pieces, axis=0))
    dk_ref[...] = join_heads(dk, tokens, heads_kv, wide)
    dv_ref[...] = join_heads(dv, tokens, heads_kv, wide)


VMEM = pl.BlockSpec(memory_space=pltpu.VMEM)


HBM = pl.BlockSpec(memory_space=pltpu.HBM)


def call(kernel, name, operands, outputs, scratch, flops, transcendentals=0, place=VMEM):
    sizes = [a.size * a.dtype.itemsize for a in (*operands, *outputs)]
    if place is HBM:
        operands = [pltpu.with_memory_space_constraint(a, pltpu.HBM) for a in operands]
    return pl.pallas_call(
        kernel,
        in_specs=[place] * len(operands),
        out_specs=[VMEM] * len(outputs),
        out_shape=outputs,
        scratch_shapes=scratch,
        compiler_params=pltpu.CompilerParams(vmem_limit_bytes=28 * 1024 * 1024),
        cost_estimate=pl.CostEstimate(flops=flops, bytes_accessed=sum(sizes), transcendentals=transcendentals),
        name=name,
    )(*operands)


def load(order, keys, values, parents, lengths, tokens):
    rows, head_size = keys.shape
    heads_kv = rows // tokens
    array = jax.ShapeDtypeStruct
    return call(
        functools.partial(load_kernel, order, heads_kv),
        "load",
        (parents, lengths, keys, values),
        [array((2 * CAP * TILE * heads_kv, head_size), BF16), array((rows, head_size), BF16)]
        + [array((heads_kv, tokens, head_size), BF16)] * 2
        + [array((2 * tokens + len(order) * CAP * TILE, 128), F32), array((8, tokens * 8), F32)],
        [pltpu.SMEM(parents.shape, jnp.int32), pltpu.SMEM(lengths.shape, jnp.int32)]
        + [pltpu.VMEM((rows, head_size), BF16)] * 2
        + [pltpu.VMEM((rows, head_size), F32), pltpu.SemaphoreType.DMA((4,))],
        flops=1 << 20,
        place=HBM,
    )


def pack(queries, grad_out, heads_kv):
    tokens, heads_q, head_size = queries.shape
    array = jax.ShapeDtypeStruct
    return call(
        functools.partial(pack_kernel, heads_kv),
        "pack",
        (queries, grad_out),
        [array((heads_kv, tokens * 8, head_size), BF16)] * 2,
        [pltpu.VMEM((heads_kv, tokens, 16, head_size), BF16), pltpu.SemaphoreType.DMA((heads_kv,))],
        flops=1 << 20,
        place=HBM,
    )


def probs(sources, targets, prompt_k, prompt_v, qh, gh, own, blocks):
    own_k, own_v, bias, weight = own
    heads_kv, tokens, head_size = own_k.shape
    rows = tokens * heads_kv
    front = CAP * TILE
    unit = 2 * front * heads_kv
    before = tokens + len(sources) * front
    sizes = [max(start for target, start in targets if target == t) + unit for t in range(1 + max(targets)[0])]
    array = jax.ShapeDtypeStruct
    work = heads_kv * tokens * 8 * (before + tokens)
    return call(
        functools.partial(probs_kernel, sources, targets, heads_kv, head_size**-0.5),
        "probs",
        (prompt_k, prompt_v, own_k, own_v, qh, gh, bias, weight, *blocks),
        [array((size, head_size), BF16) for size in sizes]
        + [
            array((heads_kv, before + tokens, head_size), BF16),
            array((heads_kv, before + tokens, tokens * 8), BF16),
            array((heads_kv, tokens, tokens * 8), BF16),
        ],
        [
            pltpu.VMEM((heads_kv, before + tokens, head_size), BF16),
            pltpu.VMEM((before, tokens * 8), BF16),
            pltpu.VMEM((2, heads_kv, before, head_size), F32),
            pltpu.VMEM((rows, head_size), F32),
        ],
        flops=8 * work * head_size,
        transcendentals=work,
    )


def grads(qh, gh, kh, ds, p_own):
    heads_kv, tokens, _ = p_own.shape
    head_size = kh.shape[2]
    array = jax.ShapeDtypeStruct
    return call(
        functools.partial(grads_kernel, heads_kv),
        "grads",
        (qh, gh, kh, ds, p_own),
        [
            array((tokens, heads_kv * 8, head_size), BF16),
            array((tokens * heads_kv, head_size), F32),
            array((tokens * heads_kv, head_size), F32),
        ],
        [pltpu.VMEM((tokens * heads_kv, head_size), F32)],
        flops=4 * heads_kv * tokens * 8 * kh.shape[1] * head_size,
    )


def shift_route(distance, size):
    return [(i, i + distance) for i in range(size - distance)]


def back(route):
    return [(j, i) for i, j in route]


def added(*blocks):
    total = blocks[0].astype(F32)
    for block in blocks[1:]:
        total = total + block.astype(F32)
    return total


def after(array, *earlier):
    return lax.optimization_barrier((array, *earlier))[0]


def per_device(size, queries, keys, values, grad_out, parents, lengths):
    tokens, heads_kv, head_size = keys.shape
    rows = tokens * heads_kv
    one = CAP * TILE * heads_kv
    unit = 2 * one
    device = lax.axis_index("node")
    even = lax.rem(device, 2) == 0
    lower = lax.rem(device, 4) < 2
    keys = keys.reshape(rows, head_size)
    values = values.reshape(rows, head_size)
    strides = [2**i for i in range(2, size.bit_length()) if 2**i < size]
    top = strides[-1]
    neighbours = [(i, i ^ 1) for i in range(size)]
    far_route = shift_route(4, size)[1:]
    near_route = shift_route(2, size)
    six_route = [(1, 7)]
    small = size == W + 1
    if small:
        order = [(1, 3), (2, 2), (3, 1), (4, 4), (5, 5), (6, 6)]
        sources = [(0, rows), (1, rows), (2, 0), (3, 0), (2, unit), (4, 0)]
        targets = [(k % 2, rows + k // 2 * unit) for k in range(6)]
    else:
        order = [(k, k) for k in range(1, W + 1)]
        sources = [(0, 0), (1, rows), (0, unit), (2, 0), (0, 2 * unit), (1, rows + unit), (0, 3 * unit)]
        targets = [(1 - k % 2, rows + (k - 1) // 2 * unit) for k in range(1, W + 1)]

    def prompt_route(stride):
        return [(i + j, i + j + stride) for i in range(0, size, 2 * stride) for j in (0, 1)]

    def units(array, start, count):
        return [array[start + i * unit : start + (i + 1) * unit] for i in range(count)]

    head, held, *own = load(order, keys, values, parents, lengths, tokens)
    qh, gh = pack(queries, grad_out, heads_kv)
    keys_far = permuted(keys, [(0, top)])
    values_far = permuted(values, [(0, top + 1)])
    values_next = permuted(values, [(0, 1)])
    head = after(head, keys_far)
    far = permuted(head, far_route)
    held = added(held, values_next, values_far, keys_far).astype(BF16)
    for stride in reversed(strides[:-1]):
        held = added(held, permuted(held, prompt_route(stride))).astype(BF16)
    if small:
        six = permuted(head, six_route)
        held = after(held, far, six, qh)
        second = permuted(jnp.concatenate([held, head]), near_route)
        crossed = jnp.where(even, jnp.concatenate([head, far]), jnp.concatenate([far, six]))
        crossed = permuted(crossed, neighbours)
        held = jnp.where(lower, held, second[:rows])
        third = permuted(after(jnp.concatenate([held, second[rows:]]), crossed), neighbours)
        other = third[:rows]
        blocks = (third, second, crossed, far, six)
    else:
        second = permuted(jnp.concatenate([held, head, far]), near_route)
        held = jnp.where(lower, held, second[:rows])
        third = permuted(jnp.concatenate([head, second[rows : rows + unit], far, second[rows + unit :]]), shift_route(1, size))
        other = permuted(held, neighbours)
        blocks = (third, second, far)

    *sent, kh, ds, p_own = probs(
        sources, targets, jnp.where(even, held, other), jnp.where(even, other, held), qh, gh, own, blocks
    )
    grad_queries, dk, dv = grads(qh, gh, kh, ds, p_own)

    send, keep = sent[:2]
    two, four, six = units(keep, rows, 3)
    if small:
        third = permuted(send, neighbours)
        total = after(added(keep[:rows], third[:rows]).astype(BF16), dk)
        near, first, last = units(third, rows, 3)
        none = jnp.zeros_like(first)
        second = permuted(jnp.concatenate([total, added(two, near).astype(BF16)]), back(near_route))
        four = added(four, jnp.where(even, last, first))
        six = permuted(added(six, jnp.where(even, none, last)).astype(BF16), back(six_route))
        mine = added(jnp.where(even, first, none), second[rows:], six)
    else:
        zero, *third = units(permuted(send[rows:], back(shift_route(1, size))), 0, 4)
        total = added(keep[:rows], permuted(send[:rows], neighbours)).astype(BF16)
        two, four, six = (added(x, y).astype(BF16) for x, y in zip((two, four, six), third))
        second = permuted(jnp.concatenate([total, two, six]), back(near_route))
        mine = added(zero, second[rows : rows + unit])
        four = added(four, second[rows + unit :])
    four = permuted(four.astype(BF16), back(far_route))
    mine = added(mine, four)
    total = added(total, jnp.where(lower, second[:rows], jnp.zeros_like(total))).astype(BF16)
    if small:
        total = after(total, four, six)
    for stride in strides[:-1]:
        total = added(total, permuted(total, back(prompt_route(stride)))).astype(BF16)
    keys_far = permuted(total, [(top, 0)])
    values_far = permuted(total, [(top + 1, 0)])
    values_next = permuted(total, [(1, 0)])
    own = []
    for side, local, prompt in ((0, dk, added(total, keys_far)), (1, dv, added(values_far, values_next))):
        whole = local + jnp.where(device == 0, prompt, 0.0)
        own.append(whole.at[:one].add(mine[side * one : (side + 1) * one]).reshape(tokens, heads_kv, head_size))
    return grad_queries, own[0], own[1]


def solution(mesh):
    by_token = P(("leaf", "node"), "tensor", None)
    return jax.shard_map(
        functools.partial(per_device, mesh.shape["node"]),
        mesh=mesh,
        in_specs=(by_token, by_token, by_token, by_token, P("leaf"), P("leaf")),
        out_specs=(by_token, by_token, by_token),
        check_vma=False,
    )
```

```python
import functools
import math

import jax
import jax.numpy as jnp
from jax import lax
from jax.experimental import pallas as pl
from jax.experimental.pallas import tpu as pltpu
from jax.sharding import PartitionSpec as P

TILE = 16
TD = 8
CAP = 2
W = 7
CHUNK = 32
MASKED = -1e30
BF16 = jnp.bfloat16
F32 = jnp.float32


def permuted(block, route):
    return lax.ppermute(block, "node", route)


def column_limits(device, window, parents, lengths):
    cursor = parents[device * TD]
    need = [jnp.int32(0)] * (window + 1)
    for _ in range(W):
        owner = jnp.where(cursor < 0, -1, lax.div(jnp.maximum(cursor, 0), TD))
        distance = device - owner
        active = (owner >= 1) & (distance >= 1) & (distance <= W)
        depth = lax.rem(jnp.maximum(cursor, 0), TD) + 1
        for k in range(1, window + 1):
            need[k] = jnp.where(active & (distance == k), depth, need[k])
        cursor = jnp.where(active, parents[jnp.maximum(owner, 0) * TD], cursor)
    prompt = [jnp.where(device >= 1, lengths[t], 0) for t in range(TD)]
    behind = []
    for k in range(1, window + 1):
        owner = device - k
        seen = [(owner >= 1) & (c < need[k]) for c in range(CAP)]
        behind.append([jnp.where(seen[c], lengths[jnp.maximum(owner, 0) * TD + c], 0) for c in range(CAP)])
    return prompt, behind, [lengths[device * TD + t] for t in range(TD)]


def split_heads(block, heads_ref, start, count, heads_kv, wide):
    wide[: count * heads_kv] = block.astype(F32)
    for h in range(heads_kv):
        heads_ref[h, start : start + count] = wide[pl.ds(h, count, stride=heads_kv), :].astype(BF16)


def join_heads(blocks, count, heads_kv, wide):
    for h in range(heads_kv):
        wide[pl.ds(h, count, stride=heads_kv), :] = blocks[h]
    return wide[: count * heads_kv]


def load_kernel(order, heads_kv, *refs):
    sources, outs, scratch = refs[:4], refs[4:10], refs[10:]
    head, held, own_k, own_v, bias, weight = outs
    parents, lengths, keys, values, wide, arrived = scratch
    copies = [pltpu.make_async_copy(a, b, arrived.at[i]) for i, (a, b) in enumerate(zip(sources, scratch))]
    for copy in copies:
        copy.start()
    tokens = TD * TILE
    front = CAP * TILE * heads_kv
    device = lax.axis_index("node")
    for copy in copies:
        copy.wait()
    head[:front] = keys[:front]
    head[front:] = values[:front]
    held[...] = jnp.where(device == 0, keys[...], jnp.zeros_like(keys))
    split_heads(keys[...], own_k, 0, tokens, heads_kv, wide)
    split_heads(values[...], own_v, 0, tokens, heads_kv, wide)
    place = lax.broadcasted_iota(jnp.int32, (TILE, 128), 0)
    prompt, behind, own = column_limits(device, len(order), parents, lengths)
    even = lax.rem(device, 2) == 0
    limits = prompt
    for on_even, on_odd in order:
        limits = limits + [jnp.where(even, x, y) for x, y in zip(behind[on_even - 1], behind[on_odd - 1])]
    for t, limit in enumerate(limits + own):
        bias[t * TILE : (t + 1) * TILE] = jnp.where(place < limit, 0.0, MASKED)
    lane_place = lax.broadcasted_iota(jnp.int32, (8, 128), 1) // 8
    for t in range(TD):
        weight[:, t * 128 : (t + 1) * 128] = jnp.where(lane_place < lengths[device * TD + t], 1.0, 0.0)


def pack_kernel(heads_kv, q_ref, g_ref, qh, gh, blocks, arrived):
    tokens = TD * TILE
    copies = []
    for pair in range(heads_kv // 2):
        for ref, out in ((q_ref, qh), (g_ref, gh)):
            i = len(copies)
            copy = pltpu.make_async_copy(ref.at[:, pair * 16 : (pair + 1) * 16], blocks.at[i], arrived.at[i])
            copy.start()
            copies.append((copy, out, pair))
    for i, (copy, out, pair) in enumerate(copies):
        copy.wait()
        both = blocks[i].astype(F32)
        for part in range(2):
            out[2 * pair + part] = both[:, part * 8 : (part + 1) * 8].reshape(tokens * 8, 128).astype(BF16)


def probs_kernel(sources, targets, heads_kv, scale, *refs):
    prompt_k, prompt_v, own_k, own_v, qh, gh, bias, weight_ref = refs[:8]
    n_in = 1 + max(source for source, _ in sources)
    n_out = 1 + max(target for target, _ in targets)
    blocks = refs[8 : 8 + n_in]
    outs = refs[8 + n_in : 8 + n_in + n_out]
    kh, ds_ref, p_own, vh, p_ref, grads, wide = refs[8 + n_in + n_out :]
    window = len(sources)
    tokens = TD * TILE
    front = CAP * TILE
    before = tokens + window * front
    columns = CHUNK * 8
    device = lax.axis_index("node")

    for side, heads_ref, prompt, own in ((0, kh, prompt_k, own_k), (1, vh, prompt_v, own_v)):
        split_heads(prompt[...], heads_ref, 0, tokens, heads_kv, wide)
        for k, (source, start) in enumerate(sources):
            start += side * front * heads_kv
            block = blocks[source][start : start + front * heads_kv]
            split_heads(block, heads_ref, tokens + k * front, front, heads_kv, wide)
        heads_ref[:, before:] = own[...]

    column_token = lax.broadcasted_iota(jnp.int32, (CHUNK, columns), 1) // 8
    causal = jnp.where(lax.broadcasted_iota(jnp.int32, (CHUNK, columns), 0) <= column_token, 0.0, MASKED)
    for head in range(heads_kv):
        for c in range(tokens // CHUNK):
            rows = before + (c + 1) * CHUNK
            span = slice(c * columns, (c + 1) * columns)
            q = qh[head, span]
            g = gh[head, span]
            s = lax.dot_general(kh[head, :rows], q, (((1,), (1,)), ((), ())), preferred_element_type=F32)
            dp = lax.dot_general(vh[head, :rows], g, (((1,), (1,)), ((), ())), preferred_element_type=F32)
            s = s + jnp.concatenate([bias[:rows]] * (columns // 128), axis=1)
            s = jnp.concatenate([s[: rows - CHUNK], s[rows - CHUNK :] + causal], axis=0)
            top = jnp.max(s, axis=0, keepdims=True)
            e = jnp.exp2((s - top) * (scale * math.log2(math.e)))
            total = jnp.sum(e, axis=0, keepdims=True)
            p = e * (weight_ref[:1, span] / total)
            delta = jnp.sum(p * dp, axis=0, keepdims=True)
            ds_ref[head, :rows, span] = (p * (dp - delta) * scale).astype(BF16)
            p_ref[:, span] = p[:before].astype(BF16)
            p_own[head, : rows - before, span] = p[before:].astype(BF16)
        grads[0, head] = jnp.dot(ds_ref[head, :before], qh[head], preferred_element_type=F32)
        grads[1, head] = jnp.dot(p_ref[...], gh[head], preferred_element_type=F32)

    rows = tokens * heads_kv
    rows_front = front * heads_kv
    even = lax.rem(device, 2) == 0
    for side in range(2):
        dprompt = join_heads([grads[side, h, :tokens] for h in range(heads_kv)], tokens, heads_kv, wide).astype(BF16)
        kept = even if side == 0 else jnp.logical_not(even)

        @pl.when(kept)
        def _():
            outs[1][:rows] = dprompt

        @pl.when(jnp.logical_not(kept))
        def _():
            outs[0][:rows] = dprompt

        for k, (target, start) in enumerate(targets):
            span = slice(tokens + k * front, tokens + (k + 1) * front)
            block = join_heads([grads[side, h, span] for h in range(heads_kv)], front, heads_kv, wide).astype(BF16)
            start += side * rows_front
            outs[target][start : start + rows_front] = block


def grads_kernel(heads_kv, *refs):
    qh, gh, kh, ds_ref, p_own, dq_ref, dk_ref, dv_ref, wide = refs
    tokens = TD * TILE
    before = kh.shape[1] - tokens
    columns = CHUNK * 8
    dk = []
    dv = []
    for pair in range(heads_kv // 2):
        for c in range(tokens // CHUNK):
            rows = before + (c + 1) * CHUNK
            span = slice(c * columns, (c + 1) * columns)
            parts = []
            for head in (2 * pair, 2 * pair + 1):
                dq = lax.dot_general(
                    kh[head, :rows], ds_ref[head, :rows, span], (((0,), (0,)), ((), ())), preferred_element_type=F32
                )
                parts.append(dq.T.reshape(CHUNK, 8, 128))
            dq_ref[c * CHUNK : (c + 1) * CHUNK, pair * 16 : (pair + 1) * 16] = jnp.concatenate(parts, axis=1).astype(BF16)
        for head in (2 * pair, 2 * pair + 1):
            for source, factor, out in ((ds_ref.at[head, before:], qh, dk), (p_own.at[head], gh, dv)):
                pieces = []
                for c in range(tokens // CHUNK):
                    start = c * columns
                    pieces.append(
                        jnp.dot(
                            source[c * CHUNK : (c + 1) * CHUNK, start:], factor[head, start:], preferred_element_type=F32
                        )
                    )
                out.append(jnp.concatenate(pieces, axis=0))
    dk_ref[...] = join_heads(dk, tokens, heads_kv, wide)
    dv_ref[...] = join_heads(dv, tokens, heads_kv, wide)


VMEM = pl.BlockSpec(memory_space=pltpu.VMEM)


HBM = pl.BlockSpec(memory_space=pltpu.HBM)


def call(kernel, name, operands, outputs, scratch, flops, transcendentals=0, place=VMEM):
    sizes = [a.size * a.dtype.itemsize for a in (*operands, *outputs)]
    if place is HBM:
        operands = [pltpu.with_memory_space_constraint(a, pltpu.HBM) for a in operands]
    return pl.pallas_call(
        kernel,
        in_specs=[place] * len(operands),
        out_specs=[VMEM] * len(outputs),
        out_shape=outputs,
        scratch_shapes=scratch,
        compiler_params=pltpu.CompilerParams(vmem_limit_bytes=28 * 1024 * 1024),
        cost_estimate=pl.CostEstimate(flops=flops, bytes_accessed=sum(sizes), transcendentals=transcendentals),
        name=name,
    )(*operands)


def load(order, keys, values, parents, lengths, tokens):
    rows, head_size = keys.shape
    heads_kv = rows // tokens
    array = jax.ShapeDtypeStruct
    return call(
        functools.partial(load_kernel, order, heads_kv),
        "load",
        (parents, lengths, keys, values),
        [array((2 * CAP * TILE * heads_kv, head_size), BF16), array((rows, head_size), BF16)]
        + [array((heads_kv, tokens, head_size), BF16)] * 2
        + [array((2 * tokens + len(order) * CAP * TILE, 128), F32), array((8, tokens * 8), F32)],
        [pltpu.SMEM(parents.shape, jnp.int32), pltpu.SMEM(lengths.shape, jnp.int32)]
        + [pltpu.VMEM((rows, head_size), BF16)] * 2
        + [pltpu.VMEM((rows, head_size), F32), pltpu.SemaphoreType.DMA((4,))],
        flops=1 << 20,
        place=HBM,
    )


def pack(queries, grad_out, heads_kv):
    tokens, heads_q, head_size = queries.shape
    array = jax.ShapeDtypeStruct
    return call(
        functools.partial(pack_kernel, heads_kv),
        "pack",
        (queries, grad_out),
        [array((heads_kv, tokens * 8, head_size), BF16)] * 2,
        [pltpu.VMEM((heads_kv, tokens, 16, head_size), BF16), pltpu.SemaphoreType.DMA((heads_kv,))],
        flops=1 << 20,
        place=HBM,
    )


def probs(sources, targets, prompt_k, prompt_v, qh, gh, own, blocks):
    own_k, own_v, bias, weight = own
    heads_kv, tokens, head_size = own_k.shape
    rows = tokens * heads_kv
    front = CAP * TILE
    unit = 2 * front * heads_kv
    before = tokens + len(sources) * front
    sizes = [max(start for target, start in targets if target == t) + unit for t in range(1 + max(targets)[0])]
    array = jax.ShapeDtypeStruct
    work = heads_kv * tokens * 8 * (before + tokens)
    return call(
        functools.partial(probs_kernel, sources, targets, heads_kv, head_size**-0.5),
        "probs",
        (prompt_k, prompt_v, own_k, own_v, qh, gh, bias, weight, *blocks),
        [array((size, head_size), BF16) for size in sizes]
        + [
            array((heads_kv, before + tokens, head_size), BF16),
            array((heads_kv, before + tokens, tokens * 8), BF16),
            array((heads_kv, tokens, tokens * 8), BF16),
        ],
        [
            pltpu.VMEM((heads_kv, before + tokens, head_size), BF16),
            pltpu.VMEM((before, tokens * 8), BF16),
            pltpu.VMEM((2, heads_kv, before, head_size), F32),
            pltpu.VMEM((rows, head_size), F32),
        ],
        flops=8 * work * head_size,
        transcendentals=work,
    )


def grads(qh, gh, kh, ds, p_own):
    heads_kv, tokens, _ = p_own.shape
    head_size = kh.shape[2]
    array = jax.ShapeDtypeStruct
    return call(
        functools.partial(grads_kernel, heads_kv),
        "grads",
        (qh, gh, kh, ds, p_own),
        [
            array((tokens, heads_kv * 8, head_size), BF16),
            array((tokens * heads_kv, head_size), F32),
            array((tokens * heads_kv, head_size), F32),
        ],
        [pltpu.VMEM((tokens * heads_kv, head_size), F32)],
        flops=4 * heads_kv * tokens * 8 * kh.shape[1] * head_size,
    )


def shift_route(distance, size):
    return [(i, i + distance) for i in range(size - distance)]


def back(route):
    return [(j, i) for i, j in route]


def added(*blocks):
    total = blocks[0].astype(F32)
    for block in blocks[1:]:
        total = total + block.astype(F32)
    return total


def after(array, *earlier):
    return lax.optimization_barrier((array, *earlier))[0]


def per_device(size, queries, keys, values, grad_out, parents, lengths):
    tokens, heads_kv, head_size = keys.shape
    rows = tokens * heads_kv
    one = CAP * TILE * heads_kv
    unit = 2 * one
    device = lax.axis_index("node")
    even = lax.rem(device, 2) == 0
    lower = lax.rem(device, 4) < 2
    keys = keys.reshape(rows, head_size)
    values = values.reshape(rows, head_size)
    strides = [2**i for i in range(2, size.bit_length()) if 2**i < size]
    top = strides[-1]
    neighbours = [(i, i ^ 1) for i in range(size)]
    far_route = shift_route(4, size)[1:]
    near_route = shift_route(2, size)
    six_route = [(1, 7)]
    small = size == W + 1
    if small:
        order = [(1, 3), (2, 2), (3, 1), (4, 4), (5, 5), (6, 6)]
        sources = [(0, rows), (1, rows), (2, 0), (3, 0), (2, unit), (4, 0)]
        targets = [(k % 2, rows + k // 2 * unit) for k in range(6)]
    else:
        order = [(k, k) for k in range(1, W + 1)]
        sources = [(0, 0), (1, rows), (0, unit), (2, 0), (0, 2 * unit), (1, rows + unit), (0, 3 * unit)]
        targets = [(1 - k % 2, rows + (k - 1) // 2 * unit) for k in range(1, W + 1)]

    def prompt_route(stride):
        return [(i + j, i + j + stride) for i in range(0, size, 2 * stride) for j in (0, 1)]

    def units(array, start, count):
        return [array[start + i * unit : start + (i + 1) * unit] for i in range(count)]

    head, held, *own = load(order, keys, values, parents, lengths, tokens)
    keys_far = permuted(keys, [(0, top)])
    values_far = permuted(values, [(0, top + 1)])
    values_next = permuted(values, [(0, 1)])
    head, queries = lax.optimization_barrier((head, queries, keys_far))[:2]
    qh, gh = pack(queries, grad_out, heads_kv)
    far = permuted(head, far_route)
    held = added(held, values_next, values_far, keys_far).astype(BF16)
    for stride in reversed(strides[:-1]):
        held = added(held, permuted(held, prompt_route(stride))).astype(BF16)
    if small:
        six = permuted(head, six_route)
        held = after(held, far, six, qh)
        second = permuted(jnp.concatenate([held, head]), near_route)
        crossed = jnp.where(even, jnp.concatenate([head, far]), jnp.concatenate([far, six]))
        crossed = permuted(crossed, neighbours)
        held = jnp.where(lower, held, second[:rows])
        third = permuted(after(jnp.concatenate([held, second[rows:]]), crossed), neighbours)
        other = third[:rows]
        blocks = (third, second, crossed, far, six)
    else:
        second = permuted(jnp.concatenate([held, head, far]), near_route)
        held = jnp.where(lower, held, second[:rows])
        third = permuted(jnp.concatenate([head, second[rows : rows + unit], far, second[rows + unit :]]), shift_route(1, size))
        other = permuted(held, neighbours)
        blocks = (third, second, far)

    *sent, kh, ds, p_own = probs(
        sources, targets, jnp.where(even, held, other), jnp.where(even, other, held), qh, gh, own, blocks
    )
    grad_queries, dk, dv = grads(qh, gh, kh, ds, p_own)

    send, keep = sent[:2]
    two, four, six = units(keep, rows, 3)
    if small:
        third = permuted(send, neighbours)
        total = after(added(keep[:rows], third[:rows]).astype(BF16), dk)
        near, first, last = units(third, rows, 3)
        none = jnp.zeros_like(first)
        second = permuted(jnp.concatenate([total, added(two, near).astype(BF16)]), back(near_route))
        four = added(four, jnp.where(even, last, first))
        six = permuted(added(six, jnp.where(even, none, last)).astype(BF16), back(six_route))
        mine = added(jnp.where(even, first, none), second[rows:], six)
    else:
        zero, *third = units(permuted(send[rows:], back(shift_route(1, size))), 0, 4)
        total = added(keep[:rows], permuted(send[:rows], neighbours)).astype(BF16)
        two, four, six = (added(x, y).astype(BF16) for x, y in zip((two, four, six), third))
        second = permuted(jnp.concatenate([total, two, six]), back(near_route))
        mine = added(zero, second[rows : rows + unit])
        four = added(four, second[rows + unit :])
    four = permuted(four.astype(BF16), back(far_route))
    mine = added(mine, four)
    total = added(total, jnp.where(lower, second[:rows], jnp.zeros_like(total))).astype(BF16)
    for stride in strides[:-1]:
        total = added(total, permuted(total, back(prompt_route(stride)))).astype(BF16)
    if small:
        total = after(total, four, six)
    keys_far = permuted(total, [(top, 0)])
    values_far = permuted(total, [(top + 1, 0)])
    values_next = permuted(total, [(1, 0)])
    prompt_v, prompt_k = lax.optimization_barrier((added(values_next, values_far), added(total, keys_far)))
    own = []
    for side, local, prompt in ((0, dk, prompt_k), (1, dv, prompt_v)):
        whole = local + jnp.where(device == 0, prompt, 0.0)
        own.append(whole.at[:one].add(mine[side * one : (side + 1) * one]).reshape(tokens, heads_kv, head_size))
    return grad_queries, own[0], own[1]


def solution(mesh):
    by_token = P(("leaf", "node"), "tensor", None)
    return jax.shard_map(
        functools.partial(per_device, mesh.shape["node"]),
        mesh=mesh,
        in_specs=(by_token, by_token, by_token, by_token, P("leaf"), P("leaf")),
        out_specs=(by_token, by_token, by_token),
        check_vma=False,
    )
```

```python
import functools
import math

import jax
import jax.numpy as jnp
from jax import lax
from jax.experimental import pallas as pl
from jax.experimental.pallas import tpu as pltpu
from jax.sharding import PartitionSpec as P

TILE = 16
TD = 8
CAP = 2
W = 7
CHUNK = 32
MASKED = -1e30
BF16 = jnp.bfloat16
F32 = jnp.float32


def permuted(block, route):
    return lax.ppermute(block, "node", route)


def column_limits(device, window, parents, lengths):
    cursor = parents[device * TD]
    need = [jnp.int32(0)] * (window + 1)
    for _ in range(W):
        owner = jnp.where(cursor < 0, -1, lax.div(jnp.maximum(cursor, 0), TD))
        distance = device - owner
        active = (owner >= 1) & (distance >= 1) & (distance <= W)
        depth = lax.rem(jnp.maximum(cursor, 0), TD) + 1
        for k in range(1, window + 1):
            need[k] = jnp.where(active & (distance == k), depth, need[k])
        cursor = jnp.where(active, parents[jnp.maximum(owner, 0) * TD], cursor)
    prompt = [jnp.where(device >= 1, lengths[t], 0) for t in range(TD)]
    behind = []
    for k in range(1, window + 1):
        owner = device - k
        seen = [(owner >= 1) & (c < need[k]) for c in range(CAP)]
        behind.append([jnp.where(seen[c], lengths[jnp.maximum(owner, 0) * TD + c], 0) for c in range(CAP)])
    return prompt, behind, [lengths[device * TD + t] for t in range(TD)]


def split_heads(block, heads_ref, start, count, heads_kv, wide):
    wide[: count * heads_kv] = block.astype(F32)
    for h in range(heads_kv):
        heads_ref[h, start : start + count] = wide[pl.ds(h, count, stride=heads_kv), :].astype(BF16)


def join_heads(blocks, count, heads_kv, wide):
    for h in range(heads_kv):
        wide[pl.ds(h, count, stride=heads_kv), :] = blocks[h]
    return wide[: count * heads_kv]


def load_kernel(order, heads_kv, *refs):
    sources, outs, scratch = refs[:4], refs[4:10], refs[10:]
    head, held, own_k, own_v, bias, weight = outs
    parents, lengths, keys, values, wide, arrived = scratch
    copies = [pltpu.make_async_copy(a, b, arrived.at[i]) for i, (a, b) in enumerate(zip(sources, scratch))]
    for copy in copies:
        copy.start()
    tokens = TD * TILE
    front = CAP * TILE * heads_kv
    device = lax.axis_index("node")
    for copy in copies:
        copy.wait()
    head[:front] = keys[:front]
    head[front:] = values[:front]
    held[...] = jnp.where(device == 0, keys[...], jnp.zeros_like(keys))
    split_heads(keys[...], own_k, 0, tokens, heads_kv, wide)
    split_heads(values[...], own_v, 0, tokens, heads_kv, wide)
    place = lax.broadcasted_iota(jnp.int32, (TILE, 128), 0)
    prompt, behind, own = column_limits(device, len(order), parents, lengths)
    even = lax.rem(device, 2) == 0
    limits = prompt
    for on_even, on_odd in order:
        limits = limits + [jnp.where(even, x, y) for x, y in zip(behind[on_even - 1], behind[on_odd - 1])]
    for t, limit in enumerate(limits + own):
        bias[t * TILE : (t + 1) * TILE] = jnp.where(place < limit, 0.0, MASKED)
    lane_place = lax.broadcasted_iota(jnp.int32, (8, 128), 1) // 8
    for t in range(TD):
        weight[:, t * 128 : (t + 1) * 128] = jnp.where(lane_place < lengths[device * TD + t], 1.0, 0.0)


def pack_kernel(heads_kv, q_ref, g_ref, qh, gh, blocks, arrived):
    tokens = TD * TILE
    copies = []
    for pair in range(heads_kv // 2):
        for ref, out in ((q_ref, qh), (g_ref, gh)):
            i = len(copies)
            copy = pltpu.make_async_copy(ref.at[:, pair * 16 : (pair + 1) * 16], blocks.at[i], arrived.at[i])
            copy.start()
            copies.append((copy, out, pair))
    for i, (copy, out, pair) in enumerate(copies):
        copy.wait()
        both = blocks[i].astype(F32)
        for part in range(2):
            out[2 * pair + part] = both[:, part * 8 : (part + 1) * 8].reshape(tokens * 8, 128).astype(BF16)


def probs_kernel(sources, targets, heads_kv, scale, *refs):
    prompt_k, prompt_v, own_k, own_v, qh, gh, bias, weight_ref = refs[:8]
    n_in = 1 + max(source for source, _ in sources)
    n_out = 1 + max(target for target, _ in targets)
    blocks = refs[8 : 8 + n_in]
    outs = refs[8 + n_in : 8 + n_in + n_out]
    kh, ds_ref, p_own, vh, p_ref, grads, wide = refs[8 + n_in + n_out :]
    window = len(sources)
    tokens = TD * TILE
    front = CAP * TILE
    before = tokens + window * front
    columns = CHUNK * 8
    device = lax.axis_index("node")

    for side, heads_ref, prompt, own in ((0, kh, prompt_k, own_k), (1, vh, prompt_v, own_v)):
        split_heads(prompt[...], heads_ref, 0, tokens, heads_kv, wide)
        for k, (source, start) in enumerate(sources):
            start += side * front * heads_kv
            block = blocks[source][start : start + front * heads_kv]
            split_heads(block, heads_ref, tokens + k * front, front, heads_kv, wide)
        heads_ref[:, before:] = own[...]

    column_token = lax.broadcasted_iota(jnp.int32, (CHUNK, columns), 1) // 8
    causal = jnp.where(lax.broadcasted_iota(jnp.int32, (CHUNK, columns), 0) <= column_token, 0.0, MASKED)
    for head in range(heads_kv):
        for c in range(tokens // CHUNK):
            rows = before + (c + 1) * CHUNK
            span = slice(c * columns, (c + 1) * columns)
            q = qh[head, span]
            g = gh[head, span]
            s = lax.dot_general(kh[head, :rows], q, (((1,), (1,)), ((), ())), preferred_element_type=F32)
            dp = lax.dot_general(vh[head, :rows], g, (((1,), (1,)), ((), ())), preferred_element_type=F32)
            s = s + jnp.concatenate([bias[:rows]] * (columns // 128), axis=1)
            s = jnp.concatenate([s[: rows - CHUNK], s[rows - CHUNK :] + causal], axis=0)
            top = jnp.max(s, axis=0, keepdims=True)
            e = jnp.exp2((s - top) * (scale * math.log2(math.e)))
            total = jnp.sum(e, axis=0, keepdims=True)
            p = e * (weight_ref[:1, span] / total)
            delta = jnp.sum(p * dp, axis=0, keepdims=True)
            ds_ref[head, :rows, span] = (p * (dp - delta) * scale).astype(BF16)
            p_ref[:, span] = p[:before].astype(BF16)
            p_own[head, : rows - before, span] = p[before:].astype(BF16)
        grads[0, head] = jnp.dot(ds_ref[head, :before], qh[head], preferred_element_type=F32)
        grads[1, head] = jnp.dot(p_ref[...], gh[head], preferred_element_type=F32)

    rows = tokens * heads_kv
    rows_front = front * heads_kv
    even = lax.rem(device, 2) == 0
    for side in range(2):
        dprompt = join_heads([grads[side, h, :tokens] for h in range(heads_kv)], tokens, heads_kv, wide).astype(BF16)
        kept = even if side == 0 else jnp.logical_not(even)

        @pl.when(kept)
        def _():
            outs[1][:rows] = dprompt

        @pl.when(jnp.logical_not(kept))
        def _():
            outs[0][:rows] = dprompt

        for k, (target, start) in enumerate(targets):
            span = slice(tokens + k * front, tokens + (k + 1) * front)
            block = join_heads([grads[side, h, span] for h in range(heads_kv)], front, heads_kv, wide).astype(BF16)
            start += side * rows_front
            outs[target][start : start + rows_front] = block


def grads_kernel(heads_kv, *refs):
    qh, gh, kh, ds_ref, p_own, dq_ref, dk_ref, dv_ref, wide = refs
    tokens = TD * TILE
    before = kh.shape[1] - tokens
    columns = CHUNK * 8
    dk = []
    dv = []
    for pair in range(heads_kv // 2):
        for c in range(tokens // CHUNK):
            rows = before + (c + 1) * CHUNK
            span = slice(c * columns, (c + 1) * columns)
            parts = []
            for head in (2 * pair, 2 * pair + 1):
                dq = lax.dot_general(
                    kh[head, :rows], ds_ref[head, :rows, span], (((0,), (0,)), ((), ())), preferred_element_type=F32
                )
                parts.append(dq.T.reshape(CHUNK, 8, 128))
            dq_ref[c * CHUNK : (c + 1) * CHUNK, pair * 16 : (pair + 1) * 16] = jnp.concatenate(parts, axis=1).astype(BF16)
        for head in (2 * pair, 2 * pair + 1):
            for source, factor, out in ((ds_ref.at[head, before:], qh, dk), (p_own.at[head], gh, dv)):
                pieces = []
                for c in range(tokens // CHUNK):
                    start = c * columns
                    pieces.append(
                        jnp.dot(
                            source[c * CHUNK : (c + 1) * CHUNK, start:], factor[head, start:], preferred_element_type=F32
                        )
                    )
                out.append(jnp.concatenate(pieces, axis=0))
    dk_ref[...] = join_heads(dk, tokens, heads_kv, wide)
    dv_ref[...] = join_heads(dv, tokens, heads_kv, wide)


VMEM = pl.BlockSpec(memory_space=pltpu.VMEM)


HBM = pl.BlockSpec(memory_space=pltpu.HBM)


def call(kernel, name, operands, outputs, scratch, flops, transcendentals=0, place=VMEM):
    sizes = [a.size * a.dtype.itemsize for a in (*operands, *outputs)]
    if place is HBM:
        operands = [pltpu.with_memory_space_constraint(a, pltpu.HBM) for a in operands]
    return pl.pallas_call(
        kernel,
        in_specs=[place] * len(operands),
        out_specs=[VMEM] * len(outputs),
        out_shape=outputs,
        scratch_shapes=scratch,
        compiler_params=pltpu.CompilerParams(vmem_limit_bytes=28 * 1024 * 1024),
        cost_estimate=pl.CostEstimate(flops=flops, bytes_accessed=sum(sizes), transcendentals=transcendentals),
        name=name,
    )(*operands)


def load(order, keys, values, parents, lengths, tokens):
    rows, head_size = keys.shape
    heads_kv = rows // tokens
    array = jax.ShapeDtypeStruct
    return call(
        functools.partial(load_kernel, order, heads_kv),
        "load",
        (parents, lengths, keys, values),
        [array((2 * CAP * TILE * heads_kv, head_size), BF16), array((rows, head_size), BF16)]
        + [array((heads_kv, tokens, head_size), BF16)] * 2
        + [array((2 * tokens + len(order) * CAP * TILE, 128), F32), array((8, tokens * 8), F32)],
        [pltpu.SMEM(parents.shape, jnp.int32), pltpu.SMEM(lengths.shape, jnp.int32)]
        + [pltpu.VMEM((rows, head_size), BF16)] * 2
        + [pltpu.VMEM((rows, head_size), F32), pltpu.SemaphoreType.DMA((4,))],
        flops=1 << 20,
        place=HBM,
    )


def pack(queries, grad_out, heads_kv):
    tokens, heads_q, head_size = queries.shape
    array = jax.ShapeDtypeStruct
    return call(
        functools.partial(pack_kernel, heads_kv),
        "pack",
        (queries, grad_out),
        [array((heads_kv, tokens * 8, head_size), BF16)] * 2,
        [pltpu.VMEM((heads_kv, tokens, 16, head_size), BF16), pltpu.SemaphoreType.DMA((heads_kv,))],
        flops=1 << 20,
        place=HBM,
    )


def probs(sources, targets, prompt_k, prompt_v, qh, gh, own, blocks):
    own_k, own_v, bias, weight = own
    heads_kv, tokens, head_size = own_k.shape
    rows = tokens * heads_kv
    front = CAP * TILE
    unit = 2 * front * heads_kv
    before = tokens + len(sources) * front
    sizes = [max(start for target, start in targets if target == t) + unit for t in range(1 + max(targets)[0])]
    array = jax.ShapeDtypeStruct
    work = heads_kv * tokens * 8 * (before + tokens)
    return call(
        functools.partial(probs_kernel, sources, targets, heads_kv, head_size**-0.5),
        "probs",
        (prompt_k, prompt_v, own_k, own_v, qh, gh, bias, weight, *blocks),
        [array((size, head_size), BF16) for size in sizes]
        + [
            array((heads_kv, before + tokens, head_size), BF16),
            array((heads_kv, before + tokens, tokens * 8), BF16),
            array((heads_kv, tokens, tokens * 8), BF16),
        ],
        [
            pltpu.VMEM((heads_kv, before + tokens, head_size), BF16),
            pltpu.VMEM((before, tokens * 8), BF16),
            pltpu.VMEM((2, heads_kv, before, head_size), F32),
            pltpu.VMEM((rows, head_size), F32),
        ],
        flops=8 * work * head_size,
        transcendentals=work,
    )


def grads(qh, gh, kh, ds, p_own):
    heads_kv, tokens, _ = p_own.shape
    head_size = kh.shape[2]
    array = jax.ShapeDtypeStruct
    return call(
        functools.partial(grads_kernel, heads_kv),
        "grads",
        (qh, gh, kh, ds, p_own),
        [
            array((tokens, heads_kv * 8, head_size), BF16),
            array((tokens * heads_kv, head_size), F32),
            array((tokens * heads_kv, head_size), F32),
        ],
        [pltpu.VMEM((tokens * heads_kv, head_size), F32)],
        flops=4 * heads_kv * tokens * 8 * kh.shape[1] * head_size,
    )


def shift_route(distance, size):
    return [(i, i + distance) for i in range(size - distance)]


def back(route):
    return [(j, i) for i, j in route]


def added(*blocks):
    total = blocks[0].astype(F32)
    for block in blocks[1:]:
        total = total + block.astype(F32)
    return total


def after(array, *earlier):
    return lax.optimization_barrier((array, *earlier))[0]


def units(array, start, unit, count):
    return [array[start + i * unit : start + (i + 1) * unit] for i in range(count)]


def prompt_route(stride, size):
    return [(i + j, i + j + stride) for i in range(0, size, 2 * stride) for j in (0, 1)]


def collect(size, unit, rows, device, keys, values, head, held, queries):
    even = lax.rem(device, 2) == 0
    lower = lax.rem(device, 4) < 2
    neighbours = [(i, i ^ 1) for i in range(size)]
    far_route = shift_route(4, size)[1:]
    near_route = shift_route(2, size)
    if size == W + 1:
        keys_far = permuted(keys, [(0, 4)])
        values_far = permuted(values, [(0, 5)])
        values_next = permuted(values, [(0, 1)])
        head, queries = lax.optimization_barrier((head, queries, keys_far))[:2]
        far = permuted(head, far_route)
        six = permuted(head, [(1, 7)])
        held = after(added(held, values_far, values_next, keys_far).astype(BF16), far, six)
        second = permuted(jnp.concatenate([held, head]), near_route)
        crossed = jnp.where(even, jnp.concatenate([head, far]), jnp.concatenate([far, six]))
        crossed = permuted(crossed, neighbours)
        held = jnp.where(lower, held, second[:rows])
        third = permuted(after(jnp.concatenate([held, second[rows:]]), crossed), neighbours)
        sources = [(0, rows), (1, rows), (2, 0), (3, 0), (2, unit), (4, 0)]
        return held, third[:rows], sources, (third, second, crossed, far, six), queries
    strides = [2**i for i in range(2, size.bit_length()) if 2**i < size]
    top = strides[-1]
    keys_far = permuted(keys, [(0, top)])
    values_far = permuted(values, [(0, top + 1)])
    values_next = permuted(values, [(0, 1)])
    far = permuted(head, far_route)
    held = added(held, values_next, values_far, keys_far).astype(BF16)
    for stride in reversed(strides[:-1]):
        held = added(held, permuted(held, prompt_route(stride, size))).astype(BF16)
    second = permuted(jnp.concatenate([held, head, far]), near_route)
    held = jnp.where(lower, held, second[:rows])
    near, six = units(second, rows, unit, 2)
    third = permuted(jnp.concatenate([head, near, far, six]), shift_route(1, size))
    other = permuted(held, neighbours)
    sources = [(0, 0), (1, rows), (0, unit), (2, 0), (0, 2 * unit), (1, rows + unit), (0, 3 * unit)]
    return held, other, sources, (third, second, far), queries


def give_back(size, unit, rows, device, send, keep, ready):
    even = lax.rem(device, 2) == 0
    lower = lax.rem(device, 4) < 2
    neighbours = [(i, i ^ 1) for i in range(size)]
    far_route = back(shift_route(4, size)[1:])
    two, four, six = units(keep, rows, unit, 3)
    if size == W + 1:
        third = permuted(send, neighbours)
        total = after(added(keep[:rows], third[:rows]).astype(BF16), ready)
        near, first, last = units(third, rows, unit, 3)
        none = jnp.zeros_like(first)
        parts = [permuted(total, [(j, 0), (j + 1, 1)]) for j in range(2, size, 2)]
        two = permuted(added(two, near).astype(BF16), back(shift_route(2, size)[1:]))
        four = permuted(added(four, jnp.where(even, last, first)).astype(BF16), far_route)
        six = permuted(added(six, jnp.where(even, none, last)).astype(BF16), [(7, 1)])
        total = added(total, *parts).astype(BF16)
        mine = added(jnp.where(even, first, none), two, four, six)
        return total, permuted(total, [(1, 0)]).astype(F32), mine
    strides = [2**i for i in range(2, size.bit_length()) if 2**i < size]
    top = strides[-1]
    zero, *third = units(permuted(send[rows:], back(shift_route(1, size))), 0, unit, 4)
    total = added(keep[:rows], permuted(send[:rows], neighbours)).astype(BF16)
    two, four, six = (added(x, y).astype(BF16) for x, y in zip((two, four, six), third))
    second = permuted(jnp.concatenate([total, two, six]), back(shift_route(2, size)))
    four = added(four, second[rows + unit :])
    mine = added(zero, second[rows : rows + unit], permuted(four.astype(BF16), far_route))
    total = added(total, jnp.where(lower, second[:rows], jnp.zeros_like(total))).astype(BF16)
    for stride in strides[:-1]:
        total = added(total, permuted(total, back(prompt_route(stride, size)))).astype(BF16)
    keys_far = permuted(total, [(top, 0)])
    values_far = permuted(total, [(top + 1, 0)])
    values_next = permuted(total, [(1, 0)])
    return added(total, keys_far), added(values_next, values_far), mine


def per_device(size, queries, keys, values, grad_out, parents, lengths):
    tokens, heads_kv, head_size = keys.shape
    rows = tokens * heads_kv
    one = CAP * TILE * heads_kv
    unit = 2 * one
    window = min(W, size - 2)
    device = lax.axis_index("node")
    even = lax.rem(device, 2) == 0
    keys = keys.reshape(rows, head_size)
    values = values.reshape(rows, head_size)

    order = [(k, k) for k in range(1, window + 1)]
    if size == W + 1:
        order[0], order[2] = (1, 3), (3, 1)
    head, held, *own = load(order, keys, values, parents, lengths, tokens)
    held, other, sources, blocks, queries = collect(size, unit, rows, device, keys, values, head, held, queries)
    qh, gh = pack(queries, grad_out, heads_kv)
    prompt_k, prompt_v = jnp.where(even, held, other), jnp.where(even, other, held)
    targets = [(1 - k % 2, rows + (k - 1) // 2 * unit) for k in range(1, window + 1)]
    send, keep, kh, ds, p_own = probs(sources, targets, prompt_k, prompt_v, qh, gh, own, blocks)
    grad_queries, dk, dv = grads(qh, gh, kh, ds, p_own)
    prompt_k, prompt_v, mine = give_back(size, unit, rows, device, send, keep, dk)
    own = []
    for side, local, prompt in ((0, dk, prompt_k), (1, dv, prompt_v)):
        whole = local + jnp.where(device == 0, prompt.astype(F32), 0.0)
        own.append(whole.at[:one].add(mine[side * one : (side + 1) * one]).reshape(tokens, heads_kv, head_size))
    return grad_queries, own[0], own[1]


def solution(mesh):
    by_token = P(("leaf", "node"), "tensor", None)
    return jax.shard_map(
        functools.partial(per_device, mesh.shape["node"]),
        mesh=mesh,
        in_specs=(by_token, by_token, by_token, by_token, P("leaf"), P("leaf")),
        out_specs=(by_token, by_token, by_token),
        check_vma=False,
    )
```

```python
import functools
import math

import jax
import jax.numpy as jnp
from jax import lax
from jax.experimental import pallas as pl
from jax.experimental.pallas import tpu as pltpu
from jax.sharding import PartitionSpec as P

TILE = 16
TD = 8
CAP = 2
W = 7
CHUNK = 32
MASKED = -1e30
BF16 = jnp.bfloat16
F32 = jnp.float32


def permuted(block, route):
    return lax.ppermute(block, "node", route)


def column_limits(device, window, parents, lengths):
    cursor = parents[device * TD]
    need = [jnp.int32(0)] * (window + 1)
    for _ in range(W):
        owner = jnp.where(cursor < 0, -1, lax.div(jnp.maximum(cursor, 0), TD))
        distance = device - owner
        active = (owner >= 1) & (distance >= 1) & (distance <= W)
        depth = lax.rem(jnp.maximum(cursor, 0), TD) + 1
        for k in range(1, window + 1):
            need[k] = jnp.where(active & (distance == k), depth, need[k])
        cursor = jnp.where(active, parents[jnp.maximum(owner, 0) * TD], cursor)
    prompt = [jnp.where(device >= 1, lengths[t], 0) for t in range(TD)]
    behind = []
    for k in range(1, window + 1):
        owner = device - k
        seen = [(owner >= 1) & (c < need[k]) for c in range(CAP)]
        behind.append([jnp.where(seen[c], lengths[jnp.maximum(owner, 0) * TD + c], 0) for c in range(CAP)])
    return prompt, behind, [lengths[device * TD + t] for t in range(TD)]


def split_heads(block, heads_ref, start, count, heads_kv, wide):
    wide[: count * heads_kv] = block.astype(F32)
    for h in range(heads_kv):
        heads_ref[h, start : start + count] = wide[pl.ds(h, count, stride=heads_kv), :].astype(BF16)


def join_heads(blocks, count, heads_kv, wide):
    for h in range(heads_kv):
        wide[pl.ds(h, count, stride=heads_kv), :] = blocks[h]
    return wide[: count * heads_kv]


def load_kernel(order, heads_kv, *refs):
    sources, outs, scratch = refs[:4], refs[4:10], refs[10:]
    head, held, own_k, own_v, bias, weight = outs
    parents, lengths, keys, values, wide, arrived = scratch
    copies = [pltpu.make_async_copy(a, b, arrived.at[i]) for i, (a, b) in enumerate(zip(sources, scratch))]
    for copy in copies:
        copy.start()
    tokens = TD * TILE
    front = CAP * TILE * heads_kv
    device = lax.axis_index("node")
    for copy in copies:
        copy.wait()
    head[:front] = keys[:front]
    head[front:] = values[:front]
    held[...] = jnp.where(device == 0, keys[...], jnp.zeros_like(keys))
    split_heads(keys[...], own_k, 0, tokens, heads_kv, wide)
    split_heads(values[...], own_v, 0, tokens, heads_kv, wide)
    place = lax.broadcasted_iota(jnp.int32, (TILE, 128), 0)
    prompt, behind, own = column_limits(device, len(order), parents, lengths)
    even = lax.rem(device, 2) == 0
    limits = prompt
    for on_even, on_odd in order:
        limits = limits + [jnp.where(even, x, y) for x, y in zip(behind[on_even - 1], behind[on_odd - 1])]
    for t, limit in enumerate(limits + own):
        bias[t * TILE : (t + 1) * TILE] = jnp.where(place < limit, 0.0, MASKED)
    lane_place = lax.broadcasted_iota(jnp.int32, (8, 128), 1) // 8
    for t in range(TD):
        weight[:, t * 128 : (t + 1) * 128] = jnp.where(lane_place < lengths[device * TD + t], 1.0, 0.0)


def pack_kernel(heads_kv, q_ref, g_ref, qh, gh, blocks, arrived):
    tokens = TD * TILE
    copies = []
    for pair in range(heads_kv // 2):
        for ref, out in ((q_ref, qh), (g_ref, gh)):
            i = len(copies)
            copy = pltpu.make_async_copy(ref.at[:, pair * 16 : (pair + 1) * 16], blocks.at[i], arrived.at[i])
            copy.start()
            copies.append((copy, out, pair))
    for i, (copy, out, pair) in enumerate(copies):
        copy.wait()
        both = blocks[i].astype(F32)
        for part in range(2):
            out[2 * pair + part] = both[:, part * 8 : (part + 1) * 8].reshape(tokens * 8, 128).astype(BF16)


def probs_kernel(sources, targets, heads_kv, scale, *refs):
    prompt_k, prompt_v, own_k, own_v, qh, gh, bias, weight_ref = refs[:8]
    n_in = 1 + max(source for source, _ in sources)
    n_out = 1 + max(target for target, _ in targets)
    blocks = refs[8 : 8 + n_in]
    outs = refs[8 + n_in : 8 + n_in + n_out]
    kh, ds_ref, p_own, vh, p_ref, grads, wide = refs[8 + n_in + n_out :]
    window = len(sources)
    tokens = TD * TILE
    front = CAP * TILE
    before = tokens + window * front
    columns = CHUNK * 8
    device = lax.axis_index("node")

    for side, heads_ref, prompt, own in ((0, kh, prompt_k, own_k), (1, vh, prompt_v, own_v)):
        split_heads(prompt[...], heads_ref, 0, tokens, heads_kv, wide)
        for k, (source, start) in enumerate(sources):
            start += side * front * heads_kv
            block = blocks[source][start : start + front * heads_kv]
            split_heads(block, heads_ref, tokens + k * front, front, heads_kv, wide)
        heads_ref[:, before:] = own[...]

    column_token = lax.broadcasted_iota(jnp.int32, (CHUNK, columns), 1) // 8
    causal = jnp.where(lax.broadcasted_iota(jnp.int32, (CHUNK, columns), 0) <= column_token, 0.0, MASKED)
    for head in range(heads_kv):
        for c in range(tokens // CHUNK):
            rows = before + (c + 1) * CHUNK
            span = slice(c * columns, (c + 1) * columns)
            q = qh[head, span]
            g = gh[head, span]
            s = lax.dot_general(kh[head, :rows], q, (((1,), (1,)), ((), ())), preferred_element_type=F32)
            dp = lax.dot_general(vh[head, :rows], g, (((1,), (1,)), ((), ())), preferred_element_type=F32)
            s = s + jnp.concatenate([bias[:rows]] * (columns // 128), axis=1)
            s = jnp.concatenate([s[: rows - CHUNK], s[rows - CHUNK :] + causal], axis=0)
            top = jnp.max(s, axis=0, keepdims=True)
            e = jnp.exp2((s - top) * (scale * math.log2(math.e)))
            total = jnp.sum(e, axis=0, keepdims=True)
            p = e * (weight_ref[:1, span] / total)
            delta = jnp.sum(p * dp, axis=0, keepdims=True)
            ds_ref[head, :rows, span] = (p * (dp - delta) * scale).astype(BF16)
            p_ref[:, span] = p[:before].astype(BF16)
            p_own[head, : rows - before, span] = p[before:].astype(BF16)
        grads[0, head] = jnp.dot(ds_ref[head, :before], qh[head], preferred_element_type=F32)
        grads[1, head] = jnp.dot(p_ref[...], gh[head], preferred_element_type=F32)

    rows = tokens * heads_kv
    rows_front = front * heads_kv
    even = lax.rem(device, 2) == 0
    for side in range(2):
        dprompt = join_heads([grads[side, h, :tokens] for h in range(heads_kv)], tokens, heads_kv, wide).astype(BF16)
        kept = even if side == 0 else jnp.logical_not(even)

        @pl.when(kept)
        def _():
            outs[1][:rows] = dprompt

        @pl.when(jnp.logical_not(kept))
        def _():
            outs[0][:rows] = dprompt

        for k, (target, start) in enumerate(targets):
            span = slice(tokens + k * front, tokens + (k + 1) * front)
            block = join_heads([grads[side, h, span] for h in range(heads_kv)], front, heads_kv, wide).astype(BF16)
            start += side * rows_front
            outs[target][start : start + rows_front] = block


def grads_kernel(heads_kv, *refs):
    qh, gh, kh, ds_ref, p_own, dq_ref, dk_ref, dv_ref, wide = refs
    tokens = TD * TILE
    before = kh.shape[1] - tokens
    columns = CHUNK * 8
    dk = []
    dv = []
    for pair in range(heads_kv // 2):
        for c in range(tokens // CHUNK):
            rows = before + (c + 1) * CHUNK
            span = slice(c * columns, (c + 1) * columns)
            parts = []
            for head in (2 * pair, 2 * pair + 1):
                dq = lax.dot_general(
                    kh[head, :rows], ds_ref[head, :rows, span], (((0,), (0,)), ((), ())), preferred_element_type=F32
                )
                parts.append(dq.T.reshape(CHUNK, 8, 128))
            dq_ref[c * CHUNK : (c + 1) * CHUNK, pair * 16 : (pair + 1) * 16] = jnp.concatenate(parts, axis=1).astype(BF16)
        for head in (2 * pair, 2 * pair + 1):
            for source, factor, out in ((ds_ref.at[head, before:], qh, dk), (p_own.at[head], gh, dv)):
                pieces = []
                for c in range(tokens // CHUNK):
                    start = c * columns
                    pieces.append(
                        jnp.dot(
                            source[c * CHUNK : (c + 1) * CHUNK, start:], factor[head, start:], preferred_element_type=F32
                        )
                    )
                out.append(jnp.concatenate(pieces, axis=0))
    dk_ref[...] = join_heads(dk, tokens, heads_kv, wide)
    dv_ref[...] = join_heads(dv, tokens, heads_kv, wide)


VMEM = pl.BlockSpec(memory_space=pltpu.VMEM)


HBM = pl.BlockSpec(memory_space=pltpu.HBM)


def call(kernel, name, operands, outputs, scratch, flops, transcendentals=0, place=VMEM):
    sizes = [a.size * a.dtype.itemsize for a in (*operands, *outputs)]
    if place is HBM:
        operands = [pltpu.with_memory_space_constraint(a, pltpu.HBM) for a in operands]
    return pl.pallas_call(
        kernel,
        in_specs=[place] * len(operands),
        out_specs=[VMEM] * len(outputs),
        out_shape=outputs,
        scratch_shapes=scratch,
        compiler_params=pltpu.CompilerParams(vmem_limit_bytes=16 * 1024 * 1024),
        cost_estimate=pl.CostEstimate(flops=flops, bytes_accessed=sum(sizes), transcendentals=transcendentals),
        name=name,
    )(*operands)


def load(order, keys, values, parents, lengths, tokens):
    rows, head_size = keys.shape
    heads_kv = rows // tokens
    array = jax.ShapeDtypeStruct
    return call(
        functools.partial(load_kernel, order, heads_kv),
        "load",
        (parents, lengths, keys, values),
        [array((2 * CAP * TILE * heads_kv, head_size), BF16), array((rows, head_size), BF16)]
        + [array((heads_kv, tokens, head_size), BF16)] * 2
        + [array((2 * tokens + len(order) * CAP * TILE, 128), F32), array((8, tokens * 8), F32)],
        [pltpu.SMEM(parents.shape, jnp.int32), pltpu.SMEM(lengths.shape, jnp.int32)]
        + [pltpu.VMEM((rows, head_size), BF16)] * 2
        + [pltpu.VMEM((rows, head_size), F32), pltpu.SemaphoreType.DMA((4,))],
        flops=1 << 20,
        place=HBM,
    )


def pack(queries, grad_out, heads_kv):
    tokens, heads_q, head_size = queries.shape
    array = jax.ShapeDtypeStruct
    return call(
        functools.partial(pack_kernel, heads_kv),
        "pack",
        (queries, grad_out),
        [array((heads_kv, tokens * 8, head_size), BF16)] * 2,
        [pltpu.VMEM((heads_kv, tokens, 16, head_size), BF16), pltpu.SemaphoreType.DMA((heads_kv,))],
        flops=1 << 20,
        place=HBM,
    )


def probs(sources, targets, prompt_k, prompt_v, qh, gh, own, blocks):
    own_k, own_v, bias, weight = own
    heads_kv, tokens, head_size = own_k.shape
    rows = tokens * heads_kv
    front = CAP * TILE
    unit = 2 * front * heads_kv
    before = tokens + len(sources) * front
    sizes = [max(start for target, start in targets if target == t) + unit for t in range(1 + max(targets)[0])]
    array = jax.ShapeDtypeStruct
    work = heads_kv * tokens * 8 * (before + tokens)
    return call(
        functools.partial(probs_kernel, sources, targets, heads_kv, head_size**-0.5),
        "probs",
        (prompt_k, prompt_v, own_k, own_v, qh, gh, bias, weight, *blocks),
        [array((size, head_size), BF16) for size in sizes]
        + [
            array((heads_kv, before + tokens, head_size), BF16),
            array((heads_kv, before + tokens, tokens * 8), BF16),
            array((heads_kv, tokens, tokens * 8), BF16),
        ],
        [
            pltpu.VMEM((heads_kv, before + tokens, head_size), BF16),
            pltpu.VMEM((before, tokens * 8), BF16),
            pltpu.VMEM((2, heads_kv, before, head_size), F32),
            pltpu.VMEM((rows, head_size), F32),
        ],
        flops=8 * work * head_size,
        transcendentals=work,
    )


def grads(qh, gh, kh, ds, p_own):
    heads_kv, tokens, _ = p_own.shape
    head_size = kh.shape[2]
    array = jax.ShapeDtypeStruct
    return call(
        functools.partial(grads_kernel, heads_kv),
        "grads",
        (qh, gh, kh, ds, p_own),
        [
            array((tokens, heads_kv * 8, head_size), BF16),
            array((tokens * heads_kv, head_size), F32),
            array((tokens * heads_kv, head_size), F32),
        ],
        [pltpu.VMEM((tokens * heads_kv, head_size), F32)],
        flops=4 * heads_kv * tokens * 8 * kh.shape[1] * head_size,
    )


def shift_route(distance, size):
    return [(i, i + distance) for i in range(size - distance)]


def back(route):
    return [(j, i) for i, j in route]


def added(*blocks):
    total = blocks[0].astype(F32)
    for block in blocks[1:]:
        total = total + block.astype(F32)
    return total


def after(array, *earlier):
    return lax.optimization_barrier((array, *earlier))[0]


def units(array, start, unit, count):
    return [array[start + i * unit : start + (i + 1) * unit] for i in range(count)]


def prompt_route(stride, size):
    return [(i + j, i + j + stride) for i in range(0, size, 2 * stride) for j in (0, 1)]


def collect(size, unit, rows, where, keys, values, head, held, queries):
    even, lower, _ = where
    neighbours = [(i, i ^ 1) for i in range(size)]
    far_route = shift_route(4, size)[1:]
    near_route = shift_route(2, size)
    if size == W + 1:
        keys_far = permuted(keys, [(0, 4)])
        values_far = permuted(values, [(0, 5)])
        values_next = permuted(values, [(0, 1)])
        head, queries = lax.optimization_barrier((head, queries, keys_far))[:2]
        far = permuted(head, far_route)
        six = permuted(head, [(1, 7)])
        held = after(added(held, values_far, values_next, keys_far).astype(BF16), far, six)
        second = permuted(jnp.concatenate([held, head]), near_route)
        crossed = jnp.where(even, jnp.concatenate([head, far]), jnp.concatenate([far, six]))
        crossed = permuted(crossed, neighbours)
        held = jnp.where(lower, held, second[:rows])
        third = permuted(after(jnp.concatenate([held, second[rows:]]), crossed), neighbours)
        sources = [(0, rows), (1, rows), (2, 0), (3, 0), (2, unit), (4, 0)]
        return held, third[:rows], sources, (third, second, crossed, far, six), queries
    strides = [2**i for i in range(2, size.bit_length()) if 2**i < size]
    top = strides[-1]
    keys_far = permuted(keys, [(0, top)])
    values_far = permuted(values, [(0, top + 1)])
    values_next = permuted(values, [(0, 1)])
    far = permuted(head, far_route)
    held = added(held, values_next, values_far, keys_far).astype(BF16)
    for stride in reversed(strides[:-1]):
        held = added(held, permuted(held, prompt_route(stride, size))).astype(BF16)
    second = permuted(jnp.concatenate([held, head, far]), near_route)
    held = jnp.where(lower, held, second[:rows])
    near, six = units(second, rows, unit, 2)
    third = permuted(jnp.concatenate([head, near, far, six]), shift_route(1, size))
    other = permuted(held, neighbours)
    sources = [(0, 0), (1, rows), (0, unit), (2, 0), (0, 2 * unit), (1, rows + unit), (0, 3 * unit)]
    return held, other, sources, (third, second, far), queries


def give_back(size, unit, rows, where, send, keep, ready):
    even, lower, _ = where
    neighbours = [(i, i ^ 1) for i in range(size)]
    far_route = back(shift_route(4, size)[1:])
    two, four, six = units(keep, rows, unit, 3)
    if size == W + 1:
        third = permuted(send, neighbours)
        total = after(added(keep[:rows], third[:rows]).astype(BF16), ready)
        near, first, last = units(third, rows, unit, 3)
        none = jnp.zeros_like(first)
        parts = [permuted(total, [(j, 0), (j + 1, 1)]) for j in range(2, size, 2)]
        two = permuted(added(two, near).astype(BF16), back(shift_route(2, size)[1:]))
        four = permuted(added(four, jnp.where(even, last, first)).astype(BF16), far_route)
        six = permuted(added(six, jnp.where(even, none, last)).astype(BF16), [(7, 1)])
        total = added(total, *parts).astype(BF16)
        mine = added(jnp.where(even, first, none), two, four, six)
        return total, permuted(total, [(1, 0)]).astype(F32), mine
    strides = [2**i for i in range(2, size.bit_length()) if 2**i < size]
    top = strides[-1]
    zero, *third = units(permuted(send[rows:], back(shift_route(1, size))), 0, unit, 4)
    total = added(keep[:rows], permuted(send[:rows], neighbours)).astype(BF16)
    two, four, six = (added(x, y).astype(BF16) for x, y in zip((two, four, six), third))
    second = permuted(jnp.concatenate([total, two, six]), back(shift_route(2, size)))
    four = added(four, second[rows + unit :])
    mine = added(zero, second[rows : rows + unit], permuted(four.astype(BF16), far_route))
    total = added(total, jnp.where(lower, second[:rows], jnp.zeros_like(total))).astype(BF16)
    for stride in strides[:-1]:
        total = added(total, permuted(total, back(prompt_route(stride, size)))).astype(BF16)
    keys_far = permuted(total, [(top, 0)])
    values_far = permuted(total, [(top + 1, 0)])
    values_next = permuted(total, [(1, 0)])
    return added(total, keys_far), added(values_next, values_far), mine


def per_device(size, queries, keys, values, grad_out, parents, lengths):
    tokens, heads_kv, head_size = keys.shape
    rows = tokens * heads_kv
    one = CAP * TILE * heads_kv
    unit = 2 * one
    window = min(W, size - 2)
    device = lax.axis_index("node")
    keys = keys.reshape(rows, head_size)
    values = values.reshape(rows, head_size)

    order = [(k, k) for k in range(1, window + 1)]
    if size == W + 1:
        order[0], order[2] = (1, 3), (3, 1)
    head, held, *own = load(order, keys, values, parents, lengths, tokens)
    head, *where = lax.optimization_barrier((head, lax.rem(device, 2) == 0, lax.rem(device, 4) < 2, device == 0))
    even, _, root = where
    held, other, sources, blocks, queries = collect(size, unit, rows, where, keys, values, head, held, queries)
    qh, gh = pack(queries, grad_out, heads_kv)
    prompt_k, prompt_v = jnp.where(even, held, other), jnp.where(even, other, held)
    targets = [(1 - k % 2, rows + (k - 1) // 2 * unit) for k in range(1, window + 1)]
    send, keep, kh, ds, p_own = probs(sources, targets, prompt_k, prompt_v, qh, gh, own, blocks)
    grad_queries, dk, dv = grads(qh, gh, kh, ds, p_own)
    prompt_k, prompt_v, mine = give_back(size, unit, rows, where, send, keep, dk)
    own = []
    for side, local, prompt in ((0, dk, prompt_k), (1, dv, prompt_v)):
        whole = local + jnp.where(root, prompt.astype(F32), 0.0)
        own.append(whole.at[:one].add(mine[side * one : (side + 1) * one]).reshape(tokens, heads_kv, head_size))
    return grad_queries, own[0], own[1]


def solution(mesh):
    by_token = P(("leaf", "node"), "tensor", None)
    return jax.shard_map(
        functools.partial(per_device, mesh.shape["node"]),
        mesh=mesh,
        in_specs=(by_token, by_token, by_token, by_token, P("leaf"), P("leaf")),
        out_specs=(by_token, by_token, by_token),
        check_vma=False,
    )
```

```python
import functools
import math

import jax
import jax.numpy as jnp
from jax import lax
from jax.experimental import pallas as pl
from jax.experimental.pallas import tpu as pltpu
from jax.sharding import PartitionSpec as P

TILE = 16
TD = 8
CAP = 2
W = 7
CHUNK = 32
MASKED = -1e30
BF16 = jnp.bfloat16
F32 = jnp.float32


def permuted(block, route):
    return lax.ppermute(block, "node", route)


def column_limits(device, window, parents, lengths):
    cursor = parents[device * TD]
    need = [jnp.int32(0)] * (window + 1)
    for _ in range(W):
        owner = jnp.where(cursor < 0, -1, lax.div(jnp.maximum(cursor, 0), TD))
        distance = device - owner
        active = (owner >= 1) & (distance >= 1) & (distance <= W)
        depth = lax.rem(jnp.maximum(cursor, 0), TD) + 1
        for k in range(1, window + 1):
            need[k] = jnp.where(active & (distance == k), depth, need[k])
        cursor = jnp.where(active, parents[jnp.maximum(owner, 0) * TD], cursor)
    prompt = [jnp.where(device >= 1, lengths[t], 0) for t in range(TD)]
    behind = []
    for k in range(1, window + 1):
        owner = device - k
        seen = [(owner >= 1) & (c < need[k]) for c in range(CAP)]
        behind.append([jnp.where(seen[c], lengths[jnp.maximum(owner, 0) * TD + c], 0) for c in range(CAP)])
    return prompt, behind, [lengths[device * TD + t] for t in range(TD)]


def split_heads(block, heads_ref, start, count, heads_kv, wide):
    wide[: count * heads_kv] = block.astype(F32)
    for h in range(heads_kv):
        heads_ref[h, start : start + count] = wide[pl.ds(h, count, stride=heads_kv), :].astype(BF16)


def join_heads(blocks, count, heads_kv, wide):
    for h in range(heads_kv):
        wide[pl.ds(h, count, stride=heads_kv), :] = blocks[h]
    return wide[: count * heads_kv]


def load_kernel(order, heads_kv, *refs):
    sources, outs, scratch = refs[:4], refs[4:10], refs[10:]
    head, held, own_k, own_v, bias, weight = outs
    parents, lengths, keys, values, wide, arrived = scratch
    copies = [pltpu.make_async_copy(a, b, arrived.at[i]) for i, (a, b) in enumerate(zip(sources, scratch))]
    for copy in copies:
        copy.start()
    tokens = TD * TILE
    front = CAP * TILE * heads_kv
    device = lax.axis_index("node")
    for copy in copies:
        copy.wait()
    head[:front] = keys[:front]
    head[front:] = values[:front]
    held[...] = jnp.where(device == 0, keys[...], jnp.zeros_like(keys))
    split_heads(keys[...], own_k, 0, tokens, heads_kv, wide)
    split_heads(values[...], own_v, 0, tokens, heads_kv, wide)
    place = lax.broadcasted_iota(jnp.int32, (TILE, 128), 0)
    prompt, behind, own = column_limits(device, len(order), parents, lengths)
    even = lax.rem(device, 2) == 0
    limits = prompt
    for on_even, on_odd in order:
        limits = limits + [jnp.where(even, x, y) for x, y in zip(behind[on_even - 1], behind[on_odd - 1])]
    for t, limit in enumerate(limits + own):
        bias[t * TILE : (t + 1) * TILE] = jnp.where(place < limit, 0.0, MASKED)
    lane_place = lax.broadcasted_iota(jnp.int32, (8, 128), 1) // 8
    for t in range(TD):
        weight[:, t * 128 : (t + 1) * 128] = jnp.where(lane_place < lengths[device * TD + t], 1.0, 0.0)


def pack_kernel(heads_kv, q_ref, g_ref, qh, gh, blocks, arrived):
    tokens = TD * TILE
    copies = []
    for pair in range(heads_kv // 2):
        for ref, out in ((q_ref, qh), (g_ref, gh)):
            i = len(copies)
            copy = pltpu.make_async_copy(ref.at[:, pair * 16 : (pair + 1) * 16], blocks.at[i], arrived.at[i])
            copy.start()
            copies.append((copy, out, pair))
    for i, (copy, out, pair) in enumerate(copies):
        copy.wait()
        both = blocks[i].astype(F32)
        for part in range(2):
            out[2 * pair + part] = both[:, part * 8 : (part + 1) * 8].reshape(tokens * 8, 128).astype(BF16)


def probs_kernel(sources, targets, heads_kv, scale, *refs):
    prompt_k, prompt_v, own_k, own_v, qh, gh, bias, weight_ref = refs[:8]
    n_in = 1 + max(source for source, _ in sources)
    n_out = 1 + max(target for target, _ in targets)
    blocks = refs[8 : 8 + n_in]
    outs = refs[8 + n_in : 8 + n_in + n_out]
    kh, ds_ref, p_own, vh, p_ref, grads, wide = refs[8 + n_in + n_out :]
    window = len(sources)
    tokens = TD * TILE
    front = CAP * TILE
    before = tokens + window * front
    columns = CHUNK * 8
    device = lax.axis_index("node")

    for side, heads_ref, prompt, own in ((0, kh, prompt_k, own_k), (1, vh, prompt_v, own_v)):
        split_heads(prompt[...], heads_ref, 0, tokens, heads_kv, wide)
        for k, (source, start) in enumerate(sources):
            start += side * front * heads_kv
            block = blocks[source][start : start + front * heads_kv]
            split_heads(block, heads_ref, tokens + k * front, front, heads_kv, wide)
        heads_ref[:, before:] = own[...]

    column_token = lax.broadcasted_iota(jnp.int32, (CHUNK, columns), 1) // 8
    causal = jnp.where(lax.broadcasted_iota(jnp.int32, (CHUNK, columns), 0) <= column_token, 0.0, MASKED)
    for head in range(heads_kv):
        for c in range(tokens // CHUNK):
            rows = before + (c + 1) * CHUNK
            span = slice(c * columns, (c + 1) * columns)
            q = qh[head, span]
            g = gh[head, span]
            s = lax.dot_general(kh[head, :rows], q, (((1,), (1,)), ((), ())), preferred_element_type=F32)
            dp = lax.dot_general(vh[head, :rows], g, (((1,), (1,)), ((), ())), preferred_element_type=F32)
            s = s + jnp.concatenate([bias[:rows]] * (columns // 128), axis=1)
            s = jnp.concatenate([s[: rows - CHUNK], s[rows - CHUNK :] + causal], axis=0)
            top = jnp.max(s, axis=0, keepdims=True)
            e = jnp.exp2((s - top) * (scale * math.log2(math.e)))
            total = jnp.sum(e, axis=0, keepdims=True)
            p = e * (weight_ref[:1, span] / total)
            delta = jnp.sum(p * dp, axis=0, keepdims=True)
            ds_ref[head, :rows, span] = (p * (dp - delta) * scale).astype(BF16)
            p_ref[:, span] = p[:before].astype(BF16)
            p_own[head, : rows - before, span] = p[before:].astype(BF16)
        grads[0, head] = jnp.dot(ds_ref[head, :before], qh[head], preferred_element_type=F32)
        grads[1, head] = jnp.dot(p_ref[...], gh[head], preferred_element_type=F32)

    rows = tokens * heads_kv
    rows_front = front * heads_kv
    even = lax.rem(device, 2) == 0
    for side in range(2):
        dprompt = join_heads([grads[side, h, :tokens] for h in range(heads_kv)], tokens, heads_kv, wide).astype(BF16)
        kept = even if side == 0 else jnp.logical_not(even)

        @pl.when(kept)
        def _():
            outs[1][:rows] = dprompt

        @pl.when(jnp.logical_not(kept))
        def _():
            outs[0][:rows] = dprompt

        for k, (target, start) in enumerate(targets):
            span = slice(tokens + k * front, tokens + (k + 1) * front)
            block = join_heads([grads[side, h, span] for h in range(heads_kv)], front, heads_kv, wide).astype(BF16)
            start += side * rows_front
            outs[target][start : start + rows_front] = block


def grads_kernel(heads_kv, *refs):
    qh, gh, kh, ds_ref, p_own, dq_ref, dk_ref, dv_ref, wide = refs
    tokens = TD * TILE
    before = kh.shape[1] - tokens
    columns = CHUNK * 8
    dk = []
    dv = []
    for pair in range(heads_kv // 2):
        for c in range(tokens // CHUNK):
            rows = before + (c + 1) * CHUNK
            span = slice(c * columns, (c + 1) * columns)
            parts = []
            for head in (2 * pair, 2 * pair + 1):
                dq = lax.dot_general(
                    kh[head, :rows], ds_ref[head, :rows, span], (((0,), (0,)), ((), ())), preferred_element_type=F32
                )
                parts.append(dq.T.reshape(CHUNK, 8, 128))
            dq_ref[c * CHUNK : (c + 1) * CHUNK, pair * 16 : (pair + 1) * 16] = jnp.concatenate(parts, axis=1).astype(BF16)
        for head in (2 * pair, 2 * pair + 1):
            for source, factor, out in ((ds_ref.at[head, before:], qh, dk), (p_own.at[head], gh, dv)):
                pieces = []
                for c in range(tokens // CHUNK):
                    start = c * columns
                    pieces.append(
                        jnp.dot(
                            source[c * CHUNK : (c + 1) * CHUNK, start:], factor[head, start:], preferred_element_type=F32
                        )
                    )
                out.append(jnp.concatenate(pieces, axis=0))
    dk_ref[...] = join_heads(dk, tokens, heads_kv, wide)
    dv_ref[...] = join_heads(dv, tokens, heads_kv, wide)


VMEM = pl.BlockSpec(memory_space=pltpu.VMEM)


HBM = pl.BlockSpec(memory_space=pltpu.HBM)


def call(kernel, name, operands, outputs, scratch, flops, transcendentals=0, place=VMEM):
    sizes = [a.size * a.dtype.itemsize for a in (*operands, *outputs)]
    if place is HBM:
        operands = [pltpu.with_memory_space_constraint(a, pltpu.HBM) for a in operands]
    return pl.pallas_call(
        kernel,
        in_specs=[place] * len(operands),
        out_specs=[VMEM] * len(outputs),
        out_shape=outputs,
        scratch_shapes=scratch,
        compiler_params=pltpu.CompilerParams(vmem_limit_bytes=16 * 1024 * 1024),
        cost_estimate=pl.CostEstimate(flops=flops, bytes_accessed=sum(sizes), transcendentals=transcendentals),
        name=name,
    )(*operands)


def load(order, keys, values, parents, lengths, tokens):
    rows, head_size = keys.shape
    heads_kv = rows // tokens
    array = jax.ShapeDtypeStruct
    return call(
        functools.partial(load_kernel, order, heads_kv),
        "load",
        (parents, lengths, keys, values),
        [array((2 * CAP * TILE * heads_kv, head_size), BF16), array((rows, head_size), BF16)]
        + [array((heads_kv, tokens, head_size), BF16)] * 2
        + [array((2 * tokens + len(order) * CAP * TILE, 128), F32), array((8, tokens * 8), F32)],
        [pltpu.SMEM(parents.shape, jnp.int32), pltpu.SMEM(lengths.shape, jnp.int32)]
        + [pltpu.VMEM((rows, head_size), BF16)] * 2
        + [pltpu.VMEM((rows, head_size), F32), pltpu.SemaphoreType.DMA((4,))],
        flops=1 << 20,
        place=HBM,
    )


def pack(queries, grad_out, heads_kv):
    tokens, heads_q, head_size = queries.shape
    array = jax.ShapeDtypeStruct
    return call(
        functools.partial(pack_kernel, heads_kv),
        "pack",
        (queries, grad_out),
        [array((heads_kv, tokens * 8, head_size), BF16)] * 2,
        [pltpu.VMEM((heads_kv, tokens, 16, head_size), BF16), pltpu.SemaphoreType.DMA((heads_kv,))],
        flops=1 << 20,
        place=HBM,
    )


def probs(sources, targets, prompt_k, prompt_v, qh, gh, own, blocks):
    own_k, own_v, bias, weight = own
    heads_kv, tokens, head_size = own_k.shape
    rows = tokens * heads_kv
    front = CAP * TILE
    unit = 2 * front * heads_kv
    before = tokens + len(sources) * front
    sizes = [max(start for target, start in targets if target == t) + unit for t in range(1 + max(targets)[0])]
    array = jax.ShapeDtypeStruct
    work = heads_kv * tokens * 8 * (before + tokens)
    return call(
        functools.partial(probs_kernel, sources, targets, heads_kv, head_size**-0.5),
        "probs",
        (prompt_k, prompt_v, own_k, own_v, qh, gh, bias, weight, *blocks),
        [array((size, head_size), BF16) for size in sizes]
        + [
            array((heads_kv, before + tokens, head_size), BF16),
            array((heads_kv, before + tokens, tokens * 8), BF16),
            array((heads_kv, tokens, tokens * 8), BF16),
        ],
        [
            pltpu.VMEM((heads_kv, before + tokens, head_size), BF16),
            pltpu.VMEM((before, tokens * 8), BF16),
            pltpu.VMEM((2, heads_kv, before, head_size), F32),
            pltpu.VMEM((rows, head_size), F32),
        ],
        flops=8 * work * head_size,
        transcendentals=work,
    )


def grads(qh, gh, kh, ds, p_own):
    heads_kv, tokens, _ = p_own.shape
    head_size = kh.shape[2]
    array = jax.ShapeDtypeStruct
    return call(
        functools.partial(grads_kernel, heads_kv),
        "grads",
        (qh, gh, kh, ds, p_own),
        [
            array((tokens, heads_kv * 8, head_size), BF16),
            array((tokens * heads_kv, head_size), F32),
            array((tokens * heads_kv, head_size), F32),
        ],
        [pltpu.VMEM((tokens * heads_kv, head_size), F32)],
        flops=4 * heads_kv * tokens * 8 * kh.shape[1] * head_size,
    )


def shift_route(distance, size):
    return [(i, i + distance) for i in range(size - distance)]


def back(route):
    return [(j, i) for i, j in route]


def added(*blocks):
    total = blocks[0].astype(F32)
    for block in blocks[1:]:
        total = total + block.astype(F32)
    return total


def after(array, *earlier):
    return lax.optimization_barrier((array, *earlier))[0]


def units(array, start, unit, count):
    return [array[start + i * unit : start + (i + 1) * unit] for i in range(count)]


def prompt_route(stride, size):
    return [(i + j, i + j + stride) for i in range(0, size, 2 * stride) for j in (0, 1)]


def collect(size, unit, rows, where, keys, values, head, held, queries):
    even, lower, _ = where
    neighbours = [(i, i ^ 1) for i in range(size)]
    far_route = shift_route(4, size)[1:]
    near_route = shift_route(2, size)
    if size == W + 1:
        keys_far = permuted(keys, [(0, 4)])
        values_far = permuted(values, [(0, 5)])
        values_next = permuted(values, [(0, 1)])
        head, queries = lax.optimization_barrier((head, queries, keys_far))[:2]
        far = permuted(head, far_route)
        six = permuted(head, [(1, 7)])
        held = after(added(held, values_far, values_next, keys_far).astype(BF16), far, six)
        second = permuted(jnp.concatenate([held, head]), near_route)
        crossed = jnp.where(even, jnp.concatenate([head, far]), jnp.concatenate([far, six]))
        crossed = permuted(crossed, neighbours)
        held = jnp.where(lower, held, second[:rows])
        third = permuted(after(jnp.concatenate([held, second[rows:]]), crossed), neighbours)
        sources = [(0, rows), (1, rows), (2, 0), (3, 0), (2, unit), (4, 0)]
        return held, third[:rows], sources, (third, second, crossed, far, six), queries
    strides = [2**i for i in range(2, size.bit_length()) if 2**i < size]
    top = strides[-1]
    keys_far = permuted(keys, [(0, top)])
    values_far = permuted(values, [(0, top + 1)])
    values_next = permuted(values, [(0, 1)])
    far = permuted(head, far_route)
    held = added(held, values_next, values_far, keys_far).astype(BF16)
    for stride in reversed(strides[:-1]):
        held = added(held, permuted(held, prompt_route(stride, size))).astype(BF16)
    second = permuted(jnp.concatenate([held, head, far]), near_route)
    held = jnp.where(lower, held, second[:rows])
    near, six = units(second, rows, unit, 2)
    third = permuted(jnp.concatenate([head, near, far, six]), shift_route(1, size))
    other = permuted(held, neighbours)
    sources = [(0, 0), (1, rows), (0, unit), (2, 0), (0, 2 * unit), (1, rows + unit), (0, 3 * unit)]
    return held, other, sources, (third, second, far), queries


def give_back(size, unit, rows, where, sent, ready):
    even, lower, _ = where
    neighbours = [(i, i ^ 1) for i in range(size)]
    far_route = back(shift_route(4, size)[1:])
    send, keep = sent[:2]
    two, four, six = units(keep, rows, unit, 3)
    if size == W + 1:
        third = permuted(send, neighbours)
        total = after(added(keep[:rows], third[:rows]).astype(BF16), ready)
        near = third[rows:]
        first, last = units(permuted(after(sent[2], third), neighbours), 0, unit, 2)
        none = jnp.zeros_like(first)
        parts = [permuted(total, [(j, 0), (j + 1, 1)]) for j in range(2, size, 2)]
        total = added(total, *parts).astype(BF16)
        two, near, first, last, _ = lax.optimization_barrier((two, near, first, last, total))
        two = added(two, near).astype(BF16)
        four = added(four, jnp.where(even, last, first)).astype(BF16)
        six = added(six, jnp.where(even, none, last)).astype(BF16)
        two = permuted(two, back(shift_route(2, size)[1:]))
        four = permuted(four, far_route)
        six = permuted(six, [(7, 1)])
        values_next = permuted(total, [(1, 0)])
        two, four, six, values_next = lax.optimization_barrier((two, four, six, values_next))
        return total, values_next, added(jnp.where(even, first, none), two, four, six)
    strides = [2**i for i in range(2, size.bit_length()) if 2**i < size]
    top = strides[-1]
    zero, *third = units(permuted(send[rows:], back(shift_route(1, size))), 0, unit, 4)
    total = added(keep[:rows], permuted(send[:rows], neighbours)).astype(BF16)
    two, four, six = (added(x, y).astype(BF16) for x, y in zip((two, four, six), third))
    second = permuted(jnp.concatenate([total, two, six]), back(shift_route(2, size)))
    four = added(four, second[rows + unit :])
    mine = added(zero, second[rows : rows + unit], permuted(four.astype(BF16), far_route))
    total = added(total, jnp.where(lower, second[:rows], jnp.zeros_like(total))).astype(BF16)
    for stride in strides[:-1]:
        total = added(total, permuted(total, back(prompt_route(stride, size)))).astype(BF16)
    keys_far = permuted(total, [(top, 0)])
    values_far = permuted(total, [(top + 1, 0)])
    values_next = permuted(total, [(1, 0)])
    return added(total, keys_far), added(values_next, values_far), mine


def per_device(size, queries, keys, values, grad_out, parents, lengths):
    tokens, heads_kv, head_size = keys.shape
    rows = tokens * heads_kv
    one = CAP * TILE * heads_kv
    unit = 2 * one
    window = min(W, size - 2)
    device = lax.axis_index("node")
    keys = keys.reshape(rows, head_size)
    values = values.reshape(rows, head_size)

    order = [(k, k) for k in range(1, window + 1)]
    if size == W + 1:
        order[0], order[2] = (1, 3), (3, 1)
    head, held, *own = load(order, keys, values, parents, lengths, tokens)
    head, *where = lax.optimization_barrier((head, lax.rem(device, 2) == 0, lax.rem(device, 4) < 2, device == 0))
    even, _, root = where
    held, other, sources, blocks, queries = collect(size, unit, rows, where, keys, values, head, held, queries)
    qh, gh = pack(queries, grad_out, heads_kv)
    prompt_k, prompt_v = jnp.where(even, held, other), jnp.where(even, other, held)
    targets = [(1 - k % 2, rows + (k - 1) // 2 * unit) for k in range(1, window + 1)]
    if size == W + 1:
        targets[2], targets[4] = (2, 0), (2, unit)
    *sent, kh, ds, p_own = probs(sources, targets, prompt_k, prompt_v, qh, gh, own, blocks)
    grad_queries, dk, dv = grads(qh, gh, kh, ds, p_own)
    prompt_k, prompt_v, mine = give_back(size, unit, rows, where, sent, dk)
    own = []
    for side, local, prompt in ((0, dk, prompt_k), (1, dv, prompt_v)):
        whole = local + jnp.where(root, prompt.astype(F32), 0.0)
        own.append(whole.at[:one].add(mine[side * one : (side + 1) * one]).reshape(tokens, heads_kv, head_size))
    return grad_queries, own[0], own[1]


def solution(mesh):
    by_token = P(("leaf", "node"), "tensor", None)
    return jax.shard_map(
        functools.partial(per_device, mesh.shape["node"]),
        mesh=mesh,
        in_specs=(by_token, by_token, by_token, by_token, P("leaf"), P("leaf")),
        out_specs=(by_token, by_token, by_token),
        check_vma=False,
    )
```

```python
import functools
import math

import jax
import jax.numpy as jnp
from jax import lax
from jax.experimental import pallas as pl
from jax.experimental.pallas import tpu as pltpu
from jax.sharding import PartitionSpec as P

TILE = 16
TD = 8
CAP = 2
W = 7
CHUNK = 32
MASKED = -1e30
BF16 = jnp.bfloat16
F32 = jnp.float32


def permuted(block, route):
    return lax.ppermute(block, "node", route)


def column_limits(device, window, parents, lengths):
    cursor = parents[device * TD]
    need = [jnp.int32(0)] * (window + 1)
    for _ in range(W):
        owner = jnp.where(cursor < 0, -1, lax.div(jnp.maximum(cursor, 0), TD))
        distance = device - owner
        active = (owner >= 1) & (distance >= 1) & (distance <= W)
        depth = lax.rem(jnp.maximum(cursor, 0), TD) + 1
        for k in range(1, window + 1):
            need[k] = jnp.where(active & (distance == k), depth, need[k])
        cursor = jnp.where(active, parents[jnp.maximum(owner, 0) * TD], cursor)
    prompt = [jnp.where(device >= 1, lengths[t], 0) for t in range(TD)]
    behind = []
    for k in range(1, window + 1):
        owner = device - k
        seen = [(owner >= 1) & (c < need[k]) for c in range(CAP)]
        behind.append([jnp.where(seen[c], lengths[jnp.maximum(owner, 0) * TD + c], 0) for c in range(CAP)])
    return prompt, behind, [lengths[device * TD + t] for t in range(TD)]


def split_heads(block, heads_ref, start, count, heads_kv, wide):
    wide[: count * heads_kv] = block.astype(F32)
    for h in range(heads_kv):
        heads_ref[h, start : start + count] = wide[pl.ds(h, count, stride=heads_kv), :].astype(BF16)


def join_heads(blocks, count, heads_kv, wide):
    for h in range(heads_kv):
        wide[pl.ds(h, count, stride=heads_kv), :] = blocks[h]
    return wide[: count * heads_kv]


def load_kernel(order, heads_kv, *refs):
    sources, outs, scratch = refs[:4], refs[4:10], refs[10:]
    head, held, own_k, own_v, bias, weight = outs
    parents, lengths, keys, values, wide, arrived = scratch
    copies = [pltpu.make_async_copy(a, b, arrived.at[i]) for i, (a, b) in enumerate(zip(sources, scratch))]
    for copy in copies:
        copy.start()
    tokens = TD * TILE
    front = CAP * TILE * heads_kv
    device = lax.axis_index("node")
    for copy in copies:
        copy.wait()
    head[:front] = keys[:front]
    head[front:] = values[:front]
    held[...] = jnp.where(device == 0, keys[...], jnp.zeros_like(keys))
    split_heads(keys[...], own_k, 0, tokens, heads_kv, wide)
    split_heads(values[...], own_v, 0, tokens, heads_kv, wide)
    place = lax.broadcasted_iota(jnp.int32, (TILE, 128), 0)
    prompt, behind, own = column_limits(device, len(order), parents, lengths)
    even = lax.rem(device, 2) == 0
    limits = prompt
    for on_even, on_odd in order:
        limits = limits + [jnp.where(even, x, y) for x, y in zip(behind[on_even - 1], behind[on_odd - 1])]
    for t, limit in enumerate(limits + own):
        bias[t * TILE : (t + 1) * TILE] = jnp.where(place < limit, 0.0, MASKED)
    lane_place = lax.broadcasted_iota(jnp.int32, (8, 128), 1) // 8
    for t in range(TD):
        weight[:, t * 128 : (t + 1) * 128] = jnp.where(lane_place < lengths[device * TD + t], 1.0, 0.0)


def pack_kernel(heads_kv, q_ref, g_ref, qh, gh, blocks, arrived):
    tokens = TD * TILE
    copies = []
    for pair in range(heads_kv // 2):
        for ref, out in ((q_ref, qh), (g_ref, gh)):
            i = len(copies)
            copy = pltpu.make_async_copy(ref.at[:, pair * 16 : (pair + 1) * 16], blocks.at[i], arrived.at[i])
            copy.start()
            copies.append((copy, out, pair))
    for i, (copy, out, pair) in enumerate(copies):
        copy.wait()
        both = blocks[i].astype(F32)
        for part in range(2):
            out[2 * pair + part] = both[:, part * 8 : (part + 1) * 8].reshape(tokens * 8, 128).astype(BF16)


def probs_kernel(sources, targets, heads_kv, scale, *refs):
    prompt_k, prompt_v, own_k, own_v, qh, gh, bias, weight_ref = refs[:8]
    n_in = 1 + max(source for source, _ in sources)
    n_out = 1 + max(target for target, _ in targets)
    blocks_in = refs[8 : 8 + n_in]
    outs = refs[8 + n_in : 8 + n_in + n_out]
    kh, ds_ref, p_own, vh, p_ref, grads, wide = refs[8 + n_in + n_out :]
    window = len(sources)
    tokens = TD * TILE
    front = CAP * TILE
    before = tokens + window * front
    columns = CHUNK * 8
    device = lax.axis_index("node")

    for side, heads_ref, prompt, own in ((0, kh, prompt_k, own_k), (1, vh, prompt_v, own_v)):
        split_heads(prompt[...], heads_ref, 0, tokens, heads_kv, wide)
        for k, (source, start) in enumerate(sources):
            start += side * front * heads_kv
            block = blocks_in[source][start : start + front * heads_kv]
            split_heads(block, heads_ref, tokens + k * front, front, heads_kv, wide)
        heads_ref[:, before:] = own[...]

    column_token = lax.broadcasted_iota(jnp.int32, (CHUNK, columns), 1) // 8
    causal = jnp.where(lax.broadcasted_iota(jnp.int32, (CHUNK, columns), 0) <= column_token, 0.0, MASKED)
    blocks = [(head, c) for head in range(heads_kv) for c in range(tokens // CHUNK)]

    def scores(head, c):
        rows = before + (c + 1) * CHUNK
        span = slice(c * columns, (c + 1) * columns)
        outer = (((1,), (1,)), ((), ()))
        s = lax.dot_general(kh[head, :rows], qh[head, span], outer, preferred_element_type=F32)
        dp = lax.dot_general(vh[head, :rows], gh[head, span], outer, preferred_element_type=F32)
        return s, dp

    coming = scores(*blocks[0])
    for i, (head, c) in enumerate(blocks):
        s, dp = coming
        if i + 1 < len(blocks):
            coming = scores(*blocks[i + 1])
        rows = before + (c + 1) * CHUNK
        span = slice(c * columns, (c + 1) * columns)
        s = s + jnp.concatenate([bias[:rows]] * (columns // 128), axis=1)
        s = jnp.concatenate([s[: rows - CHUNK], s[rows - CHUNK :] + causal], axis=0)
        top = jnp.max(s, axis=0, keepdims=True)
        e = jnp.exp2((s - top) * (scale * math.log2(math.e)))
        total = jnp.sum(e, axis=0, keepdims=True)
        p = e * (weight_ref[:1, span] / total)
        delta = jnp.sum(p * dp, axis=0, keepdims=True)
        ds_ref[head, :rows, span] = (p * (dp - delta)).astype(BF16)
        p_ref[head % 2, :, span] = p[:before].astype(BF16)
        p_own[head, : rows - before, span] = p[before:].astype(BF16)
        if c == tokens // CHUNK - 1:
            grads[0, head] = scale * jnp.dot(ds_ref[head, :before], qh[head], preferred_element_type=F32)
            grads[1, head] = jnp.dot(p_ref[head % 2], gh[head], preferred_element_type=F32)

    rows = tokens * heads_kv
    rows_front = front * heads_kv
    even = lax.rem(device, 2) == 0
    for side in range(2):
        dprompt = join_heads([grads[side, h, :tokens] for h in range(heads_kv)], tokens, heads_kv, wide).astype(BF16)
        kept = even if side == 0 else jnp.logical_not(even)

        @pl.when(kept)
        def _():
            outs[1][:rows] = dprompt

        @pl.when(jnp.logical_not(kept))
        def _():
            outs[0][:rows] = dprompt

        for k, (target, start) in enumerate(targets):
            span = slice(tokens + k * front, tokens + (k + 1) * front)
            block = join_heads([grads[side, h, span] for h in range(heads_kv)], front, heads_kv, wide).astype(BF16)
            start += side * rows_front
            outs[target][start : start + rows_front] = block


def grads_kernel(heads_kv, scale, *refs):
    qh, gh, kh, ds_ref, p_own, dq_ref, dk_ref, dv_ref, wide = refs
    tokens = TD * TILE
    before = kh.shape[1] - tokens
    columns = CHUNK * 8
    dk = []
    dv = []
    for pair in range(heads_kv // 2):
        for c in range(tokens // CHUNK):
            rows = before + (c + 1) * CHUNK
            span = slice(c * columns, (c + 1) * columns)
            parts = []
            for head in (2 * pair, 2 * pair + 1):
                dq = lax.dot_general(
                    kh[head, :rows], ds_ref[head, :rows, span], (((0,), (0,)), ((), ())), preferred_element_type=F32
                )
                parts.append((scale * dq.T).reshape(CHUNK, 8, 128))
            dq_ref[c * CHUNK : (c + 1) * CHUNK, pair * 16 : (pair + 1) * 16] = jnp.concatenate(parts, axis=1).astype(BF16)
        for head in (2 * pair, 2 * pair + 1):
            for source, factor, out in ((ds_ref.at[head, before:], qh, dk), (p_own.at[head], gh, dv)):
                pieces = []
                for c in range(tokens // CHUNK):
                    start = c * columns
                    pieces.append(
                        jnp.dot(
                            source[c * CHUNK : (c + 1) * CHUNK, start:], factor[head, start:], preferred_element_type=F32
                        )
                    )
                out.append(jnp.concatenate(pieces, axis=0))
    dk_ref[...] = scale * join_heads(dk, tokens, heads_kv, wide)
    dv_ref[...] = join_heads(dv, tokens, heads_kv, wide)


VMEM = pl.BlockSpec(memory_space=pltpu.VMEM)


HBM = pl.BlockSpec(memory_space=pltpu.HBM)


def call(kernel, name, operands, outputs, scratch, flops, transcendentals=0, place=VMEM):
    sizes = [a.size * a.dtype.itemsize for a in (*operands, *outputs)]
    if place is HBM:
        operands = [pltpu.with_memory_space_constraint(a, pltpu.HBM) for a in operands]
    return pl.pallas_call(
        kernel,
        in_specs=[place] * len(operands),
        out_specs=[VMEM] * len(outputs),
        out_shape=outputs,
        scratch_shapes=scratch,
        compiler_params=pltpu.CompilerParams(vmem_limit_bytes=16 * 1024 * 1024),
        cost_estimate=pl.CostEstimate(flops=flops, bytes_accessed=sum(sizes), transcendentals=transcendentals),
        name=name,
    )(*operands)


def load(order, keys, values, parents, lengths, tokens):
    rows, head_size = keys.shape
    heads_kv = rows // tokens
    array = jax.ShapeDtypeStruct
    return call(
        functools.partial(load_kernel, order, heads_kv),
        "load",
        (parents, lengths, keys, values),
        [array((2 * CAP * TILE * heads_kv, head_size), BF16), array((rows, head_size), BF16)]
        + [array((heads_kv, tokens, head_size), BF16)] * 2
        + [array((2 * tokens + len(order) * CAP * TILE, 128), F32), array((8, tokens * 8), F32)],
        [pltpu.SMEM(parents.shape, jnp.int32), pltpu.SMEM(lengths.shape, jnp.int32)]
        + [pltpu.VMEM((rows, head_size), BF16)] * 2
        + [pltpu.VMEM((rows, head_size), F32), pltpu.SemaphoreType.DMA((4,))],
        flops=1 << 20,
        place=HBM,
    )


def pack(queries, grad_out, heads_kv):
    tokens, heads_q, head_size = queries.shape
    array = jax.ShapeDtypeStruct
    return call(
        functools.partial(pack_kernel, heads_kv),
        "pack",
        (queries, grad_out),
        [array((heads_kv, tokens * 8, head_size), BF16)] * 2,
        [pltpu.VMEM((heads_kv, tokens, 16, head_size), BF16), pltpu.SemaphoreType.DMA((heads_kv,))],
        flops=1 << 20,
        place=HBM,
    )


def probs(sources, targets, prompt_k, prompt_v, qh, gh, own, blocks):
    own_k, own_v, bias, weight = own
    heads_kv, tokens, head_size = own_k.shape
    rows = tokens * heads_kv
    front = CAP * TILE
    unit = 2 * front * heads_kv
    before = tokens + len(sources) * front
    sizes = [max(start for target, start in targets if target == t) + unit for t in range(1 + max(targets)[0])]
    array = jax.ShapeDtypeStruct
    work = heads_kv * tokens * 8 * (before + tokens)
    return call(
        functools.partial(probs_kernel, sources, targets, heads_kv, head_size**-0.5),
        "probs",
        (prompt_k, prompt_v, own_k, own_v, qh, gh, bias, weight, *blocks),
        [array((size, head_size), BF16) for size in sizes]
        + [
            array((heads_kv, before + tokens, head_size), BF16),
            array((heads_kv, before + tokens, tokens * 8), BF16),
            array((heads_kv, tokens, tokens * 8), BF16),
        ],
        [
            pltpu.VMEM((heads_kv, before + tokens, head_size), BF16),
            pltpu.VMEM((2, before, tokens * 8), BF16),
            pltpu.VMEM((2, heads_kv, before, head_size), F32),
            pltpu.VMEM((rows, head_size), F32),
        ],
        flops=8 * work * head_size,
        transcendentals=work,
    )


def grads(qh, gh, kh, ds, p_own):
    heads_kv, tokens, _ = p_own.shape
    head_size = kh.shape[2]
    array = jax.ShapeDtypeStruct
    return call(
        functools.partial(grads_kernel, heads_kv, head_size**-0.5),
        "grads",
        (qh, gh, kh, ds, p_own),
        [
            array((tokens, heads_kv * 8, head_size), BF16),
            array((tokens * heads_kv, head_size), F32),
            array((tokens * heads_kv, head_size), F32),
        ],
        [pltpu.VMEM((tokens * heads_kv, head_size), F32)],
        flops=4 * heads_kv * tokens * 8 * kh.shape[1] * head_size,
    )


def shift_route(distance, size):
    return [(i, i + distance) for i in range(size - distance)]


def back(route):
    return [(j, i) for i, j in route]


def added(*blocks):
    total = blocks[0].astype(F32)
    for block in blocks[1:]:
        total = total + block.astype(F32)
    return total


def after(array, *earlier):
    return lax.optimization_barrier((array, *earlier))[0]


def units(array, start, unit, count):
    return [array[start + i * unit : start + (i + 1) * unit] for i in range(count)]


def prompt_route(stride, size):
    return [(i + j, i + j + stride) for i in range(0, size, 2 * stride) for j in (0, 1)]


def collect(size, unit, rows, where, keys, values, head, held, queries):
    even, lower, _ = where
    neighbours = [(i, i ^ 1) for i in range(size)]
    far_route = shift_route(4, size)[1:]
    near_route = shift_route(2, size)
    if size == W + 1:
        keys_far = permuted(keys, [(0, 4)])
        values_far = permuted(values, [(0, 5)])
        values_next = permuted(values, [(0, 1)])
        head, queries = lax.optimization_barrier((head, queries, keys_far))[:2]
        far = permuted(head, far_route)
        six = permuted(head, [(1, 7)])
        held = after(added(held, values_far, values_next, keys_far).astype(BF16), far, six)
        second = permuted(jnp.concatenate([held, head]), near_route)
        crossed = jnp.where(even, jnp.concatenate([head, far]), jnp.concatenate([far, six]))
        crossed = permuted(crossed, neighbours)
        held = jnp.where(lower, held, second[:rows])
        third = permuted(after(jnp.concatenate([held, second[rows:]]), crossed), neighbours)
        sources = [(0, rows), (1, rows), (2, 0), (3, 0), (2, unit), (4, 0)]
        return held, third[:rows], sources, (third, second, crossed, far, six), queries
    strides = [2**i for i in range(2, size.bit_length()) if 2**i < size]
    top = strides[-1]
    keys_far = permuted(keys, [(0, top)])
    values_far = permuted(values, [(0, top + 1)])
    values_next = permuted(values, [(0, 1)])
    far = permuted(head, far_route)
    held = added(held, values_next, values_far, keys_far).astype(BF16)
    for stride in reversed(strides[:-1]):
        held = added(held, permuted(held, prompt_route(stride, size))).astype(BF16)
    second = permuted(jnp.concatenate([held, head, far]), near_route)
    held = jnp.where(lower, held, second[:rows])
    near, six = units(second, rows, unit, 2)
    third = permuted(jnp.concatenate([head, near, far, six]), shift_route(1, size))
    other = permuted(held, neighbours)
    sources = [(0, 0), (1, rows), (0, unit), (2, 0), (0, 2 * unit), (1, rows + unit), (0, 3 * unit)]
    return held, other, sources, (third, second, far), queries


def give_back(size, unit, rows, where, send, keep, ready):
    even, lower, _ = where
    neighbours = [(i, i ^ 1) for i in range(size)]
    far_route = back(shift_route(4, size)[1:])
    two, four, six = units(keep, rows, unit, 3)
    if size == W + 1:
        third = permuted(send, neighbours)
        total = after(added(keep[:rows], third[:rows]).astype(BF16), ready)
        near, first, last = units(third, rows, unit, 3)
        none = jnp.zeros_like(first)
        parts = [permuted(total, [(j, 0), (j + 1, 1)]) for j in range(2, size, 2)]
        two = permuted(added(two, near).astype(BF16), back(shift_route(2, size)[1:]))
        four = permuted(added(four, jnp.where(even, last, first)).astype(BF16), far_route)
        six = permuted(added(six, jnp.where(even, none, last)).astype(BF16), [(7, 1)])
        total = added(total, *parts).astype(BF16)
        mine = added(jnp.where(even, first, none), two, four, six)
        return total, permuted(total, [(1, 0)]).astype(F32), mine
    strides = [2**i for i in range(2, size.bit_length()) if 2**i < size]
    top = strides[-1]
    zero, *third = units(permuted(send[rows:], back(shift_route(1, size))), 0, unit, 4)
    total = added(keep[:rows], permuted(send[:rows], neighbours)).astype(BF16)
    two, four, six = (added(x, y).astype(BF16) for x, y in zip((two, four, six), third))
    second = permuted(jnp.concatenate([total, two, six]), back(shift_route(2, size)))
    four = added(four, second[rows + unit :])
    mine = added(zero, second[rows : rows + unit], permuted(four.astype(BF16), far_route))
    total = added(total, jnp.where(lower, second[:rows], jnp.zeros_like(total))).astype(BF16)
    for stride in strides[:-1]:
        total = added(total, permuted(total, back(prompt_route(stride, size)))).astype(BF16)
    keys_far = permuted(total, [(top, 0)])
    values_far = permuted(total, [(top + 1, 0)])
    values_next = permuted(total, [(1, 0)])
    return added(total, keys_far), added(values_next, values_far), mine


def per_device(size, queries, keys, values, grad_out, parents, lengths):
    tokens, heads_kv, head_size = keys.shape
    rows = tokens * heads_kv
    one = CAP * TILE * heads_kv
    unit = 2 * one
    window = min(W, size - 2)
    device = lax.axis_index("node")
    keys = keys.reshape(rows, head_size)
    values = values.reshape(rows, head_size)

    order = [(k, k) for k in range(1, window + 1)]
    if size == W + 1:
        order[0], order[2] = (1, 3), (3, 1)
    head, held, *own = load(order, keys, values, parents, lengths, tokens)
    head, *where = lax.optimization_barrier((head, lax.rem(device, 2) == 0, lax.rem(device, 4) < 2, device == 0))
    even, _, root = where
    held, other, sources, blocks, queries = collect(size, unit, rows, where, keys, values, head, held, queries)
    qh, gh = pack(queries, grad_out, heads_kv)
    prompt_k, prompt_v = jnp.where(even, held, other), jnp.where(even, other, held)
    targets = [(1 - k % 2, rows + (k - 1) // 2 * unit) for k in range(1, window + 1)]
    send, keep, kh, ds, p_own = probs(sources, targets, prompt_k, prompt_v, qh, gh, own, blocks)
    grad_queries, dk, dv = grads(qh, gh, kh, ds, p_own)
    prompt_k, prompt_v, mine = give_back(size, unit, rows, where, send, keep, dk)
    own = []
    for side, local, prompt in ((0, dk, prompt_k), (1, dv, prompt_v)):
        whole = local + jnp.where(root, prompt.astype(F32), 0.0)
        own.append(whole.at[:one].add(mine[side * one : (side + 1) * one]).reshape(tokens, heads_kv, head_size))
    return grad_queries, own[0], own[1]


def solution(mesh):
    by_token = P(("leaf", "node"), "tensor", None)
    return jax.shard_map(
        functools.partial(per_device, mesh.shape["node"]),
        mesh=mesh,
        in_specs=(by_token, by_token, by_token, by_token, P("leaf"), P("leaf")),
        out_specs=(by_token, by_token, by_token),
        check_vma=False,
    )
```

```python
import functools
import math

import jax
import jax.numpy as jnp
from jax import lax
from jax.experimental import pallas as pl
from jax.experimental.pallas import tpu as pltpu
from jax.sharding import PartitionSpec as P

TILE = 16
TD = 8
CAP = 2
W = 7
CHUNK = 32
MASKED = -1e30
BF16 = jnp.bfloat16
F32 = jnp.float32


def permuted(block, route):
    return lax.ppermute(block, "node", route)


def column_limits(device, window, parents, lengths):
    cursor = parents[device * TD]
    need = [jnp.int32(0)] * (window + 1)
    for _ in range(W):
        owner = jnp.where(cursor < 0, -1, lax.div(jnp.maximum(cursor, 0), TD))
        distance = device - owner
        active = (owner >= 1) & (distance >= 1) & (distance <= W)
        depth = lax.rem(jnp.maximum(cursor, 0), TD) + 1
        for k in range(1, window + 1):
            need[k] = jnp.where(active & (distance == k), depth, need[k])
        cursor = jnp.where(active, parents[jnp.maximum(owner, 0) * TD], cursor)
    prompt = [jnp.where(device >= 1, lengths[t], 0) for t in range(TD)]
    behind = []
    for k in range(1, window + 1):
        owner = device - k
        seen = [(owner >= 1) & (c < need[k]) for c in range(CAP)]
        behind.append([jnp.where(seen[c], lengths[jnp.maximum(owner, 0) * TD + c], 0) for c in range(CAP)])
    return prompt, behind, [lengths[device * TD + t] for t in range(TD)]


def split_heads(block, heads_ref, start, count, heads_kv, wide):
    wide[: count * heads_kv] = block.astype(F32)
    for h in range(heads_kv):
        heads_ref[h, start : start + count] = wide[pl.ds(h, count, stride=heads_kv), :].astype(BF16)


def join_heads(blocks, count, heads_kv, wide):
    for h in range(heads_kv):
        wide[pl.ds(h, count, stride=heads_kv), :] = blocks[h]
    return wide[: count * heads_kv]


def load_kernel(order, heads_kv, *refs):
    sources, outs, scratch = refs[:4], refs[4:10], refs[10:]
    head, held, own_k, own_v, bias, weight = outs
    parents, lengths, keys, values, wide, arrived = scratch
    copies = [pltpu.make_async_copy(a, b, arrived.at[i]) for i, (a, b) in enumerate(zip(sources, scratch))]
    for copy in copies:
        copy.start()
    tokens = TD * TILE
    front = CAP * TILE * heads_kv
    device = lax.axis_index("node")
    for copy in copies:
        copy.wait()
    head[:front] = keys[:front]
    head[front:] = values[:front]
    held[...] = jnp.where(device == 0, keys[...], jnp.zeros_like(keys))
    split_heads(keys[...], own_k, 0, tokens, heads_kv, wide)
    split_heads(values[...], own_v, 0, tokens, heads_kv, wide)
    place = lax.broadcasted_iota(jnp.int32, (TILE, 128), 0)
    prompt, behind, own = column_limits(device, len(order), parents, lengths)
    even = lax.rem(device, 2) == 0
    limits = prompt
    for on_even, on_odd in order:
        limits = limits + [jnp.where(even, x, y) for x, y in zip(behind[on_even - 1], behind[on_odd - 1])]
    for t, limit in enumerate(limits + own):
        bias[t * TILE : (t + 1) * TILE] = jnp.where(place < limit, 0.0, MASKED)
    lane_place = lax.broadcasted_iota(jnp.int32, (8, 128), 1) // 8
    for t in range(TD):
        weight[:, t * 128 : (t + 1) * 128] = jnp.where(lane_place < lengths[device * TD + t], 1.0, 0.0)


def pack_kernel(heads_kv, q_ref, g_ref, qh, gh, blocks, arrived):
    tokens = TD * TILE
    copies = []
    for pair in range(heads_kv // 2):
        for ref, out in ((q_ref, qh), (g_ref, gh)):
            i = len(copies)
            copy = pltpu.make_async_copy(ref.at[:, pair * 16 : (pair + 1) * 16], blocks.at[i], arrived.at[i])
            copy.start()
            copies.append((copy, out, pair))
    for i, (copy, out, pair) in enumerate(copies):
        copy.wait()
        both = blocks[i].astype(F32)
        for part in range(2):
            out[2 * pair + part] = both[:, part * 8 : (part + 1) * 8].reshape(tokens * 8, 128).astype(BF16)


def causal_bias(columns):
    column_token = lax.broadcasted_iota(jnp.int32, (CHUNK, columns), 1) // 8
    return jnp.where(lax.broadcasted_iota(jnp.int32, (CHUNK, columns), 0) <= column_token, 0.0, MASKED)


def outer_product(rows, columns):
    return lax.dot_general(rows, columns, (((1,), (1,)), ((), ())), preferred_element_type=F32)


def early_kernel(fresh, sources, heads_kv, scale, *refs):
    own_k, own_v, qh, gh, bias = refs[:5]
    blocks, (kh, e_ref, dp_ref, stats, vh, wide) = refs[5:-6], refs[-6:]
    tokens = TD * TILE
    front = CAP * TILE
    behind = len(sources) * front
    start = tokens + fresh * front
    columns = CHUNK * 8
    for side, heads_ref, own in ((0, kh, own_k), (1, vh, own_v)):
        for k, (source, at) in enumerate(sources):
            at += side * front * heads_kv
            split_heads(blocks[source][at : at + front * heads_kv], heads_ref, k * front, front, heads_kv, wide)
        heads_ref[:, behind:] = own[...]
    causal = causal_bias(columns)
    for head in range(heads_kv):
        for c in range(tokens // CHUNK):
            rows = behind + (c + 1) * CHUNK
            span = slice(c * columns, (c + 1) * columns)
            s = outer_product(kh[head, :rows], qh[head, span])
            dp = outer_product(vh[head, :rows], gh[head, span])
            s = s + jnp.concatenate([bias[start : start + rows]] * (columns // 128), axis=1)
            s = jnp.concatenate([s[: rows - CHUNK], s[rows - CHUNK :] + causal], axis=0)
            top = jnp.max(s, axis=0, keepdims=True)
            e = jnp.exp2((s - top) * (scale * math.log2(math.e)))
            e_ref[head, :rows, span] = e
            dp_ref[head, :rows, span] = dp
            stats[head, 0:1, span] = top
            stats[head, 1:2, span] = jnp.sum(e, axis=0, keepdims=True)
            stats[head, 2:3, span] = jnp.sum(e * dp, axis=0, keepdims=True)


def probs_kernel(sources, targets, heads_kv, scale, *refs):
    prompt_k, prompt_v, qh, gh, bias, weight_ref, e_ref, dp_ref, stats, block_ref = refs[:10]
    n_out = 1 + max(target for target, _ in targets)
    outs = refs[10 : 10 + n_out]
    kh, ds_ref, p_own, vh, p_ref, grads, wide = refs[10 + n_out :]
    tokens = TD * TILE
    front = CAP * TILE
    fresh = tokens + len(sources) * front
    before = tokens + len(targets) * front
    columns = CHUNK * 8
    rate = scale * math.log2(math.e)
    device = lax.axis_index("node")

    for side, heads_ref, prompt in ((0, kh, prompt_k), (1, vh, prompt_v)):
        split_heads(prompt[...], heads_ref, 0, tokens, heads_kv, wide)
        for k, (_, at) in enumerate(sources):
            at += side * front * heads_kv
            split_heads(block_ref[at : at + front * heads_kv], heads_ref, tokens + k * front, front, heads_kv, wide)

    for head in range(heads_kv):
        for c in range(tokens // CHUNK):
            rows = before - fresh + (c + 1) * CHUNK
            span = slice(c * columns, (c + 1) * columns)
            s = outer_product(kh[head], qh[head, span])
            dp = outer_product(vh[head], gh[head, span])
            s = s + jnp.concatenate([bias[:fresh]] * (columns // 128), axis=1)
            top_early = stats[head, 0:1, span]
            top = jnp.maximum(jnp.max(s, axis=0, keepdims=True), top_early)
            e = jnp.exp2((s - top) * rate)
            shrink = jnp.exp2((top_early - top) * rate)
            total = jnp.sum(e, axis=0, keepdims=True) + shrink * stats[head, 1:2, span]
            weight = weight_ref[:1, span] / total
            weight_early = weight * shrink
            p = e * weight
            delta = jnp.sum(p * dp, axis=0, keepdims=True) + weight_early * stats[head, 2:3, span]
            ds_ref[head, :fresh, span] = (p * (dp - delta)).astype(BF16)
            p_ref[head % 2, :fresh, span] = p.astype(BF16)
            p = e_ref[head, :rows, span] * weight_early
            ds_ref[head, fresh : fresh + rows, span] = (p * (dp_ref[head, :rows, span] - delta)).astype(BF16)
            p_ref[head % 2, fresh:, span] = p[: before - fresh].astype(BF16)
            p_own[head, : fresh + rows - before, span] = p[before - fresh :].astype(BF16)
        grads[0, head] = scale * jnp.dot(ds_ref[head, :before], qh[head], preferred_element_type=F32)
        grads[1, head] = jnp.dot(p_ref[head % 2], gh[head], preferred_element_type=F32)

    rows = tokens * heads_kv
    rows_front = front * heads_kv
    even = lax.rem(device, 2) == 0
    for side in range(2):
        dprompt = join_heads([grads[side, h, :tokens] for h in range(heads_kv)], tokens, heads_kv, wide).astype(BF16)
        kept = even if side == 0 else jnp.logical_not(even)

        @pl.when(kept)
        def _():
            outs[1][:rows] = dprompt

        @pl.when(jnp.logical_not(kept))
        def _():
            outs[0][:rows] = dprompt

        for k, (target, start) in enumerate(targets):
            span = slice(tokens + k * front, tokens + (k + 1) * front)
            block = join_heads([grads[side, h, span] for h in range(heads_kv)], front, heads_kv, wide).astype(BF16)
            start += side * rows_front
            outs[target][start : start + rows_front] = block


def grads_kernel(heads_kv, scale, *refs):
    qh, gh, kh_fresh, kh_early, ds_ref, p_own, dq_ref, dk_ref, dv_ref, wide = refs
    tokens = TD * TILE
    kh = [jnp.concatenate([kh_fresh[h], kh_early[h]], axis=0) for h in range(heads_kv)]
    before = kh[0].shape[0] - tokens
    columns = CHUNK * 8
    dk = []
    dv = []
    for pair in range(heads_kv // 2):
        for c in range(tokens // CHUNK):
            rows = before + (c + 1) * CHUNK
            span = slice(c * columns, (c + 1) * columns)
            parts = []
            for head in (2 * pair, 2 * pair + 1):
                dq = lax.dot_general(
                    kh[head][:rows], ds_ref[head, :rows, span], (((0,), (0,)), ((), ())), preferred_element_type=F32
                )
                parts.append((scale * dq.T).reshape(CHUNK, 8, 128))
            dq_ref[c * CHUNK : (c + 1) * CHUNK, pair * 16 : (pair + 1) * 16] = jnp.concatenate(parts, axis=1).astype(BF16)
        for head in (2 * pair, 2 * pair + 1):
            for source, factor, out in ((ds_ref.at[head, before:], qh, dk), (p_own.at[head], gh, dv)):
                pieces = []
                for c in range(tokens // CHUNK):
                    start = c * columns
                    pieces.append(
                        jnp.dot(
                            source[c * CHUNK : (c + 1) * CHUNK, start:], factor[head, start:], preferred_element_type=F32
                        )
                    )
                out.append(jnp.concatenate(pieces, axis=0))
    dk_ref[...] = scale * join_heads(dk, tokens, heads_kv, wide)
    dv_ref[...] = join_heads(dv, tokens, heads_kv, wide)


VMEM = pl.BlockSpec(memory_space=pltpu.VMEM)


HBM = pl.BlockSpec(memory_space=pltpu.HBM)


def call(kernel, name, operands, outputs, scratch, flops, transcendentals=0, place=VMEM):
    sizes = [a.size * a.dtype.itemsize for a in (*operands, *outputs)]
    if place is HBM:
        operands = [pltpu.with_memory_space_constraint(a, pltpu.HBM) for a in operands]
    return pl.pallas_call(
        kernel,
        in_specs=[place] * len(operands),
        out_specs=[VMEM] * len(outputs),
        out_shape=outputs,
        scratch_shapes=scratch,
        compiler_params=pltpu.CompilerParams(vmem_limit_bytes=16 * 1024 * 1024),
        cost_estimate=pl.CostEstimate(flops=flops, bytes_accessed=sum(sizes), transcendentals=transcendentals),
        name=name,
    )(*operands)


def load(order, keys, values, parents, lengths, tokens):
    rows, head_size = keys.shape
    heads_kv = rows // tokens
    array = jax.ShapeDtypeStruct
    return call(
        functools.partial(load_kernel, order, heads_kv),
        "load",
        (parents, lengths, keys, values),
        [array((2 * CAP * TILE * heads_kv, head_size), BF16), array((rows, head_size), BF16)]
        + [array((heads_kv, tokens, head_size), BF16)] * 2
        + [array((2 * tokens + len(order) * CAP * TILE, 128), F32), array((8, tokens * 8), F32)],
        [pltpu.SMEM(parents.shape, jnp.int32), pltpu.SMEM(lengths.shape, jnp.int32)]
        + [pltpu.VMEM((rows, head_size), BF16)] * 2
        + [pltpu.VMEM((rows, head_size), F32), pltpu.SemaphoreType.DMA((4,))],
        flops=1 << 20,
        place=HBM,
    )


def pack(queries, grad_out, heads_kv):
    tokens, heads_q, head_size = queries.shape
    array = jax.ShapeDtypeStruct
    return call(
        functools.partial(pack_kernel, heads_kv),
        "pack",
        (queries, grad_out),
        [array((heads_kv, tokens * 8, head_size), BF16)] * 2,
        [pltpu.VMEM((heads_kv, tokens, 16, head_size), BF16), pltpu.SemaphoreType.DMA((heads_kv,))],
        flops=1 << 20,
        place=HBM,
    )


def early(fresh, sources, qh, gh, own, blocks):
    own_k, own_v, bias, _ = own
    heads_kv, tokens, head_size = own_k.shape
    rows = len(sources) * CAP * TILE + tokens
    array = jax.ShapeDtypeStruct
    work = heads_kv * tokens * 8 * rows
    return call(
        functools.partial(early_kernel, fresh, sources, heads_kv, head_size**-0.5),
        "early",
        (own_k, own_v, qh, gh, bias, *blocks),
        [array((heads_kv, rows, head_size), BF16)]
        + [array((heads_kv, rows, tokens * 8), F32)] * 2
        + [array((heads_kv, 8, tokens * 8), F32)],
        [pltpu.VMEM((heads_kv, rows, head_size), BF16), pltpu.VMEM((CAP * TILE * heads_kv, head_size), F32)],
        flops=4 * work * head_size,
        transcendentals=work,
    )


def probs(sources, targets, prompt_k, prompt_v, qh, gh, own, parts, block):
    _, own_v, bias, weight = own
    heads_kv, tokens, head_size = own_v.shape
    rows = tokens * heads_kv
    front = CAP * TILE
    unit = 2 * front * heads_kv
    fresh = tokens + len(sources) * front
    before = tokens + len(targets) * front
    sizes = [max(start for target, start in targets if target == t) + unit for t in range(1 + max(targets)[0])]
    array = jax.ShapeDtypeStruct
    work = heads_kv * tokens * 8 * (before + tokens)
    return call(
        functools.partial(probs_kernel, sources, targets, heads_kv, head_size**-0.5),
        "probs",
        (prompt_k, prompt_v, qh, gh, bias, weight, *parts, block),
        [array((size, head_size), BF16) for size in sizes]
        + [
            array((heads_kv, fresh, head_size), BF16),
            array((heads_kv, before + tokens, tokens * 8), BF16),
            array((heads_kv, tokens, tokens * 8), BF16),
        ],
        [
            pltpu.VMEM((heads_kv, fresh, head_size), BF16),
            pltpu.VMEM((2, before, tokens * 8), BF16),
            pltpu.VMEM((2, heads_kv, before, head_size), F32),
            pltpu.VMEM((rows, head_size), F32),
        ],
        flops=6 * work * head_size,
        transcendentals=work,
    )


def grads(qh, gh, kh_fresh, kh_early, ds, p_own):
    heads_kv, tokens, _ = p_own.shape
    head_size = kh_fresh.shape[2]
    array = jax.ShapeDtypeStruct
    return call(
        functools.partial(grads_kernel, heads_kv, head_size**-0.5),
        "grads",
        (qh, gh, kh_fresh, kh_early, ds, p_own),
        [
            array((tokens, heads_kv * 8, head_size), BF16),
            array((tokens * heads_kv, head_size), F32),
            array((tokens * heads_kv, head_size), F32),
        ],
        [pltpu.VMEM((tokens * heads_kv, head_size), F32)],
        flops=2 * heads_kv * tokens * 8 * ds.shape[1] * head_size,
    )


def shift_route(distance, size):
    return [(i, i + distance) for i in range(size - distance)]


def back(route):
    return [(j, i) for i, j in route]


def added(*blocks):
    total = blocks[0].astype(F32)
    for block in blocks[1:]:
        total = total + block.astype(F32)
    return total


def after(array, *earlier):
    return lax.optimization_barrier((array, *earlier))[0]


def units(array, start, unit, count):
    return [array[start + i * unit : start + (i + 1) * unit] for i in range(count)]


def prompt_route(stride, size):
    return [(i + j, i + j + stride) for i in range(0, size, 2 * stride) for j in (0, 1)]


def collect(size, unit, rows, where, keys, values, head, held, queries, grad_out):
    even, lower, _ = where
    neighbours = [(i, i ^ 1) for i in range(size)]
    far_route = shift_route(4, size)[1:]
    near_route = shift_route(2, size)
    if size == W + 1:
        keys_far = permuted(keys, [(0, 4)])
        values_far = permuted(values, [(0, 5)])
        values_next = permuted(values, [(0, 1)])
        head, queries = lax.optimization_barrier((head, queries, keys_far))[:2]
        qh, gh = pack(queries, grad_out, keys.shape[0] // queries.shape[0])
        far = permuted(head, far_route)
        six = permuted(head, [(1, 7)])
        held = after(added(held, values_far, values_next, keys_far).astype(BF16), far, six, qh)
        second = permuted(jnp.concatenate([held, head]), near_route)
        crossed = jnp.where(even, jnp.concatenate([head, far]), jnp.concatenate([far, six]))
        crossed = permuted(crossed, neighbours)
        held = jnp.where(lower, held, second[:rows])
        third = permuted(after(jnp.concatenate([held, second[rows:]]), crossed), neighbours)
        early_sources = [(0, rows), (1, 0), (2, 0), (1, unit), (3, 0)]
        return held, third[:rows], third, [(0, rows)], early_sources, (second, crossed, far, six), (qh, gh)
    strides = [2**i for i in range(2, size.bit_length()) if 2**i < size]
    top = strides[-1]
    keys_far = permuted(keys, [(0, top)])
    values_far = permuted(values, [(0, top + 1)])
    values_next = permuted(values, [(0, 1)])
    far = permuted(head, far_route)
    held = added(held, values_next, values_far, keys_far).astype(BF16)
    for stride in reversed(strides[:-1]):
        held = added(held, permuted(held, prompt_route(stride, size))).astype(BF16)
    second = permuted(jnp.concatenate([held, head, far]), near_route)
    held = jnp.where(lower, held, second[:rows])
    near, six = units(second, rows, unit, 2)
    third = permuted(jnp.concatenate([head, near, far, six]), shift_route(1, size))
    other = permuted(held, neighbours)
    fresh_sources = [(0, i * unit) for i in range(4)]
    early_sources = [(0, rows), (1, 0), (0, rows + unit)]
    return held, other, third, fresh_sources, early_sources, (second, far), pack(queries, grad_out, keys.shape[0] // queries.shape[0])


def give_back(size, unit, rows, where, send, keep, ready):
    even, lower, _ = where
    neighbours = [(i, i ^ 1) for i in range(size)]
    far_route = back(shift_route(4, size)[1:])
    two, four, six = units(keep, rows, unit, 3)
    if size == W + 1:
        third = permuted(send, neighbours)
        total = after(added(keep[:rows], third[:rows]).astype(BF16), ready)
        near, first, last = units(third, rows, unit, 3)
        none = jnp.zeros_like(first)
        parts = [permuted(total, [(j, 0), (j + 1, 1)]) for j in range(2, size, 2)]
        two = permuted(added(two, near).astype(BF16), back(shift_route(2, size)[1:]))
        four = permuted(added(four, jnp.where(even, last, first)).astype(BF16), far_route)
        six = permuted(added(six, jnp.where(even, none, last)).astype(BF16), [(7, 1)])
        total = added(total, *parts).astype(BF16)
        mine = added(jnp.where(even, first, none), two, four, six)
        return total, permuted(total, [(1, 0)]).astype(F32), mine
    strides = [2**i for i in range(2, size.bit_length()) if 2**i < size]
    top = strides[-1]
    zero, *third = units(permuted(send[rows:], back(shift_route(1, size))), 0, unit, 4)
    total = added(keep[:rows], permuted(send[:rows], neighbours)).astype(BF16)
    two, four, six = (added(x, y).astype(BF16) for x, y in zip((two, four, six), third))
    second = permuted(jnp.concatenate([total, two, six]), back(shift_route(2, size)))
    four = added(four, second[rows + unit :])
    mine = added(zero, second[rows : rows + unit], permuted(four.astype(BF16), far_route))
    total = added(total, jnp.where(lower, second[:rows], jnp.zeros_like(total))).astype(BF16)
    for stride in strides[:-1]:
        total = added(total, permuted(total, back(prompt_route(stride, size)))).astype(BF16)
    keys_far = permuted(total, [(top, 0)])
    values_far = permuted(total, [(top + 1, 0)])
    values_next = permuted(total, [(1, 0)])
    return added(total, keys_far), added(values_next, values_far), mine


def per_device(size, queries, keys, values, grad_out, parents, lengths):
    tokens, heads_kv, head_size = keys.shape
    rows = tokens * heads_kv
    one = CAP * TILE * heads_kv
    unit = 2 * one
    window = min(W, size - 2)
    device = lax.axis_index("node")
    keys = keys.reshape(rows, head_size)
    values = values.reshape(rows, head_size)

    if size == W + 1:
        order = [(1, 3), (2, 2), (3, 1), (4, 4), (5, 5), (6, 6)]
        targets = [(k % 2, rows + k // 2 * unit) for k in range(window)]
    else:
        order = [(k, k) for k in (1, 3, 5, 7, 2, 4, 6)]
        targets = [(0, rows + i * unit) for i in range(4)] + [(1, rows + i * unit) for i in range(3)]
    head, held, *own = load(order, keys, values, parents, lengths, tokens)
    head, *where = lax.optimization_barrier((head, lax.rem(device, 2) == 0, lax.rem(device, 4) < 2, device == 0))
    even, _, root = where
    held, other, block, fresh_sources, early_sources, blocks, (qh, gh) = collect(
        size, unit, rows, where, keys, values, head, held, queries, grad_out
    )
    kh_early, *parts = early(len(fresh_sources), early_sources, qh, gh, own, blocks)
    prompt_k, prompt_v = jnp.where(even, held, other), jnp.where(even, other, held)
    send, keep, kh, ds, p_own = probs(fresh_sources, targets, prompt_k, prompt_v, qh, gh, own, parts, block)
    grad_queries, dk, dv = grads(qh, gh, kh, kh_early, ds, p_own)
    prompt_k, prompt_v, mine = give_back(size, unit, rows, where, send, keep, dk)
    own = []
    for side, local, prompt in ((0, dk, prompt_k), (1, dv, prompt_v)):
        whole = local + jnp.where(root, prompt.astype(F32), 0.0)
        own.append(whole.at[:one].add(mine[side * one : (side + 1) * one]).reshape(tokens, heads_kv, head_size))
    return grad_queries, own[0], own[1]


def solution(mesh):
    by_token = P(("leaf", "node"), "tensor", None)
    return jax.shard_map(
        functools.partial(per_device, mesh.shape["node"]),
        mesh=mesh,
        in_specs=(by_token, by_token, by_token, by_token, P("leaf"), P("leaf")),
        out_specs=(by_token, by_token, by_token),
        check_vma=False,
    )
```

```python
import functools
import math

import jax
import jax.numpy as jnp
from jax import lax
from jax.experimental import pallas as pl
from jax.experimental.pallas import tpu as pltpu
from jax.sharding import PartitionSpec as P

TILE = 16
TD = 8
CAP = 2
W = 7
CHUNK = 32
MASKED = -1e30
BF16 = jnp.bfloat16
F32 = jnp.float32


def permuted(block, route):
    return lax.ppermute(block, "node", route)


def column_limits(device, window, parents, lengths):
    cursor = parents[device * TD]
    need = [jnp.int32(0)] * (window + 1)
    for _ in range(W):
        owner = jnp.where(cursor < 0, -1, lax.div(jnp.maximum(cursor, 0), TD))
        distance = device - owner
        active = (owner >= 1) & (distance >= 1) & (distance <= W)
        depth = lax.rem(jnp.maximum(cursor, 0), TD) + 1
        for k in range(1, window + 1):
            need[k] = jnp.where(active & (distance == k), depth, need[k])
        cursor = jnp.where(active, parents[jnp.maximum(owner, 0) * TD], cursor)
    prompt = [jnp.where(device >= 1, lengths[t], 0) for t in range(TD)]
    behind = []
    for k in range(1, window + 1):
        owner = device - k
        seen = [(owner >= 1) & (c < need[k]) for c in range(CAP)]
        behind.append([jnp.where(seen[c], lengths[jnp.maximum(owner, 0) * TD + c], 0) for c in range(CAP)])
    return prompt, behind, [lengths[device * TD + t] for t in range(TD)]


def split_heads(block, heads_ref, start, count, heads_kv, wide):
    wide[: count * heads_kv] = block.astype(F32)
    for h in range(heads_kv):
        heads_ref[h, start : start + count] = wide[pl.ds(h, count, stride=heads_kv), :].astype(BF16)


def join_heads(blocks, count, heads_kv, wide):
    for h in range(heads_kv):
        wide[pl.ds(h, count, stride=heads_kv), :] = blocks[h]
    return wide[: count * heads_kv]


def load_kernel(order, heads_kv, *refs):
    sources, outs, scratch = refs[:4], refs[4:10], refs[10:]
    head, held, own_k, own_v, bias, weight = outs
    parents, lengths, keys, values, wide, arrived = scratch
    copies = [pltpu.make_async_copy(a, b, arrived.at[i]) for i, (a, b) in enumerate(zip(sources, scratch))]
    for copy in copies:
        copy.start()
    tokens = TD * TILE
    front = CAP * TILE * heads_kv
    device = lax.axis_index("node")
    for copy in copies:
        copy.wait()
    head[:front] = keys[:front]
    head[front:] = values[:front]
    held[...] = jnp.where(device == 0, keys[...], jnp.zeros_like(keys))
    split_heads(keys[...], own_k, 0, tokens, heads_kv, wide)
    split_heads(values[...], own_v, 0, tokens, heads_kv, wide)
    place = lax.broadcasted_iota(jnp.int32, (TILE, 128), 0)
    prompt, behind, own = column_limits(device, len(order), parents, lengths)
    even = lax.rem(device, 2) == 0
    limits = prompt
    for on_even, on_odd in order:
        limits = limits + [jnp.where(even, x, y) for x, y in zip(behind[on_even - 1], behind[on_odd - 1])]
    for t, limit in enumerate(limits + own):
        bias[t * TILE : (t + 1) * TILE] = jnp.where(place < limit, 0.0, MASKED)
    lane_place = lax.broadcasted_iota(jnp.int32, (8, 128), 1) // 8
    for t in range(TD):
        weight[:, t * 128 : (t + 1) * 128] = jnp.where(lane_place < lengths[device * TD + t], 1.0, 0.0)


def pack_kernel(heads_kv, q_ref, g_ref, qh, gh, blocks, arrived):
    tokens = TD * TILE
    copies = []
    for pair in range(heads_kv // 2):
        for ref, out in ((q_ref, qh), (g_ref, gh)):
            i = len(copies)
            copy = pltpu.make_async_copy(ref.at[:, pair * 16 : (pair + 1) * 16], blocks.at[i], arrived.at[i])
            copy.start()
            copies.append((copy, out, pair))
    for i, (copy, out, pair) in enumerate(copies):
        copy.wait()
        both = blocks[i].astype(F32)
        for part in range(2):
            out[2 * pair + part] = both[:, part * 8 : (part + 1) * 8].reshape(tokens * 8, 128).astype(BF16)


def causal_bias(columns):
    column_token = lax.broadcasted_iota(jnp.int32, (CHUNK, columns), 1) // 8
    return jnp.where(lax.broadcasted_iota(jnp.int32, (CHUNK, columns), 0) <= column_token, 0.0, MASKED)


def outer_product(rows, columns):
    return lax.dot_general(rows, columns, (((1,), (1,)), ((), ())), preferred_element_type=F32)


def early_kernel(fresh, sources, heads_kv, scale, *refs):
    own_k, own_v, qh, gh, bias = refs[:5]
    blocks, (kh, e_ref, dp_ref, stats, vh, wide) = refs[5:-6], refs[-6:]
    tokens = TD * TILE
    front = CAP * TILE
    behind = len(sources) * front
    start = tokens + fresh * front
    columns = CHUNK * 8
    for side, heads_ref, own in ((0, kh, own_k), (1, vh, own_v)):
        for k, (source, at) in enumerate(sources):
            at += side * front * heads_kv
            split_heads(blocks[source][at : at + front * heads_kv], heads_ref, k * front, front, heads_kv, wide)
        heads_ref[:, behind:] = own[...]
    causal = causal_bias(columns)
    for head in range(heads_kv):
        for c in range(tokens // CHUNK):
            rows = behind + (c + 1) * CHUNK
            span = slice(c * columns, (c + 1) * columns)
            s = outer_product(kh[head, :rows], qh[head, span])
            dp = outer_product(vh[head, :rows], gh[head, span])
            s = s + jnp.concatenate([bias[start : start + rows]] * (columns // 128), axis=1)
            s = jnp.concatenate([s[: rows - CHUNK], s[rows - CHUNK :] + causal], axis=0)
            top = jnp.max(s, axis=0, keepdims=True)
            e = jnp.exp2((s - top) * (scale * math.log2(math.e)))
            e_ref[head, :rows, span] = e
            dp_ref[head, :rows, span] = dp
            stats[head, 0:1, span] = top
            stats[head, 1:2, span] = jnp.sum(e, axis=0, keepdims=True)
            stats[head, 2:3, span] = jnp.sum(e * dp, axis=0, keepdims=True)


def probs_kernel(sources, heads_kv, scale, *refs):
    prompt_k, prompt_v, qh, gh, bias, weight_ref, e_ref, dp_ref, stats, block_ref = refs[:10]
    send_ref, keep_ref, kh, ds_ref, p_behind, p_own, vh, p_ref, grads, wide = refs[10:]
    tokens = TD * TILE
    front = CAP * TILE
    fresh = tokens + len(sources) * front
    behind = p_behind.shape[1]
    before = tokens + behind
    columns = CHUNK * 8
    rate = scale * math.log2(math.e)
    device = lax.axis_index("node")

    for side, heads_ref, prompt in ((0, kh, prompt_k), (1, vh, prompt_v)):
        split_heads(prompt[...], heads_ref, 0, tokens, heads_kv, wide)
        for k, (_, at) in enumerate(sources):
            at += side * front * heads_kv
            split_heads(block_ref[at : at + front * heads_kv], heads_ref, tokens + k * front, front, heads_kv, wide)

    for head in range(heads_kv):
        for c in range(tokens // CHUNK):
            rows = before - fresh + (c + 1) * CHUNK
            span = slice(c * columns, (c + 1) * columns)
            s = outer_product(kh[head], qh[head, span])
            dp = outer_product(vh[head], gh[head, span])
            s = s + jnp.concatenate([bias[:fresh]] * (columns // 128), axis=1)
            top_early = stats[head, 0:1, span]
            top = jnp.maximum(jnp.max(s, axis=0, keepdims=True), top_early)
            e = jnp.exp2((s - top) * rate)
            shrink = jnp.exp2((top_early - top) * rate)
            total = jnp.sum(e, axis=0, keepdims=True) + shrink * stats[head, 1:2, span]
            weight = weight_ref[:1, span] / total
            weight_early = weight * shrink
            p = e * weight
            delta = jnp.sum(p * dp, axis=0, keepdims=True) + weight_early * stats[head, 2:3, span]
            ds_ref[head, :fresh, span] = (p * (dp - delta)).astype(BF16)
            p_ref[head % 2, :, span] = p[:tokens].astype(BF16)
            p_behind[head, : fresh - tokens, span] = p[tokens:].astype(BF16)
            p = e_ref[head, :rows, span] * weight_early
            ds_ref[head, fresh : fresh + rows, span] = (p * (dp_ref[head, :rows, span] - delta)).astype(BF16)
            p_behind[head, fresh - tokens :, span] = p[: before - fresh].astype(BF16)
            p_own[head, : fresh + rows - before, span] = p[before - fresh :].astype(BF16)
        grads[0, head] = scale * jnp.dot(ds_ref[head, :tokens], qh[head], preferred_element_type=F32)
        grads[1, head] = jnp.dot(p_ref[head % 2], gh[head], preferred_element_type=F32)

    even = lax.rem(device, 2) == 0
    for side in range(2):
        dprompt = join_heads([grads[side, h] for h in range(heads_kv)], tokens, heads_kv, wide).astype(BF16)
        kept = even if side == 0 else jnp.logical_not(even)

        @pl.when(kept)
        def _():
            keep_ref[...] = dprompt

        @pl.when(jnp.logical_not(kept))
        def _():
            send_ref[...] = dprompt


def windows_kernel(targets, heads_kv, scale, qh, gh, ds_ref, p_behind, send_ref, keep_ref, grads, wide):
    front = CAP * TILE
    tokens = TD * TILE
    behind = p_behind.shape[1]
    for head in range(heads_kv):
        ds = ds_ref[head, tokens : tokens + behind]
        grads[0, head] = scale * jnp.dot(ds, qh[head], preferred_element_type=F32)
        grads[1, head] = jnp.dot(p_behind[head], gh[head], preferred_element_type=F32)
    for side in range(2):
        for k, (target, start) in enumerate(targets):
            span = slice(k * front, (k + 1) * front)
            block = join_heads([grads[side, h, span] for h in range(heads_kv)], front, heads_kv, wide).astype(BF16)
            start += side * front * heads_kv
            (send_ref, keep_ref)[target][start : start + front * heads_kv] = block


def grads_kernel(heads_kv, scale, *refs):
    qh, gh, kh_fresh, kh_early, ds_ref, p_own, dq_ref, dk_ref, dv_ref, wide = refs
    tokens = TD * TILE
    kh = [jnp.concatenate([kh_fresh[h], kh_early[h]], axis=0) for h in range(heads_kv)]
    before = kh[0].shape[0] - tokens
    columns = CHUNK * 8
    dk = []
    dv = []
    for pair in range(heads_kv // 2):
        for c in range(tokens // CHUNK):
            rows = before + (c + 1) * CHUNK
            span = slice(c * columns, (c + 1) * columns)
            parts = []
            for head in (2 * pair, 2 * pair + 1):
                dq = lax.dot_general(
                    kh[head][:rows], ds_ref[head, :rows, span], (((0,), (0,)), ((), ())), preferred_element_type=F32
                )
                parts.append((scale * dq.T).reshape(CHUNK, 8, 128))
            dq_ref[c * CHUNK : (c + 1) * CHUNK, pair * 16 : (pair + 1) * 16] = jnp.concatenate(parts, axis=1).astype(BF16)
        for head in (2 * pair, 2 * pair + 1):
            for source, factor, out in ((ds_ref.at[head, before:], qh, dk), (p_own.at[head], gh, dv)):
                pieces = []
                for c in range(tokens // CHUNK):
                    start = c * columns
                    pieces.append(
                        jnp.dot(
                            source[c * CHUNK : (c + 1) * CHUNK, start:], factor[head, start:], preferred_element_type=F32
                        )
                    )
                out.append(jnp.concatenate(pieces, axis=0))
    dk_ref[...] = scale * join_heads(dk, tokens, heads_kv, wide)
    dv_ref[...] = join_heads(dv, tokens, heads_kv, wide)


VMEM = pl.BlockSpec(memory_space=pltpu.VMEM)


HBM = pl.BlockSpec(memory_space=pltpu.HBM)


def call(kernel, name, operands, outputs, scratch, flops, transcendentals=0, place=VMEM):
    sizes = [a.size * a.dtype.itemsize for a in (*operands, *outputs)]
    if place is HBM:
        operands = [pltpu.with_memory_space_constraint(a, pltpu.HBM) for a in operands]
    return pl.pallas_call(
        kernel,
        in_specs=[place] * len(operands),
        out_specs=[VMEM] * len(outputs),
        out_shape=outputs,
        scratch_shapes=scratch,
        compiler_params=pltpu.CompilerParams(vmem_limit_bytes=16 * 1024 * 1024),
        cost_estimate=pl.CostEstimate(flops=flops, bytes_accessed=sum(sizes), transcendentals=transcendentals),
        name=name,
    )(*operands)


def load(order, keys, values, parents, lengths, tokens):
    rows, head_size = keys.shape
    heads_kv = rows // tokens
    array = jax.ShapeDtypeStruct
    return call(
        functools.partial(load_kernel, order, heads_kv),
        "load",
        (parents, lengths, keys, values),
        [array((2 * CAP * TILE * heads_kv, head_size), BF16), array((rows, head_size), BF16)]
        + [array((heads_kv, tokens, head_size), BF16)] * 2
        + [array((2 * tokens + len(order) * CAP * TILE, 128), F32), array((8, tokens * 8), F32)],
        [pltpu.SMEM(parents.shape, jnp.int32), pltpu.SMEM(lengths.shape, jnp.int32)]
        + [pltpu.VMEM((rows, head_size), BF16)] * 2
        + [pltpu.VMEM((rows, head_size), F32), pltpu.SemaphoreType.DMA((4,))],
        flops=1 << 20,
        place=HBM,
    )


def pack(queries, grad_out, heads_kv):
    tokens, heads_q, head_size = queries.shape
    array = jax.ShapeDtypeStruct
    return call(
        functools.partial(pack_kernel, heads_kv),
        "pack",
        (queries, grad_out),
        [array((heads_kv, tokens * 8, head_size), BF16)] * 2,
        [pltpu.VMEM((heads_kv, tokens, 16, head_size), BF16), pltpu.SemaphoreType.DMA((heads_kv,))],
        flops=1 << 20,
        place=HBM,
    )


def early(fresh, sources, qh, gh, own, blocks):
    own_k, own_v, bias, _ = own
    heads_kv, tokens, head_size = own_k.shape
    rows = len(sources) * CAP * TILE + tokens
    array = jax.ShapeDtypeStruct
    work = heads_kv * tokens * 8 * rows
    return call(
        functools.partial(early_kernel, fresh, sources, heads_kv, head_size**-0.5),
        "early",
        (own_k, own_v, qh, gh, bias, *blocks),
        [array((heads_kv, rows, head_size), BF16)]
        + [array((heads_kv, rows, tokens * 8), F32)] * 2
        + [array((heads_kv, 8, tokens * 8), F32)],
        [pltpu.VMEM((heads_kv, rows, head_size), BF16), pltpu.VMEM((CAP * TILE * heads_kv, head_size), F32)],
        flops=4 * work * head_size,
        transcendentals=work,
    )


def probs(sources, behind, prompt_k, prompt_v, qh, gh, own, parts, block):
    _, own_v, bias, weight = own
    heads_kv, tokens, head_size = own_v.shape
    rows = tokens * heads_kv
    front = CAP * TILE
    fresh = tokens + len(sources) * front
    before = tokens + behind * front
    array = jax.ShapeDtypeStruct
    work = heads_kv * tokens * 8 * (before + tokens)
    return call(
        functools.partial(probs_kernel, sources, heads_kv, head_size**-0.5),
        "probs",
        (prompt_k, prompt_v, qh, gh, bias, weight, *parts, block),
        [array((rows, head_size), BF16)] * 2
        + [
            array((heads_kv, fresh, head_size), BF16),
            array((heads_kv, before + tokens, tokens * 8), BF16),
            array((heads_kv, behind * front, tokens * 8), BF16),
            array((heads_kv, tokens, tokens * 8), BF16),
        ],
        [
            pltpu.VMEM((heads_kv, fresh, head_size), BF16),
            pltpu.VMEM((2, tokens, tokens * 8), BF16),
            pltpu.VMEM((2, heads_kv, tokens, head_size), F32),
            pltpu.VMEM((rows, head_size), F32),
        ],
        flops=5 * work * head_size,
        transcendentals=work,
    )


def windows(targets, qh, gh, ds, p_behind):
    heads_kv, behind, _ = p_behind.shape
    head_size = qh.shape[2]
    front = CAP * TILE * heads_kv
    count = [sum(target == t for target, _ in targets) for t in (0, 1)]
    array = jax.ShapeDtypeStruct
    return call(
        functools.partial(windows_kernel, targets, heads_kv, head_size**-0.5),
        "windows",
        (qh, gh, ds, p_behind),
        [array((2 * front * n, head_size), BF16) for n in count],
        [pltpu.VMEM((2, heads_kv, behind, head_size), F32), pltpu.VMEM((front, head_size), F32)],
        flops=4 * p_behind.size * head_size,
    )


def grads(qh, gh, kh_fresh, kh_early, ds, p_own):
    heads_kv, tokens, _ = p_own.shape
    head_size = kh_fresh.shape[2]
    array = jax.ShapeDtypeStruct
    return call(
        functools.partial(grads_kernel, heads_kv, head_size**-0.5),
        "grads",
        (qh, gh, kh_fresh, kh_early, ds, p_own),
        [
            array((tokens, heads_kv * 8, head_size), BF16),
            array((tokens * heads_kv, head_size), F32),
            array((tokens * heads_kv, head_size), F32),
        ],
        [pltpu.VMEM((tokens * heads_kv, head_size), F32)],
        flops=2 * heads_kv * tokens * 8 * ds.shape[1] * head_size,
    )


def shift_route(distance, size):
    return [(i, i + distance) for i in range(size - distance)]


def back(route):
    return [(j, i) for i, j in route]


def added(*blocks):
    total = blocks[0].astype(F32)
    for block in blocks[1:]:
        total = total + block.astype(F32)
    return total


def after(array, *earlier):
    return lax.optimization_barrier((array, *earlier))[0]


def units(array, start, unit, count):
    return [array[start + i * unit : start + (i + 1) * unit] for i in range(count)]


def prompt_route(stride, size):
    return [(i + j, i + j + stride) for i in range(0, size, 2 * stride) for j in (0, 1)]


def collect(size, unit, rows, where, keys, values, head, held, queries, grad_out):
    even, lower, _ = where
    neighbours = [(i, i ^ 1) for i in range(size)]
    far_route = shift_route(4, size)[1:]
    near_route = shift_route(2, size)
    if size == W + 1:
        keys_far = permuted(keys, [(0, 4)])
        values_far = permuted(values, [(0, 5)])
        values_next = permuted(values, [(0, 1)])
        head, queries = lax.optimization_barrier((head, queries, keys_far))[:2]
        qh, gh = pack(queries, grad_out, keys.shape[0] // queries.shape[0])
        far = permuted(head, far_route)
        six = permuted(head, [(1, 7)])
        held = after(added(held, values_far, values_next, keys_far).astype(BF16), far, six, qh)
        second = permuted(jnp.concatenate([held, head]), near_route)
        crossed = jnp.where(even, jnp.concatenate([head, far]), jnp.concatenate([far, six]))
        crossed = permuted(crossed, neighbours)
        held = jnp.where(lower, held, second[:rows])
        third = permuted(after(jnp.concatenate([held, second[rows:]]), crossed), neighbours)
        early_sources = [(0, rows), (1, 0), (2, 0), (1, unit), (3, 0)]
        return held, third[:rows], third, [(0, rows)], early_sources, (second, crossed, far, six), (qh, gh)
    strides = [2**i for i in range(2, size.bit_length()) if 2**i < size]
    top = strides[-1]
    keys_far = permuted(keys, [(0, top)])
    values_far = permuted(values, [(0, top + 1)])
    values_next = permuted(values, [(0, 1)])
    far = permuted(head, far_route)
    held = added(held, values_next, values_far, keys_far).astype(BF16)
    for stride in reversed(strides[:-1]):
        held = added(held, permuted(held, prompt_route(stride, size))).astype(BF16)
    second = permuted(jnp.concatenate([held, head, far]), near_route)
    held = jnp.where(lower, held, second[:rows])
    near, six = units(second, rows, unit, 2)
    third = permuted(jnp.concatenate([head, near, far, six]), shift_route(1, size))
    other = permuted(held, neighbours)
    fresh_sources = [(0, i * unit) for i in range(4)]
    early_sources = [(0, rows), (1, 0), (0, rows + unit)]
    return held, other, third, fresh_sources, early_sources, (second, far), pack(queries, grad_out, keys.shape[0] // queries.shape[0])


def give_back(size, unit, where, prompt, behind, finish):
    even, lower, _ = where
    neighbours = [(i, i ^ 1) for i in range(size)]
    far_route = back(shift_route(4, size)[1:])
    send, keep = prompt
    rows = keep.shape[0]
    two, four, six = units(behind[1], 0, unit, 3)
    if size == W + 1:
        total = added(keep, permuted(send, neighbours)).astype(BF16)
        finished = finish(total)
        near, first, last = units(permuted(behind[0], neighbours), 0, unit, 3)
        none = jnp.zeros_like(first)
        parts = [permuted(total, [(j, 0), (j + 1, 1)]) for j in range(2, size, 2)]
        two = permuted(added(two, near).astype(BF16), back(shift_route(2, size)[1:]))
        four = after(added(four, jnp.where(even, last, first)).astype(BF16), finished[1])
        four = permuted(four, far_route)
        six = permuted(added(six, jnp.where(even, none, last)).astype(BF16), [(7, 1)])
        total = added(total, *parts).astype(BF16)
        mine = added(jnp.where(even, first, none), two, four, six)
        return finished, total, permuted(total, [(1, 0)]).astype(F32), mine
    strides = [2**i for i in range(2, size.bit_length()) if 2**i < size]
    top = strides[-1]
    zero, *third = units(permuted(behind[0], back(shift_route(1, size))), 0, unit, 4)
    total = added(keep, permuted(send, neighbours)).astype(BF16)
    two, four, six = (added(x, y).astype(BF16) for x, y in zip((two, four, six), third))
    second = permuted(jnp.concatenate([total, two, six]), back(shift_route(2, size)))
    four = added(four, second[rows + unit :])
    mine = added(zero, second[rows : rows + unit], permuted(four.astype(BF16), far_route))
    total = added(total, jnp.where(lower, second[:rows], jnp.zeros_like(total))).astype(BF16)
    for stride in strides[:-1]:
        total = added(total, permuted(total, back(prompt_route(stride, size)))).astype(BF16)
    keys_far = permuted(total, [(top, 0)])
    values_far = permuted(total, [(top + 1, 0)])
    values_next = permuted(total, [(1, 0)])
    return finish(send), added(total, keys_far), added(values_next, values_far), mine


def per_device(size, queries, keys, values, grad_out, parents, lengths):
    tokens, heads_kv, head_size = keys.shape
    rows = tokens * heads_kv
    one = CAP * TILE * heads_kv
    unit = 2 * one
    window = min(W, size - 2)
    device = lax.axis_index("node")
    keys = keys.reshape(rows, head_size)
    values = values.reshape(rows, head_size)

    if size == W + 1:
        order = [(1, 3), (2, 2), (3, 1), (4, 4), (5, 5), (6, 6)]
        targets = [(k % 2, k // 2 * unit) for k in range(window)]
    else:
        order = [(k, k) for k in (1, 3, 5, 7, 2, 4, 6)]
        targets = [(0, i * unit) for i in range(4)] + [(1, i * unit) for i in range(3)]
    head, held, *own = load(order, keys, values, parents, lengths, tokens)
    head, *where = lax.optimization_barrier((head, lax.rem(device, 2) == 0, lax.rem(device, 4) < 2, device == 0))
    even, _, root = where
    held, other, block, fresh_sources, early_sources, blocks, (qh, gh) = collect(
        size, unit, rows, where, keys, values, head, held, queries, grad_out
    )
    kh_early, *parts = early(len(fresh_sources), early_sources, qh, gh, own, blocks)
    prompt_k, prompt_v = jnp.where(even, held, other), jnp.where(even, other, held)
    *prompt, kh, ds, p_behind, p_own = probs(
        fresh_sources, len(targets), prompt_k, prompt_v, qh, gh, own, parts, block
    )
    behind = windows(targets, qh, gh, ds, p_behind)

    def finish(earlier):
        return grads(qh, gh, kh, kh_early, ds, after(p_own, earlier))

    (grad_queries, dk, dv), prompt_k, prompt_v, mine = give_back(size, unit, where, prompt, behind, finish)
    own = []
    for side, local, prompt in ((0, dk, prompt_k), (1, dv, prompt_v)):
        whole = local + jnp.where(root, prompt.astype(F32), 0.0)
        own.append(whole.at[:one].add(mine[side * one : (side + 1) * one]).reshape(tokens, heads_kv, head_size))
    return grad_queries, own[0], own[1]


def solution(mesh):
    by_token = P(("leaf", "node"), "tensor", None)
    return jax.shard_map(
        functools.partial(per_device, mesh.shape["node"]),
        mesh=mesh,
        in_specs=(by_token, by_token, by_token, by_token, P("leaf"), P("leaf")),
        out_specs=(by_token, by_token, by_token),
        check_vma=False,
    )
```

```python
import functools
import math

import jax
import jax.numpy as jnp
from jax import lax
from jax.experimental import pallas as pl
from jax.experimental.pallas import tpu as pltpu
from jax.sharding import PartitionSpec as P

TILE = 16
TD = 8
CAP = 2
W = 7
CHUNK = 32
MASKED = -1e30
BF16 = jnp.bfloat16
F32 = jnp.float32


def permuted(block, route):
    return lax.ppermute(block, "node", route)


def column_limits(device, window, parents, lengths):
    cursor = parents[device * TD]
    need = [jnp.int32(0)] * (window + 1)
    for _ in range(W):
        owner = jnp.where(cursor < 0, -1, lax.div(jnp.maximum(cursor, 0), TD))
        distance = device - owner
        active = (owner >= 1) & (distance >= 1) & (distance <= W)
        depth = lax.rem(jnp.maximum(cursor, 0), TD) + 1
        for k in range(1, window + 1):
            need[k] = jnp.where(active & (distance == k), depth, need[k])
        cursor = jnp.where(active, parents[jnp.maximum(owner, 0) * TD], cursor)
    prompt = [jnp.where(device >= 1, lengths[t], 0) for t in range(TD)]
    behind = []
    for k in range(1, window + 1):
        owner = device - k
        seen = [(owner >= 1) & (c < need[k]) for c in range(CAP)]
        behind.append([jnp.where(seen[c], lengths[jnp.maximum(owner, 0) * TD + c], 0) for c in range(CAP)])
    return prompt, behind, [lengths[device * TD + t] for t in range(TD)]


def split_heads(block, heads_ref, start, count, heads_kv, wide):
    wide[: count * heads_kv] = block.astype(F32)
    for h in range(heads_kv):
        heads_ref[h, start : start + count] = wide[pl.ds(h, count, stride=heads_kv), :].astype(BF16)


def join_heads(blocks, count, heads_kv, wide):
    for h in range(heads_kv):
        wide[pl.ds(h, count, stride=heads_kv), :] = blocks[h]
    return wide[: count * heads_kv]


def load_kernel(order, heads_kv, *refs):
    sources, outs, scratch = refs[:4], refs[4:10], refs[10:]
    head, held, own_k, own_v, bias, weight = outs
    parents, lengths, keys, values, wide, arrived = scratch
    copies = [pltpu.make_async_copy(a, b, arrived.at[i]) for i, (a, b) in enumerate(zip(sources, scratch))]
    for copy in copies:
        copy.start()
    tokens = TD * TILE
    front = CAP * TILE * heads_kv
    device = lax.axis_index("node")
    for copy in copies:
        copy.wait()
    head[:front] = keys[:front]
    head[front:] = values[:front]
    held[...] = jnp.where(device == 0, keys[...], jnp.zeros_like(keys))
    split_heads(keys[...], own_k, 0, tokens, heads_kv, wide)
    split_heads(values[...], own_v, 0, tokens, heads_kv, wide)
    place = lax.broadcasted_iota(jnp.int32, (TILE, 128), 0)
    prompt, behind, own = column_limits(device, len(order), parents, lengths)
    even = lax.rem(device, 2) == 0
    limits = prompt
    for on_even, on_odd in order:
        limits = limits + [jnp.where(even, x, y) for x, y in zip(behind[on_even - 1], behind[on_odd - 1])]
    for t, limit in enumerate(limits + own):
        bias[t * TILE : (t + 1) * TILE] = jnp.where(place < limit, 0.0, MASKED)
    lane_place = lax.broadcasted_iota(jnp.int32, (8, 128), 1) // 8
    for t in range(TD):
        weight[:, t * 128 : (t + 1) * 128] = jnp.where(lane_place < lengths[device * TD + t], 1.0, 0.0)


def pack_kernel(heads_kv, q_ref, g_ref, qh, gh, blocks, arrived):
    tokens = TD * TILE
    copies = []
    for pair in range(heads_kv // 2):
        for ref, out in ((q_ref, qh), (g_ref, gh)):
            i = len(copies)
            copy = pltpu.make_async_copy(ref.at[:, pair * 16 : (pair + 1) * 16], blocks.at[i], arrived.at[i])
            copy.start()
            copies.append((copy, out, pair))
    for i, (copy, out, pair) in enumerate(copies):
        copy.wait()
        both = blocks[i].astype(F32)
        for part in range(2):
            out[2 * pair + part] = both[:, part * 8 : (part + 1) * 8].reshape(tokens * 8, 128).astype(BF16)


def causal_bias(columns):
    column_token = lax.broadcasted_iota(jnp.int32, (CHUNK, columns), 1) // 8
    return jnp.where(lax.broadcasted_iota(jnp.int32, (CHUNK, columns), 0) <= column_token, 0.0, MASKED)


def outer_product(rows, columns):
    return lax.dot_general(rows, columns, (((1,), (1,)), ((), ())), preferred_element_type=F32)


def early_kernel(fresh, sources, heads_kv, scale, *refs):
    own_k, own_v, qh, gh, bias = refs[:5]
    blocks, (kh, e_ref, dp_ref, stats, vh, wide) = refs[5:-6], refs[-6:]
    tokens = TD * TILE
    front = CAP * TILE
    behind = len(sources) * front
    start = tokens + fresh * front
    columns = CHUNK * 8
    for side, heads_ref, own in ((0, kh, own_k), (1, vh, own_v)):
        for k, (source, at) in enumerate(sources):
            at += side * front * heads_kv
            split_heads(blocks[source][at : at + front * heads_kv], heads_ref, k * front, front, heads_kv, wide)
        heads_ref[:, behind:] = own[...]
    causal = causal_bias(columns)
    for head in range(heads_kv):
        for c in range(tokens // CHUNK):
            rows = behind + (c + 1) * CHUNK
            span = slice(c * columns, (c + 1) * columns)
            s = outer_product(kh[head, :rows], qh[head, span])
            dp = outer_product(vh[head, :rows], gh[head, span])
            s = s + jnp.concatenate([bias[start : start + rows]] * (columns // 128), axis=1)
            s = jnp.concatenate([s[: rows - CHUNK], s[rows - CHUNK :] + causal], axis=0)
            top = jnp.max(s, axis=0, keepdims=True)
            e = jnp.exp2((s - top) * (scale * math.log2(math.e)))
            e_ref[head, :rows, span] = e
            dp_ref[head, :rows, span] = dp
            stats[head, 0:1, span] = top
            stats[head, 1:2, span] = jnp.sum(e, axis=0, keepdims=True)
            stats[head, 2:3, span] = jnp.sum(e * dp, axis=0, keepdims=True)


def probs_kernel(sources, heads_kv, scale, *refs):
    prompt_k, prompt_v, qh, gh, bias, weight_ref, e_ref, dp_ref, stats, block_ref = refs[:10]
    send_ref, keep_ref, kh, ds_ref, p_behind, p_own, vh, p_ref, grads, wide = refs[10:]
    tokens = TD * TILE
    front = CAP * TILE
    fresh = tokens + len(sources) * front
    behind = p_behind.shape[1]
    before = tokens + behind
    columns = CHUNK * 8
    rate = scale * math.log2(math.e)
    device = lax.axis_index("node")

    for side, heads_ref, prompt in ((0, kh, prompt_k), (1, vh, prompt_v)):
        split_heads(prompt[...], heads_ref, 0, tokens, heads_kv, wide)
        for k, (_, at) in enumerate(sources):
            at += side * front * heads_kv
            split_heads(block_ref[at : at + front * heads_kv], heads_ref, tokens + k * front, front, heads_kv, wide)

    for head in range(heads_kv):
        for c in range(tokens // CHUNK):
            rows = before - fresh + (c + 1) * CHUNK
            span = slice(c * columns, (c + 1) * columns)
            s = outer_product(kh[head], qh[head, span])
            dp = outer_product(vh[head], gh[head, span])
            s = s + jnp.concatenate([bias[:fresh]] * (columns // 128), axis=1)
            top_early = stats[head, 0:1, span]
            top = jnp.maximum(jnp.max(s, axis=0, keepdims=True), top_early)
            e = jnp.exp2((s - top) * rate)
            shrink = jnp.exp2((top_early - top) * rate)
            total = jnp.sum(e, axis=0, keepdims=True) + shrink * stats[head, 1:2, span]
            weight = weight_ref[:1, span] / total
            weight_early = weight * shrink
            p = e * weight
            delta = jnp.sum(p * dp, axis=0, keepdims=True) + weight_early * stats[head, 2:3, span]
            ds_ref[head, :fresh, span] = (p * (dp - delta)).astype(BF16)
            p_ref[head % 2, :, span] = p[:tokens].astype(BF16)
            p_behind[head, : fresh - tokens, span] = p[tokens:].astype(BF16)
            p = e_ref[head, :rows, span] * weight_early
            ds_ref[head, fresh : fresh + rows, span] = (p * (dp_ref[head, :rows, span] - delta)).astype(BF16)
            p_behind[head, fresh - tokens :, span] = p[: before - fresh].astype(BF16)
            p_own[head, : fresh + rows - before, span] = p[before - fresh :].astype(BF16)
        grads[0, head] = scale * jnp.dot(ds_ref[head, :tokens], qh[head], preferred_element_type=F32)
        grads[1, head] = jnp.dot(p_ref[head % 2], gh[head], preferred_element_type=F32)

    even = lax.rem(device, 2) == 0
    for side in range(2):
        dprompt = join_heads([grads[side, h] for h in range(heads_kv)], tokens, heads_kv, wide).astype(BF16)
        kept = even if side == 0 else jnp.logical_not(even)

        @pl.when(kept)
        def _():
            keep_ref[...] = dprompt

        @pl.when(jnp.logical_not(kept))
        def _():
            send_ref[...] = dprompt


def windows_kernel(targets, heads_kv, scale, qh, gh, ds_ref, p_behind, send_ref, keep_ref, grads, wide):
    front = CAP * TILE
    tokens = TD * TILE
    behind = p_behind.shape[1]
    for head in range(heads_kv):
        ds = ds_ref[head, tokens : tokens + behind]
        grads[0, head] = scale * jnp.dot(ds, qh[head], preferred_element_type=F32)
        grads[1, head] = jnp.dot(p_behind[head], gh[head], preferred_element_type=F32)
    for side in range(2):
        for k, (target, start) in enumerate(targets):
            span = slice(k * front, (k + 1) * front)
            block = join_heads([grads[side, h, span] for h in range(heads_kv)], front, heads_kv, wide).astype(BF16)
            start += side * front * heads_kv
            (send_ref, keep_ref)[target][start : start + front * heads_kv] = block


def grads_kernel(heads_kv, scale, *refs):
    qh, gh, kh_fresh, kh_early, ds_ref, p_own, dq_ref, dk_ref, dv_ref, wide = refs
    tokens = TD * TILE
    kh = [jnp.concatenate([kh_fresh[h], kh_early[h]], axis=0) for h in range(heads_kv)]
    before = kh[0].shape[0] - tokens
    columns = CHUNK * 8
    dk = []
    dv = []
    for pair in range(heads_kv // 2):
        for c in range(tokens // CHUNK):
            rows = before + (c + 1) * CHUNK
            span = slice(c * columns, (c + 1) * columns)
            parts = []
            for head in (2 * pair, 2 * pair + 1):
                dq = lax.dot_general(
                    kh[head][:rows], ds_ref[head, :rows, span], (((0,), (0,)), ((), ())), preferred_element_type=F32
                )
                parts.append((scale * dq.T).reshape(CHUNK, 8, 128))
            dq_ref[c * CHUNK : (c + 1) * CHUNK, pair * 16 : (pair + 1) * 16] = jnp.concatenate(parts, axis=1).astype(BF16)
        for head in (2 * pair, 2 * pair + 1):
            for source, factor, out in ((ds_ref.at[head, before:], qh, dk), (p_own.at[head], gh, dv)):
                pieces = []
                for c in range(tokens // CHUNK):
                    start = c * columns
                    pieces.append(
                        jnp.dot(
                            source[c * CHUNK : (c + 1) * CHUNK, start:], factor[head, start:], preferred_element_type=F32
                        )
                    )
                out.append(jnp.concatenate(pieces, axis=0))
    dk_ref[...] = scale * join_heads(dk, tokens, heads_kv, wide)
    dv_ref[...] = join_heads(dv, tokens, heads_kv, wide)


VMEM = pl.BlockSpec(memory_space=pltpu.VMEM)


HBM = pl.BlockSpec(memory_space=pltpu.HBM)


def call(kernel, name, operands, outputs, scratch, flops, transcendentals=0, place=VMEM):
    sizes = [a.size * a.dtype.itemsize for a in (*operands, *outputs)]
    if place is HBM:
        operands = [pltpu.with_memory_space_constraint(a, pltpu.HBM) for a in operands]
    return pl.pallas_call(
        kernel,
        in_specs=[place] * len(operands),
        out_specs=[VMEM] * len(outputs),
        out_shape=outputs,
        scratch_shapes=scratch,
        compiler_params=pltpu.CompilerParams(vmem_limit_bytes=16 * 1024 * 1024),
        cost_estimate=pl.CostEstimate(flops=flops, bytes_accessed=sum(sizes), transcendentals=transcendentals),
        name=name,
    )(*operands)


def load(order, keys, values, parents, lengths, tokens):
    rows, head_size = keys.shape
    heads_kv = rows // tokens
    array = jax.ShapeDtypeStruct
    return call(
        functools.partial(load_kernel, order, heads_kv),
        "load",
        (parents, lengths, keys, values),
        [array((2 * CAP * TILE * heads_kv, head_size), BF16), array((rows, head_size), BF16)]
        + [array((heads_kv, tokens, head_size), BF16)] * 2
        + [array((2 * tokens + len(order) * CAP * TILE, 128), F32), array((8, tokens * 8), F32)],
        [pltpu.SMEM(parents.shape, jnp.int32), pltpu.SMEM(lengths.shape, jnp.int32)]
        + [pltpu.VMEM((rows, head_size), BF16)] * 2
        + [pltpu.VMEM((rows, head_size), F32), pltpu.SemaphoreType.DMA((4,))],
        flops=1 << 20,
        place=HBM,
    )


def pack(queries, grad_out, heads_kv):
    tokens, heads_q, head_size = queries.shape
    array = jax.ShapeDtypeStruct
    return call(
        functools.partial(pack_kernel, heads_kv),
        "pack",
        (queries, grad_out),
        [array((heads_kv, tokens * 8, head_size), BF16)] * 2,
        [pltpu.VMEM((heads_kv, tokens, 16, head_size), BF16), pltpu.SemaphoreType.DMA((heads_kv,))],
        flops=1 << 20,
        place=HBM,
    )


def early(fresh, sources, qh, gh, own, blocks):
    own_k, own_v, bias, _ = own
    heads_kv, tokens, head_size = own_k.shape
    rows = len(sources) * CAP * TILE + tokens
    array = jax.ShapeDtypeStruct
    work = heads_kv * tokens * 8 * rows
    return call(
        functools.partial(early_kernel, fresh, sources, heads_kv, head_size**-0.5),
        "early",
        (own_k, own_v, qh, gh, bias, *blocks),
        [array((heads_kv, rows, head_size), BF16)]
        + [array((heads_kv, rows, tokens * 8), F32)] * 2
        + [array((heads_kv, 8, tokens * 8), F32)],
        [pltpu.VMEM((heads_kv, rows, head_size), BF16), pltpu.VMEM((CAP * TILE * heads_kv, head_size), F32)],
        flops=4 * work * head_size,
        transcendentals=work,
    )


def probs(sources, behind, prompt_k, prompt_v, qh, gh, own, parts, block):
    _, own_v, bias, weight = own
    heads_kv, tokens, head_size = own_v.shape
    rows = tokens * heads_kv
    front = CAP * TILE
    fresh = tokens + len(sources) * front
    before = tokens + behind * front
    array = jax.ShapeDtypeStruct
    work = heads_kv * tokens * 8 * (before + tokens)
    return call(
        functools.partial(probs_kernel, sources, heads_kv, head_size**-0.5),
        "probs",
        (prompt_k, prompt_v, qh, gh, bias, weight, *parts, block),
        [array((rows, head_size), BF16)] * 2
        + [
            array((heads_kv, fresh, head_size), BF16),
            array((heads_kv, before + tokens, tokens * 8), BF16),
            array((heads_kv, behind * front, tokens * 8), BF16),
            array((heads_kv, tokens, tokens * 8), BF16),
        ],
        [
            pltpu.VMEM((heads_kv, fresh, head_size), BF16),
            pltpu.VMEM((2, tokens, tokens * 8), BF16),
            pltpu.VMEM((2, heads_kv, tokens, head_size), F32),
            pltpu.VMEM((rows, head_size), F32),
        ],
        flops=5 * work * head_size,
        transcendentals=work,
    )


def windows(targets, qh, gh, ds, p_behind):
    heads_kv, behind, _ = p_behind.shape
    head_size = qh.shape[2]
    front = CAP * TILE * heads_kv
    count = [sum(target == t for target, _ in targets) for t in (0, 1)]
    array = jax.ShapeDtypeStruct
    return call(
        functools.partial(windows_kernel, targets, heads_kv, head_size**-0.5),
        "windows",
        (qh, gh, ds, p_behind),
        [array((2 * front * n, head_size), BF16) for n in count],
        [pltpu.VMEM((2, heads_kv, behind, head_size), F32), pltpu.VMEM((front, head_size), F32)],
        flops=4 * p_behind.size * head_size,
    )


def grads(qh, gh, kh_fresh, kh_early, ds, p_own):
    heads_kv, tokens, _ = p_own.shape
    head_size = kh_fresh.shape[2]
    array = jax.ShapeDtypeStruct
    return call(
        functools.partial(grads_kernel, heads_kv, head_size**-0.5),
        "grads",
        (qh, gh, kh_fresh, kh_early, ds, p_own),
        [
            array((tokens, heads_kv * 8, head_size), BF16),
            array((tokens * heads_kv, head_size), F32),
            array((tokens * heads_kv, head_size), F32),
        ],
        [pltpu.VMEM((tokens * heads_kv, head_size), F32)],
        flops=2 * heads_kv * tokens * 8 * ds.shape[1] * head_size,
    )


def shift_route(distance, size):
    return [(i, i + distance) for i in range(size - distance)]


def back(route):
    return [(j, i) for i, j in route]


def added(*blocks):
    total = blocks[0].astype(F32)
    for block in blocks[1:]:
        total = total + block.astype(F32)
    return total


def after(array, *earlier):
    return lax.optimization_barrier((array, *earlier))[0]


def units(array, start, unit, count):
    return [array[start + i * unit : start + (i + 1) * unit] for i in range(count)]


def prompt_route(stride, size):
    return [(i + j, i + j + stride) for i in range(0, size, 2 * stride) for j in (0, 1)]


def collect(size, unit, rows, where, keys, values, head, held, queries, grad_out):
    even, lower, _ = where
    neighbours = [(i, i ^ 1) for i in range(size)]
    far_route = shift_route(4, size)[1:]
    near_route = shift_route(2, size)
    if size == W + 1:
        keys_far = permuted(keys, [(0, 4)])
        values_far = permuted(values, [(0, 5)])
        values_next = permuted(values, [(0, 1)])
        head, queries = lax.optimization_barrier((head, queries, keys_far))[:2]
        qh, gh = pack(queries, grad_out, keys.shape[0] // queries.shape[0])
        far = permuted(head, far_route)
        six = permuted(head, [(1, 7)])
        held = after(added(held, values_far, values_next, keys_far).astype(BF16), far, six, qh)
        second = permuted(jnp.concatenate([held, head]), near_route)
        crossed = jnp.where(even, jnp.concatenate([head, far]), jnp.concatenate([far, six]))
        crossed = permuted(crossed, neighbours)
        held = jnp.where(lower, held, second[:rows])
        third = permuted(after(jnp.concatenate([held, second[rows:]]), crossed), neighbours)
        early_sources = [(0, rows), (1, 0), (2, 0), (1, unit), (3, 0)]
        return held, third[:rows], third, [(0, rows)], early_sources, (second, crossed, far, six), (qh, gh)
    strides = [2**i for i in range(2, size.bit_length()) if 2**i < size]
    top = strides[-1]
    keys_far = permuted(keys, [(0, top)])
    values_far = permuted(values, [(0, top + 1)])
    values_next = permuted(values, [(0, 1)])
    far = permuted(head, far_route)
    held = added(held, values_next, values_far, keys_far).astype(BF16)
    for stride in reversed(strides[:-1]):
        held = added(held, permuted(held, prompt_route(stride, size))).astype(BF16)
    second = permuted(jnp.concatenate([held, head, far]), near_route)
    held = jnp.where(lower, held, second[:rows])
    near, six = units(second, rows, unit, 2)
    third = permuted(jnp.concatenate([head, near, far, six]), shift_route(1, size))
    other = permuted(held, neighbours)
    fresh_sources = [(0, i * unit) for i in range(4)]
    early_sources = [(0, rows), (1, 0), (0, rows + unit)]
    return held, other, third, fresh_sources, early_sources, (second, far), pack(queries, grad_out, keys.shape[0] // queries.shape[0])


def give_back(size, unit, where, prompt, behind, finish):
    even, lower, _ = where
    neighbours = [(i, i ^ 1) for i in range(size)]
    far_route = back(shift_route(4, size)[1:])
    send, keep = prompt
    rows = keep.shape[0]
    two, four, six = units(behind[1], 0, unit, 3)
    if size == W + 1:
        total = added(keep, permuted(send, neighbours)).astype(BF16)
        finished = finish(total)
        near, first, last = units(permuted(behind[0], neighbours), 0, unit, 3)
        none = jnp.zeros_like(first)
        parts = [permuted(total, [(j, 0), (j + 1, 1)]) for j in (2, 4)]
        keys_last, values_last = permuted(total, [(6, 0)]), permuted(total, [(7, 0)])
        two = permuted(added(two, near).astype(BF16), back(shift_route(2, size)[1:]))
        four = after(added(four, jnp.where(even, last, first)).astype(BF16), finished[1])
        four = permuted(four, far_route)
        six = permuted(added(six, jnp.where(even, none, last)).astype(BF16), [(7, 1)])
        total = added(total, *parts).astype(BF16)
        mine = added(jnp.where(even, first, none), two, four, six)
        values_next = permuted(total, [(1, 0)])
        return finished, added(total, keys_last), added(values_next, values_last), mine
    strides = [2**i for i in range(2, size.bit_length()) if 2**i < size]
    top = strides[-1]
    zero, *third = units(permuted(behind[0], back(shift_route(1, size))), 0, unit, 4)
    total = added(keep, permuted(send, neighbours)).astype(BF16)
    two, four, six = (added(x, y).astype(BF16) for x, y in zip((two, four, six), third))
    second = permuted(jnp.concatenate([total, two, six]), back(shift_route(2, size)))
    four = added(four, second[rows + unit :])
    mine = added(zero, second[rows : rows + unit], permuted(four.astype(BF16), far_route))
    total = added(total, jnp.where(lower, second[:rows], jnp.zeros_like(total))).astype(BF16)
    for stride in strides[:-1]:
        total = added(total, permuted(total, back(prompt_route(stride, size)))).astype(BF16)
    keys_far = permuted(total, [(top, 0)])
    values_far = permuted(total, [(top + 1, 0)])
    values_next = permuted(total, [(1, 0)])
    return finish(send), added(total, keys_far), added(values_next, values_far), mine


def per_device(size, queries, keys, values, grad_out, parents, lengths):
    tokens, heads_kv, head_size = keys.shape
    rows = tokens * heads_kv
    one = CAP * TILE * heads_kv
    unit = 2 * one
    window = min(W, size - 2)
    device = lax.axis_index("node")
    keys = keys.reshape(rows, head_size)
    values = values.reshape(rows, head_size)

    if size == W + 1:
        order = [(1, 3), (2, 2), (3, 1), (4, 4), (5, 5), (6, 6)]
        targets = [(k % 2, k // 2 * unit) for k in range(window)]
    else:
        order = [(k, k) for k in (1, 3, 5, 7, 2, 4, 6)]
        targets = [(0, i * unit) for i in range(4)] + [(1, i * unit) for i in range(3)]
    head, held, *own = load(order, keys, values, parents, lengths, tokens)
    head, *where = lax.optimization_barrier((head, lax.rem(device, 2) == 0, lax.rem(device, 4) < 2, device == 0))
    even, _, root = where
    held, other, block, fresh_sources, early_sources, blocks, (qh, gh) = collect(
        size, unit, rows, where, keys, values, head, held, queries, grad_out
    )
    kh_early, *parts = early(len(fresh_sources), early_sources, qh, gh, own, blocks)
    prompt_k, prompt_v = jnp.where(even, held, other), jnp.where(even, other, held)
    *prompt, kh, ds, p_behind, p_own = probs(
        fresh_sources, len(targets), prompt_k, prompt_v, qh, gh, own, parts, block
    )
    behind = windows(targets, qh, gh, ds, p_behind)

    def finish(earlier):
        return grads(qh, gh, kh, kh_early, ds, after(p_own, earlier))

    (grad_queries, dk, dv), prompt_k, prompt_v, mine = give_back(size, unit, where, prompt, behind, finish)
    own = []
    for side, local, prompt in ((0, dk, prompt_k), (1, dv, prompt_v)):
        whole = local + jnp.where(root, prompt.astype(F32), 0.0)
        own.append(whole.at[:one].add(mine[side * one : (side + 1) * one]).reshape(tokens, heads_kv, head_size))
    return grad_queries, own[0], own[1]


def solution(mesh):
    by_token = P(("leaf", "node"), "tensor", None)
    return jax.shard_map(
        functools.partial(per_device, mesh.shape["node"]),
        mesh=mesh,
        in_specs=(by_token, by_token, by_token, by_token, P("leaf"), P("leaf")),
        out_specs=(by_token, by_token, by_token),
        check_vma=False,
    )
```

```python
import functools
import math

import jax
import jax.numpy as jnp
from jax import lax
from jax.experimental import pallas as pl
from jax.experimental.pallas import tpu as pltpu
from jax.sharding import PartitionSpec as P

TILE = 16
TD = 8
CAP = 2
W = 7
CHUNK = 32
MASKED = -1e30
BF16 = jnp.bfloat16
F32 = jnp.float32


def permuted(block, route):
    return lax.ppermute(block, "node", route)


def column_limits(device, window, parents, lengths):
    cursor = parents[device * TD]
    need = [jnp.int32(0)] * (window + 1)
    for _ in range(W):
        owner = jnp.where(cursor < 0, -1, lax.div(jnp.maximum(cursor, 0), TD))
        distance = device - owner
        active = (owner >= 1) & (distance >= 1) & (distance <= W)
        depth = lax.rem(jnp.maximum(cursor, 0), TD) + 1
        for k in range(1, window + 1):
            need[k] = jnp.where(active & (distance == k), depth, need[k])
        cursor = jnp.where(active, parents[jnp.maximum(owner, 0) * TD], cursor)
    prompt = [jnp.where(device >= 1, lengths[t], 0) for t in range(TD)]
    behind = []
    for k in range(1, window + 1):
        owner = device - k
        seen = [(owner >= 1) & (c < need[k]) for c in range(CAP)]
        behind.append([jnp.where(seen[c], lengths[jnp.maximum(owner, 0) * TD + c], 0) for c in range(CAP)])
    return prompt, behind, [lengths[device * TD + t] for t in range(TD)]


def split_heads(block, heads_ref, start, count, heads_kv, wide):
    wide[: count * heads_kv] = block.astype(F32)
    for h in range(heads_kv):
        heads_ref[h, start : start + count] = wide[pl.ds(h, count, stride=heads_kv), :].astype(BF16)


def join_heads(blocks, count, heads_kv, wide):
    for h in range(heads_kv):
        wide[pl.ds(h, count, stride=heads_kv), :] = blocks[h]
    return wide[: count * heads_kv]


def load_kernel(order, heads_kv, *refs):
    sources, outs, scratch = refs[:4], refs[4:10], refs[10:]
    head, held, own_k, own_v, bias, weight = outs
    parents, lengths, keys, values, wide, arrived = scratch
    copies = [pltpu.make_async_copy(a, b, arrived.at[i]) for i, (a, b) in enumerate(zip(sources, scratch))]
    for copy in copies:
        copy.start()
    tokens = TD * TILE
    front = CAP * TILE * heads_kv
    device = lax.axis_index("node")
    for copy in copies:
        copy.wait()
    head[:front] = keys[:front]
    head[front:] = values[:front]
    held[...] = jnp.where(device == 0, keys[...], jnp.zeros_like(keys))
    split_heads(keys[...], own_k, 0, tokens, heads_kv, wide)
    split_heads(values[...], own_v, 0, tokens, heads_kv, wide)
    place = lax.broadcasted_iota(jnp.int32, (TILE, 128), 0)
    prompt, behind, own = column_limits(device, len(order), parents, lengths)
    even = lax.rem(device, 2) == 0
    limits = prompt
    for on_even, on_odd in order:
        limits = limits + [jnp.where(even, x, y) for x, y in zip(behind[on_even - 1], behind[on_odd - 1])]
    for t, limit in enumerate(limits + own):
        bias[t * TILE : (t + 1) * TILE] = jnp.where(place < limit, 0.0, MASKED)
    lane_place = lax.broadcasted_iota(jnp.int32, (8, 128), 1) // 8
    for t in range(TD):
        weight[:, t * 128 : (t + 1) * 128] = jnp.where(lane_place < lengths[device * TD + t], 1.0, 0.0)


def pack_kernel(heads_kv, q_ref, g_ref, qh, gh, blocks, arrived):
    tokens = TD * TILE
    copies = []
    for pair in range(heads_kv // 2):
        for ref, out in ((q_ref, qh), (g_ref, gh)):
            i = len(copies)
            copy = pltpu.make_async_copy(ref.at[:, pair * 16 : (pair + 1) * 16], blocks.at[i], arrived.at[i])
            copy.start()
            copies.append((copy, out, pair))
    for i, (copy, out, pair) in enumerate(copies):
        copy.wait()
        both = blocks[i].astype(F32)
        for part in range(2):
            out[2 * pair + part] = both[:, part * 8 : (part + 1) * 8].reshape(tokens * 8, 128).astype(BF16)


def causal_bias(columns):
    column_token = lax.broadcasted_iota(jnp.int32, (CHUNK, columns), 1) // 8
    return jnp.where(lax.broadcasted_iota(jnp.int32, (CHUNK, columns), 0) <= column_token, 0.0, MASKED)


def outer_product(rows, columns):
    return lax.dot_general(rows, columns, (((1,), (1,)), ((), ())), preferred_element_type=F32)


def early_kernel(fresh, sources, heads_kv, scale, *refs):
    own_k, own_v, qh, gh, bias = refs[:5]
    blocks, (kh, e_ref, dp_ref, stats, vh, wide) = refs[5:-6], refs[-6:]
    tokens = TD * TILE
    front = CAP * TILE
    behind = len(sources) * front
    start = tokens + fresh * front
    columns = CHUNK * 8
    for side, heads_ref, own in ((0, kh, own_k), (1, vh, own_v)):
        for k, (source, at) in enumerate(sources):
            at += side * front * heads_kv
            split_heads(blocks[source][at : at + front * heads_kv], heads_ref, k * front, front, heads_kv, wide)
        heads_ref[:, behind:] = own[...]
    causal = causal_bias(columns)
    for head in range(heads_kv):
        for c in range(tokens // CHUNK):
            rows = behind + (c + 1) * CHUNK
            span = slice(c * columns, (c + 1) * columns)
            s = outer_product(kh[head, :rows], qh[head, span])
            dp = outer_product(vh[head, :rows], gh[head, span])
            s = s + jnp.concatenate([bias[start : start + rows]] * (columns // 128), axis=1)
            s = jnp.concatenate([s[: rows - CHUNK], s[rows - CHUNK :] + causal], axis=0)
            top = jnp.max(s, axis=0, keepdims=True)
            e = jnp.exp2((s - top) * (scale * math.log2(math.e)))
            e_ref[head, :rows, span] = e
            dp_ref[head, :rows, span] = dp
            stats[head, 0:1, span] = top
            stats[head, 1:2, span] = jnp.sum(e, axis=0, keepdims=True)
            stats[head, 2:3, span] = jnp.sum(e * dp, axis=0, keepdims=True)


def probs_kernel(sources, heads_kv, scale, *refs):
    prompt_k, prompt_v, qh, gh, bias, weight_ref, stats, block_ref = refs[:8]
    send_ref, keep_ref, kh, ds_ref, p_behind, terms, vh, p_ref, grads, wide = refs[8:]
    tokens = TD * TILE
    front = CAP * TILE
    columns = CHUNK * 8
    rate = scale * math.log2(math.e)
    device = lax.axis_index("node")

    for side, heads_ref, prompt in ((0, kh, prompt_k), (1, vh, prompt_v)):
        split_heads(prompt[...], heads_ref, 0, tokens, heads_kv, wide)
        for k, (_, at) in enumerate(sources):
            at += side * front * heads_kv
            split_heads(block_ref[at : at + front * heads_kv], heads_ref, tokens + k * front, front, heads_kv, wide)

    for head in range(heads_kv):
        for c in range(tokens // CHUNK):
            span = slice(c * columns, (c + 1) * columns)
            s = outer_product(kh[head], qh[head, span])
            dp = outer_product(vh[head], gh[head, span])
            s = s + jnp.concatenate([bias[: s.shape[0]]] * (columns // 128), axis=1)
            top_early = stats[head, 0:1, span]
            top = jnp.maximum(jnp.max(s, axis=0, keepdims=True), top_early)
            e = jnp.exp2((s - top) * rate)
            shrink = jnp.exp2((top_early - top) * rate)
            total = jnp.sum(e, axis=0, keepdims=True) + shrink * stats[head, 1:2, span]
            weight = weight_ref[:1, span] / total
            weight_early = weight * shrink
            p = e * weight
            delta = jnp.sum(p * dp, axis=0, keepdims=True) + weight_early * stats[head, 2:3, span]
            ds_ref[head, :, span] = (p * (dp - delta)).astype(BF16)
            p_ref[head % 2, :, span] = p[:tokens].astype(BF16)
            p_behind[head, :, span] = p[tokens:].astype(BF16)
            terms[head, 0:1, span] = weight_early
            terms[head, 1:2, span] = delta
        grads[0, head] = scale * jnp.dot(ds_ref[head, :tokens], qh[head], preferred_element_type=F32)
        grads[1, head] = jnp.dot(p_ref[head % 2], gh[head], preferred_element_type=F32)

    even = lax.rem(device, 2) == 0
    for side in range(2):
        dprompt = join_heads([grads[side, h] for h in range(heads_kv)], tokens, heads_kv, wide).astype(BF16)
        kept = even if side == 0 else jnp.logical_not(even)

        @pl.when(kept)
        def _():
            keep_ref[...] = dprompt

        @pl.when(jnp.logical_not(kept))
        def _():
            send_ref[...] = dprompt


def windows_kernel(targets, heads_kv, scale, *refs):
    qh, gh, ds_fresh, p_behind, e_ref, dp_ref, terms, send_ref, keep_ref, ds_ref, p_own, p_ref, grads, wide = refs
    front = CAP * TILE
    tokens = TD * TILE
    early = ds_ref.shape[1] - tokens
    columns = CHUNK * 8
    for head in range(heads_kv):
        for c in range(tokens // CHUNK):
            rows = early + (c + 1) * CHUNK
            span = slice(c * columns, (c + 1) * columns)
            p = e_ref[head, :rows, span] * terms[head, 0:1, span]
            ds_ref[head, :rows, span] = (p * (dp_ref[head, :rows, span] - terms[head, 1:2, span])).astype(BF16)
            p_ref[head % 2, :, span] = p[:early].astype(BF16)
            p_own[head, : rows - early, span] = p[early:].astype(BF16)
        ds = jnp.concatenate([ds_fresh[head, tokens:], ds_ref[head, :early]], axis=0)
        grads[0, head] = scale * jnp.dot(ds, qh[head], preferred_element_type=F32)
        p = jnp.concatenate([p_behind[head], p_ref[head % 2]], axis=0)
        grads[1, head] = jnp.dot(p, gh[head], preferred_element_type=F32)
    for side in range(2):
        for k, (target, start) in enumerate(targets):
            span = slice(k * front, (k + 1) * front)
            block = join_heads([grads[side, h, span] for h in range(heads_kv)], front, heads_kv, wide).astype(BF16)
            start += side * front * heads_kv
            (send_ref, keep_ref)[target][start : start + front * heads_kv] = block


def grads_kernel(heads_kv, scale, *refs):
    qh, gh, kh_fresh, kh_early, ds_fresh, ds_early, p_own, dq_ref, dk_ref, dv_ref, wide = refs
    tokens = TD * TILE
    kh = [jnp.concatenate([kh_fresh[h], kh_early[h]], axis=0) for h in range(heads_kv)]
    before = kh[0].shape[0] - tokens
    columns = CHUNK * 8
    dk = []
    dv = []
    for pair in range(heads_kv // 2):
        for c in range(tokens // CHUNK):
            rows = before + (c + 1) * CHUNK
            span = slice(c * columns, (c + 1) * columns)
            parts = []
            for head in (2 * pair, 2 * pair + 1):
                fresh = ds_fresh.shape[1]
                ds = jnp.concatenate([ds_fresh[head, :, span], ds_early[head, : rows - fresh, span]], axis=0)
                dq = lax.dot_general(kh[head][:rows], ds, (((0,), (0,)), ((), ())), preferred_element_type=F32)
                parts.append((scale * dq.T).reshape(CHUNK, 8, 128))
            dq_ref[c * CHUNK : (c + 1) * CHUNK, pair * 16 : (pair + 1) * 16] = jnp.concatenate(parts, axis=1).astype(BF16)
        for head in (2 * pair, 2 * pair + 1):
            for source, factor, out in ((ds_early.at[head, before - fresh :], qh, dk), (p_own.at[head], gh, dv)):
                pieces = []
                for c in range(tokens // CHUNK):
                    start = c * columns
                    pieces.append(
                        jnp.dot(
                            source[c * CHUNK : (c + 1) * CHUNK, start:], factor[head, start:], preferred_element_type=F32
                        )
                    )
                out.append(jnp.concatenate(pieces, axis=0))
    dk_ref[...] = scale * join_heads(dk, tokens, heads_kv, wide)
    dv_ref[...] = join_heads(dv, tokens, heads_kv, wide)


VMEM = pl.BlockSpec(memory_space=pltpu.VMEM)


HBM = pl.BlockSpec(memory_space=pltpu.HBM)


def call(kernel, name, operands, outputs, scratch, flops, transcendentals=0, place=VMEM):
    sizes = [a.size * a.dtype.itemsize for a in (*operands, *outputs)]
    if place is HBM:
        operands = [pltpu.with_memory_space_constraint(a, pltpu.HBM) for a in operands]
    return pl.pallas_call(
        kernel,
        in_specs=[place] * len(operands),
        out_specs=[VMEM] * len(outputs),
        out_shape=outputs,
        scratch_shapes=scratch,
        compiler_params=pltpu.CompilerParams(vmem_limit_bytes=16 * 1024 * 1024),
        cost_estimate=pl.CostEstimate(flops=flops, bytes_accessed=sum(sizes), transcendentals=transcendentals),
        name=name,
    )(*operands)


def load(order, keys, values, parents, lengths, tokens):
    rows, head_size = keys.shape
    heads_kv = rows // tokens
    array = jax.ShapeDtypeStruct
    return call(
        functools.partial(load_kernel, order, heads_kv),
        "load",
        (parents, lengths, keys, values),
        [array((2 * CAP * TILE * heads_kv, head_size), BF16), array((rows, head_size), BF16)]
        + [array((heads_kv, tokens, head_size), BF16)] * 2
        + [array((2 * tokens + len(order) * CAP * TILE, 128), F32), array((8, tokens * 8), F32)],
        [pltpu.SMEM(parents.shape, jnp.int32), pltpu.SMEM(lengths.shape, jnp.int32)]
        + [pltpu.VMEM((rows, head_size), BF16)] * 2
        + [pltpu.VMEM((rows, head_size), F32), pltpu.SemaphoreType.DMA((4,))],
        flops=1 << 20,
        place=HBM,
    )


def pack(queries, grad_out, heads_kv):
    tokens, heads_q, head_size = queries.shape
    array = jax.ShapeDtypeStruct
    return call(
        functools.partial(pack_kernel, heads_kv),
        "pack",
        (queries, grad_out),
        [array((heads_kv, tokens * 8, head_size), BF16)] * 2,
        [pltpu.VMEM((heads_kv, tokens, 16, head_size), BF16), pltpu.SemaphoreType.DMA((heads_kv,))],
        flops=1 << 20,
        place=HBM,
    )


def early(fresh, sources, qh, gh, own, blocks):
    own_k, own_v, bias, _ = own
    heads_kv, tokens, head_size = own_k.shape
    rows = len(sources) * CAP * TILE + tokens
    array = jax.ShapeDtypeStruct
    work = heads_kv * tokens * 8 * rows
    return call(
        functools.partial(early_kernel, fresh, sources, heads_kv, head_size**-0.5),
        "early",
        (own_k, own_v, qh, gh, bias, *blocks),
        [array((heads_kv, rows, head_size), BF16)]
        + [array((heads_kv, rows, tokens * 8), F32)] * 2
        + [array((heads_kv, 8, tokens * 8), F32)],
        [pltpu.VMEM((heads_kv, rows, head_size), BF16), pltpu.VMEM((CAP * TILE * heads_kv, head_size), F32)],
        flops=4 * work * head_size,
        transcendentals=work,
    )


def probs(sources, prompt_k, prompt_v, qh, gh, own, stats, block):
    _, own_v, bias, weight = own
    heads_kv, tokens, head_size = own_v.shape
    rows = tokens * heads_kv
    fresh = tokens + len(sources) * CAP * TILE
    array = jax.ShapeDtypeStruct
    work = heads_kv * tokens * 8 * fresh
    return call(
        functools.partial(probs_kernel, sources, heads_kv, head_size**-0.5),
        "probs",
        (prompt_k, prompt_v, qh, gh, bias, weight, stats, block),
        [array((rows, head_size), BF16)] * 2
        + [
            array((heads_kv, fresh, head_size), BF16),
            array((heads_kv, fresh, tokens * 8), BF16),
            array((heads_kv, fresh - tokens, tokens * 8), BF16),
            array((heads_kv, 8, tokens * 8), F32),
        ],
        [
            pltpu.VMEM((heads_kv, fresh, head_size), BF16),
            pltpu.VMEM((2, tokens, tokens * 8), BF16),
            pltpu.VMEM((2, heads_kv, tokens, head_size), F32),
            pltpu.VMEM((rows, head_size), F32),
        ],
        flops=8 * work * head_size,
        transcendentals=work,
    )


def windows(targets, qh, gh, ds_fresh, p_behind, e, dp, terms):
    heads_kv, early, columns = e.shape
    head_size = qh.shape[2]
    tokens = TD * TILE
    front = CAP * TILE * heads_kv
    behind = early - tokens + p_behind.shape[1]
    count = [sum(target == t for target, _ in targets) for t in (0, 1)]
    array = jax.ShapeDtypeStruct
    return call(
        functools.partial(windows_kernel, targets, heads_kv, head_size**-0.5),
        "windows",
        (qh, gh, ds_fresh, p_behind, e, dp, terms),
        [array((2 * front * n, head_size), BF16) for n in count]
        + [array((heads_kv, early, columns), BF16), array((heads_kv, tokens, columns), BF16)],
        [
            pltpu.VMEM((2, early - tokens, columns), BF16),
            pltpu.VMEM((2, heads_kv, behind, head_size), F32),
            pltpu.VMEM((front, head_size), F32),
        ],
        flops=4 * heads_kv * behind * columns * head_size,
    )


def grads(qh, gh, kh_fresh, kh_early, ds_fresh, ds_early, p_own):
    heads_kv, tokens, _ = p_own.shape
    head_size = kh_fresh.shape[2]
    array = jax.ShapeDtypeStruct
    return call(
        functools.partial(grads_kernel, heads_kv, head_size**-0.5),
        "grads",
        (qh, gh, kh_fresh, kh_early, ds_fresh, ds_early, p_own),
        [
            array((tokens, heads_kv * 8, head_size), BF16),
            array((tokens * heads_kv, head_size), F32),
            array((tokens * heads_kv, head_size), F32),
        ],
        [pltpu.VMEM((tokens * heads_kv, head_size), F32)],
        flops=2 * tokens * 8 * (ds_fresh.size + ds_early.size) // (tokens * 8) * head_size,
    )


def shift_route(distance, size):
    return [(i, i + distance) for i in range(size - distance)]


def back(route):
    return [(j, i) for i, j in route]


def added(*blocks):
    total = blocks[0].astype(F32)
    for block in blocks[1:]:
        total = total + block.astype(F32)
    return total


def after(array, *earlier):
    return lax.optimization_barrier((array, *earlier))[0]


def units(array, start, unit, count):
    return [array[start + i * unit : start + (i + 1) * unit] for i in range(count)]


def prompt_route(stride, size):
    return [(i + j, i + j + stride) for i in range(0, size, 2 * stride) for j in (0, 1)]


def collect(size, unit, rows, where, keys, values, head, held, queries, grad_out):
    even, lower, _ = where
    neighbours = [(i, i ^ 1) for i in range(size)]
    far_route = shift_route(4, size)[1:]
    near_route = shift_route(2, size)
    if size == W + 1:
        keys_far = permuted(keys, [(0, 4)])
        values_far = permuted(values, [(0, 5)])
        values_next = permuted(values, [(0, 1)])
        head, queries = lax.optimization_barrier((head, queries, keys_far))[:2]
        qh, gh = pack(queries, grad_out, keys.shape[0] // queries.shape[0])
        far = permuted(head, far_route)
        six = permuted(head, [(1, 7)])
        held = after(added(held, values_far, values_next, keys_far).astype(BF16), far, six, qh)
        second = permuted(jnp.concatenate([held, head]), near_route)
        crossed = jnp.where(even, jnp.concatenate([head, far]), jnp.concatenate([far, six]))
        crossed = permuted(crossed, neighbours)
        held = jnp.where(lower, held, second[:rows])
        third = permuted(after(jnp.concatenate([held, second[rows:]]), crossed), neighbours)
        early_sources = [(0, rows), (1, 0), (2, 0), (1, unit), (3, 0)]
        return held, third[:rows], third, [(0, rows)], early_sources, (second, crossed, far, six), (qh, gh)
    strides = [2**i for i in range(2, size.bit_length()) if 2**i < size]
    top = strides[-1]
    keys_far = permuted(keys, [(0, top)])
    values_far = permuted(values, [(0, top + 1)])
    values_next = permuted(values, [(0, 1)])
    far = permuted(head, far_route)
    held = added(held, values_next, values_far, keys_far).astype(BF16)
    for stride in reversed(strides[:-1]):
        held = added(held, permuted(held, prompt_route(stride, size))).astype(BF16)
    second = permuted(jnp.concatenate([held, head, far]), near_route)
    held = jnp.where(lower, held, second[:rows])
    near, six = units(second, rows, unit, 2)
    third = permuted(jnp.concatenate([head, near, far, six]), shift_route(1, size))
    other = permuted(held, neighbours)
    fresh_sources = [(0, i * unit) for i in range(4)]
    early_sources = [(0, rows), (1, 0), (0, rows + unit)]
    return held, other, third, fresh_sources, early_sources, (second, far), pack(queries, grad_out, keys.shape[0] // queries.shape[0])


def give_back(size, unit, where, prompt, behind, finish):
    even, lower, _ = where
    neighbours = [(i, i ^ 1) for i in range(size)]
    far_route = back(shift_route(4, size)[1:])
    send, keep = prompt
    rows = keep.shape[0]
    two, four, six = units(behind[1], 0, unit, 3)
    if size == W + 1:
        total = added(keep, permuted(send, neighbours)).astype(BF16)
        finished = finish(total)
        near, first, last = units(permuted(behind[0], neighbours), 0, unit, 3)
        none = jnp.zeros_like(first)
        parts = [permuted(total, [(j, 0), (j + 1, 1)]) for j in range(2, size, 2)]
        two = permuted(added(two, near).astype(BF16), back(shift_route(2, size)[1:]))
        four = after(added(four, jnp.where(even, last, first)).astype(BF16), finished[1])
        four = permuted(four, far_route)
        six = permuted(added(six, jnp.where(even, none, last)).astype(BF16), [(7, 1)])
        total = added(total, *parts).astype(BF16)
        mine = added(jnp.where(even, first, none), two, four, six)
        return finished, total, permuted(total, [(1, 0)]).astype(F32), mine
    strides = [2**i for i in range(2, size.bit_length()) if 2**i < size]
    top = strides[-1]
    zero, *third = units(permuted(behind[0], back(shift_route(1, size))), 0, unit, 4)
    total = added(keep, permuted(send, neighbours)).astype(BF16)
    two, four, six = (added(x, y).astype(BF16) for x, y in zip((two, four, six), third))
    second = permuted(jnp.concatenate([total, two, six]), back(shift_route(2, size)))
    four = added(four, second[rows + unit :])
    mine = added(zero, second[rows : rows + unit], permuted(four.astype(BF16), far_route))
    total = added(total, jnp.where(lower, second[:rows], jnp.zeros_like(total))).astype(BF16)
    for stride in strides[:-1]:
        total = added(total, permuted(total, back(prompt_route(stride, size)))).astype(BF16)
    keys_far = permuted(total, [(top, 0)])
    values_far = permuted(total, [(top + 1, 0)])
    values_next = permuted(total, [(1, 0)])
    return finish(send), added(total, keys_far), added(values_next, values_far), mine


def per_device(size, queries, keys, values, grad_out, parents, lengths):
    tokens, heads_kv, head_size = keys.shape
    rows = tokens * heads_kv
    one = CAP * TILE * heads_kv
    unit = 2 * one
    window = min(W, size - 2)
    device = lax.axis_index("node")
    keys = keys.reshape(rows, head_size)
    values = values.reshape(rows, head_size)

    if size == W + 1:
        order = [(1, 3), (2, 2), (3, 1), (4, 4), (5, 5), (6, 6)]
        targets = [(k % 2, k // 2 * unit) for k in range(window)]
    else:
        order = [(k, k) for k in (1, 3, 5, 7, 2, 4, 6)]
        targets = [(0, i * unit) for i in range(4)] + [(1, i * unit) for i in range(3)]
    head, held, *own = load(order, keys, values, parents, lengths, tokens)
    head, *where = lax.optimization_barrier((head, lax.rem(device, 2) == 0, lax.rem(device, 4) < 2, device == 0))
    even, _, root = where
    held, other, block, fresh_sources, early_sources, blocks, (qh, gh) = collect(
        size, unit, rows, where, keys, values, head, held, queries, grad_out
    )
    kh_early, e, dp, stats = early(len(fresh_sources), early_sources, qh, gh, own, blocks)
    prompt_k, prompt_v = jnp.where(even, held, other), jnp.where(even, other, held)
    *prompt, kh, ds, p_behind, terms = probs(fresh_sources, prompt_k, prompt_v, qh, gh, own, stats, block)
    *behind, ds_early, p_own = windows(targets, qh, gh, ds, p_behind, e, dp, terms)

    def finish(earlier):
        return grads(qh, gh, kh, kh_early, ds, ds_early, after(p_own, earlier))

    (grad_queries, dk, dv), prompt_k, prompt_v, mine = give_back(size, unit, where, prompt, behind, finish)
    own = []
    for side, local, prompt in ((0, dk, prompt_k), (1, dv, prompt_v)):
        whole = local + jnp.where(root, prompt.astype(F32), 0.0)
        own.append(whole.at[:one].add(mine[side * one : (side + 1) * one]).reshape(tokens, heads_kv, head_size))
    return grad_queries, own[0], own[1]


def solution(mesh):
    by_token = P(("leaf", "node"), "tensor", None)
    return jax.shard_map(
        functools.partial(per_device, mesh.shape["node"]),
        mesh=mesh,
        in_specs=(by_token, by_token, by_token, by_token, P("leaf"), P("leaf")),
        out_specs=(by_token, by_token, by_token),
        check_vma=False,
    )
```

```python
import functools
import math

import jax
import jax.numpy as jnp
from jax import lax
from jax.experimental import pallas as pl
from jax.experimental.pallas import tpu as pltpu
from jax.sharding import PartitionSpec as P

TILE = 16
TD = 8
CAP = 2
W = 7
CHUNK = 32
MASKED = -1e30
BF16 = jnp.bfloat16
F32 = jnp.float32


def permuted(block, route):
    return lax.ppermute(block, "node", route)


def column_limits(device, window, parents, lengths):
    cursor = parents[device * TD]
    need = [jnp.int32(0)] * (window + 1)
    for _ in range(W):
        owner = jnp.where(cursor < 0, -1, lax.div(jnp.maximum(cursor, 0), TD))
        distance = device - owner
        active = (owner >= 1) & (distance >= 1) & (distance <= W)
        depth = lax.rem(jnp.maximum(cursor, 0), TD) + 1
        for k in range(1, window + 1):
            need[k] = jnp.where(active & (distance == k), depth, need[k])
        cursor = jnp.where(active, parents[jnp.maximum(owner, 0) * TD], cursor)
    prompt = [jnp.where(device >= 1, lengths[t], 0) for t in range(TD)]
    behind = []
    for k in range(1, window + 1):
        owner = device - k
        seen = [(owner >= 1) & (c < need[k]) for c in range(CAP)]
        behind.append([jnp.where(seen[c], lengths[jnp.maximum(owner, 0) * TD + c], 0) for c in range(CAP)])
    return prompt, behind, [lengths[device * TD + t] for t in range(TD)]


def split_heads(block, heads_ref, start, count, heads_kv, wide):
    wide[: count * heads_kv] = block.astype(F32)
    for h in range(heads_kv):
        heads_ref[h, start : start + count] = wide[pl.ds(h, count, stride=heads_kv), :].astype(BF16)


def join_heads(blocks, count, heads_kv, wide):
    for h in range(heads_kv):
        wide[pl.ds(h, count, stride=heads_kv), :] = blocks[h]
    return wide[: count * heads_kv]


def load_kernel(order, heads_kv, *refs):
    sources, outs, scratch = refs[:4], refs[4:10], refs[10:]
    head, held, own_k, own_v, bias, weight = outs
    parents, lengths, keys, values, wide, arrived = scratch
    copies = [pltpu.make_async_copy(a, b, arrived.at[i]) for i, (a, b) in enumerate(zip(sources, scratch))]
    for copy in copies:
        copy.start()
    tokens = TD * TILE
    front = CAP * TILE * heads_kv
    device = lax.axis_index("node")
    for copy in copies:
        copy.wait()
    head[:front] = keys[:front]
    head[front:] = values[:front]
    held[...] = jnp.where(device == 0, keys[...], jnp.zeros_like(keys))
    split_heads(keys[...], own_k, 0, tokens, heads_kv, wide)
    split_heads(values[...], own_v, 0, tokens, heads_kv, wide)
    place = lax.broadcasted_iota(jnp.int32, (TILE, 128), 0)
    prompt, behind, own = column_limits(device, len(order), parents, lengths)
    even = lax.rem(device, 2) == 0
    limits = prompt
    for on_even, on_odd in order:
        limits = limits + [jnp.where(even, x, y) for x, y in zip(behind[on_even - 1], behind[on_odd - 1])]
    for t, limit in enumerate(limits + own):
        bias[t * TILE : (t + 1) * TILE] = jnp.where(place < limit, 0.0, MASKED)
    lane_place = lax.broadcasted_iota(jnp.int32, (8, 128), 1) // 8
    for t in range(TD):
        weight[:, t * 128 : (t + 1) * 128] = jnp.where(lane_place < lengths[device * TD + t], 1.0, 0.0)


def pack_kernel(heads_kv, q_ref, g_ref, qh, gh, blocks, arrived):
    tokens = TD * TILE
    copies = []
    for pair in range(heads_kv // 2):
        for ref, out in ((q_ref, qh), (g_ref, gh)):
            i = len(copies)
            copy = pltpu.make_async_copy(ref.at[:, pair * 16 : (pair + 1) * 16], blocks.at[i], arrived.at[i])
            copy.start()
            copies.append((copy, out, pair))
    for i, (copy, out, pair) in enumerate(copies):
        copy.wait()
        both = blocks[i].astype(F32)
        for part in range(2):
            out[2 * pair + part] = both[:, part * 8 : (part + 1) * 8].reshape(tokens * 8, 128).astype(BF16)


def causal_bias(columns):
    column_token = lax.broadcasted_iota(jnp.int32, (CHUNK, columns), 1) // 8
    return jnp.where(lax.broadcasted_iota(jnp.int32, (CHUNK, columns), 0) <= column_token, 0.0, MASKED)


def outer_product(rows, columns):
    return lax.dot_general(rows, columns, (((1,), (1,)), ((), ())), preferred_element_type=F32)


def early_kernel(fresh, sources, heads_kv, scale, *refs):
    own_k, own_v, qh, gh, bias = refs[:5]
    blocks, (kh, e_ref, dp_ref, stats, vh, wide) = refs[5:-6], refs[-6:]
    tokens = TD * TILE
    front = CAP * TILE
    behind = len(sources) * front
    start = tokens + fresh * front
    columns = CHUNK * 8
    for side, heads_ref, own in ((0, kh, own_k), (1, vh, own_v)):
        for k, (source, at) in enumerate(sources):
            at += side * front * heads_kv
            split_heads(blocks[source][at : at + front * heads_kv], heads_ref, k * front, front, heads_kv, wide)
        heads_ref[:, behind:] = own[...]
    causal = causal_bias(columns)
    for head in range(heads_kv):
        for c in range(tokens // CHUNK):
            rows = behind + (c + 1) * CHUNK
            span = slice(c * columns, (c + 1) * columns)
            s = outer_product(kh[head, :rows], qh[head, span])
            dp = outer_product(vh[head, :rows], gh[head, span])
            s = s + jnp.concatenate([bias[start : start + rows]] * (columns // 128), axis=1)
            s = jnp.concatenate([s[: rows - CHUNK], s[rows - CHUNK :] + causal], axis=0)
            top = jnp.max(s, axis=0, keepdims=True)
            e = jnp.exp2((s - top) * (scale * math.log2(math.e)))
            e_ref[head, :rows, span] = e
            dp_ref[head, :rows, span] = dp
            stats[head, 0:1, span] = top
            stats[head, 1:2, span] = jnp.sum(e, axis=0, keepdims=True)
            stats[head, 2:3, span] = jnp.sum(e * dp, axis=0, keepdims=True)


def probs_kernel(sources, heads_kv, scale, *refs):
    prompt_k, prompt_v, qh, gh, bias, weight_ref, stats, block_ref = refs[:8]
    send_ref, keep_ref, kh, ds_ref, p_behind, terms, vh, p_ref, grads, wide = refs[8:]
    tokens = TD * TILE
    front = CAP * TILE
    columns = CHUNK * 8
    rate = scale * math.log2(math.e)
    device = lax.axis_index("node")

    for side, heads_ref, prompt in ((0, kh, prompt_k), (1, vh, prompt_v)):
        split_heads(prompt[...], heads_ref, 0, tokens, heads_kv, wide)
        for k, (_, at) in enumerate(sources):
            at += side * front * heads_kv
            split_heads(block_ref[at : at + front * heads_kv], heads_ref, tokens + k * front, front, heads_kv, wide)

    for head in range(heads_kv):
        for c in range(tokens // CHUNK):
            span = slice(c * columns, (c + 1) * columns)
            s = outer_product(kh[head], qh[head, span])
            dp = outer_product(vh[head], gh[head, span])
            s = s + jnp.concatenate([bias[: s.shape[0]]] * (columns // 128), axis=1)
            top_early = stats[head, 0:1, span]
            top = jnp.maximum(jnp.max(s, axis=0, keepdims=True), top_early)
            e = jnp.exp2((s - top) * rate)
            shrink = jnp.exp2((top_early - top) * rate)
            total = jnp.sum(e, axis=0, keepdims=True) + shrink * stats[head, 1:2, span]
            weight = weight_ref[:1, span] / total
            weight_early = weight * shrink
            p = e * weight
            delta = jnp.sum(p * dp, axis=0, keepdims=True) + weight_early * stats[head, 2:3, span]
            ds_ref[head, :, span] = (p * (dp - delta)).astype(BF16)
            p_ref[head % 2, :, span] = p[:tokens].astype(BF16)
            p_behind[head, :, span] = p[tokens:].astype(BF16)
            terms[head, 0:1, span] = weight_early
            terms[head, 1:2, span] = delta
        grads[0, head] = scale * jnp.dot(ds_ref[head, :tokens], qh[head], preferred_element_type=F32)
        grads[1, head] = jnp.dot(p_ref[head % 2], gh[head], preferred_element_type=F32)

    even = lax.rem(device, 2) == 0
    for side in range(2):
        dprompt = join_heads([grads[side, h] for h in range(heads_kv)], tokens, heads_kv, wide).astype(BF16)
        kept = even if side == 0 else jnp.logical_not(even)

        @pl.when(kept)
        def _():
            keep_ref[...] = dprompt

        @pl.when(jnp.logical_not(kept))
        def _():
            send_ref[...] = dprompt


def windows_kernel(targets, heads_kv, scale, *refs):
    qh, gh, ds_fresh, p_behind, e_ref, dp_ref, terms, send_ref, keep_ref, ds_ref, p_own, p_ref, grads, wide = refs
    front = CAP * TILE
    tokens = TD * TILE
    early = ds_ref.shape[1] - tokens
    columns = CHUNK * 8
    for head in range(heads_kv):
        for c in range(tokens // CHUNK):
            rows = early + (c + 1) * CHUNK
            span = slice(c * columns, (c + 1) * columns)
            p = e_ref[head, :rows, span] * terms[head, 0:1, span]
            ds_ref[head, :rows, span] = (p * (dp_ref[head, :rows, span] - terms[head, 1:2, span])).astype(BF16)
            p_ref[head % 2, :, span] = p[:early].astype(BF16)
            p_own[head, : rows - early, span] = p[early:].astype(BF16)
        ds = jnp.concatenate([ds_fresh[head, tokens:], ds_ref[head, :early]], axis=0)
        grads[0, head] = scale * jnp.dot(ds, qh[head], preferred_element_type=F32)
        p = jnp.concatenate([p_behind[head], p_ref[head % 2]], axis=0)
        grads[1, head] = jnp.dot(p, gh[head], preferred_element_type=F32)
    for side in range(2):
        for k, (target, start) in enumerate(targets):
            span = slice(k * front, (k + 1) * front)
            block = join_heads([grads[side, h, span] for h in range(heads_kv)], front, heads_kv, wide).astype(BF16)
            start += side * front * heads_kv
            (send_ref, keep_ref)[target][start : start + front * heads_kv] = block


def grads_kernel(heads_kv, scale, *refs):
    qh, gh, kh_fresh, kh_early, ds_fresh, ds_early, p_own, dq_ref, dk_ref, dv_ref, wide = refs
    tokens = TD * TILE
    kh = [jnp.concatenate([kh_fresh[h], kh_early[h]], axis=0) for h in range(heads_kv)]
    before = kh[0].shape[0] - tokens
    columns = CHUNK * 8
    dk = []
    dv = []
    for pair in range(heads_kv // 2):
        for c in range(tokens // CHUNK):
            rows = before + (c + 1) * CHUNK
            span = slice(c * columns, (c + 1) * columns)
            parts = []
            for head in (2 * pair, 2 * pair + 1):
                fresh = ds_fresh.shape[1]
                ds = jnp.concatenate([ds_fresh[head, :, span], ds_early[head, : rows - fresh, span]], axis=0)
                dq = lax.dot_general(kh[head][:rows], ds, (((0,), (0,)), ((), ())), preferred_element_type=F32)
                parts.append((scale * dq.T).reshape(CHUNK, 8, 128))
            dq_ref[c * CHUNK : (c + 1) * CHUNK, pair * 16 : (pair + 1) * 16] = jnp.concatenate(parts, axis=1).astype(BF16)
        for head in (2 * pair, 2 * pair + 1):
            for source, factor, out in ((ds_early.at[head, before - fresh :], qh, dk), (p_own.at[head], gh, dv)):
                pieces = []
                for c in range(tokens // CHUNK):
                    start = c * columns
                    pieces.append(
                        jnp.dot(
                            source[c * CHUNK : (c + 1) * CHUNK, start:], factor[head, start:], preferred_element_type=F32
                        )
                    )
                out.append(jnp.concatenate(pieces, axis=0))
    dk_ref[...] = scale * join_heads(dk, tokens, heads_kv, wide)
    dv_ref[...] = join_heads(dv, tokens, heads_kv, wide)


VMEM = pl.BlockSpec(memory_space=pltpu.VMEM)


HBM = pl.BlockSpec(memory_space=pltpu.HBM)


def call(kernel, name, operands, outputs, scratch, flops, transcendentals=0, place=VMEM):
    sizes = [a.size * a.dtype.itemsize for a in (*operands, *outputs)]
    if place is HBM:
        operands = [pltpu.with_memory_space_constraint(a, pltpu.HBM) for a in operands]
    return pl.pallas_call(
        kernel,
        in_specs=[place] * len(operands),
        out_specs=[VMEM] * len(outputs),
        out_shape=outputs,
        scratch_shapes=scratch,
        compiler_params=pltpu.CompilerParams(vmem_limit_bytes=16 * 1024 * 1024),
        cost_estimate=pl.CostEstimate(flops=flops, bytes_accessed=sum(sizes), transcendentals=transcendentals),
        name=name,
    )(*operands)


def load(order, keys, values, parents, lengths, tokens):
    rows, head_size = keys.shape
    heads_kv = rows // tokens
    array = jax.ShapeDtypeStruct
    return call(
        functools.partial(load_kernel, order, heads_kv),
        "load",
        (parents, lengths, keys, values),
        [array((2 * CAP * TILE * heads_kv, head_size), BF16), array((rows, head_size), BF16)]
        + [array((heads_kv, tokens, head_size), BF16)] * 2
        + [array((2 * tokens + len(order) * CAP * TILE, 128), F32), array((8, tokens * 8), F32)],
        [pltpu.SMEM(parents.shape, jnp.int32), pltpu.SMEM(lengths.shape, jnp.int32)]
        + [pltpu.VMEM((rows, head_size), BF16)] * 2
        + [pltpu.VMEM((rows, head_size), F32), pltpu.SemaphoreType.DMA((4,))],
        flops=1 << 20,
        place=HBM,
    )


def pack(queries, grad_out, heads_kv):
    tokens, heads_q, head_size = queries.shape
    array = jax.ShapeDtypeStruct
    return call(
        functools.partial(pack_kernel, heads_kv),
        "pack",
        (queries, grad_out),
        [array((heads_kv, tokens * 8, head_size), BF16)] * 2,
        [pltpu.VMEM((heads_kv, tokens, 16, head_size), BF16), pltpu.SemaphoreType.DMA((heads_kv,))],
        flops=1 << 20,
        place=HBM,
    )


def early(fresh, sources, qh, gh, own, blocks):
    own_k, own_v, bias, _ = own
    heads_kv, tokens, head_size = own_k.shape
    rows = len(sources) * CAP * TILE + tokens
    array = jax.ShapeDtypeStruct
    work = heads_kv * tokens * 8 * rows
    return call(
        functools.partial(early_kernel, fresh, sources, heads_kv, head_size**-0.5),
        "early",
        (own_k, own_v, qh, gh, bias, *blocks),
        [array((heads_kv, rows, head_size), BF16)]
        + [array((heads_kv, rows, tokens * 8), F32)] * 2
        + [array((heads_kv, 8, tokens * 8), F32)],
        [pltpu.VMEM((heads_kv, rows, head_size), BF16), pltpu.VMEM((CAP * TILE * heads_kv, head_size), F32)],
        flops=4 * work * head_size,
        transcendentals=work,
    )


def probs(sources, prompt_k, prompt_v, qh, gh, own, stats, block):
    _, own_v, bias, weight = own
    heads_kv, tokens, head_size = own_v.shape
    rows = tokens * heads_kv
    fresh = tokens + len(sources) * CAP * TILE
    array = jax.ShapeDtypeStruct
    work = heads_kv * tokens * 8 * fresh
    return call(
        functools.partial(probs_kernel, sources, heads_kv, head_size**-0.5),
        "probs",
        (prompt_k, prompt_v, qh, gh, bias, weight, stats, block),
        [array((rows, head_size), BF16)] * 2
        + [
            array((heads_kv, fresh, head_size), BF16),
            array((heads_kv, fresh, tokens * 8), BF16),
            array((heads_kv, fresh - tokens, tokens * 8), BF16),
            array((heads_kv, 8, tokens * 8), F32),
        ],
        [
            pltpu.VMEM((heads_kv, fresh, head_size), BF16),
            pltpu.VMEM((2, tokens, tokens * 8), BF16),
            pltpu.VMEM((2, heads_kv, tokens, head_size), F32),
            pltpu.VMEM((rows, head_size), F32),
        ],
        flops=8 * work * head_size,
        transcendentals=work,
    )


def windows(targets, qh, gh, ds_fresh, p_behind, e, dp, terms):
    heads_kv, early, columns = e.shape
    head_size = qh.shape[2]
    tokens = TD * TILE
    front = CAP * TILE * heads_kv
    behind = early - tokens + p_behind.shape[1]
    count = [sum(target == t for target, _ in targets) for t in (0, 1)]
    array = jax.ShapeDtypeStruct
    return call(
        functools.partial(windows_kernel, targets, heads_kv, head_size**-0.5),
        "windows",
        (qh, gh, ds_fresh, p_behind, e, dp, terms),
        [array((2 * front * n, head_size), BF16) for n in count]
        + [array((heads_kv, early, columns), BF16), array((heads_kv, tokens, columns), BF16)],
        [
            pltpu.VMEM((2, early - tokens, columns), BF16),
            pltpu.VMEM((2, heads_kv, behind, head_size), F32),
            pltpu.VMEM((front, head_size), F32),
        ],
        flops=4 * heads_kv * behind * columns * head_size,
    )


def grads(qh, gh, kh_fresh, kh_early, ds_fresh, ds_early, p_own):
    heads_kv, tokens, _ = p_own.shape
    head_size = kh_fresh.shape[2]
    array = jax.ShapeDtypeStruct
    return call(
        functools.partial(grads_kernel, heads_kv, head_size**-0.5),
        "grads",
        (qh, gh, kh_fresh, kh_early, ds_fresh, ds_early, p_own),
        [
            array((tokens, heads_kv * 8, head_size), BF16),
            array((tokens * heads_kv, head_size), F32),
            array((tokens * heads_kv, head_size), F32),
        ],
        [pltpu.VMEM((tokens * heads_kv, head_size), F32)],
        flops=2 * tokens * 8 * (ds_fresh.size + ds_early.size) // (tokens * 8) * head_size,
    )


def shift_route(distance, size):
    return [(i, i + distance) for i in range(size - distance)]


def back(route):
    return [(j, i) for i, j in route]


def added(*blocks):
    total = blocks[0].astype(F32)
    for block in blocks[1:]:
        total = total + block.astype(F32)
    return total


def after(array, *earlier):
    return lax.optimization_barrier((array, *earlier))[0]


def units(array, start, unit, count):
    return [array[start + i * unit : start + (i + 1) * unit] for i in range(count)]


def prompt_route(stride, size):
    return [(i + j, i + j + stride) for i in range(0, size, 2 * stride) for j in (0, 1)]


def collect(size, unit, rows, where, keys, values, head, held, queries, grad_out):
    even, lower, _ = where
    neighbours = [(i, i ^ 1) for i in range(size)]
    far_route = shift_route(4, size)[1:]
    near_route = shift_route(2, size)
    if size == W + 1:
        keys_far = permuted(keys, [(0, 4)])
        values_far = permuted(values, [(0, 5)])
        values_next = permuted(values, [(0, 1)])
        head, queries = lax.optimization_barrier((head, queries, keys_far))[:2]
        qh, gh = pack(queries, grad_out, keys.shape[0] // queries.shape[0])
        far = permuted(head, far_route)
        six = permuted(head, [(1, 7)])
        held = after(added(held, values_far, values_next, keys_far).astype(BF16), far, six, qh)
        second = permuted(jnp.concatenate([held, head]), near_route)
        crossed = jnp.where(even, jnp.concatenate([head, far]), jnp.concatenate([far, six]))
        crossed = permuted(crossed, neighbours)
        held = jnp.where(lower, held, second[:rows])
        third = permuted(after(jnp.concatenate([held, second[rows:]]), crossed), neighbours)
        early_sources = [(0, rows), (1, 0), (2, 0), (1, unit), (3, 0)]
        return held, third[:rows], third, [(0, rows)], early_sources, (second, crossed, far, six), (qh, gh)
    strides = [2**i for i in range(2, size.bit_length()) if 2**i < size]
    top = strides[-1]
    keys_far = permuted(keys, [(0, top)])
    values_far = permuted(values, [(0, top + 1)])
    values_next = permuted(values, [(0, 1)])
    far = permuted(head, far_route)
    held = added(held, values_next, values_far, keys_far).astype(BF16)
    for stride in reversed(strides[:-1]):
        held = added(held, permuted(held, prompt_route(stride, size))).astype(BF16)
    second = permuted(jnp.concatenate([held, head, far]), near_route)
    held = jnp.where(lower, held, second[:rows])
    near, six = units(second, rows, unit, 2)
    third = permuted(jnp.concatenate([head, near, far, six]), shift_route(1, size))
    other = permuted(held, neighbours)
    fresh_sources = [(0, i * unit) for i in range(4)]
    early_sources = [(0, rows), (1, 0), (0, rows + unit)]
    return held, other, third, fresh_sources, early_sources, (second, far), pack(queries, grad_out, keys.shape[0] // queries.shape[0])


def give_back(size, unit, where, prompt, behind, finish):
    even, lower, _ = where
    neighbours = [(i, i ^ 1) for i in range(size)]
    far_route = back(shift_route(4, size)[1:])
    send, keep = prompt
    rows = keep.shape[0]
    two, four, six = units(behind[1], 0, unit, 3)
    if size == W + 1:
        total = added(keep, permuted(send, neighbours)).astype(BF16)
        finished = finish(total)
        near, first, last = units(permuted(behind[0], neighbours), 0, unit, 3)
        none = jnp.zeros_like(first)
        parts = [permuted(total, [(j, 0), (j + 1, 1)]) for j in reversed(range(2, size, 2))]
        two = permuted(added(two, near).astype(BF16), back(shift_route(2, size)[1:]))
        four = after(added(four, jnp.where(even, last, first)).astype(BF16), finished[1])
        four = permuted(four, far_route)
        six = permuted(added(six, jnp.where(even, none, last)).astype(BF16), [(7, 1)])
        total = added(total, *parts).astype(BF16)
        mine = added(jnp.where(even, first, none), two, four, six)
        return finished, total, permuted(total, [(1, 0)]).astype(F32), mine
    strides = [2**i for i in range(2, size.bit_length()) if 2**i < size]
    top = strides[-1]
    zero, *third = units(permuted(behind[0], back(shift_route(1, size))), 0, unit, 4)
    total = added(keep, permuted(send, neighbours)).astype(BF16)
    two, four, six = (added(x, y).astype(BF16) for x, y in zip((two, four, six), third))
    second = permuted(jnp.concatenate([total, two, six]), back(shift_route(2, size)))
    four = added(four, second[rows + unit :])
    mine = added(zero, second[rows : rows + unit], permuted(four.astype(BF16), far_route))
    total = added(total, jnp.where(lower, second[:rows], jnp.zeros_like(total))).astype(BF16)
    for stride in strides[:-1]:
        total = added(total, permuted(total, back(prompt_route(stride, size)))).astype(BF16)
    keys_far = permuted(total, [(top, 0)])
    values_far = permuted(total, [(top + 1, 0)])
    values_next = permuted(total, [(1, 0)])
    return finish(send), added(total, keys_far), added(values_next, values_far), mine


def per_device(size, queries, keys, values, grad_out, parents, lengths):
    tokens, heads_kv, head_size = keys.shape
    rows = tokens * heads_kv
    one = CAP * TILE * heads_kv
    unit = 2 * one
    window = min(W, size - 2)
    device = lax.axis_index("node")
    keys = keys.reshape(rows, head_size)
    values = values.reshape(rows, head_size)

    if size == W + 1:
        order = [(1, 3), (2, 2), (3, 1), (4, 4), (5, 5), (6, 6)]
        targets = [(k % 2, k // 2 * unit) for k in range(window)]
    else:
        order = [(k, k) for k in (1, 3, 5, 7, 2, 4, 6)]
        targets = [(0, i * unit) for i in range(4)] + [(1, i * unit) for i in range(3)]
    head, held, *own = load(order, keys, values, parents, lengths, tokens)
    head, *where = lax.optimization_barrier((head, lax.rem(device, 2) == 0, lax.rem(device, 4) < 2, device == 0))
    even, _, root = where
    held, other, block, fresh_sources, early_sources, blocks, (qh, gh) = collect(
        size, unit, rows, where, keys, values, head, held, queries, grad_out
    )
    kh_early, e, dp, stats = early(len(fresh_sources), early_sources, qh, gh, own, blocks)
    prompt_k, prompt_v = jnp.where(even, held, other), jnp.where(even, other, held)
    *prompt, kh, ds, p_behind, terms = probs(fresh_sources, prompt_k, prompt_v, qh, gh, own, stats, block)
    *behind, ds_early, p_own = windows(targets, qh, gh, ds, p_behind, e, dp, terms)

    def finish(earlier):
        return grads(qh, gh, kh, kh_early, ds, ds_early, after(p_own, earlier))

    (grad_queries, dk, dv), prompt_k, prompt_v, mine = give_back(size, unit, where, prompt, behind, finish)
    own = []
    for side, local, prompt in ((0, dk, prompt_k), (1, dv, prompt_v)):
        whole = local + jnp.where(root, prompt.astype(F32), 0.0)
        own.append(whole.at[:one].add(mine[side * one : (side + 1) * one]).reshape(tokens, heads_kv, head_size))
    return grad_queries, own[0], own[1]


def solution(mesh):
    by_token = P(("leaf", "node"), "tensor", None)
    return jax.shard_map(
        functools.partial(per_device, mesh.shape["node"]),
        mesh=mesh,
        in_specs=(by_token, by_token, by_token, by_token, P("leaf"), P("leaf")),
        out_specs=(by_token, by_token, by_token),
        check_vma=False,
    )
```

```python
import functools
import math

import jax
import jax.numpy as jnp
from jax import lax
from jax.experimental import pallas as pl
from jax.experimental.pallas import tpu as pltpu
from jax.sharding import PartitionSpec as P

TILE = 16
TD = 8
CAP = 2
W = 7
CHUNK = 32
MASKED = -1e30
BF16 = jnp.bfloat16
F32 = jnp.float32


def permuted(block, route):
    return lax.ppermute(block, "node", route)


def column_limits(device, window, parents, lengths):
    cursor = parents[device * TD]
    need = [jnp.int32(0)] * (window + 1)
    for _ in range(W):
        owner = jnp.where(cursor < 0, -1, lax.div(jnp.maximum(cursor, 0), TD))
        distance = device - owner
        active = (owner >= 1) & (distance >= 1) & (distance <= W)
        depth = lax.rem(jnp.maximum(cursor, 0), TD) + 1
        for k in range(1, window + 1):
            need[k] = jnp.where(active & (distance == k), depth, need[k])
        cursor = jnp.where(active, parents[jnp.maximum(owner, 0) * TD], cursor)
    prompt = [jnp.where(device >= 1, lengths[t], 0) for t in range(TD)]
    behind = []
    for k in range(1, window + 1):
        owner = device - k
        seen = [(owner >= 1) & (c < need[k]) for c in range(CAP)]
        behind.append([jnp.where(seen[c], lengths[jnp.maximum(owner, 0) * TD + c], 0) for c in range(CAP)])
    return prompt, behind, [lengths[device * TD + t] for t in range(TD)]


def split_heads(block, heads_ref, start, count, heads_kv, wide):
    wide[: count * heads_kv] = block.astype(F32)
    for h in range(heads_kv):
        heads_ref[h, start : start + count] = wide[pl.ds(h, count, stride=heads_kv), :].astype(BF16)


def join_heads(blocks, count, heads_kv, wide):
    for h in range(heads_kv):
        wide[pl.ds(h, count, stride=heads_kv), :] = blocks[h]
    return wide[: count * heads_kv]


def load_kernel(order, heads_kv, *refs):
    sources, outs, scratch = refs[:4], refs[4:10], refs[10:]
    head, held, own_k, own_v, bias, weight = outs
    parents, lengths, keys, values, wide, arrived = scratch
    copies = [pltpu.make_async_copy(a, b, arrived.at[i]) for i, (a, b) in enumerate(zip(sources, scratch))]
    for copy in copies:
        copy.start()
    tokens = TD * TILE
    front = CAP * TILE * heads_kv
    device = lax.axis_index("node")
    for copy in copies:
        copy.wait()
    head[:front] = keys[:front]
    head[front:] = values[:front]
    held[...] = jnp.where(device == 0, keys[...], jnp.zeros_like(keys))
    split_heads(keys[...], own_k, 0, tokens, heads_kv, wide)
    split_heads(values[...], own_v, 0, tokens, heads_kv, wide)
    place = lax.broadcasted_iota(jnp.int32, (TILE, 128), 0)
    prompt, behind, own = column_limits(device, len(order), parents, lengths)
    even = lax.rem(device, 2) == 0
    limits = prompt
    for on_even, on_odd in order:
        limits = limits + [jnp.where(even, x, y) for x, y in zip(behind[on_even - 1], behind[on_odd - 1])]
    for t, limit in enumerate(limits + own):
        bias[t * TILE : (t + 1) * TILE] = jnp.where(place < limit, 0.0, MASKED)
    lane_place = lax.broadcasted_iota(jnp.int32, (8, 128), 1) // 8
    for t in range(TD):
        weight[:, t * 128 : (t + 1) * 128] = jnp.where(lane_place < lengths[device * TD + t], 1.0, 0.0)


def pack_kernel(heads_kv, q_ref, g_ref, qh, gh, blocks, arrived):
    tokens = TD * TILE
    copies = []
    for pair in range(heads_kv // 2):
        for ref, out in ((q_ref, qh), (g_ref, gh)):
            i = len(copies)
            copy = pltpu.make_async_copy(ref.at[:, pair * 16 : (pair + 1) * 16], blocks.at[i], arrived.at[i])
            copy.start()
            copies.append((copy, out, pair))
    for i, (copy, out, pair) in enumerate(copies):
        copy.wait()
        both = blocks[i].astype(F32)
        for part in range(2):
            out[2 * pair + part] = both[:, part * 8 : (part + 1) * 8].reshape(tokens * 8, 128).astype(BF16)


def causal_bias(columns):
    column_token = lax.broadcasted_iota(jnp.int32, (CHUNK, columns), 1) // 8
    return jnp.where(lax.broadcasted_iota(jnp.int32, (CHUNK, columns), 0) <= column_token, 0.0, MASKED)


def outer_product(rows, columns):
    return lax.dot_general(rows, columns, (((1,), (1,)), ((), ())), preferred_element_type=F32)


def early_kernel(fresh, sources, heads_kv, scale, *refs):
    own_k, own_v, qh, gh, bias = refs[:5]
    blocks, (kh, e_ref, dp_ref, stats, vh, wide) = refs[5:-6], refs[-6:]
    tokens = TD * TILE
    front = CAP * TILE
    behind = len(sources) * front
    start = tokens + fresh * front
    columns = CHUNK * 8
    for side, heads_ref, own in ((0, kh, own_k), (1, vh, own_v)):
        for k, (source, at) in enumerate(sources):
            at += side * front * heads_kv
            split_heads(blocks[source][at : at + front * heads_kv], heads_ref, k * front, front, heads_kv, wide)
        heads_ref[:, behind:] = own[...]
    causal = causal_bias(columns)
    for head in range(heads_kv):
        for c in range(tokens // CHUNK):
            rows = behind + (c + 1) * CHUNK
            span = slice(c * columns, (c + 1) * columns)
            s = outer_product(kh[head, :rows], qh[head, span])
            dp = outer_product(vh[head, :rows], gh[head, span])
            s = s + jnp.concatenate([bias[start : start + rows]] * (columns // 128), axis=1)
            s = jnp.concatenate([s[: rows - CHUNK], s[rows - CHUNK :] + causal], axis=0)
            top = jnp.max(s, axis=0, keepdims=True)
            e = jnp.exp2((s - top) * (scale * math.log2(math.e)))
            e_ref[head, :rows, span] = e
            dp_ref[head, :rows, span] = dp
            stats[head, 0:1, span] = top
            stats[head, 1:2, span] = jnp.sum(e, axis=0, keepdims=True)
            stats[head, 2:3, span] = jnp.sum(e * dp, axis=0, keepdims=True)


def probs_kernel(sources, heads_kv, scale, *refs):
    prompt_k, prompt_v, qh, gh, bias, weight_ref, stats, block_ref = refs[:8]
    send_ref, keep_ref, kh, ds_ref, p_behind, terms, vh, p_ref, grads, wide = refs[8:]
    tokens = TD * TILE
    front = CAP * TILE
    columns = CHUNK * 8
    rate = scale * math.log2(math.e)
    device = lax.axis_index("node")

    for side, heads_ref, prompt in ((0, kh, prompt_k), (1, vh, prompt_v)):
        split_heads(prompt[...], heads_ref, 0, tokens, heads_kv, wide)
        for k, (_, at) in enumerate(sources):
            at += side * front * heads_kv
            split_heads(block_ref[at : at + front * heads_kv], heads_ref, tokens + k * front, front, heads_kv, wide)

    for head in range(heads_kv):
        for c in range(tokens // CHUNK):
            span = slice(c * columns, (c + 1) * columns)
            s = outer_product(kh[head], qh[head, span])
            dp = outer_product(vh[head], gh[head, span])
            s = s + jnp.concatenate([bias[: s.shape[0]]] * (columns // 128), axis=1)
            top_early = stats[head, 0:1, span]
            top = jnp.maximum(jnp.max(s, axis=0, keepdims=True), top_early)
            e = jnp.exp2((s - top) * rate)
            shrink = jnp.exp2((top_early - top) * rate)
            total = jnp.sum(e, axis=0, keepdims=True) + shrink * stats[head, 1:2, span]
            weight = weight_ref[:1, span] / total
            weight_early = weight * shrink
            p = e * weight
            delta = jnp.sum(p * dp, axis=0, keepdims=True) + weight_early * stats[head, 2:3, span]
            ds_ref[head, :, span] = (p * (dp - delta)).astype(BF16)
            p_ref[head % 2, :, span] = p[:tokens].astype(BF16)
            p_behind[head, :, span] = p[tokens:].astype(BF16)
            terms[head, 0:1, span] = weight_early
            terms[head, 1:2, span] = delta
        grads[0, head] = scale * jnp.dot(ds_ref[head, :tokens], qh[head], preferred_element_type=F32)
        grads[1, head] = jnp.dot(p_ref[head % 2], gh[head], preferred_element_type=F32)

    even = lax.rem(device, 2) == 0
    for side in range(2):
        dprompt = join_heads([grads[side, h] for h in range(heads_kv)], tokens, heads_kv, wide).astype(BF16)
        kept = even if side == 0 else jnp.logical_not(even)

        @pl.when(kept)
        def _():
            keep_ref[...] = dprompt

        @pl.when(jnp.logical_not(kept))
        def _():
            send_ref[...] = dprompt


def windows_kernel(targets, heads_kv, scale, *refs):
    qh, gh, ds_fresh, p_behind, e_ref, dp_ref, terms, send_ref, keep_ref, ds_ref, p_own, p_ref, grads, wide = refs
    front = CAP * TILE
    tokens = TD * TILE
    early = ds_ref.shape[1] - tokens
    columns = CHUNK * 8
    for head in range(heads_kv):
        for c in range(tokens // CHUNK):
            rows = early + (c + 1) * CHUNK
            span = slice(c * columns, (c + 1) * columns)
            p = e_ref[head, :rows, span] * terms[head, 0:1, span]
            ds_ref[head, :rows, span] = (p * (dp_ref[head, :rows, span] - terms[head, 1:2, span])).astype(BF16)
            p_ref[head % 2, :, span] = p[:early].astype(BF16)
            p_own[head, : rows - early, span] = p[early:].astype(BF16)
        ds = jnp.concatenate([ds_fresh[head, tokens:], ds_ref[head, :early]], axis=0)
        grads[0, head] = scale * jnp.dot(ds, qh[head], preferred_element_type=F32)
        p = jnp.concatenate([p_behind[head], p_ref[head % 2]], axis=0)
        grads[1, head] = jnp.dot(p, gh[head], preferred_element_type=F32)
    for side in range(2):
        for k, (target, start) in enumerate(targets):
            span = slice(k * front, (k + 1) * front)
            block = join_heads([grads[side, h, span] for h in range(heads_kv)], front, heads_kv, wide).astype(BF16)
            start += side * front * heads_kv
            (send_ref, keep_ref)[target][start : start + front * heads_kv] = block


def grads_kernel(heads_kv, scale, *refs):
    qh, gh, kh_fresh, kh_early, ds_fresh, ds_early, p_own, dq_ref, dk_ref, dv_ref, wide = refs
    tokens = TD * TILE
    kh = [jnp.concatenate([kh_fresh[h], kh_early[h]], axis=0) for h in range(heads_kv)]
    before = kh[0].shape[0] - tokens
    columns = CHUNK * 8
    dk = []
    dv = []
    for pair in range(heads_kv // 2):
        for c in range(tokens // CHUNK):
            rows = before + (c + 1) * CHUNK
            span = slice(c * columns, (c + 1) * columns)
            parts = []
            for head in (2 * pair, 2 * pair + 1):
                fresh = ds_fresh.shape[1]
                ds = jnp.concatenate([ds_fresh[head, :, span], ds_early[head, : rows - fresh, span]], axis=0)
                dq = lax.dot_general(kh[head][:rows], ds, (((0,), (0,)), ((), ())), preferred_element_type=F32)
                parts.append((scale * dq.T).reshape(CHUNK, 8, 128))
            dq_ref[c * CHUNK : (c + 1) * CHUNK, pair * 16 : (pair + 1) * 16] = jnp.concatenate(parts, axis=1).astype(BF16)
        for head in (2 * pair, 2 * pair + 1):
            for source, factor, out in ((ds_early.at[head, before - fresh :], qh, dk), (p_own.at[head], gh, dv)):
                pieces = []
                for c in range(tokens // CHUNK):
                    start = c * columns
                    pieces.append(
                        jnp.dot(
                            source[c * CHUNK : (c + 1) * CHUNK, start:], factor[head, start:], preferred_element_type=F32
                        )
                    )
                out.append(jnp.concatenate(pieces, axis=0))
    dk_ref[...] = scale * join_heads(dk, tokens, heads_kv, wide)
    dv_ref[...] = join_heads(dv, tokens, heads_kv, wide)


VMEM = pl.BlockSpec(memory_space=pltpu.VMEM)


HBM = pl.BlockSpec(memory_space=pltpu.HBM)


def call(kernel, name, operands, outputs, scratch, flops, transcendentals=0, place=VMEM):
    sizes = [a.size * a.dtype.itemsize for a in (*operands, *outputs)]
    if place is HBM:
        operands = [pltpu.with_memory_space_constraint(a, pltpu.HBM) for a in operands]
    return pl.pallas_call(
        kernel,
        in_specs=[place] * len(operands),
        out_specs=[VMEM] * len(outputs),
        out_shape=outputs,
        scratch_shapes=scratch,
        compiler_params=pltpu.CompilerParams(vmem_limit_bytes=16 * 1024 * 1024),
        cost_estimate=pl.CostEstimate(flops=flops, bytes_accessed=sum(sizes), transcendentals=transcendentals),
        name=name,
    )(*operands)


def load(order, keys, values, parents, lengths, tokens):
    rows, head_size = keys.shape
    heads_kv = rows // tokens
    array = jax.ShapeDtypeStruct
    return call(
        functools.partial(load_kernel, order, heads_kv),
        "load",
        (parents, lengths, keys, values),
        [array((2 * CAP * TILE * heads_kv, head_size), BF16), array((rows, head_size), BF16)]
        + [array((heads_kv, tokens, head_size), BF16)] * 2
        + [array((2 * tokens + len(order) * CAP * TILE, 128), F32), array((8, tokens * 8), F32)],
        [pltpu.SMEM(parents.shape, jnp.int32), pltpu.SMEM(lengths.shape, jnp.int32)]
        + [pltpu.VMEM((rows, head_size), BF16)] * 2
        + [pltpu.VMEM((rows, head_size), F32), pltpu.SemaphoreType.DMA((4,))],
        flops=1 << 20,
        place=HBM,
    )


def pack(queries, grad_out, heads_kv):
    tokens, heads_q, head_size = queries.shape
    array = jax.ShapeDtypeStruct
    return call(
        functools.partial(pack_kernel, heads_kv),
        "pack",
        (queries, grad_out),
        [array((heads_kv, tokens * 8, head_size), BF16)] * 2,
        [pltpu.VMEM((heads_kv, tokens, 16, head_size), BF16), pltpu.SemaphoreType.DMA((heads_kv,))],
        flops=1 << 20,
        place=HBM,
    )


def early(fresh, sources, qh, gh, own, blocks):
    own_k, own_v, bias, _ = own
    heads_kv, tokens, head_size = own_k.shape
    rows = len(sources) * CAP * TILE + tokens
    array = jax.ShapeDtypeStruct
    work = heads_kv * tokens * 8 * rows
    return call(
        functools.partial(early_kernel, fresh, sources, heads_kv, head_size**-0.5),
        "early",
        (own_k, own_v, qh, gh, bias, *blocks),
        [array((heads_kv, rows, head_size), BF16)]
        + [array((heads_kv, rows, tokens * 8), F32)] * 2
        + [array((heads_kv, 8, tokens * 8), F32)],
        [pltpu.VMEM((heads_kv, rows, head_size), BF16), pltpu.VMEM((CAP * TILE * heads_kv, head_size), F32)],
        flops=4 * work * head_size,
        transcendentals=work,
    )


def probs(sources, prompt_k, prompt_v, qh, gh, own, stats, block):
    _, own_v, bias, weight = own
    heads_kv, tokens, head_size = own_v.shape
    rows = tokens * heads_kv
    fresh = tokens + len(sources) * CAP * TILE
    array = jax.ShapeDtypeStruct
    work = heads_kv * tokens * 8 * fresh
    return call(
        functools.partial(probs_kernel, sources, heads_kv, head_size**-0.5),
        "probs",
        (prompt_k, prompt_v, qh, gh, bias, weight, stats, block),
        [array((rows, head_size), BF16)] * 2
        + [
            array((heads_kv, fresh, head_size), BF16),
            array((heads_kv, fresh, tokens * 8), BF16),
            array((heads_kv, fresh - tokens, tokens * 8), BF16),
            array((heads_kv, 8, tokens * 8), F32),
        ],
        [
            pltpu.VMEM((heads_kv, fresh, head_size), BF16),
            pltpu.VMEM((2, tokens, tokens * 8), BF16),
            pltpu.VMEM((2, heads_kv, tokens, head_size), F32),
            pltpu.VMEM((rows, head_size), F32),
        ],
        flops=8 * work * head_size,
        transcendentals=work,
    )


def windows(targets, qh, gh, ds_fresh, p_behind, e, dp, terms):
    heads_kv, early, columns = e.shape
    head_size = qh.shape[2]
    tokens = TD * TILE
    front = CAP * TILE * heads_kv
    behind = early - tokens + p_behind.shape[1]
    count = [sum(target == t for target, _ in targets) for t in (0, 1)]
    array = jax.ShapeDtypeStruct
    return call(
        functools.partial(windows_kernel, targets, heads_kv, head_size**-0.5),
        "windows",
        (qh, gh, ds_fresh, p_behind, e, dp, terms),
        [array((2 * front * n, head_size), BF16) for n in count]
        + [array((heads_kv, early, columns), BF16), array((heads_kv, tokens, columns), BF16)],
        [
            pltpu.VMEM((2, early - tokens, columns), BF16),
            pltpu.VMEM((2, heads_kv, behind, head_size), F32),
            pltpu.VMEM((front, head_size), F32),
        ],
        flops=4 * heads_kv * behind * columns * head_size,
    )


def grads(qh, gh, kh_fresh, kh_early, ds_fresh, ds_early, p_own):
    heads_kv, tokens, _ = p_own.shape
    head_size = kh_fresh.shape[2]
    array = jax.ShapeDtypeStruct
    return call(
        functools.partial(grads_kernel, heads_kv, head_size**-0.5),
        "grads",
        (qh, gh, kh_fresh, kh_early, ds_fresh, ds_early, p_own),
        [
            array((tokens, heads_kv * 8, head_size), BF16),
            array((tokens * heads_kv, head_size), F32),
            array((tokens * heads_kv, head_size), F32),
        ],
        [pltpu.VMEM((tokens * heads_kv, head_size), F32)],
        flops=2 * tokens * 8 * (ds_fresh.size + ds_early.size) // (tokens * 8) * head_size,
    )


def shift_route(distance, size):
    return [(i, i + distance) for i in range(size - distance)]


def back(route):
    return [(j, i) for i, j in route]


def added(*blocks):
    total = blocks[0].astype(F32)
    for block in blocks[1:]:
        total = total + block.astype(F32)
    return total


def after(array, *earlier):
    return lax.optimization_barrier((array, *earlier))[0]


def units(array, start, unit, count):
    return [array[start + i * unit : start + (i + 1) * unit] for i in range(count)]


def prompt_route(stride, size):
    return [(i + j, i + j + stride) for i in range(0, size, 2 * stride) for j in (0, 1)]


def collect(size, unit, rows, where, keys, values, head, held, queries, grad_out):
    even, lower, _ = where
    neighbours = [(i, i ^ 1) for i in range(size)]
    far_route = shift_route(4, size)[1:]
    near_route = shift_route(2, size)
    if size == W + 1:
        keys_far = permuted(keys, [(0, 4)])
        values_far = permuted(values, [(0, 5)])
        values_next = permuted(values, [(0, 1)])
        head, queries = lax.optimization_barrier((head, queries, keys_far))[:2]
        qh, gh = pack(queries, grad_out, keys.shape[0] // queries.shape[0])
        far = permuted(head, far_route)
        six = permuted(head, [(1, 7)])
        held = after(added(held, values_next, values_far, keys_far).astype(BF16), six, far, qh)
        second = permuted(jnp.concatenate([held, head]), near_route)
        crossed = jnp.where(even, jnp.concatenate([head, far]), jnp.concatenate([far, six]))
        crossed = permuted(crossed, neighbours)
        held = jnp.where(lower, held, second[:rows])
        third = permuted(after(jnp.concatenate([held, second[rows:]]), crossed), neighbours)
        early_sources = [(0, rows), (1, 0), (2, 0), (1, unit), (3, 0)]
        return held, third[:rows], third, [(0, rows)], early_sources, (second, crossed, far, six), (qh, gh)
    strides = [2**i for i in range(2, size.bit_length()) if 2**i < size]
    top = strides[-1]
    keys_far = permuted(keys, [(0, top)])
    values_far = permuted(values, [(0, top + 1)])
    values_next = permuted(values, [(0, 1)])
    far = permuted(head, far_route)
    held = added(held, values_next, values_far, keys_far).astype(BF16)
    for stride in reversed(strides[:-1]):
        held = added(held, permuted(held, prompt_route(stride, size))).astype(BF16)
    second = permuted(jnp.concatenate([held, head, far]), near_route)
    held = jnp.where(lower, held, second[:rows])
    near, six = units(second, rows, unit, 2)
    third = permuted(jnp.concatenate([head, near, far, six]), shift_route(1, size))
    other = permuted(held, neighbours)
    fresh_sources = [(0, i * unit) for i in range(4)]
    early_sources = [(0, rows), (1, 0), (0, rows + unit)]
    return held, other, third, fresh_sources, early_sources, (second, far), pack(queries, grad_out, keys.shape[0] // queries.shape[0])


def give_back(size, unit, where, prompt, behind, finish):
    even, lower, _ = where
    neighbours = [(i, i ^ 1) for i in range(size)]
    far_route = back(shift_route(4, size)[1:])
    send, keep = prompt
    rows = keep.shape[0]
    two, four, six = units(behind[1], 0, unit, 3)
    if size == W + 1:
        total = added(keep, permuted(send, neighbours)).astype(BF16)
        finished = finish(total)
        near, first, last = units(permuted(behind[0], neighbours), 0, unit, 3)
        none = jnp.zeros_like(first)
        parts = [permuted(total, [(j, 0), (j + 1, 1)]) for j in reversed(range(2, size, 2))]
        two = permuted(added(two, near).astype(BF16), back(shift_route(2, size)[1:]))
        four = after(added(four, jnp.where(even, last, first)).astype(BF16), finished[1])
        four = permuted(four, far_route)
        six = permuted(added(six, jnp.where(even, none, last)).astype(BF16), [(7, 1)])
        total = added(total, *parts).astype(BF16)
        mine = added(jnp.where(even, first, none), two, four, six)
        return finished, total, permuted(total, [(1, 0)]).astype(F32), mine
    strides = [2**i for i in range(2, size.bit_length()) if 2**i < size]
    top = strides[-1]
    zero, *third = units(permuted(behind[0], back(shift_route(1, size))), 0, unit, 4)
    total = added(keep, permuted(send, neighbours)).astype(BF16)
    two, four, six = (added(x, y).astype(BF16) for x, y in zip((two, four, six), third))
    second = permuted(jnp.concatenate([total, two, six]), back(shift_route(2, size)))
    four = added(four, second[rows + unit :])
    mine = added(zero, second[rows : rows + unit], permuted(four.astype(BF16), far_route))
    total = added(total, jnp.where(lower, second[:rows], jnp.zeros_like(total))).astype(BF16)
    for stride in strides[:-1]:
        total = added(total, permuted(total, back(prompt_route(stride, size)))).astype(BF16)
    keys_far = permuted(total, [(top, 0)])
    values_far = permuted(total, [(top + 1, 0)])
    values_next = permuted(total, [(1, 0)])
    return finish(send), added(total, keys_far), added(values_next, values_far), mine


def per_device(size, queries, keys, values, grad_out, parents, lengths):
    tokens, heads_kv, head_size = keys.shape
    rows = tokens * heads_kv
    one = CAP * TILE * heads_kv
    unit = 2 * one
    window = min(W, size - 2)
    device = lax.axis_index("node")
    keys = keys.reshape(rows, head_size)
    values = values.reshape(rows, head_size)

    if size == W + 1:
        order = [(1, 3), (2, 2), (3, 1), (4, 4), (5, 5), (6, 6)]
        targets = [(k % 2, k // 2 * unit) for k in range(window)]
    else:
        order = [(k, k) for k in (1, 3, 5, 7, 2, 4, 6)]
        targets = [(0, i * unit) for i in range(4)] + [(1, i * unit) for i in range(3)]
    head, held, *own = load(order, keys, values, parents, lengths, tokens)
    head, *where = lax.optimization_barrier((head, lax.rem(device, 2) == 0, lax.rem(device, 4) < 2, device == 0))
    even, _, root = where
    held, other, block, fresh_sources, early_sources, blocks, (qh, gh) = collect(
        size, unit, rows, where, keys, values, head, held, queries, grad_out
    )
    kh_early, e, dp, stats = early(len(fresh_sources), early_sources, qh, gh, own, blocks)
    prompt_k, prompt_v = jnp.where(even, held, other), jnp.where(even, other, held)
    *prompt, kh, ds, p_behind, terms = probs(fresh_sources, prompt_k, prompt_v, qh, gh, own, stats, block)
    *behind, ds_early, p_own = windows(targets, qh, gh, ds, p_behind, e, dp, terms)

    def finish(earlier):
        return grads(qh, gh, kh, kh_early, ds, ds_early, after(p_own, earlier))

    (grad_queries, dk, dv), prompt_k, prompt_v, mine = give_back(size, unit, where, prompt, behind, finish)
    own = []
    for side, local, prompt in ((0, dk, prompt_k), (1, dv, prompt_v)):
        whole = local + jnp.where(root, prompt.astype(F32), 0.0)
        own.append(whole.at[:one].add(mine[side * one : (side + 1) * one]).reshape(tokens, heads_kv, head_size))
    return grad_queries, own[0], own[1]


def solution(mesh):
    by_token = P(("leaf", "node"), "tensor", None)
    return jax.shard_map(
        functools.partial(per_device, mesh.shape["node"]),
        mesh=mesh,
        in_specs=(by_token, by_token, by_token, by_token, P("leaf"), P("leaf")),
        out_specs=(by_token, by_token, by_token),
        check_vma=False,
    )
```

```python
import functools
import math

import jax
import jax.numpy as jnp
from jax import lax
from jax.experimental import pallas as pl
from jax.experimental.pallas import tpu as pltpu
from jax.sharding import PartitionSpec as P

TILE = 16
TD = 8
CAP = 2
W = 7
CHUNK = 32
MASKED = -1e30
BF16 = jnp.bfloat16
F32 = jnp.float32


def permuted(block, route):
    return lax.ppermute(block, "node", route)


def column_limits(device, window, parents, lengths):
    cursor = parents[device * TD]
    need = [jnp.int32(0)] * (window + 1)
    for _ in range(W):
        owner = jnp.where(cursor < 0, -1, lax.div(jnp.maximum(cursor, 0), TD))
        distance = device - owner
        active = (owner >= 1) & (distance >= 1) & (distance <= W)
        depth = lax.rem(jnp.maximum(cursor, 0), TD) + 1
        for k in range(1, window + 1):
            need[k] = jnp.where(active & (distance == k), depth, need[k])
        cursor = jnp.where(active, parents[jnp.maximum(owner, 0) * TD], cursor)
    prompt = [jnp.where(device >= 1, lengths[t], 0) for t in range(TD)]
    behind = []
    for k in range(1, window + 1):
        owner = device - k
        seen = [(owner >= 1) & (c < need[k]) for c in range(CAP)]
        behind.append([jnp.where(seen[c], lengths[jnp.maximum(owner, 0) * TD + c], 0) for c in range(CAP)])
    return prompt, behind, [lengths[device * TD + t] for t in range(TD)]


def split_heads(block, heads_ref, start, count, heads_kv, wide):
    wide[: count * heads_kv] = block.astype(F32)
    for h in range(heads_kv):
        heads_ref[h, start : start + count] = wide[pl.ds(h, count, stride=heads_kv), :].astype(BF16)


def join_heads(blocks, count, heads_kv, wide):
    for h in range(heads_kv):
        wide[pl.ds(h, count, stride=heads_kv), :] = blocks[h]
    return wide[: count * heads_kv]


def load_kernel(order, heads_kv, *refs):
    sources, outs, scratch = refs[:4], refs[4:10], refs[10:]
    head, held, own_k, own_v, bias, weight = outs
    parents, lengths, keys, values, wide, arrived = scratch
    copies = [pltpu.make_async_copy(a, b, arrived.at[i]) for i, (a, b) in enumerate(zip(sources, scratch))]
    for copy in copies:
        copy.start()
    tokens = TD * TILE
    front = CAP * TILE * heads_kv
    device = lax.axis_index("node")
    for copy in copies:
        copy.wait()
    head[:front] = keys[:front]
    head[front:] = values[:front]
    held[...] = jnp.where(device == 0, keys[...], jnp.zeros_like(keys))
    split_heads(keys[...], own_k, 0, tokens, heads_kv, wide)
    split_heads(values[...], own_v, 0, tokens, heads_kv, wide)
    place = lax.broadcasted_iota(jnp.int32, (TILE, 128), 0)
    prompt, behind, own = column_limits(device, len(order), parents, lengths)
    even = lax.rem(device, 2) == 0
    limits = prompt
    for on_even, on_odd in order:
        limits = limits + [jnp.where(even, x, y) for x, y in zip(behind[on_even - 1], behind[on_odd - 1])]
    for t, limit in enumerate(limits + own):
        bias[t * TILE : (t + 1) * TILE] = jnp.where(place < limit, 0.0, MASKED)
    lane_place = lax.broadcasted_iota(jnp.int32, (8, 128), 1) // 8
    for t in range(TD):
        weight[:, t * 128 : (t + 1) * 128] = jnp.where(lane_place < lengths[device * TD + t], 1.0, 0.0)


def pack_kernel(heads_kv, q_ref, g_ref, qh, gh, blocks, arrived):
    tokens = TD * TILE
    copies = []
    for pair in range(heads_kv // 2):
        for ref, out in ((q_ref, qh), (g_ref, gh)):
            i = len(copies)
            copy = pltpu.make_async_copy(ref.at[:, pair * 16 : (pair + 1) * 16], blocks.at[i], arrived.at[i])
            copy.start()
            copies.append((copy, out, pair))
    for i, (copy, out, pair) in enumerate(copies):
        copy.wait()
        both = blocks[i].astype(F32)
        for part in range(2):
            out[2 * pair + part] = both[:, part * 8 : (part + 1) * 8].reshape(tokens * 8, 128).astype(BF16)


def causal_bias(columns):
    column_token = lax.broadcasted_iota(jnp.int32, (CHUNK, columns), 1) // 8
    return jnp.where(lax.broadcasted_iota(jnp.int32, (CHUNK, columns), 0) <= column_token, 0.0, MASKED)


def outer_product(rows, columns):
    return lax.dot_general(rows, columns, (((1,), (1,)), ((), ())), preferred_element_type=F32)


def early_kernel(fresh, sources, heads_kv, scale, *refs):
    own_k, own_v, qh, gh, bias = refs[:5]
    blocks, (kh, e_ref, dp_ref, stats, vh, wide) = refs[5:-6], refs[-6:]
    tokens = TD * TILE
    front = CAP * TILE
    behind = len(sources) * front
    start = tokens + fresh * front
    columns = CHUNK * 8
    for side, heads_ref, own in ((0, kh, own_k), (1, vh, own_v)):
        for k, (source, at) in enumerate(sources):
            at += side * front * heads_kv
            split_heads(blocks[source][at : at + front * heads_kv], heads_ref, k * front, front, heads_kv, wide)
        heads_ref[:, behind:] = own[...]
    causal = causal_bias(columns)
    for head in range(heads_kv):
        for c in range(tokens // CHUNK):
            rows = behind + (c + 1) * CHUNK
            span = slice(c * columns, (c + 1) * columns)
            s = outer_product(kh[head, :rows], qh[head, span])
            dp = outer_product(vh[head, :rows], gh[head, span])
            s = s + jnp.concatenate([bias[start : start + rows]] * (columns // 128), axis=1)
            s = jnp.concatenate([s[: rows - CHUNK], s[rows - CHUNK :] + causal], axis=0)
            top = jnp.max(s, axis=0, keepdims=True)
            e = jnp.exp2((s - top) * (scale * math.log2(math.e)))
            e_ref[head, :rows, span] = e
            dp_ref[head, :rows, span] = dp
            stats[head, 0:1, span] = top
            stats[head, 1:2, span] = jnp.sum(e, axis=0, keepdims=True)
            stats[head, 2:3, span] = jnp.sum(e * dp, axis=0, keepdims=True)


def probs_kernel(sources, heads_kv, scale, *refs):
    prompt_k, prompt_v, qh, gh, bias, weight_ref, stats, block_ref = refs[:8]
    send_ref, keep_ref, kh, ds_ref, p_behind, terms, vh, p_ref, grads, wide = refs[8:]
    tokens = TD * TILE
    front = CAP * TILE
    columns = CHUNK * 8
    rate = scale * math.log2(math.e)
    device = lax.axis_index("node")

    for side, heads_ref, prompt in ((0, kh, prompt_k), (1, vh, prompt_v)):
        split_heads(prompt[...], heads_ref, 0, tokens, heads_kv, wide)
        for k, (_, at) in enumerate(sources):
            at += side * front * heads_kv
            split_heads(block_ref[at : at + front * heads_kv], heads_ref, tokens + k * front, front, heads_kv, wide)

    for head in range(heads_kv):
        for c in range(tokens // CHUNK):
            span = slice(c * columns, (c + 1) * columns)
            s = outer_product(kh[head], qh[head, span])
            dp = outer_product(vh[head], gh[head, span])
            s = s + jnp.concatenate([bias[: s.shape[0]]] * (columns // 128), axis=1)
            top_early = stats[head, 0:1, span]
            top = jnp.maximum(jnp.max(s, axis=0, keepdims=True), top_early)
            e = jnp.exp2((s - top) * rate)
            shrink = jnp.exp2((top_early - top) * rate)
            total = jnp.sum(e, axis=0, keepdims=True) + shrink * stats[head, 1:2, span]
            weight = weight_ref[:1, span] / total
            weight_early = weight * shrink
            p = e * weight
            delta = jnp.sum(p * dp, axis=0, keepdims=True) + weight_early * stats[head, 2:3, span]
            ds_ref[head, :, span] = (p * (dp - delta)).astype(BF16)
            p_ref[head % 2, :, span] = p[:tokens].astype(BF16)
            p_behind[head, :, span] = p[tokens:].astype(BF16)
            terms[head, 0:1, span] = weight_early
            terms[head, 1:2, span] = delta
        grads[0, head] = scale * jnp.dot(ds_ref[head, :tokens], qh[head], preferred_element_type=F32)
        grads[1, head] = jnp.dot(p_ref[head % 2], gh[head], preferred_element_type=F32)

    even = lax.rem(device, 2) == 0
    for side in range(2):
        dprompt = join_heads([grads[side, h] for h in range(heads_kv)], tokens, heads_kv, wide).astype(BF16)
        kept = even if side == 0 else jnp.logical_not(even)

        @pl.when(kept)
        def _():
            keep_ref[...] = dprompt

        @pl.when(jnp.logical_not(kept))
        def _():
            send_ref[...] = dprompt


def windows_kernel(targets, heads_kv, scale, *refs):
    qh, gh, ds_fresh, p_behind, e_ref, dp_ref, terms, send_ref, keep_ref, ds_ref, p_own, p_ref, grads, wide = refs
    front = CAP * TILE
    tokens = TD * TILE
    early = ds_ref.shape[1] - tokens
    columns = CHUNK * 8
    for head in range(heads_kv):
        for c in range(tokens // CHUNK):
            rows = early + (c + 1) * CHUNK
            span = slice(c * columns, (c + 1) * columns)
            p = e_ref[head, :rows, span] * terms[head, 0:1, span]
            ds_ref[head, :rows, span] = (p * (dp_ref[head, :rows, span] - terms[head, 1:2, span])).astype(BF16)
            p_ref[head % 2, :, span] = p[:early].astype(BF16)
            p_own[head, : rows - early, span] = p[early:].astype(BF16)
        ds = jnp.concatenate([ds_fresh[head, tokens:], ds_ref[head, :early]], axis=0)
        grads[0, head] = scale * jnp.dot(ds, qh[head], preferred_element_type=F32)
        p = jnp.concatenate([p_behind[head], p_ref[head % 2]], axis=0)
        grads[1, head] = jnp.dot(p, gh[head], preferred_element_type=F32)
    for side in range(2):
        for k, (target, start) in enumerate(targets):
            span = slice(k * front, (k + 1) * front)
            block = join_heads([grads[side, h, span] for h in range(heads_kv)], front, heads_kv, wide).astype(BF16)
            start += side * front * heads_kv
            (send_ref, keep_ref)[target][start : start + front * heads_kv] = block


def grads_kernel(heads_kv, scale, *refs):
    qh, gh, kh_fresh, kh_early, ds_fresh, ds_early, p_own, dq_ref, dk_ref, dv_ref, wide = refs
    tokens = TD * TILE
    kh = [jnp.concatenate([kh_fresh[h], kh_early[h]], axis=0) for h in range(heads_kv)]
    before = kh[0].shape[0] - tokens
    columns = CHUNK * 8
    dk = []
    dv = []
    for pair in range(heads_kv // 2):
        for c in range(tokens // CHUNK):
            rows = before + (c + 1) * CHUNK
            span = slice(c * columns, (c + 1) * columns)
            parts = []
            for head in (2 * pair, 2 * pair + 1):
                fresh = ds_fresh.shape[1]
                ds = jnp.concatenate([ds_fresh[head, :, span], ds_early[head, : rows - fresh, span]], axis=0)
                dq = lax.dot_general(kh[head][:rows], ds, (((0,), (0,)), ((), ())), preferred_element_type=F32)
                parts.append((scale * dq.T).reshape(CHUNK, 8, 128))
            dq_ref[c * CHUNK : (c + 1) * CHUNK, pair * 16 : (pair + 1) * 16] = jnp.concatenate(parts, axis=1).astype(BF16)
        for head in (2 * pair, 2 * pair + 1):
            for source, factor, out in ((ds_early.at[head, before - fresh :], qh, dk), (p_own.at[head], gh, dv)):
                pieces = []
                for c in range(tokens // CHUNK):
                    start = c * columns
                    pieces.append(
                        jnp.dot(
                            source[c * CHUNK : (c + 1) * CHUNK, start:], factor[head, start:], preferred_element_type=F32
                        )
                    )
                out.append(jnp.concatenate(pieces, axis=0))
    dk_ref[...] = scale * join_heads(dk, tokens, heads_kv, wide)
    dv_ref[...] = join_heads(dv, tokens, heads_kv, wide)


VMEM = pl.BlockSpec(memory_space=pltpu.VMEM)


HBM = pl.BlockSpec(memory_space=pltpu.HBM)


def call(kernel, name, operands, outputs, scratch, flops, transcendentals=0, place=VMEM):
    sizes = [a.size * a.dtype.itemsize for a in (*operands, *outputs)]
    if place is HBM:
        operands = [pltpu.with_memory_space_constraint(a, pltpu.HBM) for a in operands]
    return pl.pallas_call(
        kernel,
        in_specs=[place] * len(operands),
        out_specs=[VMEM] * len(outputs),
        out_shape=outputs,
        scratch_shapes=scratch,
        compiler_params=pltpu.CompilerParams(vmem_limit_bytes=16 * 1024 * 1024),
        cost_estimate=pl.CostEstimate(flops=flops, bytes_accessed=sum(sizes), transcendentals=transcendentals),
        name=name,
    )(*operands)


def load(order, keys, values, parents, lengths, tokens):
    rows, head_size = keys.shape
    heads_kv = rows // tokens
    array = jax.ShapeDtypeStruct
    return call(
        functools.partial(load_kernel, order, heads_kv),
        "load",
        (parents, lengths, keys, values),
        [array((2 * CAP * TILE * heads_kv, head_size), BF16), array((rows, head_size), BF16)]
        + [array((heads_kv, tokens, head_size), BF16)] * 2
        + [array((2 * tokens + len(order) * CAP * TILE, 128), F32), array((8, tokens * 8), F32)],
        [pltpu.SMEM(parents.shape, jnp.int32), pltpu.SMEM(lengths.shape, jnp.int32)]
        + [pltpu.VMEM((rows, head_size), BF16)] * 2
        + [pltpu.VMEM((rows, head_size), F32), pltpu.SemaphoreType.DMA((4,))],
        flops=1 << 20,
        place=HBM,
    )


def pack(queries, grad_out, heads_kv):
    tokens, heads_q, head_size = queries.shape
    array = jax.ShapeDtypeStruct
    return call(
        functools.partial(pack_kernel, heads_kv),
        "pack",
        (queries, grad_out),
        [array((heads_kv, tokens * 8, head_size), BF16)] * 2,
        [pltpu.VMEM((heads_kv, tokens, 16, head_size), BF16), pltpu.SemaphoreType.DMA((heads_kv,))],
        flops=1 << 20,
        place=HBM,
    )


def early(fresh, sources, qh, gh, own, blocks):
    own_k, own_v, bias, _ = own
    heads_kv, tokens, head_size = own_k.shape
    rows = len(sources) * CAP * TILE + tokens
    array = jax.ShapeDtypeStruct
    work = heads_kv * tokens * 8 * rows
    return call(
        functools.partial(early_kernel, fresh, sources, heads_kv, head_size**-0.5),
        "early",
        (own_k, own_v, qh, gh, bias, *blocks),
        [array((heads_kv, rows, head_size), BF16)]
        + [array((heads_kv, rows, tokens * 8), F32)] * 2
        + [array((heads_kv, 8, tokens * 8), F32)],
        [pltpu.VMEM((heads_kv, rows, head_size), BF16), pltpu.VMEM((CAP * TILE * heads_kv, head_size), F32)],
        flops=4 * work * head_size,
        transcendentals=work,
    )


def probs(sources, prompt_k, prompt_v, qh, gh, own, stats, block):
    _, own_v, bias, weight = own
    heads_kv, tokens, head_size = own_v.shape
    rows = tokens * heads_kv
    fresh = tokens + len(sources) * CAP * TILE
    array = jax.ShapeDtypeStruct
    work = heads_kv * tokens * 8 * fresh
    return call(
        functools.partial(probs_kernel, sources, heads_kv, head_size**-0.5),
        "probs",
        (prompt_k, prompt_v, qh, gh, bias, weight, stats, block),
        [array((rows, head_size), BF16)] * 2
        + [
            array((heads_kv, fresh, head_size), BF16),
            array((heads_kv, fresh, tokens * 8), BF16),
            array((heads_kv, fresh - tokens, tokens * 8), BF16),
            array((heads_kv, 8, tokens * 8), F32),
        ],
        [
            pltpu.VMEM((heads_kv, fresh, head_size), BF16),
            pltpu.VMEM((2, tokens, tokens * 8), BF16),
            pltpu.VMEM((2, heads_kv, tokens, head_size), F32),
            pltpu.VMEM((rows, head_size), F32),
        ],
        flops=8 * work * head_size,
        transcendentals=work,
    )


def windows(targets, qh, gh, ds_fresh, p_behind, e, dp, terms):
    heads_kv, early, columns = e.shape
    head_size = qh.shape[2]
    tokens = TD * TILE
    front = CAP * TILE * heads_kv
    behind = early - tokens + p_behind.shape[1]
    count = [sum(target == t for target, _ in targets) for t in (0, 1)]
    array = jax.ShapeDtypeStruct
    return call(
        functools.partial(windows_kernel, targets, heads_kv, head_size**-0.5),
        "windows",
        (qh, gh, ds_fresh, p_behind, e, dp, terms),
        [array((2 * front * n, head_size), BF16) for n in count]
        + [array((heads_kv, early, columns), BF16), array((heads_kv, tokens, columns), BF16)],
        [
            pltpu.VMEM((2, early - tokens, columns), BF16),
            pltpu.VMEM((2, heads_kv, behind, head_size), F32),
            pltpu.VMEM((front, head_size), F32),
        ],
        flops=4 * heads_kv * behind * columns * head_size,
    )


def grads(qh, gh, kh_fresh, kh_early, ds_fresh, ds_early, p_own):
    heads_kv, tokens, _ = p_own.shape
    head_size = kh_fresh.shape[2]
    array = jax.ShapeDtypeStruct
    return call(
        functools.partial(grads_kernel, heads_kv, head_size**-0.5),
        "grads",
        (qh, gh, kh_fresh, kh_early, ds_fresh, ds_early, p_own),
        [
            array((tokens, heads_kv * 8, head_size), BF16),
            array((tokens * heads_kv, head_size), F32),
            array((tokens * heads_kv, head_size), F32),
        ],
        [pltpu.VMEM((tokens * heads_kv, head_size), F32)],
        flops=2 * tokens * 8 * (ds_fresh.size + ds_early.size) // (tokens * 8) * head_size,
    )


def shift_route(distance, size):
    return [(i, i + distance) for i in range(size - distance)]


def back(route):
    return [(j, i) for i, j in route]


def added(*blocks):
    total = blocks[0].astype(F32)
    for block in blocks[1:]:
        total = total + block.astype(F32)
    return total


def after(array, *earlier):
    return lax.optimization_barrier((array, *earlier))[0]


def units(array, start, unit, count):
    return [array[start + i * unit : start + (i + 1) * unit] for i in range(count)]


def prompt_route(stride, size):
    return [(i + j, i + j + stride) for i in range(0, size, 2 * stride) for j in (0, 1)]


def collect(size, unit, rows, where, keys, values, head, held, queries, grad_out):
    even, lower, _ = where
    neighbours = [(i, i ^ 1) for i in range(size)]
    far_route = shift_route(4, size)[1:]
    near_route = shift_route(2, size)
    if size == W + 1:
        keys_far = permuted(keys, [(0, 4)])
        values_far = permuted(values, [(0, 5)])
        values_next = permuted(values, [(0, 1)])
        head, queries = lax.optimization_barrier((head, queries, keys_far))[:2]
        qh, gh = pack(queries, grad_out, keys.shape[0] // queries.shape[0])
        far = permuted(head, far_route)
        six = permuted(head, [(1, 7)])
        held = after(added(held, values_next, values_far, keys_far).astype(BF16), six, far, qh)
        second = permuted(jnp.concatenate([held, head]), near_route)
        crossed = jnp.where(even, jnp.concatenate([head, far]), jnp.concatenate([far, six]))
        crossed = permuted(crossed, neighbours)
        held = jnp.where(lower, held, second[:rows])
        third = permuted(after(jnp.concatenate([held, second[rows:]]), crossed), neighbours)
        early_sources = [(0, rows), (1, 0), (2, 0), (1, unit), (3, 0)]
        return held, third[:rows], third, [(0, rows)], early_sources, (second, crossed, far, six), (qh, gh)
    strides = [2**i for i in range(2, size.bit_length()) if 2**i < size]
    top = strides[-1]
    keys_far = permuted(keys, [(0, top)])
    values_far = permuted(values, [(0, top + 1)])
    values_next = permuted(values, [(0, 1)])
    far = permuted(head, far_route)
    held = added(held, values_next, values_far, keys_far).astype(BF16)
    for stride in reversed(strides[:-1]):
        held = added(held, permuted(held, prompt_route(stride, size))).astype(BF16)
    second = permuted(jnp.concatenate([held, head, far]), near_route)
    held = jnp.where(lower, held, second[:rows])
    near, six = units(second, rows, unit, 2)
    third = permuted(jnp.concatenate([head, near, far, six]), shift_route(1, size))
    other = permuted(held, neighbours)
    fresh_sources = [(0, i * unit) for i in range(4)]
    early_sources = [(0, rows), (1, 0), (0, rows + unit)]
    return held, other, third, fresh_sources, early_sources, (second, far), pack(queries, grad_out, keys.shape[0] // queries.shape[0])


def give_back(size, unit, where, prompt, behind, finish):
    even, lower, _ = where
    neighbours = [(i, i ^ 1) for i in range(size)]
    far_route = back(shift_route(4, size)[1:])
    send, keep = prompt
    rows = keep.shape[0]
    two, four, six = units(behind[1], 0, unit, 3)
    if size == W + 1:
        total = added(keep, permuted(send, neighbours)).astype(BF16)
        finished = finish(total)
        near, first, last = units(permuted(behind[0], neighbours), 0, unit, 3)
        none = jnp.zeros_like(first)
        parts = [permuted(total, [(j, 0), (j + 1, 1)]) for j in (4, 2)]
        keys_last, values_last = permuted(total, [(6, 0)]), permuted(total, [(7, 0)])
        two = permuted(added(two, near).astype(BF16), back(shift_route(2, size)[1:]))
        four = after(added(four, jnp.where(even, last, first)).astype(BF16), finished[1])
        four = permuted(four, far_route)
        six = permuted(added(six, jnp.where(even, none, last)).astype(BF16), [(7, 1)])
        total = added(total, *parts).astype(BF16)
        mine = added(jnp.where(even, first, none), two, four, six)
        values_next = permuted(total, [(1, 0)])
        return finished, added(total, keys_last), added(values_next, values_last), mine
    strides = [2**i for i in range(2, size.bit_length()) if 2**i < size]
    top = strides[-1]
    zero, *third = units(permuted(behind[0], back(shift_route(1, size))), 0, unit, 4)
    total = added(keep, permuted(send, neighbours)).astype(BF16)
    two, four, six = (added(x, y).astype(BF16) for x, y in zip((two, four, six), third))
    second = permuted(jnp.concatenate([total, two, six]), back(shift_route(2, size)))
    four = added(four, second[rows + unit :])
    mine = added(zero, second[rows : rows + unit], permuted(four.astype(BF16), far_route))
    total = added(total, jnp.where(lower, second[:rows], jnp.zeros_like(total))).astype(BF16)
    for stride in strides[:-1]:
        total = added(total, permuted(total, back(prompt_route(stride, size)))).astype(BF16)
    keys_far = permuted(total, [(top, 0)])
    values_far = permuted(total, [(top + 1, 0)])
    values_next = permuted(total, [(1, 0)])
    return finish(send), added(total, keys_far), added(values_next, values_far), mine


def per_device(size, queries, keys, values, grad_out, parents, lengths):
    tokens, heads_kv, head_size = keys.shape
    rows = tokens * heads_kv
    one = CAP * TILE * heads_kv
    unit = 2 * one
    window = min(W, size - 2)
    device = lax.axis_index("node")
    keys = keys.reshape(rows, head_size)
    values = values.reshape(rows, head_size)

    if size == W + 1:
        order = [(1, 3), (2, 2), (3, 1), (4, 4), (5, 5), (6, 6)]
        targets = [(k % 2, k // 2 * unit) for k in range(window)]
    else:
        order = [(k, k) for k in (1, 3, 5, 7, 2, 4, 6)]
        targets = [(0, i * unit) for i in range(4)] + [(1, i * unit) for i in range(3)]
    head, held, *own = load(order, keys, values, parents, lengths, tokens)
    head, *where = lax.optimization_barrier((head, lax.rem(device, 2) == 0, lax.rem(device, 4) < 2, device == 0))
    even, _, root = where
    held, other, block, fresh_sources, early_sources, blocks, (qh, gh) = collect(
        size, unit, rows, where, keys, values, head, held, queries, grad_out
    )
    kh_early, e, dp, stats = early(len(fresh_sources), early_sources, qh, gh, own, blocks)
    prompt_k, prompt_v = jnp.where(even, held, other), jnp.where(even, other, held)
    *prompt, kh, ds, p_behind, terms = probs(fresh_sources, prompt_k, prompt_v, qh, gh, own, stats, block)
    *behind, ds_early, p_own = windows(targets, qh, gh, ds, p_behind, e, dp, terms)

    def finish(earlier):
        return grads(qh, gh, kh, kh_early, ds, ds_early, after(p_own, earlier))

    (grad_queries, dk, dv), prompt_k, prompt_v, mine = give_back(size, unit, where, prompt, behind, finish)
    own = []
    for side, local, prompt in ((0, dk, prompt_k), (1, dv, prompt_v)):
        whole = local + jnp.where(root, prompt.astype(F32), 0.0)
        own.append(whole.at[:one].add(mine[side * one : (side + 1) * one]).reshape(tokens, heads_kv, head_size))
    return grad_queries, own[0], own[1]


def solution(mesh):
    by_token = P(("leaf", "node"), "tensor", None)
    return jax.shard_map(
        functools.partial(per_device, mesh.shape["node"]),
        mesh=mesh,
        in_specs=(by_token, by_token, by_token, by_token, P("leaf"), P("leaf")),
        out_specs=(by_token, by_token, by_token),
        check_vma=False,
    )
```

```python
import functools
import math

import jax
import jax.numpy as jnp
from jax import lax
from jax.experimental import pallas as pl
from jax.experimental.pallas import tpu as pltpu
from jax.sharding import PartitionSpec as P

TILE = 16
TD = 8
CAP = 2
W = 7
CHUNK = 32
MASKED = -1e30
BF16 = jnp.bfloat16
F32 = jnp.float32


def permuted(block, route):
    return lax.ppermute(block, "node", route)


def column_limits(device, window, parents, lengths):
    cursor = parents[device * TD]
    need = [jnp.int32(0)] * (window + 1)
    for _ in range(W):
        owner = jnp.where(cursor < 0, -1, lax.div(jnp.maximum(cursor, 0), TD))
        distance = device - owner
        active = (owner >= 1) & (distance >= 1) & (distance <= W)
        depth = lax.rem(jnp.maximum(cursor, 0), TD) + 1
        for k in range(1, window + 1):
            need[k] = jnp.where(active & (distance == k), depth, need[k])
        cursor = jnp.where(active, parents[jnp.maximum(owner, 0) * TD], cursor)
    prompt = [jnp.where(device >= 1, lengths[t], 0) for t in range(TD)]
    behind = []
    for k in range(1, window + 1):
        owner = device - k
        seen = [(owner >= 1) & (c < need[k]) for c in range(CAP)]
        behind.append([jnp.where(seen[c], lengths[jnp.maximum(owner, 0) * TD + c], 0) for c in range(CAP)])
    return prompt, behind, [lengths[device * TD + t] for t in range(TD)]


def split_heads(block, heads_ref, start, count, heads_kv, wide):
    wide[: count * heads_kv] = block.astype(F32)
    for h in range(heads_kv):
        heads_ref[h, start : start + count] = wide[pl.ds(h, count, stride=heads_kv), :].astype(BF16)


def join_heads(blocks, count, heads_kv, wide):
    for h in range(heads_kv):
        wide[pl.ds(h, count, stride=heads_kv), :] = blocks[h]
    return wide[: count * heads_kv]


def load_kernel(order, heads_kv, *refs):
    sources, outs, scratch = refs[:4], refs[4:10], refs[10:]
    head, held, own_k, own_v, bias, weight = outs
    parents, lengths, keys, values, wide, arrived = scratch
    copies = [pltpu.make_async_copy(a, b, arrived.at[i]) for i, (a, b) in enumerate(zip(sources, scratch))]
    for copy in copies:
        copy.start()
    tokens = TD * TILE
    front = CAP * TILE * heads_kv
    device = lax.axis_index("node")
    for copy in copies:
        copy.wait()
    head[:front] = keys[:front]
    head[front:] = values[:front]
    held[...] = jnp.where(device == 0, keys[...], jnp.zeros_like(keys))
    split_heads(keys[...], own_k, 0, tokens, heads_kv, wide)
    split_heads(values[...], own_v, 0, tokens, heads_kv, wide)
    place = lax.broadcasted_iota(jnp.int32, (TILE, 128), 0)
    prompt, behind, own = column_limits(device, len(order), parents, lengths)
    even = lax.rem(device, 2) == 0
    limits = prompt
    for on_even, on_odd in order:
        limits = limits + [jnp.where(even, x, y) for x, y in zip(behind[on_even - 1], behind[on_odd - 1])]
    for t, limit in enumerate(limits + own):
        bias[t * TILE : (t + 1) * TILE] = jnp.where(place < limit, 0.0, MASKED)
    lane_place = lax.broadcasted_iota(jnp.int32, (8, 128), 1) // 8
    for t in range(TD):
        weight[:, t * 128 : (t + 1) * 128] = jnp.where(lane_place < lengths[device * TD + t], 1.0, 0.0)


def pack_kernel(heads_kv, q_ref, g_ref, qh, gh, blocks, arrived):
    tokens = TD * TILE
    copies = []
    for pair in range(heads_kv // 2):
        for ref, out in ((q_ref, qh), (g_ref, gh)):
            i = len(copies)
            copy = pltpu.make_async_copy(ref.at[:, pair * 16 : (pair + 1) * 16], blocks.at[i], arrived.at[i])
            copy.start()
            copies.append((copy, out, pair))
    for i, (copy, out, pair) in enumerate(copies):
        copy.wait()
        both = blocks[i].astype(F32)
        for part in range(2):
            out[2 * pair + part] = both[:, part * 8 : (part + 1) * 8].reshape(tokens * 8, 128).astype(BF16)


def causal_bias(columns):
    column_token = lax.broadcasted_iota(jnp.int32, (CHUNK, columns), 1) // 8
    return jnp.where(lax.broadcasted_iota(jnp.int32, (CHUNK, columns), 0) <= column_token, 0.0, MASKED)


def outer_product(rows, columns):
    return lax.dot_general(rows, columns, (((1,), (1,)), ((), ())), preferred_element_type=F32)


def early_kernel(fresh, sources, heads_kv, scale, *refs):
    own_k, own_v, qh, gh, bias = refs[:5]
    blocks, (kh, e_ref, dp_ref, stats, vh, wide) = refs[5:-6], refs[-6:]
    tokens = TD * TILE
    front = CAP * TILE
    behind = len(sources) * front
    start = tokens + fresh * front
    columns = CHUNK * 8
    for side, heads_ref, own in ((0, kh, own_k), (1, vh, own_v)):
        for k, (source, at) in enumerate(sources):
            at += side * front * heads_kv
            split_heads(blocks[source][at : at + front * heads_kv], heads_ref, k * front, front, heads_kv, wide)
        heads_ref[:, behind:] = own[...]
    causal = causal_bias(columns)
    for head in range(heads_kv):
        for c in range(tokens // CHUNK):
            rows = behind + (c + 1) * CHUNK
            span = slice(c * columns, (c + 1) * columns)
            s = outer_product(kh[head, :rows], qh[head, span])
            dp = outer_product(vh[head, :rows], gh[head, span])
            s = s + jnp.concatenate([bias[start : start + rows]] * (columns // 128), axis=1)
            s = jnp.concatenate([s[: rows - CHUNK], s[rows - CHUNK :] + causal], axis=0)
            top = jnp.max(s, axis=0, keepdims=True)
            e = jnp.exp2((s - top) * (scale * math.log2(math.e)))
            e_ref[head, :rows, span] = e
            dp_ref[head, :rows, span] = dp
            stats[head, 0:1, span] = top
            stats[head, 1:2, span] = jnp.sum(e, axis=0, keepdims=True)
            stats[head, 2:3, span] = jnp.sum(e * dp, axis=0, keepdims=True)


def probs_kernel(sources, heads_kv, scale, *refs):
    prompt_k, prompt_v, qh, gh, bias, weight_ref, stats, block_ref = refs[:8]
    send_ref, keep_ref, kh, ds_ref, p_behind, terms, vh, p_ref, grads, wide = refs[8:]
    tokens = TD * TILE
    front = CAP * TILE
    columns = CHUNK * 8
    rate = scale * math.log2(math.e)
    device = lax.axis_index("node")

    for side, heads_ref, prompt in ((0, kh, prompt_k), (1, vh, prompt_v)):
        split_heads(prompt[...], heads_ref, 0, tokens, heads_kv, wide)
        for k, (_, at) in enumerate(sources):
            at += side * front * heads_kv
            split_heads(block_ref[at : at + front * heads_kv], heads_ref, tokens + k * front, front, heads_kv, wide)

    for head in range(heads_kv):
        for c in range(tokens // CHUNK):
            span = slice(c * columns, (c + 1) * columns)
            s = outer_product(kh[head], qh[head, span])
            dp = outer_product(vh[head], gh[head, span])
            s = s + jnp.concatenate([bias[: s.shape[0]]] * (columns // 128), axis=1)
            top_early = stats[head, 0:1, span]
            top = jnp.maximum(jnp.max(s, axis=0, keepdims=True), top_early)
            e = jnp.exp2((s - top) * rate)
            shrink = jnp.exp2((top_early - top) * rate)
            total = jnp.sum(e, axis=0, keepdims=True) + shrink * stats[head, 1:2, span]
            weight = weight_ref[:1, span] / total
            weight_early = weight * shrink
            p = e * weight
            delta = jnp.sum(p * dp, axis=0, keepdims=True) + weight_early * stats[head, 2:3, span]
            ds_ref[head, :, span] = (p * (dp - delta)).astype(BF16)
            p_ref[head % 2, :, span] = p[:tokens].astype(BF16)
            p_behind[head, :, span] = p[tokens:].astype(BF16)
            terms[head, 0:1, span] = weight_early
            terms[head, 1:2, span] = delta
        grads[0, head] = scale * jnp.dot(ds_ref[head, :tokens], qh[head], preferred_element_type=F32)
        grads[1, head] = jnp.dot(p_ref[head % 2], gh[head], preferred_element_type=F32)

    even = lax.rem(device, 2) == 0
    for side in range(2):
        dprompt = join_heads([grads[side, h] for h in range(heads_kv)], tokens, heads_kv, wide).astype(BF16)
        kept = even if side == 0 else jnp.logical_not(even)

        @pl.when(kept)
        def _():
            keep_ref[...] = dprompt

        @pl.when(jnp.logical_not(kept))
        def _():
            send_ref[...] = dprompt


def windows_kernel(targets, heads_kv, scale, *refs):
    qh, gh, ds_fresh, p_behind, e_ref, dp_ref, terms, send_ref, keep_ref, ds_ref, p_own, p_ref, grads, wide = refs
    front = CAP * TILE
    tokens = TD * TILE
    early = ds_ref.shape[1] - tokens
    columns = CHUNK * 8
    for head in range(heads_kv):
        for c in range(tokens // CHUNK):
            rows = early + (c + 1) * CHUNK
            span = slice(c * columns, (c + 1) * columns)
            p = e_ref[head, :rows, span] * terms[head, 0:1, span]
            ds_ref[head, :rows, span] = (p * (dp_ref[head, :rows, span] - terms[head, 1:2, span])).astype(BF16)
            p_ref[head % 2, :, span] = p[:early].astype(BF16)
            p_own[head, : rows - early, span] = p[early:].astype(BF16)
        ds = jnp.concatenate([ds_fresh[head, tokens:], ds_ref[head, :early]], axis=0)
        grads[0, head] = scale * jnp.dot(ds, qh[head], preferred_element_type=F32)
        p = jnp.concatenate([p_behind[head], p_ref[head % 2]], axis=0)
        grads[1, head] = jnp.dot(p, gh[head], preferred_element_type=F32)
    for side in range(2):
        for k, (target, start) in enumerate(targets):
            span = slice(k * front, (k + 1) * front)
            block = join_heads([grads[side, h, span] for h in range(heads_kv)], front, heads_kv, wide).astype(BF16)
            start += side * front * heads_kv
            (send_ref, keep_ref)[target][start : start + front * heads_kv] = block


def grads_kernel(heads_kv, scale, *refs):
    qh, gh, kh_fresh, kh_early, ds_fresh, ds_early, p_own, dq_ref, dk_ref, dv_ref, wide = refs
    tokens = TD * TILE
    kh = [jnp.concatenate([kh_fresh[h], kh_early[h]], axis=0) for h in range(heads_kv)]
    before = kh[0].shape[0] - tokens
    columns = CHUNK * 8
    dk = []
    dv = []
    for pair in range(heads_kv // 2):
        for c in range(tokens // CHUNK):
            rows = before + (c + 1) * CHUNK
            span = slice(c * columns, (c + 1) * columns)
            parts = []
            for head in (2 * pair, 2 * pair + 1):
                fresh = ds_fresh.shape[1]
                ds = jnp.concatenate([ds_fresh[head, :, span], ds_early[head, : rows - fresh, span]], axis=0)
                dq = lax.dot_general(kh[head][:rows], ds, (((0,), (0,)), ((), ())), preferred_element_type=F32)
                parts.append((scale * dq.T).reshape(CHUNK, 8, 128))
            dq_ref[c * CHUNK : (c + 1) * CHUNK, pair * 16 : (pair + 1) * 16] = jnp.concatenate(parts, axis=1).astype(BF16)
        for head in (2 * pair, 2 * pair + 1):
            for source, factor, out in ((ds_early.at[head, before - fresh :], qh, dk), (p_own.at[head], gh, dv)):
                pieces = []
                for c in range(tokens // CHUNK):
                    start = c * columns
                    pieces.append(
                        jnp.dot(
                            source[c * CHUNK : (c + 1) * CHUNK, start:], factor[head, start:], preferred_element_type=F32
                        )
                    )
                out.append(jnp.concatenate(pieces, axis=0))
    dk_ref[...] = scale * join_heads(dk, tokens, heads_kv, wide)
    dv_ref[...] = join_heads(dv, tokens, heads_kv, wide)


VMEM = pl.BlockSpec(memory_space=pltpu.VMEM)


HBM = pl.BlockSpec(memory_space=pltpu.HBM)


def call(kernel, name, operands, outputs, scratch, flops, transcendentals=0, place=VMEM):
    sizes = [a.size * a.dtype.itemsize for a in (*operands, *outputs)]
    if place is HBM:
        operands = [pltpu.with_memory_space_constraint(a, pltpu.HBM) for a in operands]
    return pl.pallas_call(
        kernel,
        in_specs=[place] * len(operands),
        out_specs=[VMEM] * len(outputs),
        out_shape=outputs,
        scratch_shapes=scratch,
        compiler_params=pltpu.CompilerParams(vmem_limit_bytes=16 * 1024 * 1024),
        cost_estimate=pl.CostEstimate(flops=flops, bytes_accessed=sum(sizes), transcendentals=transcendentals),
        name=name,
    )(*operands)


def load(order, keys, values, parents, lengths, tokens):
    rows, head_size = keys.shape
    heads_kv = rows // tokens
    array = jax.ShapeDtypeStruct
    return call(
        functools.partial(load_kernel, order, heads_kv),
        "load",
        (parents, lengths, keys, values),
        [array((2 * CAP * TILE * heads_kv, head_size), BF16), array((rows, head_size), BF16)]
        + [array((heads_kv, tokens, head_size), BF16)] * 2
        + [array((2 * tokens + len(order) * CAP * TILE, 128), F32), array((8, tokens * 8), F32)],
        [pltpu.SMEM(parents.shape, jnp.int32), pltpu.SMEM(lengths.shape, jnp.int32)]
        + [pltpu.VMEM((rows, head_size), BF16)] * 2
        + [pltpu.VMEM((rows, head_size), F32), pltpu.SemaphoreType.DMA((4,))],
        flops=1 << 20,
        place=HBM,
    )


def pack(queries, grad_out, heads_kv):
    tokens, heads_q, head_size = queries.shape
    array = jax.ShapeDtypeStruct
    return call(
        functools.partial(pack_kernel, heads_kv),
        "pack",
        (queries, grad_out),
        [array((heads_kv, tokens * 8, head_size), BF16)] * 2,
        [pltpu.VMEM((heads_kv, tokens, 16, head_size), BF16), pltpu.SemaphoreType.DMA((heads_kv,))],
        flops=1 << 20,
        place=HBM,
    )


def early(fresh, sources, qh, gh, own, blocks):
    own_k, own_v, bias, _ = own
    heads_kv, tokens, head_size = own_k.shape
    rows = len(sources) * CAP * TILE + tokens
    array = jax.ShapeDtypeStruct
    work = heads_kv * tokens * 8 * rows
    return call(
        functools.partial(early_kernel, fresh, sources, heads_kv, head_size**-0.5),
        "early",
        (own_k, own_v, qh, gh, bias, *blocks),
        [array((heads_kv, rows, head_size), BF16)]
        + [array((heads_kv, rows, tokens * 8), F32)] * 2
        + [array((heads_kv, 8, tokens * 8), F32)],
        [pltpu.VMEM((heads_kv, rows, head_size), BF16), pltpu.VMEM((CAP * TILE * heads_kv, head_size), F32)],
        flops=4 * work * head_size,
        transcendentals=work,
    )


def probs(sources, prompt_k, prompt_v, qh, gh, own, stats, block):
    _, own_v, bias, weight = own
    heads_kv, tokens, head_size = own_v.shape
    rows = tokens * heads_kv
    fresh = tokens + len(sources) * CAP * TILE
    array = jax.ShapeDtypeStruct
    work = heads_kv * tokens * 8 * fresh
    return call(
        functools.partial(probs_kernel, sources, heads_kv, head_size**-0.5),
        "probs",
        (prompt_k, prompt_v, qh, gh, bias, weight, stats, block),
        [array((rows, head_size), BF16)] * 2
        + [
            array((heads_kv, fresh, head_size), BF16),
            array((heads_kv, fresh, tokens * 8), BF16),
            array((heads_kv, fresh - tokens, tokens * 8), BF16),
            array((heads_kv, 8, tokens * 8), F32),
        ],
        [
            pltpu.VMEM((heads_kv, fresh, head_size), BF16),
            pltpu.VMEM((2, tokens, tokens * 8), BF16),
            pltpu.VMEM((2, heads_kv, tokens, head_size), F32),
            pltpu.VMEM((rows, head_size), F32),
        ],
        flops=8 * work * head_size,
        transcendentals=work,
    )


def windows(targets, qh, gh, ds_fresh, p_behind, e, dp, terms):
    heads_kv, early, columns = e.shape
    head_size = qh.shape[2]
    tokens = TD * TILE
    front = CAP * TILE * heads_kv
    behind = early - tokens + p_behind.shape[1]
    count = [sum(target == t for target, _ in targets) for t in (0, 1)]
    array = jax.ShapeDtypeStruct
    return call(
        functools.partial(windows_kernel, targets, heads_kv, head_size**-0.5),
        "windows",
        (qh, gh, ds_fresh, p_behind, e, dp, terms),
        [array((2 * front * n, head_size), BF16) for n in count]
        + [array((heads_kv, early, columns), BF16), array((heads_kv, tokens, columns), BF16)],
        [
            pltpu.VMEM((2, early - tokens, columns), BF16),
            pltpu.VMEM((2, heads_kv, behind, head_size), F32),
            pltpu.VMEM((front, head_size), F32),
        ],
        flops=4 * heads_kv * behind * columns * head_size,
    )


def grads(qh, gh, kh_fresh, kh_early, ds_fresh, ds_early, p_own):
    heads_kv, tokens, _ = p_own.shape
    head_size = kh_fresh.shape[2]
    array = jax.ShapeDtypeStruct
    return call(
        functools.partial(grads_kernel, heads_kv, head_size**-0.5),
        "grads",
        (qh, gh, kh_fresh, kh_early, ds_fresh, ds_early, p_own),
        [
            array((tokens, heads_kv * 8, head_size), BF16),
            array((tokens * heads_kv, head_size), F32),
            array((tokens * heads_kv, head_size), F32),
        ],
        [pltpu.VMEM((tokens * heads_kv, head_size), F32)],
        flops=2 * tokens * 8 * (ds_fresh.size + ds_early.size) // (tokens * 8) * head_size,
    )


def shift_route(distance, size):
    return [(i, i + distance) for i in range(size - distance)]


def back(route):
    return [(j, i) for i, j in route]


def added(*blocks):
    total = blocks[0].astype(F32)
    for block in blocks[1:]:
        total = total + block.astype(F32)
    return total


def after(array, *earlier):
    return lax.optimization_barrier((array, *earlier))[0]


def units(array, start, unit, count):
    return [array[start + i * unit : start + (i + 1) * unit] for i in range(count)]


def prompt_route(stride, size):
    return [(i + j, i + j + stride) for i in range(0, size, 2 * stride) for j in (0, 1)]


def collect(size, unit, rows, where, keys, values, head, held, queries, grad_out):
    even, lower, _ = where
    neighbours = [(i, i ^ 1) for i in range(size)]
    far_route = shift_route(4, size)[1:]
    near_route = shift_route(2, size)
    if size == W + 1:
        keys_far = permuted(keys, [(0, 4)])
        values_far = permuted(values, [(0, 5)])
        values_next = permuted(values, [(0, 1)])
        head, queries = lax.optimization_barrier((head, queries, keys_far))[:2]
        qh, gh = pack(queries, grad_out, keys.shape[0] // queries.shape[0])
        far = permuted(head, far_route)
        six = permuted(head, [(1, 7)])
        held = after(added(held, values_next, values_far, keys_far).astype(BF16), six, far)
        second = permuted(jnp.concatenate([held, head]), near_route)
        crossed = jnp.where(even, jnp.concatenate([head, far]), jnp.concatenate([far, six]))
        crossed = permuted(crossed, neighbours)
        held = jnp.where(lower, held, second[:rows])
        third = permuted(after(jnp.concatenate([held, second[rows:]]), crossed), neighbours)
        early_sources = [(0, rows), (1, 0), (2, 0), (1, unit), (3, 0)]
        return held, third[:rows], third, [(0, rows)], early_sources, (second, crossed, far, six), (qh, gh)
    strides = [2**i for i in range(2, size.bit_length()) if 2**i < size]
    top = strides[-1]
    keys_far = permuted(keys, [(0, top)])
    values_far = permuted(values, [(0, top + 1)])
    values_next = permuted(values, [(0, 1)])
    far = permuted(head, far_route)
    held = added(held, values_next, values_far, keys_far).astype(BF16)
    for stride in reversed(strides[:-1]):
        held = added(held, permuted(held, prompt_route(stride, size))).astype(BF16)
    second = permuted(jnp.concatenate([held, head, far]), near_route)
    held = jnp.where(lower, held, second[:rows])
    near, six = units(second, rows, unit, 2)
    third = permuted(jnp.concatenate([head, near, far, six]), shift_route(1, size))
    other = permuted(held, neighbours)
    fresh_sources = [(0, i * unit) for i in range(4)]
    early_sources = [(0, rows), (1, 0), (0, rows + unit)]
    return held, other, third, fresh_sources, early_sources, (second, far), pack(queries, grad_out, keys.shape[0] // queries.shape[0])


def give_back(size, unit, where, prompt, behind, finish):
    even, lower, _ = where
    neighbours = [(i, i ^ 1) for i in range(size)]
    far_route = back(shift_route(4, size)[1:])
    send, keep = prompt
    rows = keep.shape[0]
    two, four, six = units(behind[1], 0, unit, 3)
    if size == W + 1:
        total = added(keep, permuted(send, neighbours)).astype(BF16)
        finished = finish(total)
        near, first, last = units(permuted(behind[0], neighbours), 0, unit, 3)
        none = jnp.zeros_like(first)
        parts = [permuted(total, [(j, 0), (j + 1, 1)]) for j in reversed(range(2, size, 2))]
        two = permuted(added(two, near).astype(BF16), back(shift_route(2, size)[1:]))
        four = after(added(four, jnp.where(even, last, first)).astype(BF16), finished[1])
        four = permuted(four, far_route)
        six = permuted(added(six, jnp.where(even, none, last)).astype(BF16), [(7, 1)])
        total = added(total, *parts).astype(BF16)
        mine = added(jnp.where(even, first, none), two, four, six)
        return finished, total, permuted(total, [(1, 0)]).astype(F32), mine
    strides = [2**i for i in range(2, size.bit_length()) if 2**i < size]
    top = strides[-1]
    zero, *third = units(permuted(behind[0], back(shift_route(1, size))), 0, unit, 4)
    total = added(keep, permuted(send, neighbours)).astype(BF16)
    two, four, six = (added(x, y).astype(BF16) for x, y in zip((two, four, six), third))
    second = permuted(jnp.concatenate([total, two, six]), back(shift_route(2, size)))
    four = added(four, second[rows + unit :])
    mine = added(zero, second[rows : rows + unit], permuted(four.astype(BF16), far_route))
    total = added(total, jnp.where(lower, second[:rows], jnp.zeros_like(total))).astype(BF16)
    for stride in strides[:-1]:
        total = added(total, permuted(total, back(prompt_route(stride, size)))).astype(BF16)
    keys_far = permuted(total, [(top, 0)])
    values_far = permuted(total, [(top + 1, 0)])
    values_next = permuted(total, [(1, 0)])
    return finish(send), added(total, keys_far), added(values_next, values_far), mine


def per_device(size, queries, keys, values, grad_out, parents, lengths):
    tokens, heads_kv, head_size = keys.shape
    rows = tokens * heads_kv
    one = CAP * TILE * heads_kv
    unit = 2 * one
    window = min(W, size - 2)
    device = lax.axis_index("node")
    keys = keys.reshape(rows, head_size)
    values = values.reshape(rows, head_size)

    if size == W + 1:
        order = [(1, 3), (2, 2), (3, 1), (4, 4), (5, 5), (6, 6)]
        targets = [(k % 2, k // 2 * unit) for k in range(window)]
    else:
        order = [(k, k) for k in (1, 3, 5, 7, 2, 4, 6)]
        targets = [(0, i * unit) for i in range(4)] + [(1, i * unit) for i in range(3)]
    head, held, *own = load(order, keys, values, parents, lengths, tokens)
    head, *where = lax.optimization_barrier((head, lax.rem(device, 2) == 0, lax.rem(device, 4) < 2, device == 0))
    even, _, root = where
    held, other, block, fresh_sources, early_sources, blocks, (qh, gh) = collect(
        size, unit, rows, where, keys, values, head, held, queries, grad_out
    )
    kh_early, e, dp, stats = early(len(fresh_sources), early_sources, qh, gh, own, blocks)
    prompt_k, prompt_v = jnp.where(even, held, other), jnp.where(even, other, held)
    *prompt, kh, ds, p_behind, terms = probs(fresh_sources, prompt_k, prompt_v, qh, gh, own, stats, block)
    *behind, ds_early, p_own = windows(targets, qh, gh, ds, p_behind, e, dp, terms)

    def finish(earlier):
        return grads(qh, gh, kh, kh_early, ds, ds_early, after(p_own, earlier))

    (grad_queries, dk, dv), prompt_k, prompt_v, mine = give_back(size, unit, where, prompt, behind, finish)
    own = []
    for side, local, prompt in ((0, dk, prompt_k), (1, dv, prompt_v)):
        whole = local + jnp.where(root, prompt.astype(F32), 0.0)
        own.append(whole.at[:one].add(mine[side * one : (side + 1) * one]).reshape(tokens, heads_kv, head_size))
    return grad_queries, own[0], own[1]


def solution(mesh):
    by_token = P(("leaf", "node"), "tensor", None)
    return jax.shard_map(
        functools.partial(per_device, mesh.shape["node"]),
        mesh=mesh,
        in_specs=(by_token, by_token, by_token, by_token, P("leaf"), P("leaf")),
        out_specs=(by_token, by_token, by_token),
        check_vma=False,
    )
```

```python
import functools
import math

import jax
import jax.numpy as jnp
from jax import lax
from jax.experimental import pallas as pl
from jax.experimental.pallas import tpu as pltpu
from jax.sharding import PartitionSpec as P

TILE = 16
TD = 8
CAP = 2
W = 7
CHUNK = 32
MASKED = -1e30
BF16 = jnp.bfloat16
F32 = jnp.float32


def permuted(block, route):
    return lax.ppermute(block, "node", route)


def column_limits(device, window, parents, lengths):
    cursor = parents[device * TD]
    need = [jnp.int32(0)] * (window + 1)
    for _ in range(W):
        owner = jnp.where(cursor < 0, -1, lax.div(jnp.maximum(cursor, 0), TD))
        distance = device - owner
        active = (owner >= 1) & (distance >= 1) & (distance <= W)
        depth = lax.rem(jnp.maximum(cursor, 0), TD) + 1
        for k in range(1, window + 1):
            need[k] = jnp.where(active & (distance == k), depth, need[k])
        cursor = jnp.where(active, parents[jnp.maximum(owner, 0) * TD], cursor)
    prompt = [jnp.where(device >= 1, lengths[t], 0) for t in range(TD)]
    behind = []
    for k in range(1, window + 1):
        owner = device - k
        seen = [(owner >= 1) & (c < need[k]) for c in range(CAP)]
        behind.append([jnp.where(seen[c], lengths[jnp.maximum(owner, 0) * TD + c], 0) for c in range(CAP)])
    return prompt, behind, [lengths[device * TD + t] for t in range(TD)]


def split_heads(block, heads_ref, start, count, heads_kv, wide):
    wide[: count * heads_kv] = block.astype(F32)
    for h in range(heads_kv):
        heads_ref[h, start : start + count] = wide[pl.ds(h, count, stride=heads_kv), :].astype(BF16)


def join_heads(blocks, count, heads_kv, wide):
    for h in range(heads_kv):
        wide[pl.ds(h, count, stride=heads_kv), :] = blocks[h]
    return wide[: count * heads_kv]


def load_kernel(order, heads_kv, *refs):
    sources, outs, scratch = refs[:4], refs[4:10], refs[10:]
    head, held, own_k, own_v, bias, weight = outs
    parents, lengths, keys, values, wide, arrived = scratch
    copies = [pltpu.make_async_copy(a, b, arrived.at[i]) for i, (a, b) in enumerate(zip(sources, scratch))]
    for copy in copies:
        copy.start()
    tokens = TD * TILE
    front = CAP * TILE * heads_kv
    device = lax.axis_index("node")
    for copy in copies:
        copy.wait()
    head[:front] = keys[:front]
    head[front:] = values[:front]
    held[...] = jnp.where(device == 0, keys[...], jnp.zeros_like(keys))
    split_heads(keys[...], own_k, 0, tokens, heads_kv, wide)
    split_heads(values[...], own_v, 0, tokens, heads_kv, wide)
    place = lax.broadcasted_iota(jnp.int32, (TILE, 128), 0)
    prompt, behind, own = column_limits(device, len(order), parents, lengths)
    even = lax.rem(device, 2) == 0
    limits = prompt
    for on_even, on_odd in order:
        limits = limits + [jnp.where(even, x, y) for x, y in zip(behind[on_even - 1], behind[on_odd - 1])]
    for t, limit in enumerate(limits + own):
        bias[t * TILE : (t + 1) * TILE] = jnp.where(place < limit, 0.0, MASKED)
    lane_place = lax.broadcasted_iota(jnp.int32, (8, 128), 1) // 8
    for t in range(TD):
        weight[:, t * 128 : (t + 1) * 128] = jnp.where(lane_place < lengths[device * TD + t], 1.0, 0.0)


def pack_kernel(heads_kv, q_ref, g_ref, qh, gh, blocks, arrived):
    tokens = TD * TILE
    copies = []
    for pair in range(heads_kv // 2):
        for ref, out in ((q_ref, qh), (g_ref, gh)):
            i = len(copies)
            copy = pltpu.make_async_copy(ref.at[:, pair * 16 : (pair + 1) * 16], blocks.at[i], arrived.at[i])
            copy.start()
            copies.append((copy, out, pair))
    for i, (copy, out, pair) in enumerate(copies):
        copy.wait()
        both = blocks[i].astype(F32)
        for part in range(2):
            out[2 * pair + part] = both[:, part * 8 : (part + 1) * 8].reshape(tokens * 8, 128).astype(BF16)


def causal_bias(columns):
    column_token = lax.broadcasted_iota(jnp.int32, (CHUNK, columns), 1) // 8
    return jnp.where(lax.broadcasted_iota(jnp.int32, (CHUNK, columns), 0) <= column_token, 0.0, MASKED)


def outer_product(rows, columns):
    return lax.dot_general(rows, columns, (((1,), (1,)), ((), ())), preferred_element_type=F32)


def early_kernel(fresh, sources, heads_kv, scale, *refs):
    own_k, own_v, qh, gh, bias = refs[:5]
    blocks, (kh, e_ref, dp_ref, stats, vh, wide) = refs[5:-6], refs[-6:]
    tokens = TD * TILE
    front = CAP * TILE
    behind = len(sources) * front
    start = tokens + fresh * front
    columns = CHUNK * 8
    for side, heads_ref, own in ((0, kh, own_k), (1, vh, own_v)):
        for k, (source, at) in enumerate(sources):
            at += side * front * heads_kv
            split_heads(blocks[source][at : at + front * heads_kv], heads_ref, k * front, front, heads_kv, wide)
        heads_ref[:, behind:] = own[...]
    causal = causal_bias(columns)
    for head in range(heads_kv):
        for c in range(tokens // CHUNK):
            rows = behind + (c + 1) * CHUNK
            span = slice(c * columns, (c + 1) * columns)
            s = outer_product(kh[head, :rows], qh[head, span])
            dp = outer_product(vh[head, :rows], gh[head, span])
            s = s + jnp.concatenate([bias[start : start + rows]] * (columns // 128), axis=1)
            s = jnp.concatenate([s[: rows - CHUNK], s[rows - CHUNK :] + causal], axis=0)
            top = jnp.max(s, axis=0, keepdims=True)
            e = jnp.exp2((s - top) * (scale * math.log2(math.e)))
            e_ref[head, :rows, span] = e
            dp_ref[head, :rows, span] = dp
            stats[head, 0:1, span] = top
            stats[head, 1:2, span] = jnp.sum(e, axis=0, keepdims=True)
            stats[head, 2:3, span] = jnp.sum(e * dp, axis=0, keepdims=True)


def probs_kernel(sources, heads_kv, scale, *refs):
    prompt_k, prompt_v, qh, gh, bias, weight_ref, stats, block_ref = refs[:8]
    send_ref, keep_ref, kh, ds_ref, p_behind, terms, vh, p_ref, grads, wide = refs[8:]
    tokens = TD * TILE
    front = CAP * TILE
    columns = CHUNK * 8
    rate = scale * math.log2(math.e)
    device = lax.axis_index("node")

    for side, heads_ref, prompt in ((0, kh, prompt_k), (1, vh, prompt_v)):
        split_heads(prompt[...], heads_ref, 0, tokens, heads_kv, wide)
        for k, (_, at) in enumerate(sources):
            at += side * front * heads_kv
            split_heads(block_ref[at : at + front * heads_kv], heads_ref, tokens + k * front, front, heads_kv, wide)

    for head in range(heads_kv):
        for c in range(tokens // CHUNK):
            span = slice(c * columns, (c + 1) * columns)
            s = outer_product(kh[head], qh[head, span])
            dp = outer_product(vh[head], gh[head, span])
            s = s + jnp.concatenate([bias[: s.shape[0]]] * (columns // 128), axis=1)
            top_early = stats[head, 0:1, span]
            top = jnp.maximum(jnp.max(s, axis=0, keepdims=True), top_early)
            e = jnp.exp2((s - top) * rate)
            shrink = jnp.exp2((top_early - top) * rate)
            total = jnp.sum(e, axis=0, keepdims=True) + shrink * stats[head, 1:2, span]
            weight = weight_ref[:1, span] / total
            weight_early = weight * shrink
            p = e * weight
            delta = jnp.sum(p * dp, axis=0, keepdims=True) + weight_early * stats[head, 2:3, span]
            ds_ref[head, :, span] = (p * (dp - delta)).astype(BF16)
            p_ref[head % 2, :, span] = p[:tokens].astype(BF16)
            p_behind[head, :, span] = p[tokens:].astype(BF16)
            terms[head, 0:1, span] = weight_early
            terms[head, 1:2, span] = delta
        grads[0, head] = scale * jnp.dot(ds_ref[head, :tokens], qh[head], preferred_element_type=F32)
        grads[1, head] = jnp.dot(p_ref[head % 2], gh[head], preferred_element_type=F32)

    even = lax.rem(device, 2) == 0
    for side in range(2):
        dprompt = join_heads([grads[side, h] for h in range(heads_kv)], tokens, heads_kv, wide).astype(BF16)
        kept = even if side == 0 else jnp.logical_not(even)

        @pl.when(kept)
        def _():
            keep_ref[...] = dprompt

        @pl.when(jnp.logical_not(kept))
        def _():
            send_ref[...] = dprompt


def windows_kernel(targets, heads_kv, scale, *refs):
    qh, gh, ds_fresh, p_behind, e_ref, dp_ref, terms, send_ref, keep_ref, ds_ref, p_own, p_ref, grads, wide = refs
    front = CAP * TILE
    tokens = TD * TILE
    early = ds_ref.shape[1] - tokens
    columns = CHUNK * 8
    for head in range(heads_kv):
        for c in range(tokens // CHUNK):
            rows = early + (c + 1) * CHUNK
            span = slice(c * columns, (c + 1) * columns)
            p = e_ref[head, :rows, span] * terms[head, 0:1, span]
            ds_ref[head, :rows, span] = (p * (dp_ref[head, :rows, span] - terms[head, 1:2, span])).astype(BF16)
            p_ref[head % 2, :, span] = p[:early].astype(BF16)
            p_own[head, : rows - early, span] = p[early:].astype(BF16)
        ds = jnp.concatenate([ds_fresh[head, tokens:], ds_ref[head, :early]], axis=0)
        grads[0, head] = scale * jnp.dot(ds, qh[head], preferred_element_type=F32)
        p = jnp.concatenate([p_behind[head], p_ref[head % 2]], axis=0)
        grads[1, head] = jnp.dot(p, gh[head], preferred_element_type=F32)
    for side in range(2):
        for k, (target, start) in enumerate(targets):
            span = slice(k * front, (k + 1) * front)
            block = join_heads([grads[side, h, span] for h in range(heads_kv)], front, heads_kv, wide).astype(BF16)
            start += side * front * heads_kv
            (send_ref, keep_ref)[target][start : start + front * heads_kv] = block


def grads_kernel(heads_kv, scale, *refs):
    qh, gh, kh_fresh, kh_early, ds_fresh, ds_early, p_own, dq_ref, dk_ref, dv_ref, wide = refs
    tokens = TD * TILE
    kh = [jnp.concatenate([kh_fresh[h], kh_early[h]], axis=0) for h in range(heads_kv)]
    before = kh[0].shape[0] - tokens
    columns = CHUNK * 8
    dk = []
    dv = []
    for pair in range(heads_kv // 2):
        for c in range(tokens // CHUNK):
            rows = before + (c + 1) * CHUNK
            span = slice(c * columns, (c + 1) * columns)
            parts = []
            for head in (2 * pair, 2 * pair + 1):
                fresh = ds_fresh.shape[1]
                ds = jnp.concatenate([ds_fresh[head, :, span], ds_early[head, : rows - fresh, span]], axis=0)
                dq = lax.dot_general(kh[head][:rows], ds, (((0,), (0,)), ((), ())), preferred_element_type=F32)
                parts.append((scale * dq.T).reshape(CHUNK, 8, 128))
            dq_ref[c * CHUNK : (c + 1) * CHUNK, pair * 16 : (pair + 1) * 16] = jnp.concatenate(parts, axis=1).astype(BF16)
        for head in (2 * pair, 2 * pair + 1):
            for source, factor, out in ((ds_early.at[head, before - fresh :], qh, dk), (p_own.at[head], gh, dv)):
                pieces = []
                for c in range(tokens // CHUNK):
                    start = c * columns
                    pieces.append(
                        jnp.dot(
                            source[c * CHUNK : (c + 1) * CHUNK, start:], factor[head, start:], preferred_element_type=F32
                        )
                    )
                out.append(jnp.concatenate(pieces, axis=0))
    dk_ref[...] = scale * join_heads(dk, tokens, heads_kv, wide)
    dv_ref[...] = join_heads(dv, tokens, heads_kv, wide)


VMEM = pl.BlockSpec(memory_space=pltpu.VMEM)


HBM = pl.BlockSpec(memory_space=pltpu.HBM)


def call(kernel, name, operands, outputs, scratch, flops, transcendentals=0, place=VMEM):
    sizes = [a.size * a.dtype.itemsize for a in (*operands, *outputs)]
    if place is HBM:
        operands = [pltpu.with_memory_space_constraint(a, pltpu.HBM) for a in operands]
    return pl.pallas_call(
        kernel,
        in_specs=[place] * len(operands),
        out_specs=[VMEM] * len(outputs),
        out_shape=outputs,
        scratch_shapes=scratch,
        compiler_params=pltpu.CompilerParams(vmem_limit_bytes=16 * 1024 * 1024),
        cost_estimate=pl.CostEstimate(flops=flops, bytes_accessed=sum(sizes), transcendentals=transcendentals),
        name=name,
    )(*operands)


def load(order, keys, values, parents, lengths, tokens):
    rows, head_size = keys.shape
    heads_kv = rows // tokens
    array = jax.ShapeDtypeStruct
    return call(
        functools.partial(load_kernel, order, heads_kv),
        "load",
        (parents, lengths, keys, values),
        [array((2 * CAP * TILE * heads_kv, head_size), BF16), array((rows, head_size), BF16)]
        + [array((heads_kv, tokens, head_size), BF16)] * 2
        + [array((2 * tokens + len(order) * CAP * TILE, 128), F32), array((8, tokens * 8), F32)],
        [pltpu.SMEM(parents.shape, jnp.int32), pltpu.SMEM(lengths.shape, jnp.int32)]
        + [pltpu.VMEM((rows, head_size), BF16)] * 2
        + [pltpu.VMEM((rows, head_size), F32), pltpu.SemaphoreType.DMA((4,))],
        flops=1 << 20,
        place=HBM,
    )


def pack(queries, grad_out, heads_kv):
    tokens, heads_q, head_size = queries.shape
    array = jax.ShapeDtypeStruct
    return call(
        functools.partial(pack_kernel, heads_kv),
        "pack",
        (queries, grad_out),
        [array((heads_kv, tokens * 8, head_size), BF16)] * 2,
        [pltpu.VMEM((heads_kv, tokens, 16, head_size), BF16), pltpu.SemaphoreType.DMA((heads_kv,))],
        flops=1 << 20,
        place=HBM,
    )


def early(fresh, sources, qh, gh, own, blocks):
    own_k, own_v, bias, _ = own
    heads_kv, tokens, head_size = own_k.shape
    rows = len(sources) * CAP * TILE + tokens
    array = jax.ShapeDtypeStruct
    work = heads_kv * tokens * 8 * rows
    return call(
        functools.partial(early_kernel, fresh, sources, heads_kv, head_size**-0.5),
        "early",
        (own_k, own_v, qh, gh, bias, *blocks),
        [array((heads_kv, rows, head_size), BF16)]
        + [array((heads_kv, rows, tokens * 8), F32)] * 2
        + [array((heads_kv, 8, tokens * 8), F32)],
        [pltpu.VMEM((heads_kv, rows, head_size), BF16), pltpu.VMEM((CAP * TILE * heads_kv, head_size), F32)],
        flops=4 * work * head_size,
        transcendentals=work,
    )


def probs(sources, prompt_k, prompt_v, qh, gh, own, stats, block):
    _, own_v, bias, weight = own
    heads_kv, tokens, head_size = own_v.shape
    rows = tokens * heads_kv
    fresh = tokens + len(sources) * CAP * TILE
    array = jax.ShapeDtypeStruct
    work = heads_kv * tokens * 8 * fresh
    return call(
        functools.partial(probs_kernel, sources, heads_kv, head_size**-0.5),
        "probs",
        (prompt_k, prompt_v, qh, gh, bias, weight, stats, block),
        [array((rows, head_size), BF16)] * 2
        + [
            array((heads_kv, fresh, head_size), BF16),
            array((heads_kv, fresh, tokens * 8), BF16),
            array((heads_kv, fresh - tokens, tokens * 8), BF16),
            array((heads_kv, 8, tokens * 8), F32),
        ],
        [
            pltpu.VMEM((heads_kv, fresh, head_size), BF16),
            pltpu.VMEM((2, tokens, tokens * 8), BF16),
            pltpu.VMEM((2, heads_kv, tokens, head_size), F32),
            pltpu.VMEM((rows, head_size), F32),
        ],
        flops=8 * work * head_size,
        transcendentals=work,
    )


def windows(targets, qh, gh, ds_fresh, p_behind, e, dp, terms):
    heads_kv, early, columns = e.shape
    head_size = qh.shape[2]
    tokens = TD * TILE
    front = CAP * TILE * heads_kv
    behind = early - tokens + p_behind.shape[1]
    count = [sum(target == t for target, _ in targets) for t in (0, 1)]
    array = jax.ShapeDtypeStruct
    return call(
        functools.partial(windows_kernel, targets, heads_kv, head_size**-0.5),
        "windows",
        (qh, gh, ds_fresh, p_behind, e, dp, terms),
        [array((2 * front * n, head_size), BF16) for n in count]
        + [array((heads_kv, early, columns), BF16), array((heads_kv, tokens, columns), BF16)],
        [
            pltpu.VMEM((2, early - tokens, columns), BF16),
            pltpu.VMEM((2, heads_kv, behind, head_size), F32),
            pltpu.VMEM((front, head_size), F32),
        ],
        flops=4 * heads_kv * behind * columns * head_size,
    )


def grads(qh, gh, kh_fresh, kh_early, ds_fresh, ds_early, p_own):
    heads_kv, tokens, _ = p_own.shape
    head_size = kh_fresh.shape[2]
    array = jax.ShapeDtypeStruct
    return call(
        functools.partial(grads_kernel, heads_kv, head_size**-0.5),
        "grads",
        (qh, gh, kh_fresh, kh_early, ds_fresh, ds_early, p_own),
        [
            array((tokens, heads_kv * 8, head_size), BF16),
            array((tokens * heads_kv, head_size), F32),
            array((tokens * heads_kv, head_size), F32),
        ],
        [pltpu.VMEM((tokens * heads_kv, head_size), F32)],
        flops=2 * tokens * 8 * (ds_fresh.size + ds_early.size) // (tokens * 8) * head_size,
    )


def shift_route(distance, size):
    return [(i, i + distance) for i in range(size - distance)]


def back(route):
    return [(j, i) for i, j in route]


def added(*blocks):
    total = blocks[0].astype(F32)
    for block in blocks[1:]:
        total = total + block.astype(F32)
    return total


def after(array, *earlier):
    return lax.optimization_barrier((array, *earlier))[0]


def units(array, start, unit, count):
    return [array[start + i * unit : start + (i + 1) * unit] for i in range(count)]


def prompt_route(stride, size):
    return [(i + j, i + j + stride) for i in range(0, size, 2 * stride) for j in (0, 1)]


def collect(size, unit, rows, where, keys, values, head, held, queries, grad_out):
    even, lower, _ = where
    neighbours = [(i, i ^ 1) for i in range(size)]
    far_route = shift_route(4, size)[1:]
    near_route = shift_route(2, size)
    if size == W + 1:
        keys_far = permuted(keys, [(0, 4)])
        values_far = permuted(values, [(0, 5)])
        values_next = permuted(values, [(0, 1)])
        head, queries = lax.optimization_barrier((head, queries, keys_far))[:2]
        qh, gh = pack(queries, grad_out, keys.shape[0] // queries.shape[0])
        far = permuted(head, far_route)
        six = permuted(head, [(1, 7)])
        held = after(added(held, values_next, values_far, keys_far).astype(BF16), six, far, qh)
        second = permuted(jnp.concatenate([held, head]), near_route)
        crossed = jnp.where(even, jnp.concatenate([head, far]), jnp.concatenate([far, six]))
        crossed = permuted(crossed, neighbours)
        held = jnp.where(lower, held, second[:rows])
        third = permuted(after(jnp.concatenate([held, second[rows:]]), crossed), neighbours)
        early_sources = [(0, rows), (1, 0), (2, 0), (1, unit), (3, 0)]
        return held, third[:rows], third, [(0, rows)], early_sources, (second, crossed, far, six), (qh, gh)
    strides = [2**i for i in range(2, size.bit_length()) if 2**i < size]
    top = strides[-1]
    keys_far = permuted(keys, [(0, top)])
    values_far = permuted(values, [(0, top + 1)])
    values_next = permuted(values, [(0, 1)])
    far = permuted(head, far_route)
    held = added(held, values_next, values_far, keys_far).astype(BF16)
    for stride in reversed(strides[:-1]):
        held = added(held, permuted(held, prompt_route(stride, size))).astype(BF16)
    second = permuted(jnp.concatenate([held, head, far]), near_route)
    held = jnp.where(lower, held, second[:rows])
    near, six = units(second, rows, unit, 2)
    third = permuted(jnp.concatenate([head, near, far, six]), shift_route(1, size))
    other = permuted(held, neighbours)
    fresh_sources = [(0, i * unit) for i in range(4)]
    early_sources = [(0, rows), (1, 0), (0, rows + unit)]
    return held, other, third, fresh_sources, early_sources, (second, far), pack(queries, grad_out, keys.shape[0] // queries.shape[0])


def give_back(size, unit, where, prompt, behind, finish):
    even, lower, _ = where
    neighbours = [(i, i ^ 1) for i in range(size)]
    far_route = back(shift_route(4, size)[1:])
    send, keep = prompt
    rows = keep.shape[0]
    two, four, six = units(behind[1], 0, unit, 3)
    if size == W + 1:
        total = added(keep, permuted(send, neighbours)).astype(BF16)
        finished = finish(total)
        near, first, last = units(permuted(behind[0], neighbours), 0, unit, 3)
        none = jnp.zeros_like(first)
        parts = [permuted(total, [(j, 0), (j + 1, 1)]) for j in reversed(range(2, size, 2))]
        two = permuted(added(two, near).astype(BF16), back(shift_route(2, size)[1:]))
        four = after(added(four, jnp.where(even, last, first)).astype(BF16), finished[1])
        four = permuted(four, far_route)
        six = permuted(added(six, jnp.where(even, none, last)).astype(BF16), [(7, 1)])
        total = added(total, *parts).astype(BF16)
        mine = added(jnp.where(even, first, none), six, four, two)
        return finished, total, permuted(total, [(1, 0)]).astype(F32), mine
    strides = [2**i for i in range(2, size.bit_length()) if 2**i < size]
    top = strides[-1]
    zero, *third = units(permuted(behind[0], back(shift_route(1, size))), 0, unit, 4)
    total = added(keep, permuted(send, neighbours)).astype(BF16)
    two, four, six = (added(x, y).astype(BF16) for x, y in zip((two, four, six), third))
    second = permuted(jnp.concatenate([total, two, six]), back(shift_route(2, size)))
    four = added(four, second[rows + unit :])
    mine = added(zero, second[rows : rows + unit], permuted(four.astype(BF16), far_route))
    total = added(total, jnp.where(lower, second[:rows], jnp.zeros_like(total))).astype(BF16)
    for stride in strides[:-1]:
        total = added(total, permuted(total, back(prompt_route(stride, size)))).astype(BF16)
    keys_far = permuted(total, [(top, 0)])
    values_far = permuted(total, [(top + 1, 0)])
    values_next = permuted(total, [(1, 0)])
    return finish(send), added(total, keys_far), added(values_next, values_far), mine


def per_device(size, queries, keys, values, grad_out, parents, lengths):
    tokens, heads_kv, head_size = keys.shape
    rows = tokens * heads_kv
    one = CAP * TILE * heads_kv
    unit = 2 * one
    window = min(W, size - 2)
    device = lax.axis_index("node")
    keys = keys.reshape(rows, head_size)
    values = values.reshape(rows, head_size)

    if size == W + 1:
        order = [(1, 3), (2, 2), (3, 1), (4, 4), (5, 5), (6, 6)]
        targets = [(k % 2, k // 2 * unit) for k in range(window)]
    else:
        order = [(k, k) for k in (1, 3, 5, 7, 2, 4, 6)]
        targets = [(0, i * unit) for i in range(4)] + [(1, i * unit) for i in range(3)]
    head, held, *own = load(order, keys, values, parents, lengths, tokens)
    head, *where = lax.optimization_barrier((head, lax.rem(device, 2) == 0, lax.rem(device, 4) < 2, device == 0))
    even, _, root = where
    held, other, block, fresh_sources, early_sources, blocks, (qh, gh) = collect(
        size, unit, rows, where, keys, values, head, held, queries, grad_out
    )
    kh_early, e, dp, stats = early(len(fresh_sources), early_sources, qh, gh, own, blocks)
    prompt_k, prompt_v = jnp.where(even, held, other), jnp.where(even, other, held)
    *prompt, kh, ds, p_behind, terms = probs(fresh_sources, prompt_k, prompt_v, qh, gh, own, stats, block)
    *behind, ds_early, p_own = windows(targets, qh, gh, ds, p_behind, e, dp, terms)

    def finish(earlier):
        return grads(qh, gh, kh, kh_early, ds, ds_early, after(p_own, earlier))

    (grad_queries, dk, dv), prompt_k, prompt_v, mine = give_back(size, unit, where, prompt, behind, finish)
    own = []
    for side, local, prompt in ((0, dk, prompt_k), (1, dv, prompt_v)):
        whole = local + jnp.where(root, prompt.astype(F32), 0.0)
        own.append(whole.at[:one].add(mine[side * one : (side + 1) * one]).reshape(tokens, heads_kv, head_size))
    return grad_queries, own[0], own[1]


def solution(mesh):
    by_token = P(("leaf", "node"), "tensor", None)
    return jax.shard_map(
        functools.partial(per_device, mesh.shape["node"]),
        mesh=mesh,
        in_specs=(by_token, by_token, by_token, by_token, P("leaf"), P("leaf")),
        out_specs=(by_token, by_token, by_token),
        check_vma=False,
    )
```

```python
import functools
import math

import jax
import jax.numpy as jnp
from jax import lax
from jax.experimental import pallas as pl
from jax.experimental.pallas import tpu as pltpu
from jax.sharding import PartitionSpec as P

TILE = 16
TD = 8
CAP = 2
W = 7
CHUNK = 32
MASKED = -1e30
BF16 = jnp.bfloat16
F32 = jnp.float32


def permuted(block, route):
    return lax.ppermute(block, "node", route)


def column_limits(device, window, parents, lengths):
    cursor = parents[device * TD]
    need = [jnp.int32(0)] * (window + 1)
    for _ in range(W):
        owner = jnp.where(cursor < 0, -1, lax.div(jnp.maximum(cursor, 0), TD))
        distance = device - owner
        active = (owner >= 1) & (distance >= 1) & (distance <= W)
        depth = lax.rem(jnp.maximum(cursor, 0), TD) + 1
        for k in range(1, window + 1):
            need[k] = jnp.where(active & (distance == k), depth, need[k])
        cursor = jnp.where(active, parents[jnp.maximum(owner, 0) * TD], cursor)
    prompt = [jnp.where(device >= 1, lengths[t], 0) for t in range(TD)]
    behind = []
    for k in range(1, window + 1):
        owner = device - k
        seen = [(owner >= 1) & (c < need[k]) for c in range(CAP)]
        behind.append([jnp.where(seen[c], lengths[jnp.maximum(owner, 0) * TD + c], 0) for c in range(CAP)])
    return prompt, behind, [lengths[device * TD + t] for t in range(TD)]


def split_heads(block, heads_ref, start, count, heads_kv, wide):
    wide[: count * heads_kv] = block.astype(F32)
    for h in range(heads_kv):
        heads_ref[h, start : start + count] = wide[pl.ds(h, count, stride=heads_kv), :].astype(BF16)


def join_heads(blocks, count, heads_kv, wide):
    for h in range(heads_kv):
        wide[pl.ds(h, count, stride=heads_kv), :] = blocks[h]
    return wide[: count * heads_kv]


def load_kernel(order, heads_kv, *refs):
    sources, outs, scratch = refs[:4], refs[4:10], refs[10:]
    head, held, own_k, own_v, bias, weight = outs
    parents, lengths, keys, values, wide, arrived = scratch
    copies = [pltpu.make_async_copy(a, b, arrived.at[i]) for i, (a, b) in enumerate(zip(sources, scratch))]
    for copy in copies:
        copy.start()
    tokens = TD * TILE
    front = CAP * TILE * heads_kv
    device = lax.axis_index("node")
    for copy in copies:
        copy.wait()
    head[:front] = keys[:front]
    head[front:] = values[:front]
    held[...] = jnp.where(device == 0, keys[...], jnp.zeros_like(keys))
    split_heads(keys[...], own_k, 0, tokens, heads_kv, wide)
    split_heads(values[...], own_v, 0, tokens, heads_kv, wide)
    place = lax.broadcasted_iota(jnp.int32, (TILE, 128), 0)
    prompt, behind, own = column_limits(device, len(order), parents, lengths)
    even = lax.rem(device, 2) == 0
    limits = prompt
    for on_even, on_odd in order:
        limits = limits + [jnp.where(even, x, y) for x, y in zip(behind[on_even - 1], behind[on_odd - 1])]
    for t, limit in enumerate(limits + own):
        bias[t * TILE : (t + 1) * TILE] = jnp.where(place < limit, 0.0, MASKED)
    lane_place = lax.broadcasted_iota(jnp.int32, (8, 128), 1) // 8
    for t in range(TD):
        weight[:, t * 128 : (t + 1) * 128] = jnp.where(lane_place < lengths[device * TD + t], 1.0, 0.0)


def pack_kernel(heads_kv, q_ref, g_ref, qh, gh, blocks, arrived):
    tokens = TD * TILE
    copies = []
    for pair in range(heads_kv // 2):
        for ref, out in ((q_ref, qh), (g_ref, gh)):
            i = len(copies)
            copy = pltpu.make_async_copy(ref.at[:, pair * 16 : (pair + 1) * 16], blocks.at[i], arrived.at[i])
            copy.start()
            copies.append((copy, out, pair))
    for i, (copy, out, pair) in enumerate(copies):
        copy.wait()
        both = blocks[i].astype(F32)
        for part in range(2):
            out[2 * pair + part] = both[:, part * 8 : (part + 1) * 8].reshape(tokens * 8, 128).astype(BF16)


def causal_bias(columns):
    column_token = lax.broadcasted_iota(jnp.int32, (CHUNK, columns), 1) // 8
    return jnp.where(lax.broadcasted_iota(jnp.int32, (CHUNK, columns), 0) <= column_token, 0.0, MASKED)


def outer_product(rows, columns):
    return lax.dot_general(rows, columns, (((1,), (1,)), ((), ())), preferred_element_type=F32)


def early_kernel(fresh, sources, heads_kv, scale, *refs):
    own_k, own_v, qh, gh, bias = refs[:5]
    blocks, (kh, e_ref, dp_ref, stats, vh, wide) = refs[5:-6], refs[-6:]
    tokens = TD * TILE
    front = CAP * TILE
    behind = len(sources) * front
    start = tokens + fresh * front
    columns = CHUNK * 8
    for side, heads_ref, own in ((0, kh, own_k), (1, vh, own_v)):
        for k, (source, at) in enumerate(sources):
            at += side * front * heads_kv
            split_heads(blocks[source][at : at + front * heads_kv], heads_ref, k * front, front, heads_kv, wide)
        heads_ref[:, behind:] = own[...]
    causal = causal_bias(columns)
    for head in range(heads_kv):
        for c in range(tokens // CHUNK):
            rows = behind + (c + 1) * CHUNK
            span = slice(c * columns, (c + 1) * columns)
            s = outer_product(kh[head, :rows], qh[head, span])
            dp = outer_product(vh[head, :rows], gh[head, span])
            s = s + jnp.concatenate([bias[start : start + rows]] * (columns // 128), axis=1)
            s = jnp.concatenate([s[: rows - CHUNK], s[rows - CHUNK :] + causal], axis=0)
            top = jnp.max(s, axis=0, keepdims=True)
            e = jnp.exp2((s - top) * (scale * math.log2(math.e)))
            e_ref[head, :rows, span] = e
            dp_ref[head, :rows, span] = dp
            stats[head, 0:1, span] = top
            stats[head, 1:2, span] = jnp.sum(e, axis=0, keepdims=True)
            stats[head, 2:3, span] = jnp.sum(e * dp, axis=0, keepdims=True)


def probs_kernel(sources, heads_kv, scale, *refs):
    prompt_k, prompt_v, qh, gh, bias, weight_ref, stats, block_ref = refs[:8]
    send_ref, keep_ref, kh, ds_ref, p_behind, terms, vh, p_ref, grads, wide = refs[8:]
    tokens = TD * TILE
    front = CAP * TILE
    columns = 2 * CHUNK * 8
    rate = scale * math.log2(math.e)
    device = lax.axis_index("node")

    for side, heads_ref, prompt in ((0, kh, prompt_k), (1, vh, prompt_v)):
        split_heads(prompt[...], heads_ref, 0, tokens, heads_kv, wide)
        for k, (_, at) in enumerate(sources):
            at += side * front * heads_kv
            split_heads(block_ref[at : at + front * heads_kv], heads_ref, tokens + k * front, front, heads_kv, wide)

    for head in range(heads_kv):
        for c in range(tokens * 8 // columns):
            span = slice(c * columns, (c + 1) * columns)
            s = outer_product(kh[head], qh[head, span])
            dp = outer_product(vh[head], gh[head, span])
            s = s + jnp.concatenate([bias[: s.shape[0]]] * (columns // 128), axis=1)
            top_early = stats[head, 0:1, span]
            top = jnp.maximum(jnp.max(s, axis=0, keepdims=True), top_early)
            e = jnp.exp2((s - top) * rate)
            shrink = jnp.exp2((top_early - top) * rate)
            total = jnp.sum(e, axis=0, keepdims=True) + shrink * stats[head, 1:2, span]
            weight = weight_ref[:1, span] / total
            weight_early = weight * shrink
            p = e * weight
            delta = jnp.sum(p * dp, axis=0, keepdims=True) + weight_early * stats[head, 2:3, span]
            ds_ref[head, :, span] = (p * (dp - delta)).astype(BF16)
            p_ref[head % 2, :, span] = p[:tokens].astype(BF16)
            p_behind[head, :, span] = p[tokens:].astype(BF16)
            terms[head, 0:1, span] = weight_early
            terms[head, 1:2, span] = delta
        grads[0, head] = scale * jnp.dot(ds_ref[head, :tokens], qh[head], preferred_element_type=F32)
        grads[1, head] = jnp.dot(p_ref[head % 2], gh[head], preferred_element_type=F32)

    even = lax.rem(device, 2) == 0
    for side in range(2):
        dprompt = join_heads([grads[side, h] for h in range(heads_kv)], tokens, heads_kv, wide).astype(BF16)
        kept = even if side == 0 else jnp.logical_not(even)

        @pl.when(kept)
        def _():
            keep_ref[...] = dprompt

        @pl.when(jnp.logical_not(kept))
        def _():
            send_ref[...] = dprompt


def windows_kernel(targets, heads_kv, scale, *refs):
    qh, gh, ds_fresh, p_behind, e_ref, dp_ref, terms, send_ref, keep_ref, ds_ref, p_own, p_ref, grads, wide = refs
    front = CAP * TILE
    tokens = TD * TILE
    early = ds_ref.shape[1] - tokens
    columns = CHUNK * 8
    for head in range(heads_kv):
        for c in range(tokens // CHUNK):
            rows = early + (c + 1) * CHUNK
            span = slice(c * columns, (c + 1) * columns)
            p = e_ref[head, :rows, span] * terms[head, 0:1, span]
            ds_ref[head, :rows, span] = (p * (dp_ref[head, :rows, span] - terms[head, 1:2, span])).astype(BF16)
            p_ref[head % 2, :, span] = p[:early].astype(BF16)
            p_own[head, : rows - early, span] = p[early:].astype(BF16)
        ds = jnp.concatenate([ds_fresh[head, tokens:], ds_ref[head, :early]], axis=0)
        grads[0, head] = scale * jnp.dot(ds, qh[head], preferred_element_type=F32)
        p = jnp.concatenate([p_behind[head], p_ref[head % 2]], axis=0)
        grads[1, head] = jnp.dot(p, gh[head], preferred_element_type=F32)
    for side in range(2):
        for k, (target, start) in enumerate(targets):
            span = slice(k * front, (k + 1) * front)
            block = join_heads([grads[side, h, span] for h in range(heads_kv)], front, heads_kv, wide).astype(BF16)
            start += side * front * heads_kv
            (send_ref, keep_ref)[target][start : start + front * heads_kv] = block


def grads_kernel(heads_kv, scale, *refs):
    qh, gh, kh_fresh, kh_early, ds_fresh, ds_early, p_own, dq_ref, dk_ref, dv_ref, wide = refs
    tokens = TD * TILE
    kh = [jnp.concatenate([kh_fresh[h], kh_early[h]], axis=0) for h in range(heads_kv)]
    before = kh[0].shape[0] - tokens
    columns = CHUNK * 8
    dk = []
    dv = []
    for pair in range(heads_kv // 2):
        for c in range(tokens // CHUNK):
            rows = before + (c + 1) * CHUNK
            span = slice(c * columns, (c + 1) * columns)
            parts = []
            for head in (2 * pair, 2 * pair + 1):
                fresh = ds_fresh.shape[1]
                ds = jnp.concatenate([ds_fresh[head, :, span], ds_early[head, : rows - fresh, span]], axis=0)
                dq = lax.dot_general(kh[head][:rows], ds, (((0,), (0,)), ((), ())), preferred_element_type=F32)
                parts.append((scale * dq.T).reshape(CHUNK, 8, 128))
            dq_ref[c * CHUNK : (c + 1) * CHUNK, pair * 16 : (pair + 1) * 16] = jnp.concatenate(parts, axis=1).astype(BF16)
        for head in (2 * pair, 2 * pair + 1):
            for source, factor, out in ((ds_early.at[head, before - fresh :], qh, dk), (p_own.at[head], gh, dv)):
                pieces = []
                for c in range(tokens // CHUNK):
                    start = c * columns
                    pieces.append(
                        jnp.dot(
                            source[c * CHUNK : (c + 1) * CHUNK, start:], factor[head, start:], preferred_element_type=F32
                        )
                    )
                out.append(jnp.concatenate(pieces, axis=0))
    dk_ref[...] = scale * join_heads(dk, tokens, heads_kv, wide)
    dv_ref[...] = join_heads(dv, tokens, heads_kv, wide)


VMEM = pl.BlockSpec(memory_space=pltpu.VMEM)


HBM = pl.BlockSpec(memory_space=pltpu.HBM)


def call(kernel, name, operands, outputs, scratch, flops, transcendentals=0, place=VMEM):
    sizes = [a.size * a.dtype.itemsize for a in (*operands, *outputs)]
    if place is HBM:
        operands = [pltpu.with_memory_space_constraint(a, pltpu.HBM) for a in operands]
    return pl.pallas_call(
        kernel,
        in_specs=[place] * len(operands),
        out_specs=[VMEM] * len(outputs),
        out_shape=outputs,
        scratch_shapes=scratch,
        compiler_params=pltpu.CompilerParams(vmem_limit_bytes=16 * 1024 * 1024),
        cost_estimate=pl.CostEstimate(flops=flops, bytes_accessed=sum(sizes), transcendentals=transcendentals),
        name=name,
    )(*operands)


def load(order, keys, values, parents, lengths, tokens):
    rows, head_size = keys.shape
    heads_kv = rows // tokens
    array = jax.ShapeDtypeStruct
    return call(
        functools.partial(load_kernel, order, heads_kv),
        "load",
        (parents, lengths, keys, values),
        [array((2 * CAP * TILE * heads_kv, head_size), BF16), array((rows, head_size), BF16)]
        + [array((heads_kv, tokens, head_size), BF16)] * 2
        + [array((2 * tokens + len(order) * CAP * TILE, 128), F32), array((8, tokens * 8), F32)],
        [pltpu.SMEM(parents.shape, jnp.int32), pltpu.SMEM(lengths.shape, jnp.int32)]
        + [pltpu.VMEM((rows, head_size), BF16)] * 2
        + [pltpu.VMEM((rows, head_size), F32), pltpu.SemaphoreType.DMA((4,))],
        flops=1 << 20,
        place=HBM,
    )


def pack(queries, grad_out, heads_kv):
    tokens, heads_q, head_size = queries.shape
    array = jax.ShapeDtypeStruct
    return call(
        functools.partial(pack_kernel, heads_kv),
        "pack",
        (queries, grad_out),
        [array((heads_kv, tokens * 8, head_size), BF16)] * 2,
        [pltpu.VMEM((heads_kv, tokens, 16, head_size), BF16), pltpu.SemaphoreType.DMA((heads_kv,))],
        flops=1 << 20,
        place=HBM,
    )


def early(fresh, sources, qh, gh, own, blocks):
    own_k, own_v, bias, _ = own
    heads_kv, tokens, head_size = own_k.shape
    rows = len(sources) * CAP * TILE + tokens
    array = jax.ShapeDtypeStruct
    work = heads_kv * tokens * 8 * rows
    return call(
        functools.partial(early_kernel, fresh, sources, heads_kv, head_size**-0.5),
        "early",
        (own_k, own_v, qh, gh, bias, *blocks),
        [array((heads_kv, rows, head_size), BF16)]
        + [array((heads_kv, rows, tokens * 8), F32)] * 2
        + [array((heads_kv, 8, tokens * 8), F32)],
        [pltpu.VMEM((heads_kv, rows, head_size), BF16), pltpu.VMEM((CAP * TILE * heads_kv, head_size), F32)],
        flops=4 * work * head_size,
        transcendentals=work,
    )


def probs(sources, prompt_k, prompt_v, qh, gh, own, stats, block):
    _, own_v, bias, weight = own
    heads_kv, tokens, head_size = own_v.shape
    rows = tokens * heads_kv
    fresh = tokens + len(sources) * CAP * TILE
    array = jax.ShapeDtypeStruct
    work = heads_kv * tokens * 8 * fresh
    return call(
        functools.partial(probs_kernel, sources, heads_kv, head_size**-0.5),
        "probs",
        (prompt_k, prompt_v, qh, gh, bias, weight, stats, block),
        [array((rows, head_size), BF16)] * 2
        + [
            array((heads_kv, fresh, head_size), BF16),
            array((heads_kv, fresh, tokens * 8), BF16),
            array((heads_kv, fresh - tokens, tokens * 8), BF16),
            array((heads_kv, 8, tokens * 8), F32),
        ],
        [
            pltpu.VMEM((heads_kv, fresh, head_size), BF16),
            pltpu.VMEM((2, tokens, tokens * 8), BF16),
            pltpu.VMEM((2, heads_kv, tokens, head_size), F32),
            pltpu.VMEM((rows, head_size), F32),
        ],
        flops=8 * work * head_size,
        transcendentals=work,
    )


def windows(targets, qh, gh, ds_fresh, p_behind, e, dp, terms):
    heads_kv, early, columns = e.shape
    head_size = qh.shape[2]
    tokens = TD * TILE
    front = CAP * TILE * heads_kv
    behind = early - tokens + p_behind.shape[1]
    count = [sum(target == t for target, _ in targets) for t in (0, 1)]
    array = jax.ShapeDtypeStruct
    return call(
        functools.partial(windows_kernel, targets, heads_kv, head_size**-0.5),
        "windows",
        (qh, gh, ds_fresh, p_behind, e, dp, terms),
        [array((2 * front * n, head_size), BF16) for n in count]
        + [array((heads_kv, early, columns), BF16), array((heads_kv, tokens, columns), BF16)],
        [
            pltpu.VMEM((2, early - tokens, columns), BF16),
            pltpu.VMEM((2, heads_kv, behind, head_size), F32),
            pltpu.VMEM((front, head_size), F32),
        ],
        flops=4 * heads_kv * behind * columns * head_size,
    )


def grads(qh, gh, kh_fresh, kh_early, ds_fresh, ds_early, p_own):
    heads_kv, tokens, _ = p_own.shape
    head_size = kh_fresh.shape[2]
    array = jax.ShapeDtypeStruct
    return call(
        functools.partial(grads_kernel, heads_kv, head_size**-0.5),
        "grads",
        (qh, gh, kh_fresh, kh_early, ds_fresh, ds_early, p_own),
        [
            array((tokens, heads_kv * 8, head_size), BF16),
            array((tokens * heads_kv, head_size), F32),
            array((tokens * heads_kv, head_size), F32),
        ],
        [pltpu.VMEM((tokens * heads_kv, head_size), F32)],
        flops=2 * tokens * 8 * (ds_fresh.size + ds_early.size) // (tokens * 8) * head_size,
    )


def shift_route(distance, size):
    return [(i, i + distance) for i in range(size - distance)]


def back(route):
    return [(j, i) for i, j in route]


def added(*blocks):
    total = blocks[0].astype(F32)
    for block in blocks[1:]:
        total = total + block.astype(F32)
    return total


def after(array, *earlier):
    return lax.optimization_barrier((array, *earlier))[0]


def units(array, start, unit, count):
    return [array[start + i * unit : start + (i + 1) * unit] for i in range(count)]


def prompt_route(stride, size):
    return [(i + j, i + j + stride) for i in range(0, size, 2 * stride) for j in (0, 1)]


def collect(size, unit, rows, where, keys, values, head, held, queries, grad_out):
    even, lower, _ = where
    neighbours = [(i, i ^ 1) for i in range(size)]
    far_route = shift_route(4, size)[1:]
    near_route = shift_route(2, size)
    if size == W + 1:
        keys_far = permuted(keys, [(0, 4)])
        values_far = permuted(values, [(0, 5)])
        values_next = permuted(values, [(0, 1)])
        head, queries = lax.optimization_barrier((head, queries, keys_far))[:2]
        qh, gh = pack(queries, grad_out, keys.shape[0] // queries.shape[0])
        far = permuted(head, far_route)
        six = permuted(head, [(1, 7)])
        held = after(added(held, values_next, values_far, keys_far).astype(BF16), six, far, qh)
        second = permuted(jnp.concatenate([held, head]), near_route)
        crossed = jnp.where(even, jnp.concatenate([head, far]), jnp.concatenate([far, six]))
        crossed = permuted(crossed, neighbours)
        held = jnp.where(lower, held, second[:rows])
        third = permuted(after(jnp.concatenate([held, second[rows:]]), crossed), neighbours)
        early_sources = [(0, rows), (1, 0), (2, 0), (1, unit), (3, 0)]
        return held, third[:rows], third, [(0, rows)], early_sources, (second, crossed, far, six), (qh, gh)
    strides = [2**i for i in range(2, size.bit_length()) if 2**i < size]
    top = strides[-1]
    keys_far = permuted(keys, [(0, top)])
    values_far = permuted(values, [(0, top + 1)])
    values_next = permuted(values, [(0, 1)])
    far = permuted(head, far_route)
    held = added(held, values_next, values_far, keys_far).astype(BF16)
    for stride in reversed(strides[:-1]):
        held = added(held, permuted(held, prompt_route(stride, size))).astype(BF16)
    second = permuted(jnp.concatenate([held, head, far]), near_route)
    held = jnp.where(lower, held, second[:rows])
    near, six = units(second, rows, unit, 2)
    third = permuted(jnp.concatenate([head, near, far, six]), shift_route(1, size))
    other = permuted(held, neighbours)
    fresh_sources = [(0, i * unit) for i in range(4)]
    early_sources = [(0, rows), (1, 0), (0, rows + unit)]
    return held, other, third, fresh_sources, early_sources, (second, far), pack(queries, grad_out, keys.shape[0] // queries.shape[0])


def give_back(size, unit, where, prompt, behind, finish):
    even, lower, _ = where
    neighbours = [(i, i ^ 1) for i in range(size)]
    far_route = back(shift_route(4, size)[1:])
    send, keep = prompt
    rows = keep.shape[0]
    two, four, six = units(behind[1], 0, unit, 3)
    if size == W + 1:
        total = added(keep, permuted(send, neighbours)).astype(BF16)
        finished = finish(total)
        near, first, last = units(permuted(behind[0], neighbours), 0, unit, 3)
        none = jnp.zeros_like(first)
        parts = [permuted(total, [(j, 0), (j + 1, 1)]) for j in reversed(range(2, size, 2))]
        two = permuted(added(two, near).astype(BF16), back(shift_route(2, size)[1:]))
        four = after(added(four, jnp.where(even, last, first)).astype(BF16), finished[1])
        four = permuted(four, far_route)
        six = permuted(added(six, jnp.where(even, none, last)).astype(BF16), [(7, 1)])
        total = added(total, *parts).astype(BF16)
        mine = added(jnp.where(even, first, none), six, four, two)
        return finished, total, permuted(total, [(1, 0)]).astype(F32), mine
    strides = [2**i for i in range(2, size.bit_length()) if 2**i < size]
    top = strides[-1]
    zero, *third = units(permuted(behind[0], back(shift_route(1, size))), 0, unit, 4)
    total = added(keep, permuted(send, neighbours)).astype(BF16)
    two, four, six = (added(x, y).astype(BF16) for x, y in zip((two, four, six), third))
    second = permuted(jnp.concatenate([total, two, six]), back(shift_route(2, size)))
    four = added(four, second[rows + unit :])
    mine = added(zero, second[rows : rows + unit], permuted(four.astype(BF16), far_route))
    total = added(total, jnp.where(lower, second[:rows], jnp.zeros_like(total))).astype(BF16)
    for stride in strides[:-1]:
        total = added(total, permuted(total, back(prompt_route(stride, size)))).astype(BF16)
    keys_far = permuted(total, [(top, 0)])
    values_far = permuted(total, [(top + 1, 0)])
    values_next = permuted(total, [(1, 0)])
    return finish(send), added(total, keys_far), added(values_next, values_far), mine


def per_device(size, queries, keys, values, grad_out, parents, lengths):
    tokens, heads_kv, head_size = keys.shape
    rows = tokens * heads_kv
    one = CAP * TILE * heads_kv
    unit = 2 * one
    window = min(W, size - 2)
    device = lax.axis_index("node")
    keys = keys.reshape(rows, head_size)
    values = values.reshape(rows, head_size)

    if size == W + 1:
        order = [(1, 3), (2, 2), (3, 1), (4, 4), (5, 5), (6, 6)]
        targets = [(k % 2, k // 2 * unit) for k in range(window)]
    else:
        order = [(k, k) for k in (1, 3, 5, 7, 2, 4, 6)]
        targets = [(0, i * unit) for i in range(4)] + [(1, i * unit) for i in range(3)]
    head, held, *own = load(order, keys, values, parents, lengths, tokens)
    head, *where = lax.optimization_barrier((head, lax.rem(device, 2) == 0, lax.rem(device, 4) < 2, device == 0))
    even, _, root = where
    held, other, block, fresh_sources, early_sources, blocks, (qh, gh) = collect(
        size, unit, rows, where, keys, values, head, held, queries, grad_out
    )
    kh_early, e, dp, stats = early(len(fresh_sources), early_sources, qh, gh, own, blocks)
    prompt_k, prompt_v = jnp.where(even, held, other), jnp.where(even, other, held)
    *prompt, kh, ds, p_behind, terms = probs(fresh_sources, prompt_k, prompt_v, qh, gh, own, stats, block)
    *behind, ds_early, p_own = windows(targets, qh, gh, ds, p_behind, e, dp, terms)

    def finish(earlier):
        return grads(qh, gh, kh, kh_early, ds, ds_early, after(p_own, earlier))

    (grad_queries, dk, dv), prompt_k, prompt_v, mine = give_back(size, unit, where, prompt, behind, finish)
    own = []
    for side, local, prompt in ((0, dk, prompt_k), (1, dv, prompt_v)):
        whole = local + jnp.where(root, prompt.astype(F32), 0.0)
        own.append(whole.at[:one].add(mine[side * one : (side + 1) * one]).reshape(tokens, heads_kv, head_size))
    return grad_queries, own[0], own[1]


def solution(mesh):
    by_token = P(("leaf", "node"), "tensor", None)
    return jax.shard_map(
        functools.partial(per_device, mesh.shape["node"]),
        mesh=mesh,
        in_specs=(by_token, by_token, by_token, by_token, P("leaf"), P("leaf")),
        out_specs=(by_token, by_token, by_token),
        check_vma=False,
    )
```

```python
import functools
import math

import jax
import jax.numpy as jnp
from jax import lax
from jax.experimental import pallas as pl
from jax.experimental.pallas import tpu as pltpu
from jax.sharding import PartitionSpec as P

TILE = 16
TD = 8
CAP = 2
W = 7
CHUNK = 32
MASKED = -1e30
BF16 = jnp.bfloat16
F32 = jnp.float32


def permuted(block, route):
    return lax.ppermute(block, "node", route)


def column_limits(device, window, parents, lengths):
    cursor = parents[device * TD]
    need = [jnp.int32(0)] * (window + 1)
    for _ in range(W):
        owner = jnp.where(cursor < 0, -1, lax.div(jnp.maximum(cursor, 0), TD))
        distance = device - owner
        active = (owner >= 1) & (distance >= 1) & (distance <= W)
        depth = lax.rem(jnp.maximum(cursor, 0), TD) + 1
        for k in range(1, window + 1):
            need[k] = jnp.where(active & (distance == k), depth, need[k])
        cursor = jnp.where(active, parents[jnp.maximum(owner, 0) * TD], cursor)
    prompt = [jnp.where(device >= 1, lengths[t], 0) for t in range(TD)]
    behind = []
    for k in range(1, window + 1):
        owner = device - k
        seen = [(owner >= 1) & (c < need[k]) for c in range(CAP)]
        behind.append([jnp.where(seen[c], lengths[jnp.maximum(owner, 0) * TD + c], 0) for c in range(CAP)])
    return prompt, behind, [lengths[device * TD + t] for t in range(TD)]


def split_heads(block, heads_ref, start, count, heads_kv, wide):
    wide[: count * heads_kv] = block.astype(F32)
    for h in range(heads_kv):
        heads_ref[h, start : start + count] = wide[pl.ds(h, count, stride=heads_kv), :].astype(BF16)


def join_heads(blocks, count, heads_kv, wide):
    for h in range(heads_kv):
        wide[pl.ds(h, count, stride=heads_kv), :] = blocks[h]
    return wide[: count * heads_kv]


def load_kernel(order, heads_kv, *refs):
    sources, outs, scratch = refs[:4], refs[4:10], refs[10:]
    head, held, own_k, own_v, bias, weight = outs
    parents, lengths, keys, values, wide, arrived = scratch
    copies = [pltpu.make_async_copy(a, b, arrived.at[i]) for i, (a, b) in enumerate(zip(sources, scratch))]
    for copy in copies:
        copy.start()
    tokens = TD * TILE
    front = CAP * TILE * heads_kv
    device = lax.axis_index("node")
    for copy in copies:
        copy.wait()
    head[:front] = keys[:front]
    head[front:] = values[:front]
    held[...] = jnp.where(device == 0, keys[...], jnp.zeros_like(keys))
    split_heads(keys[...], own_k, 0, tokens, heads_kv, wide)
    split_heads(values[...], own_v, 0, tokens, heads_kv, wide)
    place = lax.broadcasted_iota(jnp.int32, (TILE, 128), 0)
    prompt, behind, own = column_limits(device, len(order), parents, lengths)
    even = lax.rem(device, 2) == 0
    limits = prompt
    for on_even, on_odd in order:
        limits = limits + [jnp.where(even, x, y) for x, y in zip(behind[on_even - 1], behind[on_odd - 1])]
    for t, limit in enumerate(limits + own):
        bias[t * TILE : (t + 1) * TILE] = jnp.where(place < limit, 0.0, MASKED)
    lane_place = lax.broadcasted_iota(jnp.int32, (8, 128), 1) // 8
    for t in range(TD):
        weight[:, t * 128 : (t + 1) * 128] = jnp.where(lane_place < lengths[device * TD + t], 1.0, 0.0)


def pack_kernel(heads_kv, q_ref, g_ref, qh, gh, blocks, arrived):
    tokens = TD * TILE
    copies = []
    for pair in range(heads_kv // 2):
        for ref, out in ((q_ref, qh), (g_ref, gh)):
            i = len(copies)
            copy = pltpu.make_async_copy(ref.at[:, pair * 16 : (pair + 1) * 16], blocks.at[i], arrived.at[i])
            copy.start()
            copies.append((copy, out, pair))
    for i, (copy, out, pair) in enumerate(copies):
        copy.wait()
        both = blocks[i].astype(F32)
        for part in range(2):
            out[2 * pair + part] = both[:, part * 8 : (part + 1) * 8].reshape(tokens * 8, 128).astype(BF16)


def causal_bias(columns):
    column_token = lax.broadcasted_iota(jnp.int32, (CHUNK, columns), 1) // 8
    return jnp.where(lax.broadcasted_iota(jnp.int32, (CHUNK, columns), 0) <= column_token, 0.0, MASKED)


def outer_product(rows, columns):
    return lax.dot_general(rows, columns, (((1,), (1,)), ((), ())), preferred_element_type=F32)


def early_kernel(fresh, sources, heads_kv, scale, *refs):
    own_k, own_v, qh, gh, bias = refs[:5]
    blocks, (kh, e_ref, dp_ref, stats, vh, wide) = refs[5:-6], refs[-6:]
    tokens = TD * TILE
    front = CAP * TILE
    behind = len(sources) * front
    start = tokens + fresh * front
    columns = CHUNK * 8
    for side, heads_ref, own in ((0, kh, own_k), (1, vh, own_v)):
        for k, (source, at) in enumerate(sources):
            at += side * front * heads_kv
            split_heads(blocks[source][at : at + front * heads_kv], heads_ref, k * front, front, heads_kv, wide)
        heads_ref[:, behind:] = own[...]
    causal = causal_bias(columns)
    for head in range(heads_kv):
        for c in range(tokens // CHUNK):
            rows = behind + (c + 1) * CHUNK
            span = slice(c * columns, (c + 1) * columns)
            s = outer_product(kh[head, :rows], qh[head, span])
            dp = outer_product(vh[head, :rows], gh[head, span])
            s = s + jnp.concatenate([bias[start : start + rows]] * (columns // 128), axis=1)
            s = jnp.concatenate([s[: rows - CHUNK], s[rows - CHUNK :] + causal], axis=0)
            top = jnp.max(s, axis=0, keepdims=True)
            e = jnp.exp2((s - top) * (scale * math.log2(math.e)))
            e_ref[head, :rows, span] = e
            dp_ref[head, :rows, span] = dp
            stats[head, 0:1, span] = top
            stats[head, 1:2, span] = jnp.sum(e, axis=0, keepdims=True)
            stats[head, 2:3, span] = jnp.sum(e * dp, axis=0, keepdims=True)


def probs_kernel(sources, heads_kv, scale, *refs):
    prompt_k, prompt_v, qh, gh, bias, weight_ref, stats, block_ref = refs[:8]
    send_ref, keep_ref, kh, ds_ref, p_behind, terms, vh, p_ref, grads, wide = refs[8:]
    tokens = TD * TILE
    front = CAP * TILE
    columns = TILE * 8
    rate = scale * math.log2(math.e)
    device = lax.axis_index("node")

    for side, heads_ref, prompt in ((0, kh, prompt_k), (1, vh, prompt_v)):
        split_heads(prompt[...], heads_ref, 0, tokens, heads_kv, wide)
        for k, (_, at) in enumerate(sources):
            at += side * front * heads_kv
            split_heads(block_ref[at : at + front * heads_kv], heads_ref, tokens + k * front, front, heads_kv, wide)

    for head in range(heads_kv):
        for c in range(tokens // TILE):
            span = slice(c * columns, (c + 1) * columns)
            s = outer_product(kh[head], qh[head, span])
            dp = outer_product(vh[head], gh[head, span])
            s = s + jnp.concatenate([bias[: s.shape[0]]] * (columns // 128), axis=1)
            top_early = stats[head, 0:1, span]
            top = jnp.maximum(jnp.max(s, axis=0, keepdims=True), top_early)
            e = jnp.exp2((s - top) * rate)
            shrink = jnp.exp2((top_early - top) * rate)
            total = jnp.sum(e, axis=0, keepdims=True) + shrink * stats[head, 1:2, span]
            weight = weight_ref[:1, span] / total
            weight_early = weight * shrink
            p = e * weight
            delta = jnp.sum(p * dp, axis=0, keepdims=True) + weight_early * stats[head, 2:3, span]
            ds_ref[head, :, span] = (p * (dp - delta)).astype(BF16)
            p_ref[head % 2, :, span] = p[:tokens].astype(BF16)
            p_behind[head, :, span] = p[tokens:].astype(BF16)
            terms[head, 0:1, span] = weight_early
            terms[head, 1:2, span] = delta
        grads[0, head] = scale * jnp.dot(ds_ref[head, :tokens], qh[head], preferred_element_type=F32)
        grads[1, head] = jnp.dot(p_ref[head % 2], gh[head], preferred_element_type=F32)

    even = lax.rem(device, 2) == 0
    for side in range(2):
        dprompt = join_heads([grads[side, h] for h in range(heads_kv)], tokens, heads_kv, wide).astype(BF16)
        kept = even if side == 0 else jnp.logical_not(even)

        @pl.when(kept)
        def _():
            keep_ref[...] = dprompt

        @pl.when(jnp.logical_not(kept))
        def _():
            send_ref[...] = dprompt


def windows_kernel(targets, heads_kv, scale, *refs):
    qh, gh, ds_fresh, p_behind, e_ref, dp_ref, terms, send_ref, keep_ref, ds_ref, p_own, p_ref, grads, wide = refs
    front = CAP * TILE
    tokens = TD * TILE
    early = ds_ref.shape[1] - tokens
    columns = CHUNK * 8
    for head in range(heads_kv):
        for c in range(tokens // CHUNK):
            rows = early + (c + 1) * CHUNK
            span = slice(c * columns, (c + 1) * columns)
            p = e_ref[head, :rows, span] * terms[head, 0:1, span]
            ds_ref[head, :rows, span] = (p * (dp_ref[head, :rows, span] - terms[head, 1:2, span])).astype(BF16)
            p_ref[head % 2, :, span] = p[:early].astype(BF16)
            p_own[head, : rows - early, span] = p[early:].astype(BF16)
        ds = jnp.concatenate([ds_fresh[head, tokens:], ds_ref[head, :early]], axis=0)
        grads[0, head] = scale * jnp.dot(ds, qh[head], preferred_element_type=F32)
        p = jnp.concatenate([p_behind[head], p_ref[head % 2]], axis=0)
        grads[1, head] = jnp.dot(p, gh[head], preferred_element_type=F32)
    for side in range(2):
        for k, (target, start) in enumerate(targets):
            span = slice(k * front, (k + 1) * front)
            block = join_heads([grads[side, h, span] for h in range(heads_kv)], front, heads_kv, wide).astype(BF16)
            start += side * front * heads_kv
            (send_ref, keep_ref)[target][start : start + front * heads_kv] = block


def grads_kernel(heads_kv, scale, *refs):
    qh, gh, kh_fresh, kh_early, ds_fresh, ds_early, p_own, dq_ref, dk_ref, dv_ref, wide = refs
    tokens = TD * TILE
    kh = [jnp.concatenate([kh_fresh[h], kh_early[h]], axis=0) for h in range(heads_kv)]
    before = kh[0].shape[0] - tokens
    columns = CHUNK * 8
    dk = []
    dv = []
    for pair in range(heads_kv // 2):
        for c in range(tokens // CHUNK):
            rows = before + (c + 1) * CHUNK
            span = slice(c * columns, (c + 1) * columns)
            parts = []
            for head in (2 * pair, 2 * pair + 1):
                fresh = ds_fresh.shape[1]
                ds = jnp.concatenate([ds_fresh[head, :, span], ds_early[head, : rows - fresh, span]], axis=0)
                dq = lax.dot_general(kh[head][:rows], ds, (((0,), (0,)), ((), ())), preferred_element_type=F32)
                parts.append((scale * dq.T).reshape(CHUNK, 8, 128))
            dq_ref[c * CHUNK : (c + 1) * CHUNK, pair * 16 : (pair + 1) * 16] = jnp.concatenate(parts, axis=1).astype(BF16)
        for head in (2 * pair, 2 * pair + 1):
            for source, factor, out in ((ds_early.at[head, before - fresh :], qh, dk), (p_own.at[head], gh, dv)):
                pieces = []
                for c in range(tokens // CHUNK):
                    start = c * columns
                    pieces.append(
                        jnp.dot(
                            source[c * CHUNK : (c + 1) * CHUNK, start:], factor[head, start:], preferred_element_type=F32
                        )
                    )
                out.append(jnp.concatenate(pieces, axis=0))
    dk_ref[...] = scale * join_heads(dk, tokens, heads_kv, wide)
    dv_ref[...] = join_heads(dv, tokens, heads_kv, wide)


VMEM = pl.BlockSpec(memory_space=pltpu.VMEM)


HBM = pl.BlockSpec(memory_space=pltpu.HBM)


def call(kernel, name, operands, outputs, scratch, flops, transcendentals=0, place=VMEM):
    sizes = [a.size * a.dtype.itemsize for a in (*operands, *outputs)]
    if place is HBM:
        operands = [pltpu.with_memory_space_constraint(a, pltpu.HBM) for a in operands]
    return pl.pallas_call(
        kernel,
        in_specs=[place] * len(operands),
        out_specs=[VMEM] * len(outputs),
        out_shape=outputs,
        scratch_shapes=scratch,
        compiler_params=pltpu.CompilerParams(vmem_limit_bytes=16 * 1024 * 1024),
        cost_estimate=pl.CostEstimate(flops=flops, bytes_accessed=sum(sizes), transcendentals=transcendentals),
        name=name,
    )(*operands)


def load(order, keys, values, parents, lengths, tokens):
    rows, head_size = keys.shape
    heads_kv = rows // tokens
    array = jax.ShapeDtypeStruct
    return call(
        functools.partial(load_kernel, order, heads_kv),
        "load",
        (parents, lengths, keys, values),
        [array((2 * CAP * TILE * heads_kv, head_size), BF16), array((rows, head_size), BF16)]
        + [array((heads_kv, tokens, head_size), BF16)] * 2
        + [array((2 * tokens + len(order) * CAP * TILE, 128), F32), array((8, tokens * 8), F32)],
        [pltpu.SMEM(parents.shape, jnp.int32), pltpu.SMEM(lengths.shape, jnp.int32)]
        + [pltpu.VMEM((rows, head_size), BF16)] * 2
        + [pltpu.VMEM((rows, head_size), F32), pltpu.SemaphoreType.DMA((4,))],
        flops=1 << 20,
        place=HBM,
    )


def pack(queries, grad_out, heads_kv):
    tokens, heads_q, head_size = queries.shape
    array = jax.ShapeDtypeStruct
    return call(
        functools.partial(pack_kernel, heads_kv),
        "pack",
        (queries, grad_out),
        [array((heads_kv, tokens * 8, head_size), BF16)] * 2,
        [pltpu.VMEM((heads_kv, tokens, 16, head_size), BF16), pltpu.SemaphoreType.DMA((heads_kv,))],
        flops=1 << 20,
        place=HBM,
    )


def early(fresh, sources, qh, gh, own, blocks):
    own_k, own_v, bias, _ = own
    heads_kv, tokens, head_size = own_k.shape
    rows = len(sources) * CAP * TILE + tokens
    array = jax.ShapeDtypeStruct
    work = heads_kv * tokens * 8 * rows
    return call(
        functools.partial(early_kernel, fresh, sources, heads_kv, head_size**-0.5),
        "early",
        (own_k, own_v, qh, gh, bias, *blocks),
        [array((heads_kv, rows, head_size), BF16)]
        + [array((heads_kv, rows, tokens * 8), F32)] * 2
        + [array((heads_kv, 8, tokens * 8), F32)],
        [pltpu.VMEM((heads_kv, rows, head_size), BF16), pltpu.VMEM((CAP * TILE * heads_kv, head_size), F32)],
        flops=4 * work * head_size,
        transcendentals=work,
    )


def probs(sources, prompt_k, prompt_v, qh, gh, own, stats, block):
    _, own_v, bias, weight = own
    heads_kv, tokens, head_size = own_v.shape
    rows = tokens * heads_kv
    fresh = tokens + len(sources) * CAP * TILE
    array = jax.ShapeDtypeStruct
    work = heads_kv * tokens * 8 * fresh
    return call(
        functools.partial(probs_kernel, sources, heads_kv, head_size**-0.5),
        "probs",
        (prompt_k, prompt_v, qh, gh, bias, weight, stats, block),
        [array((rows, head_size), BF16)] * 2
        + [
            array((heads_kv, fresh, head_size), BF16),
            array((heads_kv, fresh, tokens * 8), BF16),
            array((heads_kv, fresh - tokens, tokens * 8), BF16),
            array((heads_kv, 8, tokens * 8), F32),
        ],
        [
            pltpu.VMEM((heads_kv, fresh, head_size), BF16),
            pltpu.VMEM((2, tokens, tokens * 8), BF16),
            pltpu.VMEM((2, heads_kv, tokens, head_size), F32),
            pltpu.VMEM((rows, head_size), F32),
        ],
        flops=8 * work * head_size,
        transcendentals=work,
    )


def windows(targets, qh, gh, ds_fresh, p_behind, e, dp, terms):
    heads_kv, early, columns = e.shape
    head_size = qh.shape[2]
    tokens = TD * TILE
    front = CAP * TILE * heads_kv
    behind = early - tokens + p_behind.shape[1]
    count = [sum(target == t for target, _ in targets) for t in (0, 1)]
    array = jax.ShapeDtypeStruct
    return call(
        functools.partial(windows_kernel, targets, heads_kv, head_size**-0.5),
        "windows",
        (qh, gh, ds_fresh, p_behind, e, dp, terms),
        [array((2 * front * n, head_size), BF16) for n in count]
        + [array((heads_kv, early, columns), BF16), array((heads_kv, tokens, columns), BF16)],
        [
            pltpu.VMEM((2, early - tokens, columns), BF16),
            pltpu.VMEM((2, heads_kv, behind, head_size), F32),
            pltpu.VMEM((front, head_size), F32),
        ],
        flops=4 * heads_kv * behind * columns * head_size,
    )


def grads(qh, gh, kh_fresh, kh_early, ds_fresh, ds_early, p_own):
    heads_kv, tokens, _ = p_own.shape
    head_size = kh_fresh.shape[2]
    array = jax.ShapeDtypeStruct
    return call(
        functools.partial(grads_kernel, heads_kv, head_size**-0.5),
        "grads",
        (qh, gh, kh_fresh, kh_early, ds_fresh, ds_early, p_own),
        [
            array((tokens, heads_kv * 8, head_size), BF16),
            array((tokens * heads_kv, head_size), F32),
            array((tokens * heads_kv, head_size), F32),
        ],
        [pltpu.VMEM((tokens * heads_kv, head_size), F32)],
        flops=2 * tokens * 8 * (ds_fresh.size + ds_early.size) // (tokens * 8) * head_size,
    )


def shift_route(distance, size):
    return [(i, i + distance) for i in range(size - distance)]


def back(route):
    return [(j, i) for i, j in route]


def added(*blocks):
    total = blocks[0].astype(F32)
    for block in blocks[1:]:
        total = total + block.astype(F32)
    return total


def after(array, *earlier):
    return lax.optimization_barrier((array, *earlier))[0]


def units(array, start, unit, count):
    return [array[start + i * unit : start + (i + 1) * unit] for i in range(count)]


def prompt_route(stride, size):
    return [(i + j, i + j + stride) for i in range(0, size, 2 * stride) for j in (0, 1)]


def collect(size, unit, rows, where, keys, values, head, held, queries, grad_out):
    even, lower, _ = where
    neighbours = [(i, i ^ 1) for i in range(size)]
    far_route = shift_route(4, size)[1:]
    near_route = shift_route(2, size)
    if size == W + 1:
        keys_far = permuted(keys, [(0, 4)])
        values_far = permuted(values, [(0, 5)])
        values_next = permuted(values, [(0, 1)])
        head, queries = lax.optimization_barrier((head, queries, keys_far))[:2]
        qh, gh = pack(queries, grad_out, keys.shape[0] // queries.shape[0])
        far = permuted(head, far_route)
        six = permuted(head, [(1, 7)])
        held = after(added(held, values_next, values_far, keys_far).astype(BF16), six, far, qh)
        second = permuted(jnp.concatenate([held, head]), near_route)
        crossed = jnp.where(even, jnp.concatenate([head, far]), jnp.concatenate([far, six]))
        crossed = permuted(crossed, neighbours)
        held = jnp.where(lower, held, second[:rows])
        third = permuted(after(jnp.concatenate([held, second[rows:]]), crossed), neighbours)
        early_sources = [(0, rows), (1, 0), (2, 0), (1, unit), (3, 0)]
        return held, third[:rows], third, [(0, rows)], early_sources, (second, crossed, far, six), (qh, gh)
    strides = [2**i for i in range(2, size.bit_length()) if 2**i < size]
    top = strides[-1]
    keys_far = permuted(keys, [(0, top)])
    values_far = permuted(values, [(0, top + 1)])
    values_next = permuted(values, [(0, 1)])
    far = permuted(head, far_route)
    held = added(held, values_next, values_far, keys_far).astype(BF16)
    for stride in reversed(strides[:-1]):
        held = added(held, permuted(held, prompt_route(stride, size))).astype(BF16)
    second = permuted(jnp.concatenate([held, head, far]), near_route)
    held = jnp.where(lower, held, second[:rows])
    near, six = units(second, rows, unit, 2)
    third = permuted(jnp.concatenate([head, near, far, six]), shift_route(1, size))
    other = permuted(held, neighbours)
    fresh_sources = [(0, i * unit) for i in range(4)]
    early_sources = [(0, rows), (1, 0), (0, rows + unit)]
    return held, other, third, fresh_sources, early_sources, (second, far), pack(queries, grad_out, keys.shape[0] // queries.shape[0])


def give_back(size, unit, where, prompt, behind, finish):
    even, lower, _ = where
    neighbours = [(i, i ^ 1) for i in range(size)]
    far_route = back(shift_route(4, size)[1:])
    send, keep = prompt
    rows = keep.shape[0]
    two, four, six = units(behind[1], 0, unit, 3)
    if size == W + 1:
        total = added(keep, permuted(send, neighbours)).astype(BF16)
        finished = finish(total)
        near, first, last = units(permuted(behind[0], neighbours), 0, unit, 3)
        none = jnp.zeros_like(first)
        parts = [permuted(total, [(j, 0), (j + 1, 1)]) for j in reversed(range(2, size, 2))]
        two = permuted(added(two, near).astype(BF16), back(shift_route(2, size)[1:]))
        four = after(added(four, jnp.where(even, last, first)).astype(BF16), finished[1])
        four = permuted(four, far_route)
        six = permuted(added(six, jnp.where(even, none, last)).astype(BF16), [(7, 1)])
        total = added(total, *parts).astype(BF16)
        mine = added(jnp.where(even, first, none), six, four, two)
        return finished, total, permuted(total, [(1, 0)]).astype(F32), mine
    strides = [2**i for i in range(2, size.bit_length()) if 2**i < size]
    top = strides[-1]
    zero, *third = units(permuted(behind[0], back(shift_route(1, size))), 0, unit, 4)
    total = added(keep, permuted(send, neighbours)).astype(BF16)
    two, four, six = (added(x, y).astype(BF16) for x, y in zip((two, four, six), third))
    second = permuted(jnp.concatenate([total, two, six]), back(shift_route(2, size)))
    four = added(four, second[rows + unit :])
    mine = added(zero, second[rows : rows + unit], permuted(four.astype(BF16), far_route))
    total = added(total, jnp.where(lower, second[:rows], jnp.zeros_like(total))).astype(BF16)
    for stride in strides[:-1]:
        total = added(total, permuted(total, back(prompt_route(stride, size)))).astype(BF16)
    keys_far = permuted(total, [(top, 0)])
    values_far = permuted(total, [(top + 1, 0)])
    values_next = permuted(total, [(1, 0)])
    return finish(send), added(total, keys_far), added(values_next, values_far), mine


def per_device(size, queries, keys, values, grad_out, parents, lengths):
    tokens, heads_kv, head_size = keys.shape
    rows = tokens * heads_kv
    one = CAP * TILE * heads_kv
    unit = 2 * one
    window = min(W, size - 2)
    device = lax.axis_index("node")
    keys = keys.reshape(rows, head_size)
    values = values.reshape(rows, head_size)

    if size == W + 1:
        order = [(1, 3), (2, 2), (3, 1), (4, 4), (5, 5), (6, 6)]
        targets = [(k % 2, k // 2 * unit) for k in range(window)]
    else:
        order = [(k, k) for k in (1, 3, 5, 7, 2, 4, 6)]
        targets = [(0, i * unit) for i in range(4)] + [(1, i * unit) for i in range(3)]
    head, held, *own = load(order, keys, values, parents, lengths, tokens)
    head, *where = lax.optimization_barrier((head, lax.rem(device, 2) == 0, lax.rem(device, 4) < 2, device == 0))
    even, _, root = where
    held, other, block, fresh_sources, early_sources, blocks, (qh, gh) = collect(
        size, unit, rows, where, keys, values, head, held, queries, grad_out
    )
    kh_early, e, dp, stats = early(len(fresh_sources), early_sources, qh, gh, own, blocks)
    prompt_k, prompt_v = jnp.where(even, held, other), jnp.where(even, other, held)
    *prompt, kh, ds, p_behind, terms = probs(fresh_sources, prompt_k, prompt_v, qh, gh, own, stats, block)
    *behind, ds_early, p_own = windows(targets, qh, gh, ds, p_behind, e, dp, terms)

    def finish(earlier):
        return grads(qh, gh, kh, kh_early, ds, ds_early, after(p_own, earlier))

    (grad_queries, dk, dv), prompt_k, prompt_v, mine = give_back(size, unit, where, prompt, behind, finish)
    own = []
    for side, local, prompt in ((0, dk, prompt_k), (1, dv, prompt_v)):
        whole = local + jnp.where(root, prompt.astype(F32), 0.0)
        own.append(whole.at[:one].add(mine[side * one : (side + 1) * one]).reshape(tokens, heads_kv, head_size))
    return grad_queries, own[0], own[1]


def solution(mesh):
    by_token = P(("leaf", "node"), "tensor", None)
    return jax.shard_map(
        functools.partial(per_device, mesh.shape["node"]),
        mesh=mesh,
        in_specs=(by_token, by_token, by_token, by_token, P("leaf"), P("leaf")),
        out_specs=(by_token, by_token, by_token),
        check_vma=False,
    )
```
